32 devices in a mesh: dp: 16 (over z, y, core), tensor: 2 (over x).
Axes of the slice: x: 2, y: 2, z: 4, core: 2. Of those that a mesh axis runs over, the one named last changes fastest.
Arguments:
- tokens: bfloat16 [16384, 1024], P('dp'), may hold values from -6 to 6
- segments: int32 [16, 1024], P('dp'), may hold values from 0 to 3, never falling along the last dimension, each value on 1 to 800 neighbouring positions
- cotangent: bfloat16 [16384, 1024], P('dp'), may hold values from -6 to 6
- input_gain: bfloat16 [1024], replicated, may hold values from 0.5 to 1.5
- query_weight: bfloat16 [1024, 512], P(None, 'tensor'), may hold values from -0.1875 to 0.1875
- key_value_weight: bfloat16 [1024, 256], replicated, may hold values from -0.1875 to 0.1875
- attnout_weight: bfloat16 [512, 1024], P('tensor'), may hold values from -0.75 to 0.75
- gating_weight: bfloat16 [1024, 1536], P(None, 'tensor'), may hold values from -0.1875 to 0.1875
- inner_weight: bfloat16 [1024, 1536], P(None, 'tensor'), may hold values from -0.1875 to 0.1875
- state_weight: bfloat16 [1024, 256], replicated, may hold values from -0.1875 to 0.1875
- step_weight: bfloat16 [1024, 24], P(None, 'tensor'), may hold values from -0.1875 to 0.1875
- conv_inner: bfloat16 [4, 1536], P(None, 'tensor'), may hold values from -3 to 3
- conv_state: bfloat16 [4, 256], replicated, may hold values from -3 to 3
- inner_bias: bfloat16 [1536], P('tensor'), may hold values from -0.5 to 0.5
- state_bias: bfloat16 [256], replicated, may hold values from -0.5 to 0.5
- step_bias: bfloat16 [24], P('tensor'), may hold values from -5 to -1
- decay_log: bfloat16 [24], P('tensor'), may hold values from 0 to 2.765625
- skip_scale: bfloat16 [24], P('tensor'), may hold values from 0.5 to 1.5
- mixer_gain: bfloat16 [1536], P('tensor'), may hold values from 0.5 to 1.5
- mixer_out: bfloat16 [1536, 1024], P('tensor'), may hold values from -0.15625 to 0.15625
- post_gain: bfloat16 [1024], replicated, may hold values from 0.5 to 1.5
- gate_weight: bfloat16 [1024, 2048], P(None, 'tensor'), may hold values from -0.1875 to 0.1875
- up_weight: bfloat16 [1024, 2048], P(None, 'tensor'), may hold values from -0.1875 to 0.1875
- down_weight: bfloat16 [2048, 1024], P('tensor'), may hold values from -0.125 to 0.125
Outputs:
- tokens_grad: float32 [16384, 1024], P('dp')
- input_gain_grad: float32 [1024], replicated
- query_grad: float32 [1024, 512], P(None, 'tensor')
- keyval_grad: float32 [1024, 256], replicated
- attnout_grad: float32 [512, 1024], P('tensor')
- gating_grad: float32 [1024, 1536], P(None, 'tensor')
- inner_grad: float32 [1024, 1536], P(None, 'tensor')
- state_grad: float32 [1024, 256], replicated
- step_grad: float32 [1024, 24], P(None, 'tensor')
- conv_inner_grad: float32 [4, 1536], P(None, 'tensor')
- conv_state_grad: float32 [4, 256], replicated
- inner_bias_grad: float32 [1536], P('tensor')
- state_bias_grad: float32 [256], replicated
- step_bias_grad: float32 [24], P('tensor')
- decay_grad: float32 [24], P('tensor')
- skip_grad: float32 [24], P('tensor')
- mixer_gain_grad: float32 [1536], P('tensor')
- mixer_out_grad: float32 [1536, 1024], P('tensor')
- post_gain_grad: float32 [1024], replicated
- gate_grad: float32 [1024, 2048], P(None, 'tensor')
- up_grad: float32 [1024, 2048], P(None, 'tensor')
- down_grad: float32 [2048, 1024], P('tensor')
The draws below stay inside these ranges and needn't reach their ends.
Inputs may be any that keep to these rules, and one draw needn't show every extreme that they name: `segments`: within a sequence the numbers never fall; a document holds 1 to 1024 * 25 // 32 tokens and one holds exactly that many.
All inputs are finite; a program needn't handle non-finite values.
Results may differ from the reference program's by a relative error of at most 0.028.
Values may be sent and summed in bfloat16 or wider, within the bound.
No kernel may reach another device: no remote copies, remote signals or barrier semaphores. Data moves between devices by JAX's collectives and lax.ppermute only.
A program may use at most 192 MiB of HBM per device.

```python
import math
import jax
import jax.numpy as jnp
import numpy as np
from jax import lax

MODEL_WIDTH = 1024
QUERY_HEADS = 8
KEYVALUE_HEADS = 2
HEAD_SIZE = 64
NH = 24
P_SIZE = 64
NS = 128
KC = 4
FF = 2048
LEN = 1024
DSSM = 1536
SEQS = 16
TOKENS = 16384


def block_scale(stream_key, extent, cuts, smallest, top_value):
    def one(axis_at, parts):
        steps = jax.random.uniform(jax.random.fold_in(jax.random.fold_in(stream_key, 6), axis_at), (parts,), jnp.float32, smallest / len(cuts), top_value / len(cuts))
        return jnp.repeat(jnp.exp(steps), extent[axis_at] // parts).reshape((-1,) + (1,) * (len(extent) - axis_at - 1))

    factor_of = one(*cuts[0])
    for cut in cuts[1:]:
        factor_of = factor_of * one(*cut)
    return factor_of


def length_profile(amount, total, reach, lean):
    portions = [(1 << 20) // math.isqrt(rank ** lean) + 1 for rank in range(2, amount + 1)]
    surplus, given = total - reach - (amount - 1), [1] * (amount - 1)
    while surplus > 0:
        movable = [i for i in range(amount - 1) if given[i] < reach]
        whole, remaining = sum([portions[i] for i in movable]), surplus
        for i in movable:
            extra = min(reach - given[i], max(1, remaining * portions[i] // whole), surplus)
            given[i] = given[i] + extra
            surplus = surplus - extra
    return np.array([reach] + given)


def ragged_sizes(own_key, count, total, bound, slope):
    if count == 2:
        one = jax.random.randint(own_key, (), max(1, total - bound), min(bound, total - 1) + 1)
        return jnp.stack([one, total - one])
    lengths = jnp.asarray(length_profile(count, total, bound, slope), jnp.int32)
    twos = (count - 1) // 2
    source_of, taker = lengths[1:1 + 2 * twos:2], lengths[2:2 + 2 * twos:2]
    margin = jnp.minimum(source_of - 1, bound - taker)
    moved = jax.random.randint(jax.random.fold_in(own_key, 1), (twos,), 0, 1 << 20) % (margin + 1)
    lengths = lengths.at[1:1 + 2 * twos:2].set(source_of - moved).at[2:2 + 2 * twos:2].set(taker + moved)
    return lengths[jax.random.permutation(jax.random.fold_in(own_key, 2), count)]


def centred(own_key, extent, scale, most, split=(), held_as=jnp.bfloat16):
    array = scale * jax.random.normal(own_key, extent, jnp.float32)
    if split:
        array = array * block_scale(own_key, extent, split, -0.22, 0.18)
    return jnp.clip(array, -most, most).astype(held_as)


def setup_inputs(seed: int = 0) -> dict:
    arg_keys = jax.random.split(jax.random.key(seed), 25)
    return {
        "tokens": centred(arg_keys[0], (TOKENS, MODEL_WIDTH), 1.0, 6.0, ((0, 16),)),
        "segments": jax.vmap(lambda own: jnp.searchsorted(jnp.cumsum(ragged_sizes(own, 4, LEN, LEN * 25 // 32, 0)), jnp.arange(LEN), side="right"))(jax.random.split(arg_keys[1], SEQS)).reshape((SEQS, LEN)).astype(jnp.int32),
        "cotangent": centred(arg_keys[2], (TOKENS, MODEL_WIDTH), 1.0, 6.0, ((0, 16),)),
        "input_gain": jnp.clip(1.0 + 0.1 * jax.random.normal(arg_keys[3], (MODEL_WIDTH,), jnp.float32), 0.5, 1.5).astype(jnp.bfloat16),
        "query_weight": centred(arg_keys[4], (MODEL_WIDTH, QUERY_HEADS * HEAD_SIZE), MODEL_WIDTH ** -0.5, 0.1875, ((1, 2),)),
        "key_value_weight": centred(arg_keys[5], (MODEL_WIDTH, 2 * KEYVALUE_HEADS * HEAD_SIZE), MODEL_WIDTH ** -0.5, 0.1875),
        "attnout_weight": centred(arg_keys[6], (QUERY_HEADS * HEAD_SIZE, MODEL_WIDTH), HEAD_SIZE ** -0.5, 0.75, ((0, 2),)),
        "gating_weight": centred(arg_keys[7], (MODEL_WIDTH, DSSM), MODEL_WIDTH ** -0.5, 0.1875, ((1, 2),)),
        "inner_weight": centred(arg_keys[8], (MODEL_WIDTH, DSSM), MODEL_WIDTH ** -0.5, 0.1875, ((1, 2),)),
        "state_weight": centred(arg_keys[9], (MODEL_WIDTH, 2 * NS), MODEL_WIDTH ** -0.5, 0.1875),
        "step_weight": centred(arg_keys[10], (MODEL_WIDTH, NH), MODEL_WIDTH ** -0.5, 0.1875, ((1, 2),)),
        "conv_inner": centred(arg_keys[11], (KC, DSSM), KC ** -0.5, 3.0, ((1, 2),)),
        "conv_state": centred(arg_keys[12], (KC, 2 * NS), KC ** -0.5, 3.0),
        "inner_bias": jnp.clip(jax.random.uniform(arg_keys[13], (DSSM,), jnp.float32, -0.5, 0.5) * block_scale(arg_keys[13], (DSSM,), ((0, 2),), -0.4, 0.0), -0.5, 0.5).astype(jnp.bfloat16),
        "state_bias": jnp.clip(jax.random.uniform(arg_keys[14], (2 * NS,), jnp.float32, -0.5, 0.5), -0.5, 0.5).astype(jnp.bfloat16),
        "step_bias": jnp.clip(-5.0 + 4.0 * jax.random.uniform(arg_keys[15], (NH,), jnp.float32) ** block_scale(arg_keys[15], (NH,), ((0, 2),), -0.2, 0.2), -5.0, -1.0).astype(jnp.bfloat16),
        "decay_log": jnp.clip(2.765625 * jax.random.uniform(arg_keys[16], (NH,), jnp.float32) ** block_scale(arg_keys[16], (NH,), ((0, 2),), -0.2, 0.2), 0.0, 2.765625).astype(jnp.bfloat16),
        "skip_scale": jnp.clip(0.5 + 1.0 * jax.random.uniform(arg_keys[17], (NH,), jnp.float32) ** block_scale(arg_keys[17], (NH,), ((0, 2),), -0.2, 0.2), 0.5, 1.5).astype(jnp.bfloat16),
        "mixer_gain": jnp.clip(1.0 + 0.1 * jax.random.normal(arg_keys[18], (DSSM,), jnp.float32), 0.5, 1.5).astype(jnp.bfloat16),
        "mixer_out": centred(arg_keys[19], (DSSM, MODEL_WIDTH), DSSM ** -0.5, 0.15625, ((0, 2),)),
        "post_gain": jnp.clip(1.0 + 0.1 * jax.random.normal(arg_keys[20], (MODEL_WIDTH,), jnp.float32), 0.5, 1.5).astype(jnp.bfloat16),
        "gate_weight": centred(arg_keys[21], (MODEL_WIDTH, FF), MODEL_WIDTH ** -0.5, 0.1875, ((1, 2),)),
        "up_weight": centred(arg_keys[22], (MODEL_WIDTH, FF), MODEL_WIDTH ** -0.5, 0.1875, ((1, 2),)),
        "down_weight": centred(arg_keys[23], (FF, MODEL_WIDTH), FF ** -0.5, 0.125, ((0, 2),)),
    }


EPS = 1e-05
ROPE_BASE = 100000000000.0
NEG_FILL = -1e+30
HIGH = lax.Precision.HIGHEST

@jax.custom_vjp
def low(v):
    return lax.optimization_barrier(v.astype(jnp.bfloat16)).astype(jnp.float32)

@jax.custom_vjp
def low_back(v):
    return v

def low_keep(v):
    return (low(v), None)

def low_pass(kept, grad):
    return (grad,)

def back_keep(v):
    return (v, None)

def back_low(kept, grad):
    return (low(grad),)
low.defvjp(low_keep, low_pass)
low_back.defvjp(back_keep, back_low)

def matmul(left, right):
    return jnp.dot(left, right, precision=HIGH, preferred_element_type=jnp.float32)

def rms_norm(value, gain):
    return value * lax.rsqrt(lax.optimization_barrier(jnp.mean(value * value, axis=-1, keepdims=True)) + EPS) * gain

def rotary_tables(document_length):
    half = HEAD_SIZE // 2
    freqs = jnp.exp(-jnp.log(ROPE_BASE) * (2.0 * jnp.arange(half, dtype=jnp.float32) / HEAD_SIZE))
    angles = jnp.arange(document_length, dtype=jnp.float32)[:, None] * freqs[None, :]
    return (jnp.cos(angles), jnp.sin(angles))

def rotate(value, cosine, sine):
    half = value.shape[-1] // 2
    first = value[..., :half]
    second = value[..., half:]
    return jnp.concatenate([first * cosine - second * sine, first * sine + second * cosine], -1)

def shifted(value, seg_ids, offset):
    document_length = value.shape[0]
    moved = jnp.pad(value, ((offset, 0), (0, 0)))[:document_length]
    seg_moved = jnp.pad(seg_ids, (offset, 0), constant_values=-1)[:document_length]
    keep = (seg_moved == seg_ids).astype(jnp.float32)
    return moved * keep[:, None]

def causal_conv(value, kernel, bias, seg_ids):
    total = bias[None, :] + jnp.zeros_like(value)
    for tap in range(KC):
        total = total + kernel[tap][None, :] * shifted(value, seg_ids, KC - 1 - tap)
    return total

def forward_seq(params, seq_in, seg_ids):
    input_gain, query_weight, key_value_weight, attnout_weight, gating_weight, inner_weight, state_weight, step_weight, conv_inner, conv_state, inner_bias, state_bias, step_bias, decay_log, skip_scale, mixer_gain, mixer_out, post_gain, gate_weight, up_weight, down_weight = params
    document_length = seq_in.shape[0]
    normed = low(rms_norm(seq_in, input_gain))
    cosine, sine = rotary_tables(document_length)
    positions = jnp.arange(document_length)
    allowed = (positions[:, None] >= positions[None, :]) & (seg_ids[:, None] == seg_ids[None, :])
    queries = matmul(normed, query_weight).reshape(document_length, QUERY_HEADS, HEAD_SIZE).transpose(1, 0, 2)
    key_value_rows = matmul(normed, key_value_weight)
    key_rows = key_value_rows[:, :KEYVALUE_HEADS * HEAD_SIZE].reshape(document_length, KEYVALUE_HEADS, HEAD_SIZE).transpose(1, 0, 2)
    value_rows = key_value_rows[:, KEYVALUE_HEADS * HEAD_SIZE:].reshape(document_length, KEYVALUE_HEADS, HEAD_SIZE).transpose(1, 0, 2)
    query_group = QUERY_HEADS // KEYVALUE_HEADS
    key_rows = jnp.repeat(key_rows, query_group, axis=0)
    value_rows = jnp.repeat(value_rows, query_group, axis=0)
    queries = low(rotate(low_back(queries), cosine, sine))
    key_rows = low(rotate(low_back(key_rows), cosine, sine))
    value_rows = low_back(low(value_rows))
    scores = jnp.einsum('htd,hsd->hts', queries, key_rows, precision=HIGH) * HEAD_SIZE ** (-0.5)
    scores = low_back(jnp.where(allowed[None], scores, NEG_FILL))
    top = lax.optimization_barrier(jnp.max(scores, -1, keepdims=True))
    weights = jnp.exp(scores - top)
    probs = weights / lax.optimization_barrier(jnp.sum(weights, -1, keepdims=True))
    attended = jnp.einsum('hts,hsd->htd', low(probs), value_rows, precision=HIGH)
    attended = low_back(low(attended)).transpose(1, 0, 2).reshape(document_length, QUERY_HEADS * HEAD_SIZE)
    attn_part = matmul(attended, attnout_weight)
    gating = low_back(matmul(normed, gating_weight))
    inner = low_back(matmul(normed, inner_weight))
    state_in = low_back(matmul(normed, state_weight))
    step_raw = low_back(matmul(normed, step_weight))
    inner_act = jax.nn.silu(causal_conv(inner, conv_inner, inner_bias, seg_ids))
    state_act = jax.nn.silu(causal_conv(state_in, conv_state, state_bias, seg_ids))
    coef_b = low(state_act[:, :NS])
    coef_c = low(state_act[:, NS:])
    coupling = matmul(coef_c, coef_b.T)
    step = jax.nn.softplus(step_raw + step_bias)
    rate = -jnp.exp(decay_log)
    cumulative = jnp.cumsum(step * rate[None, :], axis=0).T
    difference = cumulative[:, :, None] - cumulative[:, None, :]
    decay = jnp.where(allowed[None], jnp.exp(jnp.where(allowed[None], difference, 0.0)), 0.0)
    mixing = low(low_back(jnp.broadcast_to(coupling, (NH, document_length, document_length))) * decay)
    heads_in = inner_act.reshape(document_length, NH, P_SIZE).transpose(1, 0, 2)
    driven = low(heads_in * step.T[:, :, None])
    core = low_back(jnp.einsum('hts,hsp->htp', mixing, driven, precision=HIGH))
    ssm_out = core + skip_scale[:, None, None] * heads_in
    ssm_out = ssm_out.transpose(1, 0, 2).reshape(document_length, NH * P_SIZE)
    gated = ssm_out * jax.nn.silu(gating)
    mixed = low(rms_norm(gated, mixer_gain))
    mamba_part = matmul(mixed, mixer_out)
    branch = low_back(attn_part + mamba_part)
    middle = seq_in + branch
    post = low(rms_norm(middle, post_gain))
    gate = low_back(matmul(post, gate_weight))
    upward = low_back(matmul(post, up_weight))
    hidden = low(jax.nn.silu(gate) * upward)
    return middle + matmul(hidden, down_weight)

def reference(tokens, segments, cotangent, input_gain, query_weight, key_value_weight, attnout_weight, gating_weight, inner_weight, state_weight, step_weight, conv_inner, conv_state, inner_bias, state_bias, step_bias, decay_log, skip_scale, mixer_gain, mixer_out, post_gain, gate_weight, up_weight, down_weight):
    params = tuple((weight.astype(jnp.float32) for weight in (input_gain, query_weight, key_value_weight, attnout_weight, gating_weight, inner_weight, state_weight, step_weight, conv_inner, conv_state, inner_bias, state_bias, step_bias, decay_log, skip_scale, mixer_gain, mixer_out, post_gain, gate_weight, up_weight, down_weight)))
    seq_tokens = tokens.astype(jnp.float32).reshape(SEQS, LEN, MODEL_WIDTH)
    seq_cots = cotangent.astype(jnp.float32).reshape(SEQS, LEN, MODEL_WIDTH)

    def step_fn(totals, seq_item):
        seq_in, seg_ids, seq_cot = seq_item
        _, pull = jax.vjp(lambda weights_all, value: forward_seq(weights_all, value, seg_ids), params, seq_in)
        grads_par, grad_in = pull(seq_cot)
        return (jax.tree.map(lambda left, right: left + right, totals, grads_par), grad_in)
    zeros = jax.tree.map(jnp.zeros_like, params)
    totals, grads_in = lax.scan(step_fn, zeros, (seq_tokens, segments, seq_cots))
    return (grads_in.reshape(TOKENS, MODEL_WIDTH), totals[0], totals[1], totals[2], totals[3], totals[4], totals[5], totals[6], totals[7], totals[8], totals[9], totals[10], totals[11], totals[12], totals[13], totals[14], totals[15], totals[16], totals[17], totals[18], totals[19], totals[20])
```

```python
import jax
import jax.numpy as jnp
from jax import lax
from jax.sharding import PartitionSpec as P

QUERY_HEADS = 8
KEYVALUE_HEADS = 2
HEAD_SIZE = 64
P_SIZE = 64
NS = 128
DSSM = 1536


EPS = 1e-05
ROPE_BASE = 100000000000.0
NEG_FILL = -1e30


def matmul(left, right):
    return jnp.dot(left, right, preferred_element_type=jnp.float32)


def rotary_tables(document_length):
    half = HEAD_SIZE // 2
    freqs = jnp.exp(-jnp.log(ROPE_BASE) * (2.0 * jnp.arange(half, dtype=jnp.float32) / HEAD_SIZE))
    angles = jnp.arange(document_length, dtype=jnp.float32)[:, None] * freqs[None, :]
    return (jnp.cos(angles), jnp.sin(angles))


def rotate(value, cosine, sine):
    half = value.shape[-1] // 2
    first = value[..., :half]
    second = value[..., half:]
    return jnp.concatenate([first * cosine - second * sine, first * sine + second * cosine], -1)


def rotate_back(grad, cosine, sine):
    half = grad.shape[-1] // 2
    first = grad[..., :half]
    second = grad[..., half:]
    return jnp.concatenate([first * cosine + second * sine, second * cosine - first * sine], -1)


def silu_slope(value):
    sigma = jax.nn.sigmoid(value)
    return sigma * (1.0 + value * (1.0 - sigma))


def seg_keep(segments, offset):
    document_length = segments.shape[1]
    moved = jnp.pad(segments, ((0, 0), (offset, 0)), constant_values=-1)[:, :document_length]
    return (moved == segments).astype(jnp.float32)[:, :, None]


def move_down(value, offset):
    document_length = value.shape[1]
    return jnp.pad(value, ((0, 0), (offset, 0), (0, 0)))[:, :document_length]


def move_up(value, offset):
    return jnp.pad(value, ((0, 0), (0, offset), (0, 0)))[:, offset:]


def conv_forward(value, kernel, bias, segments):
    taps = kernel.shape[0]
    total = jnp.zeros_like(value) + bias.astype(jnp.float32)
    for tap in range(taps):
        offset = taps - 1 - tap
        total = total + kernel[tap].astype(jnp.float32) * move_down(value, offset) * seg_keep(
            segments, offset
        )
    return total


def conv_backward(grad, value, kernel, segments):
    taps = kernel.shape[0]
    grad_in = jnp.zeros_like(value)
    kernel_rows = []
    for tap in range(taps):
        offset = taps - 1 - tap
        masked = grad * seg_keep(segments, offset)
        kernel_rows.append(jnp.sum(masked * move_down(value, offset), axis=(0, 1)))
        grad_in = grad_in + kernel[tap].astype(jnp.float32) * move_up(masked, offset)
    return (grad_in, jnp.stack(kernel_rows))


def ssd_parts(step_block, rate, coef_b, coef_c, heads_block, allowed):
    coupling = jnp.einsum("tn,sn->ts", coef_c, coef_b, preferred_element_type=jnp.float32)
    cumulative = jnp.cumsum(step_block * rate, axis=0).T
    difference = cumulative[:, :, None] - cumulative[:, None, :]
    decay = jnp.where(allowed[None], jnp.exp(jnp.where(allowed[None], difference, 0.0)), 0.0)
    mixing = (coupling[None] * decay).astype(jnp.bfloat16)
    driven = (heads_block * step_block.T[:, :, None]).astype(jnp.bfloat16)
    return (coupling, decay, mixing, driven)


def pair_sum(value):
    if lax.axis_size("tensor") == 2:
        other = lax.ppermute(value, "tensor", [(0, 1), (1, 0)])
        return value.astype(jnp.float32) + other.astype(jnp.float32)
    return lax.psum(value, "tensor").astype(jnp.float32)


def swap_bit(value, bit):
    size = lax.axis_size("dp")
    return lax.ppermute(value, "dp", [(i, i ^ bit) for i in range(size)])


def shared_sum(rows, first_shared):
    tail = pair_sum(rows[:, first_shared:]).astype(rows.dtype)
    return jnp.concatenate([rows[:, :first_shared], tail], 1) if first_shared else tail


def tree_sum(value, first_shared=None):
    size = lax.axis_size("dp")
    rows = value.shape[0]
    if size & (size - 1) or rows % (16 * size):
        total = lax.psum(value, "dp")
        return total if first_shared is None else shared_sum(total, first_shared)
    bits = [1 << i for i in range(size.bit_length() - 1)]
    me = lax.axis_index("dp")
    for bit in bits:
        half = value.shape[0] // 2
        low, high = value[:half], value[half:]
        upper = (me & bit) != 0
        got = swap_bit(jnp.where(upper, low, high), bit)
        kept = jnp.where(upper, high, low)
        value = (kept.astype(jnp.float32) + got.astype(jnp.float32)).astype(value.dtype)
    if first_shared is not None:
        value = shared_sum(value, first_shared)
    for bit in reversed(bits):
        upper = (me & bit) != 0
        got = swap_bit(value, bit)
        value = jnp.where(
            upper, jnp.concatenate([got, value], 0), jnp.concatenate([value, got], 0)
        )
    return value


def local(
    tokens,
    segments,
    cotangent,
    input_gain,
    query_weight,
    key_value_weight,
    attnout_weight,
    gating_weight,
    inner_weight,
    state_weight,
    step_weight,
    conv_inner,
    conv_state,
    inner_bias,
    state_bias,
    step_bias,
    decay_log,
    skip_scale,
    mixer_gain,
    mixer_out,
    post_gain,
    gate_weight,
    up_weight,
    down_weight,
):
    seq_count, document_length = segments.shape
    rows = seq_count * document_length
    heads = query_weight.shape[1] // HEAD_SIZE
    ssm_heads = step_weight.shape[1]
    query_group = QUERY_HEADS // KEYVALUE_HEADS
    shared_key_head = lax.axis_index("tensor") * heads // query_group
    scale = HEAD_SIZE ** (-0.5)
    cosine, sine = rotary_tables(document_length)
    positions = jnp.arange(document_length)

    def allowed_of(seg_ids):
        return (positions[:, None] >= positions[None, :]) & (seg_ids[:, None] == seg_ids[None, :])

    inputs = tokens.astype(jnp.float32)
    inv_first = lax.rsqrt(jnp.mean(inputs * inputs, -1, keepdims=True) + EPS)
    unit_first = inputs * inv_first
    in_gain = input_gain.astype(jnp.float32)
    normed = (unit_first * in_gain).astype(jnp.bfloat16)
    key_cols = lax.dynamic_slice_in_dim(key_value_weight, shared_key_head * HEAD_SIZE, HEAD_SIZE, 1)
    value_columns = lax.dynamic_slice_in_dim(
        key_value_weight, (KEYVALUE_HEADS + shared_key_head) * HEAD_SIZE, HEAD_SIZE, 1
    )
    query_pre = matmul(normed, query_weight)
    key_pre = matmul(normed, key_cols)
    value_pre = matmul(normed, value_columns)
    queries = rotate(
        query_pre.reshape(seq_count, document_length, heads, HEAD_SIZE).transpose(0, 2, 1, 3),
        cosine,
        sine,
    ).astype(jnp.bfloat16)
    key_rows = rotate(key_pre.reshape(seq_count, document_length, HEAD_SIZE), cosine, sine).astype(
        jnp.bfloat16
    )
    value_rows = value_pre.reshape(seq_count, document_length, HEAD_SIZE).astype(jnp.bfloat16)

    def attend(seq_item):
        query_block, key_block, value_block, seg_ids = seq_item
        allowed = allowed_of(seg_ids)[None]
        scores = (
            jnp.einsum("htd,sd->hts", query_block, key_block, preferred_element_type=jnp.float32)
            * scale
        )
        scores = jnp.where(allowed, scores, NEG_FILL)
        top = jnp.max(scores, -1, keepdims=True)
        weights = jnp.exp(scores - top)
        total = jnp.sum(weights, -1, keepdims=True)
        probs = (weights / total).astype(jnp.bfloat16)
        attended = jnp.einsum("hts,sd->htd", probs, value_block, preferred_element_type=jnp.float32)
        return (attended.astype(jnp.bfloat16), (top + jnp.log(total))[..., 0])

    attended, logsum = lax.map(attend, (queries, key_rows, value_rows, segments))
    attn_flat = attended.transpose(0, 2, 1, 3).reshape(rows, heads * HEAD_SIZE)
    attn_part = matmul(attn_flat, attnout_weight)
    gating = matmul(normed, gating_weight)
    inner = matmul(normed, inner_weight).reshape(seq_count, document_length, -1)
    state_in = matmul(normed, state_weight).reshape(seq_count, document_length, -1)
    step_raw = matmul(normed, step_weight)
    inner_pre = conv_forward(inner, conv_inner, inner_bias, segments)
    inner_act = jax.nn.silu(inner_pre)
    state_pre = conv_forward(state_in, conv_state, state_bias, segments)
    state_act = jax.nn.silu(state_pre)
    coef_b = state_act[..., :NS].astype(jnp.bfloat16)
    coef_c = state_act[..., NS:].astype(jnp.bfloat16)
    step_arg = step_raw.reshape(seq_count, document_length, ssm_heads) + step_bias.astype(
        jnp.float32
    )
    step = jax.nn.softplus(step_arg)
    rate = -jnp.exp(decay_log.astype(jnp.float32))
    heads_in = inner_act.reshape(seq_count, document_length, ssm_heads, P_SIZE).transpose(
        0, 2, 1, 3
    )

    def scan_forward(seq_item):
        step_block, coef_b_block, coef_c_block, heads_block, seg_ids = seq_item
        parts = ssd_parts(
            step_block, rate, coef_b_block, coef_c_block, heads_block, allowed_of(seg_ids)
        )
        return jnp.einsum("hts,hsp->htp", parts[2], parts[3], preferred_element_type=jnp.float32)

    core = lax.map(scan_forward, (step, coef_b, coef_c, heads_in, segments))
    skip = skip_scale.astype(jnp.float32)[None, :, None, None]
    ssm_out = (core + skip * heads_in).transpose(0, 2, 1, 3).reshape(rows, ssm_heads * P_SIZE)
    sigma_gate = jax.nn.sigmoid(gating)
    gate_act = gating * sigma_gate
    gated = ssm_out * gate_act
    square_sum = pair_sum(jnp.sum(gated * gated, -1))[:, None]
    inv_gate = lax.rsqrt(square_sum / DSSM + EPS)
    mixer_scale = mixer_gain.astype(jnp.float32)
    mixed = (gated * inv_gate * mixer_scale).astype(jnp.bfloat16)
    branch_part = attn_part + matmul(mixed, mixer_out)
    out_gain = post_gain.astype(jnp.float32)
    branch = pair_sum(branch_part.astype(jnp.bfloat16))
    middle = inputs + branch
    inv_second = lax.rsqrt(jnp.mean(middle * middle, -1, keepdims=True) + EPS)
    unit_second = middle * inv_second
    post = (unit_second * out_gain).astype(jnp.bfloat16)
    gate = matmul(post, gate_weight)
    upward = matmul(post, up_weight)
    sigma = jax.nn.sigmoid(gate)
    hidden = (gate * sigma * upward).astype(jnp.bfloat16)
    down_wgrad = jnp.einsum("tf,td->fd", hidden, cotangent, preferred_element_type=jnp.float32)
    hidden_grad = jnp.einsum(
        "td,fd->tf", cotangent, down_weight, preferred_element_type=jnp.float32
    )
    up_act_grad = (hidden_grad * gate * sigma).astype(jnp.bfloat16)
    gate_act_grad = (hidden_grad * upward * sigma * (1.0 + gate * (1.0 - sigma))).astype(
        jnp.bfloat16
    )
    gate_wgrad = jnp.einsum("tc,tf->cf", post, gate_act_grad, preferred_element_type=jnp.float32)
    up_wgrad = jnp.einsum("tc,tf->cf", post, up_act_grad, preferred_element_type=jnp.float32)
    post_part = jnp.einsum(
        "tf,cf->tc", gate_act_grad, gate_weight, preferred_element_type=jnp.float32
    ) + jnp.einsum("tf,cf->tc", up_act_grad, up_weight, preferred_element_type=jnp.float32)
    post_gain_part = jnp.sum(post_part * unit_second, 0)
    post_full = pair_sum(post_part.astype(jnp.bfloat16))
    down_wgrad, gate_wgrad, up_wgrad, post_full = lax.optimization_barrier(
        (
            down_wgrad.astype(jnp.bfloat16),
            gate_wgrad.astype(jnp.bfloat16),
            up_wgrad.astype(jnp.bfloat16),
            post_full,
        )
    )
    down_wgrad, gate_wgrad, up_wgrad = lax.psum((down_wgrad, gate_wgrad, up_wgrad), "dp")
    scaled_post = post_full * out_gain
    middle_grad = cotangent.astype(jnp.float32) + inv_second * (
        scaled_post - unit_second * jnp.mean(scaled_post * unit_second, -1, keepdims=True)
    )
    branch_grad = middle_grad.astype(jnp.bfloat16)
    attnout_wgrad = jnp.einsum(
        "tk,td->kd", attn_flat, branch_grad, preferred_element_type=jnp.float32
    )
    attended_grad = jnp.einsum(
        "td,kd->tk", branch_grad, attnout_weight, preferred_element_type=jnp.float32
    )
    attended_grad = (
        attended_grad.astype(jnp.bfloat16)
        .reshape(seq_count, document_length, heads, HEAD_SIZE)
        .transpose(0, 2, 1, 3)
    )

    def attend_back(seq_item):
        query_block, key_block, value_block, seg_ids, logsum_block, grad_block = seq_item
        allowed = allowed_of(seg_ids)[None]
        scores = (
            jnp.einsum("htd,sd->hts", query_block, key_block, preferred_element_type=jnp.float32)
            * scale
        )
        probs = jnp.where(allowed, jnp.exp(scores - logsum_block[..., None]), 0.0)
        value_grad = jnp.einsum(
            "hts,htd->hsd",
            probs.astype(jnp.bfloat16),
            grad_block,
            preferred_element_type=jnp.float32,
        )
        prob_grad = jnp.einsum(
            "htd,sd->hts", grad_block, value_block, preferred_element_type=jnp.float32
        )
        delta = jnp.sum(probs * prob_grad, -1, keepdims=True)
        score_grad = (probs * (prob_grad - delta)).astype(jnp.bfloat16)
        query_grad = (
            jnp.einsum("hts,sd->htd", score_grad, key_block, preferred_element_type=jnp.float32)
            * scale
        )
        key_grad = (
            jnp.einsum("hts,htd->hsd", score_grad, query_block, preferred_element_type=jnp.float32)
            * scale
        )
        return (query_grad, key_grad, value_grad)

    query_rot_grad, key_rot_grad, value_head_grad = lax.map(
        attend_back, (queries, key_rows, value_rows, segments, logsum, attended_grad)
    )
    query_pre_grad = (
        rotate_back(query_rot_grad, cosine, sine)
        .astype(jnp.bfloat16)
        .transpose(0, 2, 1, 3)
        .reshape(rows, heads * HEAD_SIZE)
    )
    key_pre_grad = rotate_back(key_rot_grad, cosine, sine).astype(jnp.bfloat16)
    value_pre_grad = value_head_grad.astype(jnp.bfloat16)
    normed_seq = normed.reshape(seq_count, document_length, -1)
    query_wgrad = jnp.einsum(
        "tc,tk->ck", normed, query_pre_grad, preferred_element_type=jnp.float32
    )
    key_wgrad = jnp.einsum(
        "slc,shld->cd", normed_seq, key_pre_grad, preferred_element_type=jnp.float32
    )
    value_weight_grad = jnp.einsum(
        "slc,shld->cd", normed_seq, value_pre_grad, preferred_element_type=jnp.float32
    )
    normed_part = (
        jnp.einsum("tk,ck->tc", query_pre_grad, query_weight, preferred_element_type=jnp.float32)
        + jnp.einsum(
            "shld,cd->slc", key_pre_grad, key_cols, preferred_element_type=jnp.float32
        ).reshape(rows, -1)
        + jnp.einsum(
            "shld,cd->slc", value_pre_grad, value_columns, preferred_element_type=jnp.float32
        ).reshape(rows, -1)
    )
    mixout_wgrad = jnp.einsum("tk,td->kd", mixed, branch_grad, preferred_element_type=jnp.float32)
    mixed_grad = jnp.einsum("td,kd->tk", branch_grad, mixer_out, preferred_element_type=jnp.float32)
    mixer_gain_wgrad = jnp.sum(mixed_grad * gated * inv_gate, 0)
    weighted = mixed_grad * mixer_scale
    cross = pair_sum(jnp.sum(weighted * gated, -1))[:, None]
    gated_grad = inv_gate * weighted - gated * (inv_gate * inv_gate * inv_gate) * cross / DSSM
    ssm_grad = gated_grad * gate_act
    gating_act_grad = (
        gated_grad * ssm_out * sigma_gate * (1.0 + gating * (1.0 - sigma_gate))
    ).astype(jnp.bfloat16)
    ssm_heads_grad = ssm_grad.reshape(seq_count, document_length, ssm_heads, P_SIZE).transpose(
        0, 2, 1, 3
    )
    core_grad = ssm_heads_grad.astype(jnp.bfloat16)
    skip_wgrad = jnp.sum(ssm_heads_grad * heads_in, axis=(0, 2, 3))

    def scan_back(seq_item):
        step_block, coef_b_block, coef_c_block, heads_block, seg_ids, core_block = seq_item
        coupling, decay, mixing, driven = ssd_parts(
            step_block, rate, coef_b_block, coef_c_block, heads_block, allowed_of(seg_ids)
        )
        mix_grad = jnp.einsum(
            "htp,hsp->hts", core_block, driven, preferred_element_type=jnp.float32
        )
        driven_grad = jnp.einsum(
            "hts,htp->hsp", mixing, core_block, preferred_element_type=jnp.float32
        )
        rounded = (mix_grad * decay).astype(jnp.bfloat16)
        coef_c_grad = jnp.einsum(
            "hts,sn->tn", rounded, coef_b_block, preferred_element_type=jnp.float32
        )
        coef_b_grad = jnp.einsum(
            "hts,tn->sn", rounded, coef_c_block, preferred_element_type=jnp.float32
        )
        spread = mix_grad * coupling[None] * decay
        cumulative_grad = jnp.sum(spread, 2) - jnp.sum(spread, 1)
        log_grad = jnp.flip(jnp.cumsum(jnp.flip(cumulative_grad, 1), 1), 1)
        heads_grad = driven_grad * step_block.T[:, :, None]
        step_grad = (jnp.sum(driven_grad * heads_block, -1) + log_grad * rate[:, None]).T
        rate_grad = jnp.sum(log_grad * step_block.T, 1)
        return (heads_grad, step_grad, rate_grad, coef_b_grad, coef_c_grad)

    heads_grad, step_grad, rate_grad, coef_b_grad, coef_c_grad = lax.map(
        scan_back, (step, coef_b, coef_c, heads_in, segments, core_grad)
    )
    heads_total = heads_grad + ssm_heads_grad * skip
    inner_act_grad = heads_total.transpose(0, 2, 1, 3).reshape(seq_count, document_length, -1)
    step_total = step_grad * jax.nn.sigmoid(step_arg)
    step_bias_wgrad = jnp.sum(step_total, axis=(0, 1))
    decay_wgrad = jnp.sum(rate_grad, 0) * rate
    step_raw_grad = step_total.reshape(rows, ssm_heads).astype(jnp.bfloat16)
    inner_pre_grad = inner_act_grad * silu_slope(inner_pre)
    inner_bias_wgrad = jnp.sum(inner_pre_grad, axis=(0, 1))
    inner_grad, conv_inner_wgrad = conv_backward(inner_pre_grad, inner, conv_inner, segments)
    inner_grad = inner_grad.reshape(rows, -1).astype(jnp.bfloat16)
    state_act_grad = jnp.concatenate([coef_b_grad, coef_c_grad], -1)
    state_pre_grad = state_act_grad * silu_slope(state_pre)
    state_bias_wgrad = jnp.sum(state_pre_grad, axis=(0, 1))
    state_grad, conv_state_wgrad = conv_backward(state_pre_grad, state_in, conv_state, segments)
    state_grad = state_grad.reshape(rows, -1).astype(jnp.bfloat16)
    gating_wgrad = jnp.einsum(
        "tc,tk->ck", normed, gating_act_grad, preferred_element_type=jnp.float32
    )
    inner_wgrad = jnp.einsum("tc,tk->ck", normed, inner_grad, preferred_element_type=jnp.float32)
    step_wgrad = jnp.einsum("tc,tk->ck", normed, step_raw_grad, preferred_element_type=jnp.float32)
    state_wgrad = jnp.einsum("tc,tk->ck", normed, state_grad, preferred_element_type=jnp.float32)
    normed_part = (
        normed_part
        + jnp.einsum(
            "tk,ck->tc", gating_act_grad, gating_weight, preferred_element_type=jnp.float32
        )
        + jnp.einsum("tk,ck->tc", inner_grad, inner_weight, preferred_element_type=jnp.float32)
        + jnp.einsum("tk,ck->tc", step_raw_grad, step_weight, preferred_element_type=jnp.float32)
        + jnp.einsum("tk,ck->tc", state_grad, state_weight, preferred_element_type=jnp.float32)
    )
    input_gain_part = jnp.sum(normed_part * unit_first, 0)
    normed_full = pair_sum(normed_part.astype(jnp.bfloat16))
    scaled_in = normed_full * in_gain
    tokens_grad = middle_grad + inv_first * (
        scaled_in - unit_first * jnp.mean(scaled_in * unit_first, -1, keepdims=True)
    )
    low = jnp.bfloat16
    if lax.axis_size("tensor") == 2 and KEYVALUE_HEADS == 2:
        keyval_part = jnp.concatenate([key_wgrad, value_weight_grad], 1)
    else:
        keyval_part = jnp.zeros(key_value_weight.shape, jnp.float32)
        keyval_part = lax.dynamic_update_slice_in_dim(
            keyval_part, key_wgrad, shared_key_head * HEAD_SIZE, 1
        )
        keyval_part = lax.dynamic_update_slice_in_dim(
            keyval_part, value_weight_grad, (KEYVALUE_HEADS + shared_key_head) * HEAD_SIZE, 1
        )
        keyval_part = lax.psum(keyval_part, "tensor")
    first_total = tree_sum(
        jnp.concatenate(
            [query_wgrad.astype(low), keyval_part.astype(low), gating_wgrad.astype(low)], 1
        )
    ).astype(jnp.float32)
    second_total = tree_sum(
        jnp.concatenate([attnout_wgrad.astype(low), mixout_wgrad.astype(low)], 0)
    ).astype(jnp.float32)
    width = query_wgrad.shape[1]
    kv_width = keyval_part.shape[1]
    query_wgrad = first_total[:, :width]
    keyval_part = first_total[:, width : width + kv_width]
    gating_wgrad = first_total[:, width + kv_width :]
    attnout_wgrad = second_total[: heads * HEAD_SIZE]
    mixout_wgrad = second_total[heads * HEAD_SIZE :]
    if lax.axis_size("tensor") == 2 and KEYVALUE_HEADS == 2:
        other = lax.ppermute(keyval_part.astype(low), "tensor", [(0, 1), (1, 0)])
        mine = keyval_part.astype(low)
        is_first = lax.axis_index("tensor") == 0
        head_0 = jnp.where(is_first, mine, other)
        head_1 = jnp.where(is_first, other, mine)
        key_value_weight_grad = jnp.concatenate(
            [
                head_0[:, :HEAD_SIZE],
                head_1[:, :HEAD_SIZE],
                head_0[:, HEAD_SIZE:],
                head_1[:, HEAD_SIZE:],
            ],
            1,
        ).astype(jnp.float32)
    else:
        key_value_weight_grad = keyval_part
    own = [
        step_bias_wgrad,
        decay_wgrad,
        skip_wgrad,
        mixer_gain_wgrad,
        inner_bias_wgrad,
        conv_inner_wgrad.reshape(-1),
    ]
    shared = [input_gain_part, post_gain_part, state_bias_wgrad, conv_state_wgrad.reshape(-1)]

    def columns_of(parts):
        flat = jnp.concatenate(parts)
        count = -(-flat.shape[0] // tokens.shape[1])
        flat = jnp.pad(flat, (0, count * tokens.shape[1] - flat.shape[0]))
        return flat.reshape(count, tokens.shape[1]).T

    def parts_of(columns, parts):
        flat = columns.T.reshape(-1)
        found, at = [], 0
        for part in parts:
            found.append(flat[at : at + part.shape[0]])
            at += part.shape[0]
        return found

    own_columns, shared_columns = columns_of(own), columns_of(shared)
    inner_width = inner_wgrad.shape[1]
    own_width = own_columns.shape[1]
    shared_from = -(-(inner_width + ssm_heads + own_width) // 128) * 128
    pad = shared_from - inner_width - ssm_heads - own_width
    third_total = tree_sum(
        jnp.concatenate(
            [
                inner_wgrad.astype(low),
                step_wgrad.astype(low),
                own_columns.astype(low),
                jnp.zeros((tokens.shape[1], pad), low),
                state_wgrad.astype(low),
                shared_columns.astype(low),
            ],
            1,
        ),
        shared_from,
    ).astype(jnp.float32)
    inner_wgrad = third_total[:, :inner_width]
    step_wgrad = third_total[:, inner_width : inner_width + ssm_heads]
    at = inner_width + ssm_heads
    (
        step_bias_wgrad,
        decay_wgrad,
        skip_wgrad,
        mixer_gain_wgrad,
        inner_bias_wgrad,
        conv_inner_flat,
    ) = parts_of(third_total[:, at : at + own_width], own)
    conv_inner_wgrad = conv_inner_flat.reshape(conv_inner.shape)
    state_width = state_wgrad.shape[1]
    state_wgrad = third_total[:, shared_from : shared_from + state_width]
    input_gain_part, post_gain_part, state_bias_wgrad, conv_state_flat = parts_of(
        third_total[:, shared_from + state_width :], shared
    )
    conv_state_wgrad = conv_state_flat.reshape(conv_state.shape)
    down_wgrad = down_wgrad.astype(jnp.float32)
    gate_wgrad = gate_wgrad.astype(jnp.float32)
    up_wgrad = up_wgrad.astype(jnp.float32)
    return (
        tokens_grad,
        input_gain_part,
        query_wgrad,
        key_value_weight_grad,
        attnout_wgrad,
        gating_wgrad,
        inner_wgrad,
        state_wgrad,
        step_wgrad,
        conv_inner_wgrad,
        conv_state_wgrad,
        inner_bias_wgrad,
        state_bias_wgrad,
        step_bias_wgrad,
        decay_wgrad,
        skip_wgrad,
        mixer_gain_wgrad,
        mixout_wgrad,
        post_gain_part,
        gate_wgrad,
        up_wgrad,
        down_wgrad,
    )


def solution(mesh):
    placed = (
        P("dp", None),
        P("dp", None),
        P("dp", None),
        P(),
        P(None, "tensor"),
        P(),
        P("tensor", None),
        P(None, "tensor"),
        P(None, "tensor"),
        P(),
        P(None, "tensor"),
        P(None, "tensor"),
        P(),
        P("tensor"),
        P(),
        P("tensor"),
        P("tensor"),
        P("tensor"),
        P("tensor"),
        P("tensor", None),
        P(),
        P(None, "tensor"),
        P(None, "tensor"),
        P("tensor", None),
    )
    return jax.shard_map(
        local,
        mesh=mesh,
        in_specs=placed,
        out_specs=(
            P("dp", None),
            P(),
            P(None, "tensor"),
            P(),
            P("tensor", None),
            P(None, "tensor"),
            P(None, "tensor"),
            P(),
            P(None, "tensor"),
            P(None, "tensor"),
            P(),
            P("tensor"),
            P(),
            P("tensor"),
            P("tensor"),
            P("tensor"),
            P("tensor"),
            P("tensor", None),
            P(),
            P(None, "tensor"),
            P(None, "tensor"),
            P("tensor", None),
        ),
        check_vma=False,
    )
```

```python
import jax
import jax.numpy as jnp
from jax import lax
from jax.experimental import pallas as pl
from jax.experimental.pallas import tpu as pltpu
from jax.sharding import PartitionSpec as P

QUERY_HEADS = 8
KEYVALUE_HEADS = 2
HEAD_SIZE = 64
P_SIZE = 64
NS = 128
DSSM = 1536


EPS = 1e-05
ROPE_BASE = 100000000000.0
NEG_FILL = -1e30


def matmul(left, right):
    return jnp.dot(left, right, preferred_element_type=jnp.float32)


def rotary_tables(document_length):
    half = HEAD_SIZE // 2
    freqs = jnp.exp(-jnp.log(ROPE_BASE) * (2.0 * jnp.arange(half, dtype=jnp.float32) / HEAD_SIZE))
    angles = jnp.arange(document_length, dtype=jnp.float32)[:, None] * freqs[None, :]
    return (jnp.cos(angles), jnp.sin(angles))


def rotate(value, cosine, sine):
    half = value.shape[-1] // 2
    first = value[..., :half]
    second = value[..., half:]
    return jnp.concatenate([first * cosine - second * sine, first * sine + second * cosine], -1)


def rotate_back(grad, cosine, sine):
    half = grad.shape[-1] // 2
    first = grad[..., :half]
    second = grad[..., half:]
    return jnp.concatenate([first * cosine + second * sine, second * cosine - first * sine], -1)


def silu_slope(value):
    sigma = jax.nn.sigmoid(value)
    return sigma * (1.0 + value * (1.0 - sigma))


def seg_keep(segments, offset):
    document_length = segments.shape[1]
    moved = jnp.pad(segments, ((0, 0), (offset, 0)), constant_values=-1)[:, :document_length]
    return (moved == segments).astype(jnp.float32)[:, :, None]


def move_down(value, offset):
    document_length = value.shape[1]
    return jnp.pad(value, ((0, 0), (offset, 0), (0, 0)))[:, :document_length]


def move_up(value, offset):
    return jnp.pad(value, ((0, 0), (0, offset), (0, 0)))[:, offset:]


def conv_forward(value, kernel, bias, segments):
    taps = kernel.shape[0]
    total = jnp.zeros_like(value) + bias.astype(jnp.float32)
    for tap in range(taps):
        offset = taps - 1 - tap
        total = total + kernel[tap].astype(jnp.float32) * move_down(value, offset) * seg_keep(
            segments, offset
        )
    return total


def conv_backward(grad, value, kernel, segments):
    taps = kernel.shape[0]
    grad_in = jnp.zeros_like(value)
    kernel_rows = []
    for tap in range(taps):
        offset = taps - 1 - tap
        masked = grad * seg_keep(segments, offset)
        kernel_rows.append(jnp.sum(masked * move_down(value, offset), axis=(0, 1)))
        grad_in = grad_in + kernel[tap].astype(jnp.float32) * move_up(masked, offset)
    return (grad_in, jnp.stack(kernel_rows))


def ssd_parts(step_block, rate, coef_b, coef_c, heads_block, allowed):
    coupling = jnp.einsum("tn,sn->ts", coef_c, coef_b, preferred_element_type=jnp.float32)
    cumulative = jnp.cumsum(step_block * rate, axis=0).T
    difference = cumulative[:, :, None] - cumulative[:, None, :]
    decay = jnp.where(allowed[None], jnp.exp(jnp.where(allowed[None], difference, 0.0)), 0.0)
    mixing = (coupling[None] * decay).astype(jnp.bfloat16)
    driven = (heads_block * step_block.T[:, :, None]).astype(jnp.bfloat16)
    return (coupling, decay, mixing, driven)


def pair_sum(value):
    if lax.axis_size("tensor") == 2:
        other = lax.ppermute(value, "tensor", [(0, 1), (1, 0)])
        return value.astype(jnp.float32) + other.astype(jnp.float32)
    return lax.psum(value, "tensor").astype(jnp.float32)


def swap_bit(value, bit):
    size = lax.axis_size("dp")
    return lax.ppermute(value, "dp", [(i, i ^ bit) for i in range(size)])


def shared_sum(rows, first_shared):
    tail = pair_sum(rows[:, first_shared:]).astype(rows.dtype)
    return jnp.concatenate([rows[:, :first_shared], tail], 1) if first_shared else tail


def tree_sum(value, first_shared=None):
    size = lax.axis_size("dp")
    rows = value.shape[0]
    if size & (size - 1) or rows % (16 * size):
        total = lax.psum(value, "dp")
        return total if first_shared is None else shared_sum(total, first_shared)
    bits = [1 << i for i in range(size.bit_length() - 1)]
    me = lax.axis_index("dp")
    for bit in bits:
        half = value.shape[0] // 2
        low, high = value[:half], value[half:]
        upper = (me & bit) != 0
        got = swap_bit(jnp.where(upper, low, high), bit)
        kept = jnp.where(upper, high, low)
        value = (kept.astype(jnp.float32) + got.astype(jnp.float32)).astype(value.dtype)
    if first_shared is not None:
        value = shared_sum(value, first_shared)
    for bit in reversed(bits):
        upper = (me & bit) != 0
        got = swap_bit(value, bit)
        value = jnp.where(
            upper, jnp.concatenate([got, value], 0), jnp.concatenate([value, got], 0)
        )
    return value


def local(
    tokens,
    segments,
    cotangent,
    input_gain,
    query_weight,
    key_value_weight,
    attnout_weight,
    gating_weight,
    inner_weight,
    state_weight,
    step_weight,
    conv_inner,
    conv_state,
    inner_bias,
    state_bias,
    step_bias,
    decay_log,
    skip_scale,
    mixer_gain,
    mixer_out,
    post_gain,
    gate_weight,
    up_weight,
    down_weight,
):
    seq_count, document_length = segments.shape
    rows = seq_count * document_length
    heads = query_weight.shape[1] // HEAD_SIZE
    ssm_heads = step_weight.shape[1]
    query_group = QUERY_HEADS // KEYVALUE_HEADS
    shared_key_head = lax.axis_index("tensor") * heads // query_group
    scale = HEAD_SIZE ** (-0.5)
    cosine, sine = rotary_tables(document_length)
    positions = jnp.arange(document_length)

    def allowed_of(seg_ids):
        return (positions[:, None] >= positions[None, :]) & (seg_ids[:, None] == seg_ids[None, :])

    inputs = tokens.astype(jnp.float32)
    inv_first = lax.rsqrt(jnp.mean(inputs * inputs, -1, keepdims=True) + EPS)
    unit_first = inputs * inv_first
    in_gain = input_gain.astype(jnp.float32)
    normed = (unit_first * in_gain).astype(jnp.bfloat16)
    key_cols = lax.dynamic_slice_in_dim(key_value_weight, shared_key_head * HEAD_SIZE, HEAD_SIZE, 1)
    value_columns = lax.dynamic_slice_in_dim(
        key_value_weight, (KEYVALUE_HEADS + shared_key_head) * HEAD_SIZE, HEAD_SIZE, 1
    )
    query_pre = matmul(normed, query_weight)
    key_pre = matmul(normed, key_cols)
    value_pre = matmul(normed, value_columns)
    queries = rotate(
        query_pre.reshape(seq_count, document_length, heads, HEAD_SIZE).transpose(0, 2, 1, 3),
        cosine,
        sine,
    ).astype(jnp.bfloat16)
    key_rows = rotate(key_pre.reshape(seq_count, document_length, HEAD_SIZE), cosine, sine).astype(
        jnp.bfloat16
    )
    value_rows = value_pre.reshape(seq_count, document_length, HEAD_SIZE).astype(jnp.bfloat16)

    def attend(seq_item):
        query_block, key_block, value_block, seg_ids = seq_item
        allowed = allowed_of(seg_ids)[None]
        scores = (
            jnp.einsum("htd,sd->hts", query_block, key_block, preferred_element_type=jnp.float32)
            * scale
        )
        scores = jnp.where(allowed, scores, NEG_FILL)
        top = jnp.max(scores, -1, keepdims=True)
        weights = jnp.exp(scores - top)
        total = jnp.sum(weights, -1, keepdims=True)
        probs = (weights / total).astype(jnp.bfloat16)
        attended = jnp.einsum("hts,sd->htd", probs, value_block, preferred_element_type=jnp.float32)
        return (attended.astype(jnp.bfloat16), (top + jnp.log(total))[..., 0])

    attended, logsum = lax.map(attend, (queries, key_rows, value_rows, segments))
    attn_flat = attended.transpose(0, 2, 1, 3).reshape(rows, heads * HEAD_SIZE)
    attn_part = matmul(attn_flat, attnout_weight)
    gating = matmul(normed, gating_weight)
    inner = matmul(normed, inner_weight).reshape(seq_count, document_length, -1)
    state_in = matmul(normed, state_weight).reshape(seq_count, document_length, -1)
    step_raw = matmul(normed, step_weight)
    inner_pre = conv_forward(inner, conv_inner, inner_bias, segments)
    inner_act = jax.nn.silu(inner_pre)
    state_pre = conv_forward(state_in, conv_state, state_bias, segments)
    state_act = jax.nn.silu(state_pre)
    coef_b = state_act[..., :NS].astype(jnp.bfloat16)
    coef_c = state_act[..., NS:].astype(jnp.bfloat16)
    step_arg = step_raw.reshape(seq_count, document_length, ssm_heads) + step_bias.astype(
        jnp.float32
    )
    step = jax.nn.softplus(step_arg)
    rate = -jnp.exp(decay_log.astype(jnp.float32))
    heads_in = inner_act.reshape(seq_count, document_length, ssm_heads, P_SIZE).transpose(
        0, 2, 1, 3
    )

    def scan_forward(seq_item):
        step_block, coef_b_block, coef_c_block, heads_block, seg_ids = seq_item
        parts = ssd_parts(
            step_block, rate, coef_b_block, coef_c_block, heads_block, allowed_of(seg_ids)
        )
        return jnp.einsum("hts,hsp->htp", parts[2], parts[3], preferred_element_type=jnp.float32)

    core = lax.map(scan_forward, (step, coef_b, coef_c, heads_in, segments))
    skip = skip_scale.astype(jnp.float32)[None, :, None, None]
    ssm_out = (core + skip * heads_in).transpose(0, 2, 1, 3).reshape(rows, ssm_heads * P_SIZE)
    sigma_gate = jax.nn.sigmoid(gating)
    gate_act = gating * sigma_gate
    gated = ssm_out * gate_act
    square_sum = pair_sum(jnp.sum(gated * gated, -1))[:, None]
    inv_gate = lax.rsqrt(square_sum / DSSM + EPS)
    mixer_scale = mixer_gain.astype(jnp.float32)
    mixed = (gated * inv_gate * mixer_scale).astype(jnp.bfloat16)
    branch_part = attn_part + matmul(mixed, mixer_out)
    out_gain = post_gain.astype(jnp.float32)
    branch = pair_sum(branch_part.astype(jnp.bfloat16))
    middle = inputs + branch
    inv_second = lax.rsqrt(jnp.mean(middle * middle, -1, keepdims=True) + EPS)
    unit_second = middle * inv_second
    post = (unit_second * out_gain).astype(jnp.bfloat16)
    gate = matmul(post, gate_weight)
    upward = matmul(post, up_weight)
    sigma = jax.nn.sigmoid(gate)
    hidden = (gate * sigma * upward).astype(jnp.bfloat16)
    down_wgrad = jnp.einsum("tf,td->fd", hidden, cotangent, preferred_element_type=jnp.float32)
    hidden_grad = jnp.einsum(
        "td,fd->tf", cotangent, down_weight, preferred_element_type=jnp.float32
    )
    up_act_grad = (hidden_grad * gate * sigma).astype(jnp.bfloat16)
    gate_act_grad = (hidden_grad * upward * sigma * (1.0 + gate * (1.0 - sigma))).astype(
        jnp.bfloat16
    )
    gate_wgrad = jnp.einsum("tc,tf->cf", post, gate_act_grad, preferred_element_type=jnp.float32)
    up_wgrad = jnp.einsum("tc,tf->cf", post, up_act_grad, preferred_element_type=jnp.float32)
    post_part = jnp.einsum(
        "tf,cf->tc", gate_act_grad, gate_weight, preferred_element_type=jnp.float32
    ) + jnp.einsum("tf,cf->tc", up_act_grad, up_weight, preferred_element_type=jnp.float32)
    post_gain_part = jnp.sum(post_part * unit_second, 0)
    post_full = pair_sum(post_part.astype(jnp.bfloat16))
    down_wgrad, gate_wgrad, up_wgrad, post_full = lax.optimization_barrier(
        (
            down_wgrad.astype(jnp.bfloat16),
            gate_wgrad.astype(jnp.bfloat16),
            up_wgrad.astype(jnp.bfloat16),
            post_full,
        )
    )
    down_wgrad, gate_wgrad, up_wgrad = lax.psum((down_wgrad, gate_wgrad, up_wgrad), "dp")
    scaled_post = post_full * out_gain
    middle_grad = cotangent.astype(jnp.float32) + inv_second * (
        scaled_post - unit_second * jnp.mean(scaled_post * unit_second, -1, keepdims=True)
    )
    branch_grad = middle_grad.astype(jnp.bfloat16)
    attnout_wgrad = jnp.einsum(
        "tk,td->kd", attn_flat, branch_grad, preferred_element_type=jnp.float32
    )
    attended_grad = jnp.einsum(
        "td,kd->tk", branch_grad, attnout_weight, preferred_element_type=jnp.float32
    )
    attended_grad = (
        attended_grad.astype(jnp.bfloat16)
        .reshape(seq_count, document_length, heads, HEAD_SIZE)
        .transpose(0, 2, 1, 3)
    )

    def attend_back(seq_item):
        query_block, key_block, value_block, seg_ids, logsum_block, grad_block = seq_item
        allowed = allowed_of(seg_ids)[None]
        scores = (
            jnp.einsum("htd,sd->hts", query_block, key_block, preferred_element_type=jnp.float32)
            * scale
        )
        probs = jnp.where(allowed, jnp.exp(scores - logsum_block[..., None]), 0.0)
        value_grad = jnp.einsum(
            "hts,htd->hsd",
            probs.astype(jnp.bfloat16),
            grad_block,
            preferred_element_type=jnp.float32,
        )
        prob_grad = jnp.einsum(
            "htd,sd->hts", grad_block, value_block, preferred_element_type=jnp.float32
        )
        delta = jnp.sum(probs * prob_grad, -1, keepdims=True)
        score_grad = (probs * (prob_grad - delta)).astype(jnp.bfloat16)
        query_grad = (
            jnp.einsum("hts,sd->htd", score_grad, key_block, preferred_element_type=jnp.float32)
            * scale
        )
        key_grad = (
            jnp.einsum("hts,htd->hsd", score_grad, query_block, preferred_element_type=jnp.float32)
            * scale
        )
        return (query_grad, key_grad, value_grad)

    query_rot_grad, key_rot_grad, value_head_grad = lax.map(
        attend_back, (queries, key_rows, value_rows, segments, logsum, attended_grad)
    )
    query_pre_grad = (
        rotate_back(query_rot_grad, cosine, sine)
        .astype(jnp.bfloat16)
        .transpose(0, 2, 1, 3)
        .reshape(rows, heads * HEAD_SIZE)
    )
    key_pre_grad = rotate_back(key_rot_grad, cosine, sine).astype(jnp.bfloat16)
    value_pre_grad = value_head_grad.astype(jnp.bfloat16)
    normed_seq = normed.reshape(seq_count, document_length, -1)
    query_wgrad = jnp.einsum(
        "tc,tk->ck", normed, query_pre_grad, preferred_element_type=jnp.float32
    )
    key_wgrad = jnp.einsum(
        "slc,shld->cd", normed_seq, key_pre_grad, preferred_element_type=jnp.float32
    )
    value_weight_grad = jnp.einsum(
        "slc,shld->cd", normed_seq, value_pre_grad, preferred_element_type=jnp.float32
    )
    normed_part = (
        jnp.einsum("tk,ck->tc", query_pre_grad, query_weight, preferred_element_type=jnp.float32)
        + jnp.einsum(
            "shld,cd->slc", key_pre_grad, key_cols, preferred_element_type=jnp.float32
        ).reshape(rows, -1)
        + jnp.einsum(
            "shld,cd->slc", value_pre_grad, value_columns, preferred_element_type=jnp.float32
        ).reshape(rows, -1)
    )
    mixout_wgrad = jnp.einsum("tk,td->kd", mixed, branch_grad, preferred_element_type=jnp.float32)
    mixed_grad = jnp.einsum("td,kd->tk", branch_grad, mixer_out, preferred_element_type=jnp.float32)
    mixer_gain_wgrad = jnp.sum(mixed_grad * gated * inv_gate, 0)
    weighted = mixed_grad * mixer_scale
    cross = pair_sum(jnp.sum(weighted * gated, -1))[:, None]
    gated_grad = inv_gate * weighted - gated * (inv_gate * inv_gate * inv_gate) * cross / DSSM
    ssm_grad = gated_grad * gate_act
    gating_act_grad = (
        gated_grad * ssm_out * sigma_gate * (1.0 + gating * (1.0 - sigma_gate))
    ).astype(jnp.bfloat16)
    ssm_heads_grad = ssm_grad.reshape(seq_count, document_length, ssm_heads, P_SIZE).transpose(
        0, 2, 1, 3
    )
    core_grad = ssm_heads_grad.astype(jnp.bfloat16)
    skip_wgrad = jnp.sum(ssm_heads_grad * heads_in, axis=(0, 2, 3))

    def scan_back(seq_item):
        step_block, coef_b_block, coef_c_block, heads_block, seg_ids, core_block = seq_item
        coupling, decay, mixing, driven = ssd_parts(
            step_block, rate, coef_b_block, coef_c_block, heads_block, allowed_of(seg_ids)
        )
        mix_grad = jnp.einsum(
            "htp,hsp->hts", core_block, driven, preferred_element_type=jnp.float32
        )
        driven_grad = jnp.einsum(
            "hts,htp->hsp", mixing, core_block, preferred_element_type=jnp.float32
        )
        rounded = (mix_grad * decay).astype(jnp.bfloat16)
        coef_c_grad = jnp.einsum(
            "hts,sn->tn", rounded, coef_b_block, preferred_element_type=jnp.float32
        )
        coef_b_grad = jnp.einsum(
            "hts,tn->sn", rounded, coef_c_block, preferred_element_type=jnp.float32
        )
        spread = mix_grad * coupling[None] * decay
        cumulative_grad = jnp.sum(spread, 2) - jnp.sum(spread, 1)
        log_grad = jnp.flip(jnp.cumsum(jnp.flip(cumulative_grad, 1), 1), 1)
        heads_grad = driven_grad * step_block.T[:, :, None]
        step_grad = (jnp.sum(driven_grad * heads_block, -1) + log_grad * rate[:, None]).T
        rate_grad = jnp.sum(log_grad * step_block.T, 1)
        return (heads_grad, step_grad, rate_grad, coef_b_grad, coef_c_grad)

    heads_grad, step_grad, rate_grad, coef_b_grad, coef_c_grad = lax.map(
        scan_back, (step, coef_b, coef_c, heads_in, segments, core_grad)
    )
    heads_total = heads_grad + ssm_heads_grad * skip
    inner_act_grad = heads_total.transpose(0, 2, 1, 3).reshape(seq_count, document_length, -1)
    step_total = step_grad * jax.nn.sigmoid(step_arg)
    step_bias_wgrad = jnp.sum(step_total, axis=(0, 1))
    decay_wgrad = jnp.sum(rate_grad, 0) * rate
    step_raw_grad = step_total.reshape(rows, ssm_heads).astype(jnp.bfloat16)
    inner_pre_grad = inner_act_grad * silu_slope(inner_pre)
    inner_bias_wgrad = jnp.sum(inner_pre_grad, axis=(0, 1))
    inner_grad, conv_inner_wgrad = conv_backward(inner_pre_grad, inner, conv_inner, segments)
    inner_grad = inner_grad.reshape(rows, -1).astype(jnp.bfloat16)
    state_act_grad = jnp.concatenate([coef_b_grad, coef_c_grad], -1)
    state_pre_grad = state_act_grad * silu_slope(state_pre)
    state_bias_wgrad = jnp.sum(state_pre_grad, axis=(0, 1))
    state_grad, conv_state_wgrad = conv_backward(state_pre_grad, state_in, conv_state, segments)
    state_grad = state_grad.reshape(rows, -1).astype(jnp.bfloat16)
    gating_wgrad = jnp.einsum(
        "tc,tk->ck", normed, gating_act_grad, preferred_element_type=jnp.float32
    )
    inner_wgrad = jnp.einsum("tc,tk->ck", normed, inner_grad, preferred_element_type=jnp.float32)
    step_wgrad = jnp.einsum("tc,tk->ck", normed, step_raw_grad, preferred_element_type=jnp.float32)
    state_wgrad = jnp.einsum("tc,tk->ck", normed, state_grad, preferred_element_type=jnp.float32)
    normed_part = (
        normed_part
        + jnp.einsum(
            "tk,ck->tc", gating_act_grad, gating_weight, preferred_element_type=jnp.float32
        )
        + jnp.einsum("tk,ck->tc", inner_grad, inner_weight, preferred_element_type=jnp.float32)
        + jnp.einsum("tk,ck->tc", step_raw_grad, step_weight, preferred_element_type=jnp.float32)
        + jnp.einsum("tk,ck->tc", state_grad, state_weight, preferred_element_type=jnp.float32)
    )
    input_gain_part = jnp.sum(normed_part * unit_first, 0)
    normed_full = pair_sum(normed_part.astype(jnp.bfloat16))
    scaled_in = normed_full * in_gain
    tokens_grad = middle_grad + inv_first * (
        scaled_in - unit_first * jnp.mean(scaled_in * unit_first, -1, keepdims=True)
    )
    low = jnp.bfloat16
    if lax.axis_size("tensor") == 2 and KEYVALUE_HEADS == 2:
        keyval_part = jnp.concatenate([key_wgrad, value_weight_grad], 1)
    else:
        keyval_part = jnp.zeros(key_value_weight.shape, jnp.float32)
        keyval_part = lax.dynamic_update_slice_in_dim(
            keyval_part, key_wgrad, shared_key_head * HEAD_SIZE, 1
        )
        keyval_part = lax.dynamic_update_slice_in_dim(
            keyval_part, value_weight_grad, (KEYVALUE_HEADS + shared_key_head) * HEAD_SIZE, 1
        )
        keyval_part = lax.psum(keyval_part, "tensor")
    first_total = tree_sum(
        jnp.concatenate(
            [query_wgrad.astype(low), keyval_part.astype(low), gating_wgrad.astype(low)], 1
        )
    ).astype(jnp.float32)
    second_total = tree_sum(
        jnp.concatenate([attnout_wgrad.astype(low), mixout_wgrad.astype(low)], 0)
    ).astype(jnp.float32)
    width = query_wgrad.shape[1]
    kv_width = keyval_part.shape[1]
    query_wgrad = first_total[:, :width]
    keyval_part = first_total[:, width : width + kv_width]
    gating_wgrad = first_total[:, width + kv_width :]
    attnout_wgrad = second_total[: heads * HEAD_SIZE]
    mixout_wgrad = second_total[heads * HEAD_SIZE :]
    if lax.axis_size("tensor") == 2 and KEYVALUE_HEADS == 2:
        other = lax.ppermute(keyval_part.astype(low), "tensor", [(0, 1), (1, 0)])
        mine = keyval_part.astype(low)
        is_first = lax.axis_index("tensor") == 0
        head_0 = jnp.where(is_first, mine, other)
        head_1 = jnp.where(is_first, other, mine)
        key_value_weight_grad = jnp.concatenate(
            [
                head_0[:, :HEAD_SIZE],
                head_1[:, :HEAD_SIZE],
                head_0[:, HEAD_SIZE:],
                head_1[:, HEAD_SIZE:],
            ],
            1,
        ).astype(jnp.float32)
    else:
        key_value_weight_grad = keyval_part
    own = [
        step_bias_wgrad,
        decay_wgrad,
        skip_wgrad,
        mixer_gain_wgrad,
        inner_bias_wgrad,
        conv_inner_wgrad.reshape(-1),
    ]
    shared = [input_gain_part, post_gain_part, state_bias_wgrad, conv_state_wgrad.reshape(-1)]

    def columns_of(parts):
        flat = jnp.concatenate(parts)
        count = -(-flat.shape[0] // tokens.shape[1])
        flat = jnp.pad(flat, (0, count * tokens.shape[1] - flat.shape[0]))
        return flat.reshape(count, tokens.shape[1]).T

    def parts_of(columns, parts):
        flat = columns.T.reshape(-1)
        found, at = [], 0
        for part in parts:
            found.append(flat[at : at + part.shape[0]])
            at += part.shape[0]
        return found

    own_columns, shared_columns = columns_of(own), columns_of(shared)
    inner_width = inner_wgrad.shape[1]
    own_width = own_columns.shape[1]
    shared_from = -(-(inner_width + ssm_heads + own_width) // 128) * 128
    pad = shared_from - inner_width - ssm_heads - own_width
    third_total = tree_sum(
        jnp.concatenate(
            [
                inner_wgrad.astype(low),
                step_wgrad.astype(low),
                own_columns.astype(low),
                jnp.zeros((tokens.shape[1], pad), low),
                state_wgrad.astype(low),
                shared_columns.astype(low),
            ],
            1,
        ),
        shared_from,
    ).astype(jnp.float32)
    inner_wgrad = third_total[:, :inner_width]
    step_wgrad = third_total[:, inner_width : inner_width + ssm_heads]
    at = inner_width + ssm_heads
    (
        step_bias_wgrad,
        decay_wgrad,
        skip_wgrad,
        mixer_gain_wgrad,
        inner_bias_wgrad,
        conv_inner_flat,
    ) = parts_of(third_total[:, at : at + own_width], own)
    conv_inner_wgrad = conv_inner_flat.reshape(conv_inner.shape)
    state_width = state_wgrad.shape[1]
    state_wgrad = third_total[:, shared_from : shared_from + state_width]
    input_gain_part, post_gain_part, state_bias_wgrad, conv_state_flat = parts_of(
        third_total[:, shared_from + state_width :], shared
    )
    conv_state_wgrad = conv_state_flat.reshape(conv_state.shape)
    down_wgrad = down_wgrad.astype(jnp.float32)
    gate_wgrad = gate_wgrad.astype(jnp.float32)
    up_wgrad = up_wgrad.astype(jnp.float32)
    return (
        tokens_grad,
        input_gain_part,
        query_wgrad,
        key_value_weight_grad,
        attnout_wgrad,
        gating_wgrad,
        inner_wgrad,
        state_wgrad,
        step_wgrad,
        conv_inner_wgrad,
        conv_state_wgrad,
        inner_bias_wgrad,
        state_bias_wgrad,
        step_bias_wgrad,
        decay_wgrad,
        skip_wgrad,
        mixer_gain_wgrad,
        mixout_wgrad,
        post_gain_part,
        gate_wgrad,
        up_wgrad,
        down_wgrad,
    )


CHUNK = 256
LANES = 128
VMEM_BYTES = 56 * 1024 * 1024


def dot_nn(left, right):
    return lax.dot_general(left, right, (((1,), (0,)), ((), ())), preferred_element_type=jnp.float32)


def dot_nt(left, right):
    return lax.dot_general(left, right, (((1,), (1,)), ((), ())), preferred_element_type=jnp.float32)


def dot_tn(left, right):
    return lax.dot_general(left, right, (((0,), (0,)), ((), ())), preferred_element_type=jnp.float32)


def split_two(value):
    high = value.astype(jnp.bfloat16)
    return high, (value - high.astype(jnp.float32)).astype(jnp.bfloat16)


def exact_nn(ones, value):
    high, low = split_two(value)
    return dot_nn(ones, high) + dot_nn(ones, low)


def grid_of(shape):
    return (
        lax.broadcasted_iota(jnp.int32, shape, 0),
        lax.broadcasted_iota(jnp.int32, shape, 1),
    )


def pick(columns, pair):
    rows = columns.shape[0]
    left = jnp.broadcast_to(columns[:, 2 * pair : 2 * pair + 1], (rows, LANES))
    right = jnp.broadcast_to(columns[:, 2 * pair + 1 : 2 * pair + 2], (rows, LANES))
    return jnp.where(grid_of((rows, LANES))[1] < P_SIZE, left, right)


def scan_terms(step, rate, aux):
    row, col = grid_of((CHUNK, CHUNK))
    lower = (row >= col).astype(jnp.bfloat16)
    cumulative = exact_nn(lower, step * rate)
    last = cumulative[CHUNK - 1 : CHUNK]
    enter = jnp.exp(cumulative) * aux[:, 1:2]
    leave = jnp.exp(last - cumulative) * aux[:, 2:3]
    across = jnp.exp(last) * aux[CHUNK - 1 : CHUNK, 1:2]
    return cumulative, enter, leave, across


def scan_kernel(step_ref, coef_ref, act_ref, aux_ref, seg_ref, rate_ref, core_ref, kept_ref, state, moved):
    @pl.when(pl.program_id(0) == 0)
    def _():
        state[...] = jnp.zeros_like(state)

    step = step_ref[...]
    aux = aux_ref[...]
    cumulative, enter, leave, across = scan_terms(step, rate_ref[...], aux)
    cum_rows = cumulative.T
    row, col = grid_of((CHUNK, CHUNK))
    blocked = jnp.where((row >= col) & (aux[:, 0:1] == seg_ref[...]), 0.0, NEG_FILL)
    coef_b = coef_ref[:, :NS]
    coef_c = coef_ref[:, NS:]
    coupling = dot_nt(coef_c, coef_b)
    low_state = state[...].astype(jnp.bfloat16)
    kept_ref[0] = low_state
    carried = dot_nn(coef_c, low_state)
    first = grid_of((CHUNK, LANES))[1] < P_SIZE
    for pair in range(act_ref.shape[1] // LANES):
        at = slice(pair * LANES, (pair + 1) * LANES)
        driven = (act_ref[:, at] * pick(step, pair)).astype(jnp.bfloat16)
        parts = []
        for head in (2 * pair, 2 * pair + 1):
            decay = jnp.exp(cumulative[:, head : head + 1] - cum_rows[head : head + 1] + blocked)
            parts.append(dot_nn((coupling * decay).astype(jnp.bfloat16), driven))
        core_ref[:, at] = jnp.where(first, parts[0], parts[1]) + carried[:, at] * pick(enter, pair)
        moved[:, at] = (driven.astype(jnp.float32) * pick(leave, pair)).astype(jnp.bfloat16)
    fresh = dot_tn(coef_b, moved[...])
    for pair in range(act_ref.shape[1] // LANES):
        at = slice(pair * LANES, (pair + 1) * LANES)
        state[:, at] = state[:, at] * pick(across, pair) + fresh[:, at]


def scan_call(step, coef, act, aux, seg_row, rate):
    rows, width = act.shape
    chunks = rows // CHUNK
    by_chunk = lambda columns: pl.BlockSpec((CHUNK, columns), lambda i: (i, 0))
    return pl.pallas_call(
        scan_kernel,
        grid=(chunks,),
        in_specs=[
            by_chunk(LANES),
            by_chunk(2 * NS),
            by_chunk(width),
            by_chunk(LANES),
            pl.BlockSpec((1, CHUNK), lambda i: (0, i)),
            pl.BlockSpec((1, LANES), lambda i: (0, 0)),
        ],
        out_specs=[by_chunk(width), pl.BlockSpec((1, NS, width), lambda i: (i, 0, 0))],
        out_shape=[
            jax.ShapeDtypeStruct((rows, width), jnp.float32),
            jax.ShapeDtypeStruct((chunks, NS, width), jnp.bfloat16),
        ],
        scratch_shapes=[
            pltpu.VMEM((NS, width), jnp.float32),
            pltpu.VMEM((CHUNK, width), jnp.bfloat16),
        ],
        compiler_params=pltpu.CompilerParams(vmem_limit_bytes=VMEM_BYTES),
        name="scan_forward",
    )(step, coef, act, aux, seg_row, rate)


def scan_back_kernel(
    step_ref,
    coef_ref,
    act_ref,
    aux_ref,
    seg_ref,
    rate_ref,
    skip_ref,
    grad_ref,
    kept_ref,
    act_grad_ref,
    step_grad_ref,
    coef_grad_ref,
    sums_ref,
    skip_sum_ref,
    state_grad,
    moved,
    entered,
    row_sums,
):
    @pl.when(pl.program_id(0) == 0)
    def _():
        state_grad[...] = jnp.zeros_like(state_grad)
        sums_ref[...] = jnp.zeros_like(sums_ref)
        skip_sum_ref[...] = jnp.zeros_like(skip_sum_ref)
        row_sums[...] = jnp.zeros_like(row_sums)

    step = step_ref[...]
    aux = aux_ref[...]
    rate = rate_ref[...]
    cumulative, enter, leave, across = scan_terms(step, rate, aux)
    cum_rows = cumulative.T
    row, col = grid_of((CHUNK, CHUNK))
    blocked = jnp.where((row <= col) & (aux[:, 0:1] == seg_ref[...]), 0.0, NEG_FILL)
    coef_b = coef_ref[:, :NS]
    coef_c = coef_ref[:, NS:]
    coupling = dot_nt(coef_b, coef_c)
    low_state = kept_ref[0]
    carried = dot_nn(coef_c, low_state)
    low_grad = state_grad[...].astype(jnp.bfloat16)
    returned = dot_nn(coef_b, low_grad)
    product = jnp.sum(low_state.astype(jnp.float32) * low_grad.astype(jnp.float32), 0, keepdims=True)
    lane = grid_of((CHUNK, LANES))[1]
    lane_row = grid_of((1, LANES))[1]
    first = lane < P_SIZE
    later = jnp.zeros((CHUNK, LANES), jnp.float32)
    earlier = jnp.zeros((CHUNK, LANES), jnp.float32)
    direct = jnp.zeros((CHUNK, LANES), jnp.float32)
    through = jnp.zeros((1, LANES), jnp.float32)
    coupling_grad = jnp.zeros((CHUNK, CHUNK), jnp.float32)
    for pair in range(act_ref.shape[1] // LANES):
        at = slice(pair * LANES, (pair + 1) * LANES)
        act = act_ref[:, at]
        spread_step = pick(step, pair)
        driven = (act * spread_step).astype(jnp.bfloat16)
        grad = grad_ref[:, at]
        core_grad = grad.astype(jnp.bfloat16)
        core_wide = core_grad.astype(jnp.float32)
        enter_grad = core_wide * pick(enter, pair)
        entered[:, at] = enter_grad.astype(jnp.bfloat16)
        row_part = enter_grad * carried[:, at]
        leave_pair = pick(leave, pair)
        moved[:, at] = (driven.astype(jnp.float32) * leave_pair).astype(jnp.bfloat16)
        back = returned[:, at] * leave_pair
        col_part = back * driven.astype(jnp.float32)
        parts = []
        for head in (2 * pair, 2 * pair + 1):
            mine = first if head % 2 == 0 else ~first
            decay = jnp.exp(cum_rows[head : head + 1] - cumulative[:, head : head + 1] + blocked)
            mix_grad = dot_nt(jnp.where(mine, driven, jnp.zeros_like(driven)), core_grad)
            share = mix_grad * decay
            coupling_grad = coupling_grad + share
            spread = share * coupling
            row_sums[head : head + 1] = jnp.sum(spread, 0, keepdims=True)
            folded = sum(spread[:, k * LANES : (k + 1) * LANES] for k in range(CHUNK // LANES))
            found = jnp.sum(jnp.where(mine, row_part, 0.0) - folded, 1, keepdims=True)
            later = jnp.where(lane == head, found, later)
            parts.append(dot_nn((coupling * decay).astype(jnp.bfloat16), core_grad))
            found = jnp.sum(jnp.where(mine, col_part, 0.0), 1, keepdims=True)
            earlier = jnp.where(lane == head, found, earlier)
        driven_grad = jnp.where(first, parts[0], parts[1]) + back
        act_grad_ref[:, at] = driven_grad * spread_step + grad * skip_ref[:, at]
        skip_sum_ref[:, at] += jnp.sum(grad * act, 0, keepdims=True)
        step_part = driven_grad * act
        product_pair = product[:, at]
        for head in (2 * pair, 2 * pair + 1):
            mine = first if head % 2 == 0 else ~first
            found = jnp.sum(jnp.where(mine, step_part, 0.0), 1, keepdims=True)
            direct = jnp.where(lane == head, found, direct)
            found = jnp.sum(jnp.where(mine[:1], product_pair, 0.0), 1, keepdims=True)
            through = jnp.where(lane_row == head, found, through)
    upper = (row <= col).astype(jnp.bfloat16)
    below = (row > col).astype(jnp.bfloat16)
    high, low = split_two(row_sums[...])
    log_grad = (
        exact_nn(upper, later)
        + dot_nt(upper, high)
        + dot_nt(upper, low)
        + exact_nn(below, earlier)
        + through * across
    )
    step_grad_ref[...] = direct + log_grad * rate
    sums_ref[...] += jnp.sum(log_grad * step, 0, keepdims=True)
    low_coupling = coupling_grad.astype(jnp.bfloat16)
    coef_grad_ref[:, :NS] = dot_nn(low_coupling, coef_c) + dot_nt(moved[...], low_grad)
    coef_grad_ref[:, NS:] = dot_tn(low_coupling, coef_b) + dot_nt(entered[...], low_state)
    fresh = dot_tn(coef_c, entered[...])
    for pair in range(act_ref.shape[1] // LANES):
        at = slice(pair * LANES, (pair + 1) * LANES)
        state_grad[:, at] = state_grad[:, at] * pick(across, pair) + fresh[:, at]


def scan_back_call(step, coef, act, aux, seg_row, rate, skip_row, grad, kept):
    rows, width = act.shape
    chunks = rows // CHUNK
    by_chunk = lambda columns: pl.BlockSpec((CHUNK, columns), lambda i: (chunks - 1 - i, 0))
    one_row = lambda columns: pl.BlockSpec((1, columns), lambda i: (0, 0))
    return pl.pallas_call(
        scan_back_kernel,
        grid=(chunks,),
        in_specs=[
            by_chunk(LANES),
            by_chunk(2 * NS),
            by_chunk(width),
            by_chunk(LANES),
            pl.BlockSpec((1, CHUNK), lambda i: (0, chunks - 1 - i)),
            one_row(LANES),
            one_row(width),
            by_chunk(width),
            pl.BlockSpec((1, NS, width), lambda i: (chunks - 1 - i, 0, 0)),
        ],
        out_specs=[
            by_chunk(width),
            by_chunk(LANES),
            by_chunk(2 * NS),
            one_row(LANES),
            one_row(width),
        ],
        out_shape=[
            jax.ShapeDtypeStruct((rows, width), jnp.float32),
            jax.ShapeDtypeStruct((rows, LANES), jnp.float32),
            jax.ShapeDtypeStruct((rows, 2 * NS), jnp.float32),
            jax.ShapeDtypeStruct((1, LANES), jnp.float32),
            jax.ShapeDtypeStruct((1, width), jnp.float32),
        ],
        scratch_shapes=[
            pltpu.VMEM((NS, width), jnp.float32),
            pltpu.VMEM((CHUNK, width), jnp.bfloat16),
            pltpu.VMEM((CHUNK, width), jnp.bfloat16),
            pltpu.VMEM((LANES, CHUNK), jnp.float32),
        ],
        compiler_params=pltpu.CompilerParams(vmem_limit_bytes=VMEM_BYTES),
        name="scan_backward",
    )(step, coef, act, aux, seg_row, rate, skip_row, grad, kept)


def swap_halves(value):
    width = value.shape[1]
    half = HEAD_SIZE // 2
    up = pltpu.roll(value, width - half, 1)
    down = pltpu.roll(value, half, 1)
    return jnp.where(grid_of(value.shape)[1] % HEAD_SIZE < half, up, down)


def turned(value, cosine, sine):
    return value * cosine + swap_halves(value) * sine


def attend_kernel(query_ref, keyval_ref, seg_ref, seg_col_ref, cos_ref, sin_ref, out_ref, turned_ref, both_ref, log_ref):
    rows = query_ref.shape[0]
    first = grid_of((rows, LANES))[1] < HEAD_SIZE
    keyval = keyval_ref[...]
    moved = pltpu.roll(keyval, HEAD_SIZE, 1)
    keys = turned(jnp.where(first, keyval, moved), cos_ref[...], sin_ref[...]).astype(jnp.bfloat16)
    values = jnp.where(first, moved, keyval).astype(jnp.bfloat16)
    both_ref[:, :LANES] = keys
    both_ref[:, LANES:] = values
    scale = HEAD_SIZE ** (-0.5)
    head_lane = grid_of((CHUNK, LANES))[1]
    first = head_lane < HEAD_SIZE
    for block in range(rows // CHUNK):
        low, high = block * CHUNK, (block + 1) * CHUNK
        row, col = grid_of((CHUNK, high))
        blocked = jnp.where(
            (row + low >= col) & (seg_col_ref[low:high, 0:1] == seg_ref[:, :high]), 0.0, NEG_FILL
        )
        logs = jnp.zeros((CHUNK, LANES), jnp.float32)
        for pair in range(query_ref.shape[1] // LANES):
            at = slice(pair * LANES, (pair + 1) * LANES)
            query = turned(query_ref[low:high, at], cos_ref[low:high], sin_ref[low:high]).astype(
                jnp.bfloat16
            )
            turned_ref[low:high, at] = query
            parts = []
            for head in (2 * pair, 2 * pair + 1):
                mine = first if head % 2 == 0 else ~first
                scores = (
                    dot_nt(jnp.where(mine, query, jnp.zeros_like(query)), keys[:high]) * scale
                    + blocked
                )
                top = jnp.max(scores, 1, keepdims=True)
                weights = jnp.exp(scores - top)
                total = jnp.sum(weights, 1, keepdims=True)
                probs = (weights * (1.0 / total)).astype(jnp.bfloat16)
                parts.append(dot_nn(probs, values[:high]))
                logs = jnp.where(head_lane == head, top + jnp.log(total), logs)
            out_ref[low:high, at] = jnp.where(first, parts[0], parts[1]).astype(jnp.bfloat16)
        log_ref[low:high] = logs


def attend_call(query, keyval, seg_row, aux, cosine, sine):
    rows, width = query.shape
    return pl.pallas_call(
        attend_kernel,
        out_shape=[
            jax.ShapeDtypeStruct((rows, width), jnp.bfloat16),
            jax.ShapeDtypeStruct((rows, width), jnp.bfloat16),
            jax.ShapeDtypeStruct((rows, 2 * LANES), jnp.bfloat16),
            jax.ShapeDtypeStruct((rows, LANES), jnp.float32),
        ],
        compiler_params=pltpu.CompilerParams(vmem_limit_bytes=VMEM_BYTES),
        name="attend_forward",
    )(query, keyval, seg_row, aux, cosine, sine)


def attend_back_kernel(
    query_ref, both_ref, seg_ref, seg_col_ref, cos_ref, sin_ref, log_ref, out_ref, grad_ref,
    query_grad_ref, keyval_grad_ref, key_sum, value_sum,
):
    rows = query_ref.shape[0]
    key_sum[...] = jnp.zeros_like(key_sum)
    value_sum[...] = jnp.zeros_like(value_sum)
    scale = HEAD_SIZE ** (-0.5)
    first = grid_of((CHUNK, LANES))[1] < HEAD_SIZE
    for block in range(rows // CHUNK):
        low, high = block * CHUNK, (block + 1) * CHUNK
        row, col = grid_of((CHUNK, high))
        blocked = jnp.where(
            (row + low >= col) & (seg_col_ref[low:high, 0:1] == seg_ref[:, :high]), 0.0, NEG_FILL
        )
        keys = both_ref[:high, :LANES]
        values = both_ref[:high, LANES:]
        for pair in range(query_ref.shape[1] // LANES):
            at = slice(pair * LANES, (pair + 1) * LANES)
            query = query_ref[low:high, at]
            grad = grad_ref[low:high, at]
            inner = grad.astype(jnp.float32) * out_ref[low:high, at].astype(jnp.float32)
            parts = []
            key_part = None
            for head in (2 * pair, 2 * pair + 1):
                mine = first if head % 2 == 0 else ~first
                query_mine = jnp.where(mine, query, jnp.zeros_like(query))
                grad_mine = jnp.where(mine, grad, jnp.zeros_like(grad))
                scores = dot_nt(query_mine, keys) * scale + blocked
                probs = jnp.exp(scores - log_ref[low:high, head : head + 1])
                delta = jnp.sum(jnp.where(mine, inner, 0.0), 1, keepdims=True)
                prob_grad = dot_nt(grad_mine, values)
                score_grad = (probs * (prob_grad - delta)).astype(jnp.bfloat16)
                parts.append(dot_nn(score_grad, keys) * scale)
                key_sum[:high] += dot_tn(score_grad, query_mine)
                value_sum[:high] += dot_tn(probs.astype(jnp.bfloat16), grad_mine)
            full = jnp.where(first, parts[0], parts[1])
            query_grad_ref[low:high, at] = turned(full, cos_ref[low:high], -sin_ref[low:high]).astype(
                jnp.bfloat16
            )
    wide = grid_of((rows, LANES))[1] < HEAD_SIZE
    key_total = key_sum[...] * scale
    key_total = key_total + pltpu.roll(key_total, HEAD_SIZE, 1)
    key_total = turned(key_total, cos_ref[...], -sin_ref[...])
    value_total = value_sum[...]
    value_total = value_total + pltpu.roll(value_total, HEAD_SIZE, 1)
    keyval_grad_ref[...] = jnp.where(wide, key_total, value_total).astype(jnp.bfloat16)


def attend_back_call(query, both, seg_row, aux, cosine, sine, logs, out, grad):
    rows, width = query.shape
    return pl.pallas_call(
        attend_back_kernel,
        out_shape=[
            jax.ShapeDtypeStruct((rows, width), jnp.bfloat16),
            jax.ShapeDtypeStruct((rows, LANES), jnp.bfloat16),
        ],
        scratch_shapes=[
            pltpu.VMEM((rows, LANES), jnp.float32),
            pltpu.VMEM((rows, LANES), jnp.float32),
        ],
        compiler_params=pltpu.CompilerParams(vmem_limit_bytes=VMEM_BYTES),
        name="attend_backward",
    )(query, both, seg_row, aux, cosine, sine, logs, out, grad)


def halve(value, bit):
    half = value.shape[0] // 2
    upper = (lax.axis_index("dp") & bit) != 0
    got = swap_bit(jnp.where(upper, value[:half], value[half:]), bit)
    kept = jnp.where(upper, value[half:], value[:half])
    return (kept.astype(jnp.float32) + got.astype(jnp.float32)).astype(value.dtype)


def double(value, bit):
    upper = (lax.axis_index("dp") & bit) != 0
    got = swap_bit(value, bit)
    return jnp.concatenate([jnp.where(upper, got, value), jnp.where(upper, value, got)], 0)


def dp_bits():
    size = lax.axis_size("dp")
    return [1 << i for i in range(size.bit_length() - 1)]


def scatter_sum(value):
    for bit in dp_bits():
        value = halve(value, bit)
    return value


def gather_rows(value):
    for bit in reversed(dp_bits()):
        value = double(value, bit)
    return value


def conv_rows(value, kernel, bias, keeps):
    taps = kernel.shape[0]
    total = bias.astype(jnp.float32)[None]
    for tap in range(taps):
        offset = taps - 1 - tap
        moved = jnp.pad(value, ((offset, 0), (0, 0)))[: value.shape[0]]
        total = total + kernel[tap].astype(jnp.float32) * moved * keeps[offset]
    return total


def conv_rows_back(grad, value, kernel, keeps):
    taps = kernel.shape[0]
    grad_in = jnp.zeros_like(grad)
    sums = []
    for tap in range(taps):
        offset = taps - 1 - tap
        masked = grad * keeps[offset]
        moved = jnp.pad(value, ((offset, 0), (0, 0)))[: value.shape[0]]
        sums.append(jnp.sum(masked * moved, 0, keepdims=True))
        grad_in = grad_in + kernel[tap].astype(jnp.float32) * jnp.pad(
            masked, ((0, offset), (0, 0))
        )[offset:]
    return grad_in, sums


def local_fast(
    tokens,
    segments,
    cotangent,
    input_gain,
    query_weight,
    key_value_weight,
    attnout_weight,
    gating_weight,
    inner_weight,
    state_weight,
    step_weight,
    conv_inner,
    conv_state,
    inner_bias,
    state_bias,
    step_bias,
    decay_log,
    skip_scale,
    mixer_gain,
    mixer_out,
    post_gain,
    gate_weight,
    up_weight,
    down_weight,
):
    low, wide = jnp.bfloat16, jnp.float32
    rows, model = tokens.shape
    heads = query_weight.shape[1] // HEAD_SIZE
    ssm_heads = step_weight.shape[1]
    ssm_width = ssm_heads * P_SIZE
    query_width = heads * HEAD_SIZE
    first_device = lax.axis_index("tensor") == 0
    pick_head = lambda at: jnp.where(
        first_device,
        key_value_weight[:, at : at + HEAD_SIZE],
        key_value_weight[:, at + HEAD_SIZE : at + 2 * HEAD_SIZE],
    )
    keyval_weight = jnp.concatenate([pick_head(0), pick_head(KEYVALUE_HEADS * HEAD_SIZE)], 1)
    lane_pad = ((0, 0), (0, LANES - ssm_heads))
    step_weight_wide = jnp.pad(step_weight, lane_pad)
    step_bias_wide = jnp.pad(step_bias.astype(wide)[None], lane_pad)
    rate = -jnp.exp(decay_log.astype(wide))
    rate_wide = jnp.pad(rate[None], lane_pad)
    skip_row = jnp.repeat(skip_scale.astype(wide), P_SIZE)[None]
    cosine, sine = rotary_tables(rows)
    cosine = jnp.concatenate([cosine] * 4, 1)
    sine = jnp.concatenate([-sine, sine, -sine, sine], 1)
    seg_row = segments.astype(wide)
    seg_chunks = seg_row.reshape(-1, CHUNK)
    ends = seg_chunks[:, -1:]
    starts = jnp.concatenate([jnp.full((1, 1), -1.0, wide), ends[:-1]], 0)
    aux = jnp.stack(
        [seg_chunks, (seg_chunks == starts).astype(wide), (seg_chunks == ends).astype(wide)], -1
    ).reshape(rows, 3)
    aux = jnp.pad(aux, ((0, 0), (0, LANES - 3)))
    keeps = [seg_keep(segments, offset)[0] for offset in range(conv_inner.shape[0])]

    inputs = tokens.astype(wide)
    inv_first = lax.rsqrt(jnp.mean(inputs * inputs, -1, keepdims=True) + EPS)
    unit_first = inputs * inv_first
    in_gain = input_gain.astype(wide)
    normed = (unit_first * in_gain).astype(low)
    inner = matmul(normed, inner_weight)
    state_in = matmul(normed, state_weight)
    step_arg = matmul(normed, step_weight_wide) + step_bias_wide
    gating = matmul(normed, gating_weight)
    inner_pre = conv_rows(inner, conv_inner, inner_bias, keeps)
    inner_act = jax.nn.silu(inner_pre)
    state_pre = conv_rows(state_in, conv_state, state_bias, keeps)
    coef = jax.nn.silu(state_pre).astype(low)
    step = jax.nn.softplus(step_arg)
    core, kept = scan_call(step, coef, inner_act, aux, seg_row, rate_wide)
    ssm_out = core + skip_row * inner_act
    sigma_gate = jax.nn.sigmoid(gating)
    gate_act = gating * sigma_gate
    gated = ssm_out * gate_act
    square_sum = pair_sum(jnp.sum(gated * gated, -1))[:, None]
    query_pre = matmul(normed, query_weight)
    keyval_pre = matmul(normed, keyval_weight)
    attended, queries, both, logs = attend_call(query_pre, keyval_pre, seg_row, aux, cosine, sine)
    attn_part = matmul(attended, attnout_weight)
    inv_gate = lax.rsqrt(square_sum / DSSM + EPS)
    mixer_scale = mixer_gain.astype(wide)
    mixed = (gated * inv_gate * mixer_scale).astype(low)
    branch_part = attn_part + matmul(mixed, mixer_out)
    out_gain = post_gain.astype(wide)
    branch = pair_sum(branch_part.astype(low))
    middle = inputs + branch
    inv_second = lax.rsqrt(jnp.mean(middle * middle, -1, keepdims=True) + EPS)
    unit_second = middle * inv_second
    post = (unit_second * out_gain).astype(low)
    gate = matmul(post, gate_weight)
    upward = matmul(post, up_weight)
    sigma = jax.nn.sigmoid(gate)
    hidden = (gate * sigma * upward).astype(low)
    hidden_grad = dot_nt(cotangent, down_weight)
    up_act_grad = (hidden_grad * gate * sigma).astype(low)
    gate_act_grad = (hidden_grad * upward * sigma * (1.0 + gate * (1.0 - sigma))).astype(low)
    post_part = dot_nt(gate_act_grad, gate_weight) + dot_nt(up_act_grad, up_weight)
    post_gain_part = jnp.sum(post_part * unit_second, 0, keepdims=True)
    post_full = pair_sum(post_part.astype(low))
    down_wgrad = dot_tn(hidden, cotangent).astype(low)
    gate_wgrad = dot_tn(post, gate_act_grad).astype(low)
    up_wgrad = dot_tn(post, up_act_grad).astype(low)
    down_wgrad, gate_wgrad, up_wgrad, post_full = lax.optimization_barrier(
        (down_wgrad, gate_wgrad, up_wgrad, post_full)
    )
    down_wgrad, gate_wgrad, up_wgrad = lax.psum((down_wgrad, gate_wgrad, up_wgrad), "dp")
    scaled_post = post_full * out_gain
    middle_grad = cotangent.astype(wide) + inv_second * (
        scaled_post - unit_second * jnp.mean(scaled_post * unit_second, -1, keepdims=True)
    )
    branch_grad = middle_grad.astype(low)
    mixed_grad = dot_nt(branch_grad, mixer_out)
    mixer_gain_part = jnp.sum(mixed_grad * gated * inv_gate, 0, keepdims=True)
    weighted = mixed_grad * mixer_scale
    cross = pair_sum(jnp.sum(weighted * gated, -1))[:, None]
    attnout_part = dot_tn(attended, branch_grad).astype(low)
    mixout_part = dot_tn(mixed, branch_grad).astype(low)
    attended_grad = dot_nt(branch_grad, attnout_weight).astype(low)
    gated_grad = inv_gate * weighted - gated * (inv_gate * inv_gate * inv_gate) * cross / DSSM
    ssm_grad = gated_grad * gate_act
    gating_grad = (
        gated_grad * ssm_out * sigma_gate * (1.0 + gating * (1.0 - sigma_gate))
    ).astype(low)
    gating_part = dot_tn(normed, gating_grad).astype(low)
    early = jnp.concatenate(
        [jnp.concatenate([attnout_part, mixout_part], 0), gating_part], 1
    )
    early, ssm_grad = lax.optimization_barrier((early, ssm_grad))
    act_grad, step_grad, coef_grad, rate_sum, skip_sum = scan_back_call(
        step, coef, inner_act, aux, seg_row, rate_wide, skip_row, ssm_grad, kept
    )
    step_total = step_grad * jax.nn.sigmoid(step_arg)
    inner_pre_grad = act_grad * silu_slope(inner_pre)
    inner_grad, conv_inner_sums = conv_rows_back(inner_pre_grad, inner, conv_inner, keeps)
    state_pre_grad = coef_grad * silu_slope(state_pre)
    state_grad, conv_state_sums = conv_rows_back(state_pre_grad, state_in, conv_state, keeps)
    scan_cat = jnp.concatenate(
        [inner_grad.astype(low), step_total.astype(low), state_grad.astype(low)], 1
    )
    scan_part = dot_tn(normed, scan_cat).astype(low)
    early_total = gather_rows(scatter_sum(early))
    scan_part, attended_grad = lax.optimization_barrier((scan_part, attended_grad))
    query_grad, keyval_grad = attend_back_call(
        queries, both, seg_row, aux, cosine, sine, logs, attended, attended_grad
    )
    attend_cat = jnp.concatenate([query_grad, keyval_grad], 1)
    attend_part = dot_tn(normed, attend_cat).astype(low)
    weight_cat = jnp.concatenate(
        [gating_weight, inner_weight, step_weight_wide, state_weight, query_weight, keyval_weight], 1
    )
    normed_part = dot_nt(jnp.concatenate([gating_grad, scan_cat, attend_cat], 1), weight_cat)
    input_gain_part = jnp.sum(normed_part * unit_first, 0, keepdims=True)
    normed_full = pair_sum(normed_part.astype(low))

    own_rows = [
        *conv_inner_sums,
        jnp.sum(inner_pre_grad, 0, keepdims=True),
        mixer_gain_part,
        skip_sum,
        jnp.sum(step_total, 0, keepdims=True),
        rate_sum * rate_wide,
    ]
    shared_rows = [
        input_gain_part,
        post_gain_part,
        *conv_state_sums,
        jnp.sum(state_pre_grad, 0, keepdims=True),
    ]
    small = jnp.concatenate(
        [jnp.pad(row, ((0, 0), (0, model - row.shape[1]))) for row in own_rows + shared_rows], 0
    )
    small_other = lax.ppermute(small, "tensor", [(0, 1), (1, 0)])
    is_shared = lax.broadcasted_iota(jnp.int32, small.shape, 0) >= len(own_rows)
    small = small + jnp.where(is_shared, small_other, 0.0)
    for bit in dp_bits():
        small = small + swap_bit(small, bit)

    scan_piece = scatter_sum(scan_part)
    scan_piece, early_total = lax.optimization_barrier((scan_piece, early_total))
    attend_piece = scatter_sum(attend_part)
    state_at = ssm_width + LANES
    trade = jnp.concatenate([scan_piece[:, state_at:], attend_piece[:, query_width:]], 1)
    other = lax.ppermute(trade, "tensor", [(0, 1), (1, 0)])
    state_cols = state_weight.shape[1]
    state_piece = (
        trade[:, :state_cols].astype(wide) + other[:, :state_cols].astype(wide)
    ).astype(low)
    mine, theirs = trade[:, state_cols:], other[:, state_cols:]
    head_0 = jnp.where(first_device, mine, theirs)
    head_1 = jnp.where(first_device, theirs, mine)
    scan_total = gather_rows(jnp.concatenate([scan_piece[:, :state_at], state_piece], 1))
    attend_total = gather_rows(
        jnp.concatenate(
            [
                attend_piece[:, :query_width],
                head_0[:, :HEAD_SIZE],
                head_1[:, :HEAD_SIZE],
                head_0[:, HEAD_SIZE:],
                head_1[:, HEAD_SIZE:],
            ],
            1,
        )
    )

    scaled_in = normed_full * in_gain
    tokens_grad = middle_grad + inv_first * (
        scaled_in - unit_first * jnp.mean(scaled_in * unit_first, -1, keepdims=True)
    )
    count = len(own_rows)
    taps = conv_inner.shape[0]
    return (
        tokens_grad,
        small[count],
        attend_total[:, :query_width].astype(wide),
        attend_total[:, query_width:].astype(wide),
        early_total[:query_width, :model].astype(wide),
        early_total[:, model:].astype(wide),
        scan_total[:, :ssm_width].astype(wide),
        scan_total[:, state_at:].astype(wide),
        scan_total[:, ssm_width : ssm_width + ssm_heads].astype(wide),
        small[:taps, :ssm_width],
        small[count + 2 : count + 2 + taps, :state_cols],
        small[taps, :ssm_width],
        small[count + 2 + taps, :state_cols],
        small[taps + 3, :ssm_heads],
        small[taps + 4, :ssm_heads],
        jnp.sum(small[taps + 2, :ssm_width].reshape(ssm_heads, P_SIZE), 1),
        small[taps + 1, :ssm_width],
        early_total[query_width:, :model].astype(wide),
        small[count + 1],
        gate_wgrad.astype(wide),
        up_wgrad.astype(wide),
        down_wgrad.astype(wide),
    )


def layer(*arrays):
    tokens, segments, query_weight, step_weight = arrays[0], arrays[1], arrays[4], arrays[10]
    size = lax.axis_size("dp")
    fits = (
        lax.axis_size("tensor") == 2
        and size & (size - 1) == 0
        and segments.shape[0] == 1
        and tokens.shape[0] % CHUNK == 0
        and tokens.shape[1] % (16 * size) == 0
        and query_weight.shape[1] == QUERY_HEADS // KEYVALUE_HEADS * HEAD_SIZE
        and KEYVALUE_HEADS == 2
        and step_weight.shape[1] % 2 == 0
        and query_weight.shape[1] + step_weight.shape[1] * P_SIZE == tokens.shape[1]
    )
    return local_fast(*arrays) if fits else local(*arrays)


def solution(mesh):
    placed = (
        P("dp", None),
        P("dp", None),
        P("dp", None),
        P(),
        P(None, "tensor"),
        P(),
        P("tensor", None),
        P(None, "tensor"),
        P(None, "tensor"),
        P(),
        P(None, "tensor"),
        P(None, "tensor"),
        P(),
        P("tensor"),
        P(),
        P("tensor"),
        P("tensor"),
        P("tensor"),
        P("tensor"),
        P("tensor", None),
        P(),
        P(None, "tensor"),
        P(None, "tensor"),
        P("tensor", None),
    )
    return jax.shard_map(
        layer,
        mesh=mesh,
        in_specs=placed,
        out_specs=(
            P("dp", None),
            P(),
            P(None, "tensor"),
            P(),
            P("tensor", None),
            P(None, "tensor"),
            P(None, "tensor"),
            P(),
            P(None, "tensor"),
            P(None, "tensor"),
            P(),
            P("tensor"),
            P(),
            P("tensor"),
            P("tensor"),
            P("tensor"),
            P("tensor"),
            P("tensor", None),
            P(),
            P(None, "tensor"),
            P(None, "tensor"),
            P("tensor", None),
        ),
        check_vma=False,
    )
```

```python
import jax
import jax.numpy as jnp
from jax import lax
from jax.experimental.layout import Layout, with_layout_constraint
from jax.experimental import pallas as pl
from jax.experimental.pallas import tpu as pltpu
from jax.sharding import PartitionSpec as P

QUERY_HEADS = 8
KEYVALUE_HEADS = 2
HEAD_SIZE = 64
P_SIZE = 64
NS = 128
DSSM = 1536


EPS = 1e-05
ROPE_BASE = 100000000000.0
NEG_FILL = -1e30


def matmul(left, right):
    return jnp.dot(left, right, preferred_element_type=jnp.float32)


def rotary_tables(document_length):
    half = HEAD_SIZE // 2
    freqs = jnp.exp(-jnp.log(ROPE_BASE) * (2.0 * jnp.arange(half, dtype=jnp.float32) / HEAD_SIZE))
    angles = jnp.arange(document_length, dtype=jnp.float32)[:, None] * freqs[None, :]
    return (jnp.cos(angles), jnp.sin(angles))


def rotate(value, cosine, sine):
    half = value.shape[-1] // 2
    first = value[..., :half]
    second = value[..., half:]
    return jnp.concatenate([first * cosine - second * sine, first * sine + second * cosine], -1)


def rotate_back(grad, cosine, sine):
    half = grad.shape[-1] // 2
    first = grad[..., :half]
    second = grad[..., half:]
    return jnp.concatenate([first * cosine + second * sine, second * cosine - first * sine], -1)


def silu_slope(value):
    sigma = jax.nn.sigmoid(value)
    return sigma * (1.0 + value * (1.0 - sigma))


def seg_keep(segments, offset):
    document_length = segments.shape[1]
    moved = jnp.pad(segments, ((0, 0), (offset, 0)), constant_values=-1)[:, :document_length]
    return (moved == segments).astype(jnp.float32)[:, :, None]


def move_down(value, offset):
    document_length = value.shape[1]
    return jnp.pad(value, ((0, 0), (offset, 0), (0, 0)))[:, :document_length]


def move_up(value, offset):
    return jnp.pad(value, ((0, 0), (0, offset), (0, 0)))[:, offset:]


def conv_forward(value, kernel, bias, segments):
    taps = kernel.shape[0]
    total = jnp.zeros_like(value) + bias.astype(jnp.float32)
    for tap in range(taps):
        offset = taps - 1 - tap
        total = total + kernel[tap].astype(jnp.float32) * move_down(value, offset) * seg_keep(
            segments, offset
        )
    return total


def conv_backward(grad, value, kernel, segments):
    taps = kernel.shape[0]
    grad_in = jnp.zeros_like(value)
    kernel_rows = []
    for tap in range(taps):
        offset = taps - 1 - tap
        masked = grad * seg_keep(segments, offset)
        kernel_rows.append(jnp.sum(masked * move_down(value, offset), axis=(0, 1)))
        grad_in = grad_in + kernel[tap].astype(jnp.float32) * move_up(masked, offset)
    return (grad_in, jnp.stack(kernel_rows))


def ssd_parts(step_block, rate, coef_b, coef_c, heads_block, allowed):
    coupling = jnp.einsum("tn,sn->ts", coef_c, coef_b, preferred_element_type=jnp.float32)
    cumulative = jnp.cumsum(step_block * rate, axis=0).T
    difference = cumulative[:, :, None] - cumulative[:, None, :]
    decay = jnp.where(allowed[None], jnp.exp(jnp.where(allowed[None], difference, 0.0)), 0.0)
    mixing = (coupling[None] * decay).astype(jnp.bfloat16)
    driven = (heads_block * step_block.T[:, :, None]).astype(jnp.bfloat16)
    return (coupling, decay, mixing, driven)


def pair_sum(value):
    if lax.axis_size("tensor") == 2:
        other = lax.ppermute(value, "tensor", [(0, 1), (1, 0)])
        return value.astype(jnp.float32) + other.astype(jnp.float32)
    return lax.psum(value, "tensor").astype(jnp.float32)


def swap_bit(value, bit):
    size = lax.axis_size("dp")
    return lax.ppermute(value, "dp", [(i, i ^ bit) for i in range(size)])


def shared_sum(rows, first_shared):
    tail = pair_sum(rows[:, first_shared:]).astype(rows.dtype)
    return jnp.concatenate([rows[:, :first_shared], tail], 1) if first_shared else tail


def tree_sum(value, first_shared=None):
    size = lax.axis_size("dp")
    rows = value.shape[0]
    if size & (size - 1) or rows % (16 * size):
        total = lax.psum(value, "dp")
        return total if first_shared is None else shared_sum(total, first_shared)
    bits = [1 << i for i in range(size.bit_length() - 1)]
    me = lax.axis_index("dp")
    for bit in bits:
        half = value.shape[0] // 2
        low, high = value[:half], value[half:]
        upper = (me & bit) != 0
        got = swap_bit(jnp.where(upper, low, high), bit)
        kept = jnp.where(upper, high, low)
        value = (kept.astype(jnp.float32) + got.astype(jnp.float32)).astype(value.dtype)
    if first_shared is not None:
        value = shared_sum(value, first_shared)
    for bit in reversed(bits):
        upper = (me & bit) != 0
        got = swap_bit(value, bit)
        value = jnp.where(
            upper, jnp.concatenate([got, value], 0), jnp.concatenate([value, got], 0)
        )
    return value


def local(
    tokens,
    segments,
    cotangent,
    input_gain,
    query_weight,
    key_value_weight,
    attnout_weight,
    gating_weight,
    inner_weight,
    state_weight,
    step_weight,
    conv_inner,
    conv_state,
    inner_bias,
    state_bias,
    step_bias,
    decay_log,
    skip_scale,
    mixer_gain,
    mixer_out,
    post_gain,
    gate_weight,
    up_weight,
    down_weight,
):
    seq_count, document_length = segments.shape
    rows = seq_count * document_length
    heads = query_weight.shape[1] // HEAD_SIZE
    ssm_heads = step_weight.shape[1]
    query_group = QUERY_HEADS // KEYVALUE_HEADS
    shared_key_head = lax.axis_index("tensor") * heads // query_group
    scale = HEAD_SIZE ** (-0.5)
    cosine, sine = rotary_tables(document_length)
    positions = jnp.arange(document_length)

    def allowed_of(seg_ids):
        return (positions[:, None] >= positions[None, :]) & (seg_ids[:, None] == seg_ids[None, :])

    inputs = tokens.astype(jnp.float32)
    inv_first = lax.rsqrt(jnp.mean(inputs * inputs, -1, keepdims=True) + EPS)
    unit_first = inputs * inv_first
    in_gain = input_gain.astype(jnp.float32)
    normed = (unit_first * in_gain).astype(jnp.bfloat16)
    key_cols = lax.dynamic_slice_in_dim(key_value_weight, shared_key_head * HEAD_SIZE, HEAD_SIZE, 1)
    value_columns = lax.dynamic_slice_in_dim(
        key_value_weight, (KEYVALUE_HEADS + shared_key_head) * HEAD_SIZE, HEAD_SIZE, 1
    )
    query_pre = matmul(normed, query_weight)
    key_pre = matmul(normed, key_cols)
    value_pre = matmul(normed, value_columns)
    queries = rotate(
        query_pre.reshape(seq_count, document_length, heads, HEAD_SIZE).transpose(0, 2, 1, 3),
        cosine,
        sine,
    ).astype(jnp.bfloat16)
    key_rows = rotate(key_pre.reshape(seq_count, document_length, HEAD_SIZE), cosine, sine).astype(
        jnp.bfloat16
    )
    value_rows = value_pre.reshape(seq_count, document_length, HEAD_SIZE).astype(jnp.bfloat16)

    def attend(seq_item):
        query_block, key_block, value_block, seg_ids = seq_item
        allowed = allowed_of(seg_ids)[None]
        scores = (
            jnp.einsum("htd,sd->hts", query_block, key_block, preferred_element_type=jnp.float32)
            * scale
        )
        scores = jnp.where(allowed, scores, NEG_FILL)
        top = jnp.max(scores, -1, keepdims=True)
        weights = jnp.exp(scores - top)
        total = jnp.sum(weights, -1, keepdims=True)
        probs = (weights / total).astype(jnp.bfloat16)
        attended = jnp.einsum("hts,sd->htd", probs, value_block, preferred_element_type=jnp.float32)
        return (attended.astype(jnp.bfloat16), (top + jnp.log(total))[..., 0])

    attended, logsum = lax.map(attend, (queries, key_rows, value_rows, segments))
    attn_flat = attended.transpose(0, 2, 1, 3).reshape(rows, heads * HEAD_SIZE)
    attn_part = matmul(attn_flat, attnout_weight)
    gating = matmul(normed, gating_weight)
    inner = matmul(normed, inner_weight).reshape(seq_count, document_length, -1)
    state_in = matmul(normed, state_weight).reshape(seq_count, document_length, -1)
    step_raw = matmul(normed, step_weight)
    inner_pre = conv_forward(inner, conv_inner, inner_bias, segments)
    inner_act = jax.nn.silu(inner_pre)
    state_pre = conv_forward(state_in, conv_state, state_bias, segments)
    state_act = jax.nn.silu(state_pre)
    coef_b = state_act[..., :NS].astype(jnp.bfloat16)
    coef_c = state_act[..., NS:].astype(jnp.bfloat16)
    step_arg = step_raw.reshape(seq_count, document_length, ssm_heads) + step_bias.astype(
        jnp.float32
    )
    step = jax.nn.softplus(step_arg)
    rate = -jnp.exp(decay_log.astype(jnp.float32))
    heads_in = inner_act.reshape(seq_count, document_length, ssm_heads, P_SIZE).transpose(
        0, 2, 1, 3
    )

    def scan_forward(seq_item):
        step_block, coef_b_block, coef_c_block, heads_block, seg_ids = seq_item
        parts = ssd_parts(
            step_block, rate, coef_b_block, coef_c_block, heads_block, allowed_of(seg_ids)
        )
        return jnp.einsum("hts,hsp->htp", parts[2], parts[3], preferred_element_type=jnp.float32)

    core = lax.map(scan_forward, (step, coef_b, coef_c, heads_in, segments))
    skip = skip_scale.astype(jnp.float32)[None, :, None, None]
    ssm_out = (core + skip * heads_in).transpose(0, 2, 1, 3).reshape(rows, ssm_heads * P_SIZE)
    sigma_gate = jax.nn.sigmoid(gating)
    gate_act = gating * sigma_gate
    gated = ssm_out * gate_act
    square_sum = pair_sum(jnp.sum(gated * gated, -1))[:, None]
    inv_gate = lax.rsqrt(square_sum / DSSM + EPS)
    mixer_scale = mixer_gain.astype(jnp.float32)
    mixed = (gated * inv_gate * mixer_scale).astype(jnp.bfloat16)
    branch_part = attn_part + matmul(mixed, mixer_out)
    out_gain = post_gain.astype(jnp.float32)
    branch = pair_sum(branch_part.astype(jnp.bfloat16))
    middle = inputs + branch
    inv_second = lax.rsqrt(jnp.mean(middle * middle, -1, keepdims=True) + EPS)
    unit_second = middle * inv_second
    post = (unit_second * out_gain).astype(jnp.bfloat16)
    gate = matmul(post, gate_weight)
    upward = matmul(post, up_weight)
    sigma = jax.nn.sigmoid(gate)
    hidden = (gate * sigma * upward).astype(jnp.bfloat16)
    down_wgrad = jnp.einsum("tf,td->fd", hidden, cotangent, preferred_element_type=jnp.float32)
    hidden_grad = jnp.einsum(
        "td,fd->tf", cotangent, down_weight, preferred_element_type=jnp.float32
    )
    up_act_grad = (hidden_grad * gate * sigma).astype(jnp.bfloat16)
    gate_act_grad = (hidden_grad * upward * sigma * (1.0 + gate * (1.0 - sigma))).astype(
        jnp.bfloat16
    )
    gate_wgrad = jnp.einsum("tc,tf->cf", post, gate_act_grad, preferred_element_type=jnp.float32)
    up_wgrad = jnp.einsum("tc,tf->cf", post, up_act_grad, preferred_element_type=jnp.float32)
    post_part = jnp.einsum(
        "tf,cf->tc", gate_act_grad, gate_weight, preferred_element_type=jnp.float32
    ) + jnp.einsum("tf,cf->tc", up_act_grad, up_weight, preferred_element_type=jnp.float32)
    post_gain_part = jnp.sum(post_part * unit_second, 0)
    post_full = pair_sum(post_part.astype(jnp.bfloat16))
    down_wgrad, gate_wgrad, up_wgrad, post_full = lax.optimization_barrier(
        (
            down_wgrad.astype(jnp.bfloat16),
            gate_wgrad.astype(jnp.bfloat16),
            up_wgrad.astype(jnp.bfloat16),
            post_full,
        )
    )
    down_wgrad, gate_wgrad, up_wgrad = lax.psum((down_wgrad, gate_wgrad, up_wgrad), "dp")
    scaled_post = post_full * out_gain
    middle_grad = cotangent.astype(jnp.float32) + inv_second * (
        scaled_post - unit_second * jnp.mean(scaled_post * unit_second, -1, keepdims=True)
    )
    branch_grad = middle_grad.astype(jnp.bfloat16)
    attnout_wgrad = jnp.einsum(
        "tk,td->kd", attn_flat, branch_grad, preferred_element_type=jnp.float32
    )
    attended_grad = jnp.einsum(
        "td,kd->tk", branch_grad, attnout_weight, preferred_element_type=jnp.float32
    )
    attended_grad = (
        attended_grad.astype(jnp.bfloat16)
        .reshape(seq_count, document_length, heads, HEAD_SIZE)
        .transpose(0, 2, 1, 3)
    )

    def attend_back(seq_item):
        query_block, key_block, value_block, seg_ids, logsum_block, grad_block = seq_item
        allowed = allowed_of(seg_ids)[None]
        scores = (
            jnp.einsum("htd,sd->hts", query_block, key_block, preferred_element_type=jnp.float32)
            * scale
        )
        probs = jnp.where(allowed, jnp.exp(scores - logsum_block[..., None]), 0.0)
        value_grad = jnp.einsum(
            "hts,htd->hsd",
            probs.astype(jnp.bfloat16),
            grad_block,
            preferred_element_type=jnp.float32,
        )
        prob_grad = jnp.einsum(
            "htd,sd->hts", grad_block, value_block, preferred_element_type=jnp.float32
        )
        delta = jnp.sum(probs * prob_grad, -1, keepdims=True)
        score_grad = (probs * (prob_grad - delta)).astype(jnp.bfloat16)
        query_grad = (
            jnp.einsum("hts,sd->htd", score_grad, key_block, preferred_element_type=jnp.float32)
            * scale
        )
        key_grad = (
            jnp.einsum("hts,htd->hsd", score_grad, query_block, preferred_element_type=jnp.float32)
            * scale
        )
        return (query_grad, key_grad, value_grad)

    query_rot_grad, key_rot_grad, value_head_grad = lax.map(
        attend_back, (queries, key_rows, value_rows, segments, logsum, attended_grad)
    )
    query_pre_grad = (
        rotate_back(query_rot_grad, cosine, sine)
        .astype(jnp.bfloat16)
        .transpose(0, 2, 1, 3)
        .reshape(rows, heads * HEAD_SIZE)
    )
    key_pre_grad = rotate_back(key_rot_grad, cosine, sine).astype(jnp.bfloat16)
    value_pre_grad = value_head_grad.astype(jnp.bfloat16)
    normed_seq = normed.reshape(seq_count, document_length, -1)
    query_wgrad = jnp.einsum(
        "tc,tk->ck", normed, query_pre_grad, preferred_element_type=jnp.float32
    )
    key_wgrad = jnp.einsum(
        "slc,shld->cd", normed_seq, key_pre_grad, preferred_element_type=jnp.float32
    )
    value_weight_grad = jnp.einsum(
        "slc,shld->cd", normed_seq, value_pre_grad, preferred_element_type=jnp.float32
    )
    normed_part = (
        jnp.einsum("tk,ck->tc", query_pre_grad, query_weight, preferred_element_type=jnp.float32)
        + jnp.einsum(
            "shld,cd->slc", key_pre_grad, key_cols, preferred_element_type=jnp.float32
        ).reshape(rows, -1)
        + jnp.einsum(
            "shld,cd->slc", value_pre_grad, value_columns, preferred_element_type=jnp.float32
        ).reshape(rows, -1)
    )
    mixout_wgrad = jnp.einsum("tk,td->kd", mixed, branch_grad, preferred_element_type=jnp.float32)
    mixed_grad = jnp.einsum("td,kd->tk", branch_grad, mixer_out, preferred_element_type=jnp.float32)
    mixer_gain_wgrad = jnp.sum(mixed_grad * gated * inv_gate, 0)
    weighted = mixed_grad * mixer_scale
    cross = pair_sum(jnp.sum(weighted * gated, -1))[:, None]
    gated_grad = inv_gate * weighted - gated * (inv_gate * inv_gate * inv_gate) * cross / DSSM
    ssm_grad = gated_grad * gate_act
    gating_act_grad = (
        gated_grad * ssm_out * sigma_gate * (1.0 + gating * (1.0 - sigma_gate))
    ).astype(jnp.bfloat16)
    ssm_heads_grad = ssm_grad.reshape(seq_count, document_length, ssm_heads, P_SIZE).transpose(
        0, 2, 1, 3
    )
    core_grad = ssm_heads_grad.astype(jnp.bfloat16)
    skip_wgrad = jnp.sum(ssm_heads_grad * heads_in, axis=(0, 2, 3))

    def scan_back(seq_item):
        step_block, coef_b_block, coef_c_block, heads_block, seg_ids, core_block = seq_item
        coupling, decay, mixing, driven = ssd_parts(
            step_block, rate, coef_b_block, coef_c_block, heads_block, allowed_of(seg_ids)
        )
        mix_grad = jnp.einsum(
            "htp,hsp->hts", core_block, driven, preferred_element_type=jnp.float32
        )
        driven_grad = jnp.einsum(
            "hts,htp->hsp", mixing, core_block, preferred_element_type=jnp.float32
        )
        rounded = (mix_grad * decay).astype(jnp.bfloat16)
        coef_c_grad = jnp.einsum(
            "hts,sn->tn", rounded, coef_b_block, preferred_element_type=jnp.float32
        )
        coef_b_grad = jnp.einsum(
            "hts,tn->sn", rounded, coef_c_block, preferred_element_type=jnp.float32
        )
        spread = mix_grad * coupling[None] * decay
        cumulative_grad = jnp.sum(spread, 2) - jnp.sum(spread, 1)
        log_grad = jnp.flip(jnp.cumsum(jnp.flip(cumulative_grad, 1), 1), 1)
        heads_grad = driven_grad * step_block.T[:, :, None]
        step_grad = (jnp.sum(driven_grad * heads_block, -1) + log_grad * rate[:, None]).T
        rate_grad = jnp.sum(log_grad * step_block.T, 1)
        return (heads_grad, step_grad, rate_grad, coef_b_grad, coef_c_grad)

    heads_grad, step_grad, rate_grad, coef_b_grad, coef_c_grad = lax.map(
        scan_back, (step, coef_b, coef_c, heads_in, segments, core_grad)
    )
    heads_total = heads_grad + ssm_heads_grad * skip
    inner_act_grad = heads_total.transpose(0, 2, 1, 3).reshape(seq_count, document_length, -1)
    step_total = step_grad * jax.nn.sigmoid(step_arg)
    step_bias_wgrad = jnp.sum(step_total, axis=(0, 1))
    decay_wgrad = jnp.sum(rate_grad, 0) * rate
    step_raw_grad = step_total.reshape(rows, ssm_heads).astype(jnp.bfloat16)
    inner_pre_grad = inner_act_grad * silu_slope(inner_pre)
    inner_bias_wgrad = jnp.sum(inner_pre_grad, axis=(0, 1))
    inner_grad, conv_inner_wgrad = conv_backward(inner_pre_grad, inner, conv_inner, segments)
    inner_grad = inner_grad.reshape(rows, -1).astype(jnp.bfloat16)
    state_act_grad = jnp.concatenate([coef_b_grad, coef_c_grad], -1)
    state_pre_grad = state_act_grad * silu_slope(state_pre)
    state_bias_wgrad = jnp.sum(state_pre_grad, axis=(0, 1))
    state_grad, conv_state_wgrad = conv_backward(state_pre_grad, state_in, conv_state, segments)
    state_grad = state_grad.reshape(rows, -1).astype(jnp.bfloat16)
    gating_wgrad = jnp.einsum(
        "tc,tk->ck", normed, gating_act_grad, preferred_element_type=jnp.float32
    )
    inner_wgrad = jnp.einsum("tc,tk->ck", normed, inner_grad, preferred_element_type=jnp.float32)
    step_wgrad = jnp.einsum("tc,tk->ck", normed, step_raw_grad, preferred_element_type=jnp.float32)
    state_wgrad = jnp.einsum("tc,tk->ck", normed, state_grad, preferred_element_type=jnp.float32)
    normed_part = (
        normed_part
        + jnp.einsum(
            "tk,ck->tc", gating_act_grad, gating_weight, preferred_element_type=jnp.float32
        )
        + jnp.einsum("tk,ck->tc", inner_grad, inner_weight, preferred_element_type=jnp.float32)
        + jnp.einsum("tk,ck->tc", step_raw_grad, step_weight, preferred_element_type=jnp.float32)
        + jnp.einsum("tk,ck->tc", state_grad, state_weight, preferred_element_type=jnp.float32)
    )
    input_gain_part = jnp.sum(normed_part * unit_first, 0)
    normed_full = pair_sum(normed_part.astype(jnp.bfloat16))
    scaled_in = normed_full * in_gain
    tokens_grad = middle_grad + inv_first * (
        scaled_in - unit_first * jnp.mean(scaled_in * unit_first, -1, keepdims=True)
    )
    low = jnp.bfloat16
    if lax.axis_size("tensor") == 2 and KEYVALUE_HEADS == 2:
        keyval_part = jnp.concatenate([key_wgrad, value_weight_grad], 1)
    else:
        keyval_part = jnp.zeros(key_value_weight.shape, jnp.float32)
        keyval_part = lax.dynamic_update_slice_in_dim(
            keyval_part, key_wgrad, shared_key_head * HEAD_SIZE, 1
        )
        keyval_part = lax.dynamic_update_slice_in_dim(
            keyval_part, value_weight_grad, (KEYVALUE_HEADS + shared_key_head) * HEAD_SIZE, 1
        )
        keyval_part = lax.psum(keyval_part, "tensor")
    first_total = tree_sum(
        jnp.concatenate(
            [query_wgrad.astype(low), keyval_part.astype(low), gating_wgrad.astype(low)], 1
        )
    ).astype(jnp.float32)
    second_total = tree_sum(
        jnp.concatenate([attnout_wgrad.astype(low), mixout_wgrad.astype(low)], 0)
    ).astype(jnp.float32)
    width = query_wgrad.shape[1]
    kv_width = keyval_part.shape[1]
    query_wgrad = first_total[:, :width]
    keyval_part = first_total[:, width : width + kv_width]
    gating_wgrad = first_total[:, width + kv_width :]
    attnout_wgrad = second_total[: heads * HEAD_SIZE]
    mixout_wgrad = second_total[heads * HEAD_SIZE :]
    if lax.axis_size("tensor") == 2 and KEYVALUE_HEADS == 2:
        other = lax.ppermute(keyval_part.astype(low), "tensor", [(0, 1), (1, 0)])
        mine = keyval_part.astype(low)
        is_first = lax.axis_index("tensor") == 0
        head_0 = jnp.where(is_first, mine, other)
        head_1 = jnp.where(is_first, other, mine)
        key_value_weight_grad = jnp.concatenate(
            [
                head_0[:, :HEAD_SIZE],
                head_1[:, :HEAD_SIZE],
                head_0[:, HEAD_SIZE:],
                head_1[:, HEAD_SIZE:],
            ],
            1,
        ).astype(jnp.float32)
    else:
        key_value_weight_grad = keyval_part
    own = [
        step_bias_wgrad,
        decay_wgrad,
        skip_wgrad,
        mixer_gain_wgrad,
        inner_bias_wgrad,
        conv_inner_wgrad.reshape(-1),
    ]
    shared = [input_gain_part, post_gain_part, state_bias_wgrad, conv_state_wgrad.reshape(-1)]

    def columns_of(parts):
        flat = jnp.concatenate(parts)
        count = -(-flat.shape[0] // tokens.shape[1])
        flat = jnp.pad(flat, (0, count * tokens.shape[1] - flat.shape[0]))
        return flat.reshape(count, tokens.shape[1]).T

    def parts_of(columns, parts):
        flat = columns.T.reshape(-1)
        found, at = [], 0
        for part in parts:
            found.append(flat[at : at + part.shape[0]])
            at += part.shape[0]
        return found

    own_columns, shared_columns = columns_of(own), columns_of(shared)
    inner_width = inner_wgrad.shape[1]
    own_width = own_columns.shape[1]
    shared_from = -(-(inner_width + ssm_heads + own_width) // 128) * 128
    pad = shared_from - inner_width - ssm_heads - own_width
    third_total = tree_sum(
        jnp.concatenate(
            [
                inner_wgrad.astype(low),
                step_wgrad.astype(low),
                own_columns.astype(low),
                jnp.zeros((tokens.shape[1], pad), low),
                state_wgrad.astype(low),
                shared_columns.astype(low),
            ],
            1,
        ),
        shared_from,
    ).astype(jnp.float32)
    inner_wgrad = third_total[:, :inner_width]
    step_wgrad = third_total[:, inner_width : inner_width + ssm_heads]
    at = inner_width + ssm_heads
    (
        step_bias_wgrad,
        decay_wgrad,
        skip_wgrad,
        mixer_gain_wgrad,
        inner_bias_wgrad,
        conv_inner_flat,
    ) = parts_of(third_total[:, at : at + own_width], own)
    conv_inner_wgrad = conv_inner_flat.reshape(conv_inner.shape)
    state_width = state_wgrad.shape[1]
    state_wgrad = third_total[:, shared_from : shared_from + state_width]
    input_gain_part, post_gain_part, state_bias_wgrad, conv_state_flat = parts_of(
        third_total[:, shared_from + state_width :], shared
    )
    conv_state_wgrad = conv_state_flat.reshape(conv_state.shape)
    down_wgrad = down_wgrad.astype(jnp.float32)
    gate_wgrad = gate_wgrad.astype(jnp.float32)
    up_wgrad = up_wgrad.astype(jnp.float32)
    return (
        tokens_grad,
        input_gain_part,
        query_wgrad,
        key_value_weight_grad,
        attnout_wgrad,
        gating_wgrad,
        inner_wgrad,
        state_wgrad,
        step_wgrad,
        conv_inner_wgrad,
        conv_state_wgrad,
        inner_bias_wgrad,
        state_bias_wgrad,
        step_bias_wgrad,
        decay_wgrad,
        skip_wgrad,
        mixer_gain_wgrad,
        mixout_wgrad,
        post_gain_part,
        gate_wgrad,
        up_wgrad,
        down_wgrad,
    )


CHUNK = 256
LANES = 128
VMEM_BYTES = 56 * 1024 * 1024


def dot_nn(left, right):
    return lax.dot_general(left, right, (((1,), (0,)), ((), ())), preferred_element_type=jnp.float32)


def dot_nt(left, right):
    return lax.dot_general(left, right, (((1,), (1,)), ((), ())), preferred_element_type=jnp.float32)


def dot_tn(left, right):
    return lax.dot_general(left, right, (((0,), (0,)), ((), ())), preferred_element_type=jnp.float32)


def split_two(value):
    high = value.astype(jnp.bfloat16)
    return high, (value - high.astype(jnp.float32)).astype(jnp.bfloat16)


def exact_nn(ones, value):
    high, low = split_two(value)
    return dot_nn(ones, high) + dot_nn(ones, low)


def grid_of(shape):
    return (
        lax.broadcasted_iota(jnp.int32, shape, 0),
        lax.broadcasted_iota(jnp.int32, shape, 1),
    )


def pick(columns, pair):
    rows = columns.shape[0]
    left = jnp.broadcast_to(columns[:, 2 * pair : 2 * pair + 1], (rows, LANES))
    right = jnp.broadcast_to(columns[:, 2 * pair + 1 : 2 * pair + 2], (rows, LANES))
    return jnp.where(grid_of((rows, LANES))[1] < P_SIZE, left, right)


def scan_terms(step, rate, aux):
    row, col = grid_of((CHUNK, CHUNK))
    lower = (row >= col).astype(jnp.bfloat16)
    cumulative = exact_nn(lower, step * rate)
    last = cumulative[CHUNK - 1 : CHUNK]
    enter = jnp.exp(cumulative) * aux[:, 1:2]
    leave = jnp.exp(last - cumulative) * aux[:, 2:3]
    across = jnp.exp(last) * aux[CHUNK - 1 : CHUNK, 1:2]
    return cumulative, enter, leave, across


def scan_kernel(step_ref, coef_ref, act_ref, aux_ref, seg_ref, rate_ref, core_ref, kept_ref, state, moved):
    @pl.when(pl.program_id(0) == 0)
    def _():
        state[...] = jnp.zeros_like(state)

    step = step_ref[...]
    aux = aux_ref[...]
    cumulative, enter, leave, across = scan_terms(step, rate_ref[...], aux)
    cum_rows = cumulative.T
    row, col = grid_of((CHUNK, CHUNK))
    blocked = jnp.where((row >= col) & (aux[:, 0:1] == seg_ref[...]), 0.0, NEG_FILL)
    coef_b = coef_ref[:, :NS]
    coef_c = coef_ref[:, NS:]
    coupling = dot_nt(coef_c, coef_b)
    low_state = state[...].astype(jnp.bfloat16)
    kept_ref[0] = low_state
    carried = dot_nn(coef_c, low_state)
    first = grid_of((CHUNK, LANES))[1] < P_SIZE
    for pair in range(act_ref.shape[1] // LANES):
        at = slice(pair * LANES, (pair + 1) * LANES)
        driven = (act_ref[:, at] * pick(step, pair)).astype(jnp.bfloat16)
        parts = []
        for head in (2 * pair, 2 * pair + 1):
            decay = jnp.exp(cumulative[:, head : head + 1] - cum_rows[head : head + 1] + blocked)
            parts.append(dot_nn((coupling * decay).astype(jnp.bfloat16), driven))
        core_ref[:, at] = jnp.where(first, parts[0], parts[1]) + carried[:, at] * pick(enter, pair)
        moved[:, at] = (driven.astype(jnp.float32) * pick(leave, pair)).astype(jnp.bfloat16)
    fresh = dot_tn(coef_b, moved[...])
    for pair in range(act_ref.shape[1] // LANES):
        at = slice(pair * LANES, (pair + 1) * LANES)
        state[:, at] = state[:, at] * pick(across, pair) + fresh[:, at]


def scan_call(step, coef, act, aux, seg_row, rate):
    rows, width = act.shape
    chunks = rows // CHUNK
    by_chunk = lambda columns: pl.BlockSpec((CHUNK, columns), lambda i: (i, 0))
    return pl.pallas_call(
        scan_kernel,
        grid=(chunks,),
        in_specs=[
            by_chunk(LANES),
            by_chunk(2 * NS),
            by_chunk(width),
            by_chunk(LANES),
            pl.BlockSpec((1, CHUNK), lambda i: (0, i)),
            pl.BlockSpec((1, LANES), lambda i: (0, 0)),
        ],
        out_specs=[by_chunk(width), pl.BlockSpec((1, NS, width), lambda i: (i, 0, 0))],
        out_shape=[
            jax.ShapeDtypeStruct((rows, width), jnp.float32),
            jax.ShapeDtypeStruct((chunks, NS, width), jnp.bfloat16),
        ],
        scratch_shapes=[
            pltpu.VMEM((NS, width), jnp.float32),
            pltpu.VMEM((CHUNK, width), jnp.bfloat16),
        ],
        compiler_params=pltpu.CompilerParams(vmem_limit_bytes=VMEM_BYTES),
        name="scan_forward",
    )(step, coef, act, aux, seg_row, rate)


def scan_back_kernel(
    step_ref,
    coef_ref,
    act_ref,
    aux_ref,
    seg_ref,
    rate_ref,
    skip_ref,
    grad_ref,
    kept_ref,
    act_grad_ref,
    step_grad_ref,
    coef_grad_ref,
    sums_ref,
    skip_sum_ref,
    state_grad,
    moved,
    entered,
    row_sums,
):
    @pl.when(pl.program_id(0) == 0)
    def _():
        state_grad[...] = jnp.zeros_like(state_grad)
        sums_ref[...] = jnp.zeros_like(sums_ref)
        skip_sum_ref[...] = jnp.zeros_like(skip_sum_ref)
        row_sums[...] = jnp.zeros_like(row_sums)

    step = step_ref[...]
    aux = aux_ref[...]
    rate = rate_ref[...]
    cumulative, enter, leave, across = scan_terms(step, rate, aux)
    cum_rows = cumulative.T
    row, col = grid_of((CHUNK, CHUNK))
    blocked = jnp.where((row <= col) & (aux[:, 0:1] == seg_ref[...]), 0.0, NEG_FILL)
    coef_b = coef_ref[:, :NS]
    coef_c = coef_ref[:, NS:]
    coupling = dot_nt(coef_b, coef_c)
    low_state = kept_ref[0]
    carried = dot_nn(coef_c, low_state)
    low_grad = state_grad[...].astype(jnp.bfloat16)
    returned = dot_nn(coef_b, low_grad)
    product = jnp.sum(low_state.astype(jnp.float32) * low_grad.astype(jnp.float32), 0, keepdims=True)
    lane = grid_of((CHUNK, LANES))[1]
    lane_row = grid_of((1, LANES))[1]
    first = lane < P_SIZE
    later = jnp.zeros((CHUNK, LANES), jnp.float32)
    earlier = jnp.zeros((CHUNK, LANES), jnp.float32)
    direct = jnp.zeros((CHUNK, LANES), jnp.float32)
    through = jnp.zeros((1, LANES), jnp.float32)
    coupling_grad = jnp.zeros((CHUNK, CHUNK), jnp.float32)
    for pair in range(act_ref.shape[1] // LANES):
        at = slice(pair * LANES, (pair + 1) * LANES)
        act = act_ref[:, at]
        spread_step = pick(step, pair)
        driven = (act * spread_step).astype(jnp.bfloat16)
        grad = grad_ref[:, at]
        core_grad = grad.astype(jnp.bfloat16)
        core_wide = core_grad.astype(jnp.float32)
        enter_grad = core_wide * pick(enter, pair)
        entered[:, at] = enter_grad.astype(jnp.bfloat16)
        row_part = enter_grad * carried[:, at]
        leave_pair = pick(leave, pair)
        moved[:, at] = (driven.astype(jnp.float32) * leave_pair).astype(jnp.bfloat16)
        back = returned[:, at] * leave_pair
        col_part = back * driven.astype(jnp.float32)
        parts = []
        for head in (2 * pair, 2 * pair + 1):
            mine = first if head % 2 == 0 else ~first
            decay = jnp.exp(cum_rows[head : head + 1] - cumulative[:, head : head + 1] + blocked)
            mix_grad = dot_nt(jnp.where(mine, driven, jnp.zeros_like(driven)), core_grad)
            share = mix_grad * decay
            coupling_grad = coupling_grad + share
            spread = share * coupling
            row_sums[head : head + 1] = jnp.sum(spread, 0, keepdims=True)
            folded = sum(spread[:, k * LANES : (k + 1) * LANES] for k in range(CHUNK // LANES))
            found = jnp.sum(jnp.where(mine, row_part, 0.0) - folded, 1, keepdims=True)
            later = jnp.where(lane == head, found, later)
            parts.append(dot_nn((coupling * decay).astype(jnp.bfloat16), core_grad))
            found = jnp.sum(jnp.where(mine, col_part, 0.0), 1, keepdims=True)
            earlier = jnp.where(lane == head, found, earlier)
        driven_grad = jnp.where(first, parts[0], parts[1]) + back
        act_grad_ref[:, at] = driven_grad * spread_step + grad * skip_ref[:, at]
        skip_sum_ref[:, at] += jnp.sum(grad * act, 0, keepdims=True)
        step_part = driven_grad * act
        product_pair = product[:, at]
        for head in (2 * pair, 2 * pair + 1):
            mine = first if head % 2 == 0 else ~first
            found = jnp.sum(jnp.where(mine, step_part, 0.0), 1, keepdims=True)
            direct = jnp.where(lane == head, found, direct)
            found = jnp.sum(jnp.where(mine[:1], product_pair, 0.0), 1, keepdims=True)
            through = jnp.where(lane_row == head, found, through)
    upper = (row <= col).astype(jnp.bfloat16)
    below = (row > col).astype(jnp.bfloat16)
    high, low = split_two(row_sums[...])
    log_grad = (
        exact_nn(upper, later)
        + dot_nt(upper, high)
        + dot_nt(upper, low)
        + exact_nn(below, earlier)
        + through * across
    )
    step_grad_ref[...] = direct + log_grad * rate
    sums_ref[...] += jnp.sum(log_grad * step, 0, keepdims=True)
    low_coupling = coupling_grad.astype(jnp.bfloat16)
    coef_grad_ref[:, :NS] = dot_nn(low_coupling, coef_c) + dot_nt(moved[...], low_grad)
    coef_grad_ref[:, NS:] = dot_tn(low_coupling, coef_b) + dot_nt(entered[...], low_state)
    fresh = dot_tn(coef_c, entered[...])
    for pair in range(act_ref.shape[1] // LANES):
        at = slice(pair * LANES, (pair + 1) * LANES)
        state_grad[:, at] = state_grad[:, at] * pick(across, pair) + fresh[:, at]


def scan_back_call(step, coef, act, aux, seg_row, rate, skip_row, grad, kept):
    rows, width = act.shape
    chunks = rows // CHUNK
    by_chunk = lambda columns: pl.BlockSpec((CHUNK, columns), lambda i: (chunks - 1 - i, 0))
    one_row = lambda columns: pl.BlockSpec((1, columns), lambda i: (0, 0))
    return pl.pallas_call(
        scan_back_kernel,
        grid=(chunks,),
        in_specs=[
            by_chunk(LANES),
            by_chunk(2 * NS),
            by_chunk(width),
            by_chunk(LANES),
            pl.BlockSpec((1, CHUNK), lambda i: (0, chunks - 1 - i)),
            one_row(LANES),
            one_row(width),
            by_chunk(width),
            pl.BlockSpec((1, NS, width), lambda i: (chunks - 1 - i, 0, 0)),
        ],
        out_specs=[
            by_chunk(width),
            by_chunk(LANES),
            by_chunk(2 * NS),
            one_row(LANES),
            one_row(width),
        ],
        out_shape=[
            jax.ShapeDtypeStruct((rows, width), jnp.float32),
            jax.ShapeDtypeStruct((rows, LANES), jnp.float32),
            jax.ShapeDtypeStruct((rows, 2 * NS), jnp.float32),
            jax.ShapeDtypeStruct((1, LANES), jnp.float32),
            jax.ShapeDtypeStruct((1, width), jnp.float32),
        ],
        scratch_shapes=[
            pltpu.VMEM((NS, width), jnp.float32),
            pltpu.VMEM((CHUNK, width), jnp.bfloat16),
            pltpu.VMEM((CHUNK, width), jnp.bfloat16),
            pltpu.VMEM((LANES, CHUNK), jnp.float32),
        ],
        compiler_params=pltpu.CompilerParams(vmem_limit_bytes=VMEM_BYTES),
        name="scan_backward",
    )(step, coef, act, aux, seg_row, rate, skip_row, grad, kept)


def swap_halves(value):
    width = value.shape[1]
    half = HEAD_SIZE // 2
    up = pltpu.roll(value, width - half, 1)
    down = pltpu.roll(value, half, 1)
    return jnp.where(grid_of(value.shape)[1] % HEAD_SIZE < half, up, down)


def turned(value, cosine, sine):
    return value * cosine + swap_halves(value) * sine


def attend_kernel(query_ref, keyval_ref, seg_ref, seg_col_ref, cos_ref, sin_ref, out_ref, turned_ref, both_ref, log_ref):
    rows = query_ref.shape[0]
    first = grid_of((rows, LANES))[1] < HEAD_SIZE
    keyval = keyval_ref[...]
    moved = pltpu.roll(keyval, HEAD_SIZE, 1)
    keys = turned(jnp.where(first, keyval, moved), cos_ref[...], sin_ref[...]).astype(jnp.bfloat16)
    values = jnp.where(first, moved, keyval).astype(jnp.bfloat16)
    both_ref[:, :LANES] = keys
    both_ref[:, LANES:] = values
    scale = HEAD_SIZE ** (-0.5)
    head_lane = grid_of((CHUNK, LANES))[1]
    first = head_lane < HEAD_SIZE
    for block in range(rows // CHUNK):
        low, high = block * CHUNK, (block + 1) * CHUNK
        row, col = grid_of((CHUNK, high))
        blocked = jnp.where(
            (row + low >= col) & (seg_col_ref[low:high, 0:1] == seg_ref[:, :high]), 0.0, NEG_FILL
        )
        logs = jnp.zeros((CHUNK, LANES), jnp.float32)
        for pair in range(query_ref.shape[1] // LANES):
            at = slice(pair * LANES, (pair + 1) * LANES)
            query = turned(query_ref[low:high, at], cos_ref[low:high], sin_ref[low:high]).astype(
                jnp.bfloat16
            )
            turned_ref[low:high, at] = query
            parts = []
            for head in (2 * pair, 2 * pair + 1):
                mine = first if head % 2 == 0 else ~first
                scores = (
                    dot_nt(jnp.where(mine, query, jnp.zeros_like(query)), keys[:high]) * scale
                    + blocked
                )
                top = jnp.max(scores, 1, keepdims=True)
                weights = jnp.exp(scores - top)
                total = jnp.sum(weights, 1, keepdims=True)
                probs = (weights * (1.0 / total)).astype(jnp.bfloat16)
                parts.append(dot_nn(probs, values[:high]))
                logs = jnp.where(head_lane == head, top + jnp.log(total), logs)
            out_ref[low:high, at] = jnp.where(first, parts[0], parts[1]).astype(jnp.bfloat16)
        log_ref[low:high] = logs


def attend_call(query, keyval, seg_row, aux, cosine, sine):
    rows, width = query.shape
    return pl.pallas_call(
        attend_kernel,
        out_shape=[
            jax.ShapeDtypeStruct((rows, width), jnp.bfloat16),
            jax.ShapeDtypeStruct((rows, width), jnp.bfloat16),
            jax.ShapeDtypeStruct((rows, 2 * LANES), jnp.bfloat16),
            jax.ShapeDtypeStruct((rows, LANES), jnp.float32),
        ],
        compiler_params=pltpu.CompilerParams(vmem_limit_bytes=VMEM_BYTES),
        name="attend_forward",
    )(query, keyval, seg_row, aux, cosine, sine)


def attend_back_kernel(
    query_ref, both_ref, seg_ref, seg_col_ref, cos_ref, sin_ref, log_ref, out_ref, grad_ref,
    query_grad_ref, keyval_grad_ref, key_sum, value_sum,
):
    rows = query_ref.shape[0]
    key_sum[...] = jnp.zeros_like(key_sum)
    value_sum[...] = jnp.zeros_like(value_sum)
    scale = HEAD_SIZE ** (-0.5)
    first = grid_of((CHUNK, LANES))[1] < HEAD_SIZE
    for block in range(rows // CHUNK):
        low, high = block * CHUNK, (block + 1) * CHUNK
        row, col = grid_of((CHUNK, high))
        blocked = jnp.where(
            (row + low >= col) & (seg_col_ref[low:high, 0:1] == seg_ref[:, :high]), 0.0, NEG_FILL
        )
        keys = both_ref[:high, :LANES]
        values = both_ref[:high, LANES:]
        for pair in range(query_ref.shape[1] // LANES):
            at = slice(pair * LANES, (pair + 1) * LANES)
            query = query_ref[low:high, at]
            grad = grad_ref[low:high, at]
            inner = grad.astype(jnp.float32) * out_ref[low:high, at].astype(jnp.float32)
            parts = []
            key_part = None
            for head in (2 * pair, 2 * pair + 1):
                mine = first if head % 2 == 0 else ~first
                query_mine = jnp.where(mine, query, jnp.zeros_like(query))
                grad_mine = jnp.where(mine, grad, jnp.zeros_like(grad))
                scores = dot_nt(query_mine, keys) * scale + blocked
                probs = jnp.exp(scores - log_ref[low:high, head : head + 1])
                delta = jnp.sum(jnp.where(mine, inner, 0.0), 1, keepdims=True)
                prob_grad = dot_nt(grad_mine, values)
                score_grad = (probs * (prob_grad - delta)).astype(jnp.bfloat16)
                parts.append(dot_nn(score_grad, keys) * scale)
                key_sum[:high] += dot_tn(score_grad, query_mine)
                value_sum[:high] += dot_tn(probs.astype(jnp.bfloat16), grad_mine)
            full = jnp.where(first, parts[0], parts[1])
            query_grad_ref[low:high, at] = turned(full, cos_ref[low:high], -sin_ref[low:high]).astype(
                jnp.bfloat16
            )
    wide = grid_of((rows, LANES))[1] < HEAD_SIZE
    key_total = key_sum[...] * scale
    key_total = key_total + pltpu.roll(key_total, HEAD_SIZE, 1)
    key_total = turned(key_total, cos_ref[...], -sin_ref[...])
    value_total = value_sum[...]
    value_total = value_total + pltpu.roll(value_total, HEAD_SIZE, 1)
    keyval_grad_ref[...] = jnp.where(wide, key_total, value_total).astype(jnp.bfloat16)


def attend_back_call(query, both, seg_row, aux, cosine, sine, logs, out, grad):
    rows, width = query.shape
    return pl.pallas_call(
        attend_back_kernel,
        out_shape=[
            jax.ShapeDtypeStruct((rows, width), jnp.bfloat16),
            jax.ShapeDtypeStruct((rows, LANES), jnp.bfloat16),
        ],
        scratch_shapes=[
            pltpu.VMEM((rows, LANES), jnp.float32),
            pltpu.VMEM((rows, LANES), jnp.float32),
        ],
        compiler_params=pltpu.CompilerParams(vmem_limit_bytes=VMEM_BYTES),
        name="attend_backward",
    )(query, both, seg_row, aux, cosine, sine, logs, out, grad)


def halve(value, bit):
    half = value.shape[0] // 2
    upper = (lax.axis_index("dp") & bit) != 0
    got = swap_bit(jnp.where(upper, value[:half], value[half:]), bit)
    kept = jnp.where(upper, value[half:], value[:half])
    return (kept.astype(jnp.float32) + got.astype(jnp.float32)).astype(value.dtype)


def double(value, bit):
    upper = (lax.axis_index("dp") & bit) != 0
    got = swap_bit(value, bit)
    return jnp.concatenate([jnp.where(upper, got, value), jnp.where(upper, value, got)], 0)


def dp_bits():
    size = lax.axis_size("dp")
    return [1 << i for i in range(size.bit_length() - 1)]


def halve_parts(values, bit):
    half = values[0].shape[0] // 2
    upper = (lax.axis_index("dp") & bit) != 0
    got = swap_bit(
        jnp.concatenate([jnp.where(upper, v[:half], v[half:]) for v in values], 1), bit
    )
    kept = jnp.concatenate([jnp.where(upper, v[half:], v[:half]) for v in values], 1)
    return (kept.astype(jnp.float32) + got.astype(jnp.float32)).astype(got.dtype)


def by_rows(value):
    return with_layout_constraint(value, Layout(major_to_minor=(0, 1)))


def tie(*values):
    return lax.optimization_barrier(values)


def conv_rows(value, kernel, bias, keeps):
    taps = kernel.shape[0]
    total = bias.astype(jnp.float32)[None]
    for tap in range(taps):
        offset = taps - 1 - tap
        moved = jnp.pad(value, ((offset, 0), (0, 0)))[: value.shape[0]]
        total = total + kernel[tap].astype(jnp.float32) * moved * keeps[offset]
    return total


def conv_rows_back(grad, value, kernel, keeps):
    taps = kernel.shape[0]
    grad_in = jnp.zeros_like(grad)
    sums = []
    for tap in range(taps):
        offset = taps - 1 - tap
        masked = grad * keeps[offset]
        moved = jnp.pad(value, ((offset, 0), (0, 0)))[: value.shape[0]]
        sums.append(jnp.sum(masked * moved, 0, keepdims=True))
        grad_in = grad_in + kernel[tap].astype(jnp.float32) * jnp.pad(
            masked, ((0, offset), (0, 0))
        )[offset:]
    return grad_in, sums


def local_fast(
    tokens,
    segments,
    cotangent,
    input_gain,
    query_weight,
    key_value_weight,
    attnout_weight,
    gating_weight,
    inner_weight,
    state_weight,
    step_weight,
    conv_inner,
    conv_state,
    inner_bias,
    state_bias,
    step_bias,
    decay_log,
    skip_scale,
    mixer_gain,
    mixer_out,
    post_gain,
    gate_weight,
    up_weight,
    down_weight,
):
    low, wide = jnp.bfloat16, jnp.float32
    rows, model = tokens.shape
    heads = query_weight.shape[1] // HEAD_SIZE
    ssm_heads = step_weight.shape[1]
    ssm_width = ssm_heads * P_SIZE
    query_width = heads * HEAD_SIZE
    first_device = lax.axis_index("tensor") == 0
    pick_head = lambda at: jnp.where(
        first_device,
        key_value_weight[:, at : at + HEAD_SIZE],
        key_value_weight[:, at + HEAD_SIZE : at + 2 * HEAD_SIZE],
    )
    keyval_weight = jnp.concatenate([pick_head(0), pick_head(KEYVALUE_HEADS * HEAD_SIZE)], 1)
    lane_pad = ((0, 0), (0, LANES - ssm_heads))
    step_weight_wide = jnp.pad(step_weight, lane_pad)
    step_bias_wide = jnp.pad(step_bias.astype(wide)[None], lane_pad)
    rate = -jnp.exp(decay_log.astype(wide))
    rate_wide = jnp.pad(rate[None], lane_pad)
    skip_row = jnp.repeat(skip_scale.astype(wide), P_SIZE)[None]
    cosine, sine = rotary_tables(rows)
    cosine = jnp.concatenate([cosine] * 4, 1)
    sine = jnp.concatenate([-sine, sine, -sine, sine], 1)
    seg_row = segments.astype(wide)
    seg_chunks = seg_row.reshape(-1, CHUNK)
    ends = seg_chunks[:, -1:]
    starts = jnp.concatenate([jnp.full((1, 1), -1.0, wide), ends[:-1]], 0)
    aux = jnp.stack(
        [seg_chunks, (seg_chunks == starts).astype(wide), (seg_chunks == ends).astype(wide)], -1
    ).reshape(rows, 3)
    aux = jnp.pad(aux, ((0, 0), (0, LANES - 3)))
    keeps = [seg_keep(segments, offset)[0] for offset in range(conv_inner.shape[0])]

    inputs = by_rows(tokens.astype(wide))
    inv_first = lax.rsqrt(jnp.mean(inputs * inputs, -1, keepdims=True) + EPS)
    unit_first = inputs * inv_first
    in_gain = input_gain.astype(wide)
    normed = by_rows((unit_first * in_gain).astype(low))
    inner = matmul(normed, inner_weight)
    state_in = matmul(normed, state_weight)
    step_arg = matmul(normed, step_weight_wide) + step_bias_wide
    gating = matmul(normed, gating_weight)
    inner_pre = conv_rows(inner, conv_inner, inner_bias, keeps)
    inner_act = jax.nn.silu(inner_pre)
    state_pre = conv_rows(state_in, conv_state, state_bias, keeps)
    coef = jax.nn.silu(state_pre).astype(low)
    step = jax.nn.softplus(step_arg)
    core, kept = scan_call(step, coef, inner_act, aux, seg_row, rate_wide)
    ssm_out = core + skip_row * inner_act
    sigma_gate = jax.nn.sigmoid(gating)
    gate_act = gating * sigma_gate
    gated = ssm_out * gate_act
    square_sum = pair_sum(jnp.sum(gated * gated, -1))[:, None]
    query_pre = matmul(normed, query_weight)
    keyval_pre = matmul(normed, keyval_weight)
    attended, queries, both, logs = attend_call(query_pre, keyval_pre, seg_row, aux, cosine, sine)
    attn_part = matmul(attended, attnout_weight)
    inv_gate = lax.rsqrt(square_sum / DSSM + EPS)
    mixer_scale = mixer_gain.astype(wide)
    mixed = (gated * inv_gate * mixer_scale).astype(low)
    branch_part = attn_part + matmul(mixed, mixer_out)
    out_gain = post_gain.astype(wide)
    branch = by_rows(pair_sum(by_rows(branch_part.astype(low))))
    middle = inputs + branch
    inv_second = lax.rsqrt(jnp.mean(middle * middle, -1, keepdims=True) + EPS)
    unit_second = middle * inv_second
    post = by_rows((unit_second * out_gain).astype(low))
    gate = matmul(post, gate_weight)
    upward = matmul(post, up_weight)
    sigma = jax.nn.sigmoid(gate)
    hidden = (gate * sigma * upward).astype(low)
    hidden_grad = dot_nt(cotangent, down_weight)
    up_act_grad = (hidden_grad * gate * sigma).astype(low)
    gate_act_grad = (hidden_grad * upward * sigma * (1.0 + gate * (1.0 - sigma))).astype(low)
    post_part = dot_nt(gate_act_grad, gate_weight) + dot_nt(up_act_grad, up_weight)
    post_gain_part = jnp.sum(post_part * unit_second, 0, keepdims=True)
    post_full = by_rows(pair_sum(by_rows(post_part.astype(low))))
    down_wgrad = dot_tn(hidden, cotangent).astype(low)
    gate_wgrad = dot_tn(post, gate_act_grad).astype(low)
    up_wgrad = dot_tn(post, up_act_grad).astype(low)
    post_full, _, _, _ = tie(post_full, down_wgrad, gate_wgrad, up_wgrad)
    forward_piece = lax.psum_scatter(
        jnp.concatenate([down_wgrad, gate_wgrad, up_wgrad], 0),
        "dp",
        scatter_dimension=0,
        tiled=True,
    )
    scaled_post = post_full * out_gain
    middle_grad = cotangent.astype(wide) + inv_second * (
        scaled_post - unit_second * jnp.mean(scaled_post * unit_second, -1, keepdims=True)
    )
    branch_grad = by_rows(middle_grad.astype(low))
    mixed_grad = dot_nt(branch_grad, mixer_out)
    mixer_gain_part = jnp.sum(mixed_grad * gated * inv_gate, 0, keepdims=True)
    weighted = mixed_grad * mixer_scale
    cross = pair_sum(jnp.sum(weighted * gated, -1))[:, None]
    out_part = dot_tn(jnp.concatenate([attended, mixed], 1), branch_grad).astype(low)
    out_part = by_rows(out_part)
    attended_grad = dot_nt(branch_grad, attnout_weight).astype(low)
    gated_grad = inv_gate * weighted - gated * (inv_gate * inv_gate * inv_gate) * cross / DSSM
    ssm_grad = gated_grad * gate_act
    gating_grad = (
        gated_grad * ssm_out * sigma_gate * (1.0 + gating * (1.0 - sigma_gate))
    ).astype(low)
    gating_part = by_rows(dot_tn(normed, gating_grad).astype(low))
    bits = dp_bits()
    early = halve_parts([out_part, gating_part], bits[0])
    early, ssm_grad, forward_piece = tie(early, ssm_grad, forward_piece)
    forward_total = lax.all_gather(forward_piece, "dp", axis=0, tiled=True)
    early = halve(early, bits[1])
    act_grad, step_grad, coef_grad, rate_sum, skip_sum = scan_back_call(
        step, coef, inner_act, aux, seg_row, rate_wide, skip_row, ssm_grad, kept
    )
    early, act_grad, step_grad, coef_grad = tie(early, act_grad, step_grad, coef_grad)
    early = halve(early, bits[2])
    step_total = step_grad * jax.nn.sigmoid(step_arg)
    inner_pre_grad = act_grad * silu_slope(inner_pre)
    inner_grad, conv_inner_sums = conv_rows_back(inner_pre_grad, inner, conv_inner, keeps)
    state_pre_grad = coef_grad * silu_slope(state_pre)
    state_grad, conv_state_sums = conv_rows_back(state_pre_grad, state_in, conv_state, keeps)
    scan_cat = jnp.concatenate(
        [inner_grad.astype(low), step_total.astype(low), state_grad.astype(low)], 1
    )
    scan_part = dot_tn(normed, scan_cat).astype(low)
    early, scan_part, attended_grad = tie(early, scan_part, attended_grad)
    early = halve(early, bits[3])
    scan_part = halve(scan_part, bits[0])
    query_grad, keyval_grad = attend_back_call(
        queries, both, seg_row, aux, cosine, sine, logs, attended, attended_grad
    )
    attend_cat = jnp.concatenate([query_grad, keyval_grad], 1)
    attend_part = dot_tn(normed, attend_cat).astype(low)
    early, scan_part, attend_part, attend_cat = tie(early, scan_part, attend_part, attend_cat)
    early = double(early, bits[3])
    scan_part = halve(scan_part, bits[1])
    attend_part = halve(attend_part, bits[0])
    weight_cat = jnp.concatenate(
        [gating_weight, inner_weight, step_weight_wide, state_weight, query_weight, keyval_weight], 1
    )
    normed_part = dot_nt(jnp.concatenate([gating_grad, scan_cat, attend_cat], 1), weight_cat)
    input_gain_part = jnp.sum(normed_part * unit_first, 0, keepdims=True)
    early, scan_part, attend_part, normed_part, input_gain_part = tie(
        early, scan_part, attend_part, normed_part, input_gain_part
    )
    normed_full = by_rows(pair_sum(by_rows(normed_part.astype(low))))
    own_rows = [
        *conv_inner_sums,
        jnp.sum(inner_pre_grad, 0, keepdims=True),
        mixer_gain_part,
        skip_sum,
        jnp.sum(step_total, 0, keepdims=True),
        rate_sum * rate_wide,
    ]
    shared_rows = [
        input_gain_part,
        post_gain_part,
        *conv_state_sums,
        jnp.sum(state_pre_grad, 0, keepdims=True),
    ]
    small = jnp.concatenate(
        [jnp.pad(row, ((0, 0), (0, model - row.shape[1]))) for row in own_rows + shared_rows], 0
    )
    small_other = lax.ppermute(small, "tensor", [(0, 1), (1, 0)])
    is_shared = lax.broadcasted_iota(jnp.int32, small.shape, 0) >= len(own_rows)
    small = small + jnp.where(is_shared, small_other, 0.0)
    early = double(early, bits[2])
    scan_part = halve(scan_part, bits[2])
    attend_part = halve(attend_part, bits[1])
    early, scan_part, attend_part, small, forward_total = tie(
        early, scan_part, attend_part, small, forward_total
    )
    hidden_units = down_weight.shape[0]
    down_wgrad = forward_total[:hidden_units].astype(wide)
    gate_wgrad = forward_total[hidden_units : hidden_units + model].astype(wide)
    up_wgrad = forward_total[hidden_units + model :].astype(wide)
    early = double(early, bits[1])
    scan_part = halve(scan_part, bits[3])
    attend_part = halve(attend_part, bits[2])
    small = small + swap_bit(small, bits[0])
    scan_part, attend_part, small = tie(scan_part, attend_part, small)
    attend_part = halve(attend_part, bits[3])
    small = small + swap_bit(small, bits[1])
    attend_part, small, early = tie(attend_part, small, early)
    small = small + swap_bit(small, bits[2])
    scan_piece, attend_piece = scan_part, attend_part
    state_at = ssm_width + LANES
    trade = jnp.concatenate([scan_piece[:, state_at:], attend_piece[:, query_width:]], 1)
    other = lax.ppermute(trade, "tensor", [(0, 1), (1, 0)])
    state_cols = state_weight.shape[1]
    state_piece = (
        trade[:, :state_cols].astype(wide) + other[:, :state_cols].astype(wide)
    ).astype(low)
    mine, theirs = trade[:, state_cols:], other[:, state_cols:]
    head_0 = jnp.where(first_device, mine, theirs)
    head_1 = jnp.where(first_device, theirs, mine)
    late = jnp.concatenate(
        [
            scan_piece[:, :state_at],
            state_piece,
            attend_piece[:, :query_width],
            head_0[:, :HEAD_SIZE],
            head_1[:, :HEAD_SIZE],
            head_0[:, HEAD_SIZE:],
            head_1[:, HEAD_SIZE:],
        ],
        1,
    )
    late, small = tie(late, small)
    late = double(late, bits[3])
    small = small + swap_bit(small, bits[3])
    late, early, small = tie(late, early, small)
    late = double(late, bits[2])
    early = double(early, bits[0])
    late, early = tie(late, early)
    late = double(late, bits[1])
    early_grads = (
        gate_wgrad,
        up_wgrad,
        down_wgrad,
        early[:query_width, :model].astype(wide),
        early[:, model:].astype(wide),
        early[query_width:, :model].astype(wide),
    )
    scaled_in = normed_full * in_gain
    tokens_grad = middle_grad + inv_first * (
        scaled_in - unit_first * jnp.mean(scaled_in * unit_first, -1, keepdims=True)
    )
    late, tokens_grad, *early_grads = tie(late, tokens_grad, *early_grads)
    late = double(late, bits[0])
    scan_total = late[:, : state_at + state_cols]
    attend_total = late[:, state_at + state_cols :]
    gate_wgrad, up_wgrad, down_wgrad, attnout_grad, gating_wgrad, mixout_grad = early_grads
    count = len(own_rows)
    taps = conv_inner.shape[0]
    return (
        tokens_grad,
        small[count],
        attend_total[:, :query_width].astype(wide),
        attend_total[:, query_width:].astype(wide),
        attnout_grad,
        gating_wgrad,
        scan_total[:, :ssm_width].astype(wide),
        scan_total[:, state_at:].astype(wide),
        scan_total[:, ssm_width : ssm_width + ssm_heads].astype(wide),
        small[:taps, :ssm_width],
        small[count + 2 : count + 2 + taps, :state_cols],
        small[taps, :ssm_width],
        small[count + 2 + taps, :state_cols],
        small[taps + 3, :ssm_heads],
        small[taps + 4, :ssm_heads],
        jnp.sum(small[taps + 2, :ssm_width].reshape(ssm_heads, P_SIZE), 1),
        small[taps + 1, :ssm_width],
        mixout_grad,
        small[count + 1],
        gate_wgrad,
        up_wgrad,
        down_wgrad,
    )


def layer(*arrays):
    tokens, segments, query_weight, step_weight = arrays[0], arrays[1], arrays[4], arrays[10]
    size = lax.axis_size("dp")
    fits = (
        lax.axis_size("tensor") == 2
        and size == 16
        and segments.shape[0] == 1
        and tokens.shape[0] % CHUNK == 0
        and tokens.shape[1] % (16 * size) == 0
        and query_weight.shape[1] == QUERY_HEADS // KEYVALUE_HEADS * HEAD_SIZE
        and KEYVALUE_HEADS == 2
        and arrays[23].shape[0] == tokens.shape[1]
        and step_weight.shape[1] % 2 == 0
        and query_weight.shape[1] + step_weight.shape[1] * P_SIZE == tokens.shape[1]
    )
    return local_fast(*arrays) if fits else local(*arrays)


def solution(mesh):
    placed = (
        P("dp", None),
        P("dp", None),
        P("dp", None),
        P(),
        P(None, "tensor"),
        P(),
        P("tensor", None),
        P(None, "tensor"),
        P(None, "tensor"),
        P(),
        P(None, "tensor"),
        P(None, "tensor"),
        P(),
        P("tensor"),
        P(),
        P("tensor"),
        P("tensor"),
        P("tensor"),
        P("tensor"),
        P("tensor", None),
        P(),
        P(None, "tensor"),
        P(None, "tensor"),
        P("tensor", None),
    )
    return jax.shard_map(
        layer,
        mesh=mesh,
        in_specs=placed,
        out_specs=(
            P("dp", None),
            P(),
            P(None, "tensor"),
            P(),
            P("tensor", None),
            P(None, "tensor"),
            P(None, "tensor"),
            P(),
            P(None, "tensor"),
            P(None, "tensor"),
            P(),
            P("tensor"),
            P(),
            P("tensor"),
            P("tensor"),
            P("tensor"),
            P("tensor"),
            P("tensor", None),
            P(),
            P(None, "tensor"),
            P(None, "tensor"),
            P("tensor", None),
        ),
        check_vma=False,
    )
```

```python
import jax
import jax.numpy as jnp
from jax import lax
from jax.experimental.layout import Layout, with_layout_constraint
from jax.experimental import pallas as pl
from jax.experimental.pallas import tpu as pltpu
from jax.sharding import PartitionSpec as P

QUERY_HEADS = 8
KEYVALUE_HEADS = 2
HEAD_SIZE = 64
P_SIZE = 64
NS = 128
DSSM = 1536


EPS = 1e-05
ROPE_BASE = 100000000000.0
NEG_FILL = -1e30


def matmul(left, right):
    return jnp.dot(left, right, preferred_element_type=jnp.float32)


def rotary_tables(document_length):
    half = HEAD_SIZE // 2
    freqs = jnp.exp(-jnp.log(ROPE_BASE) * (2.0 * jnp.arange(half, dtype=jnp.float32) / HEAD_SIZE))
    angles = jnp.arange(document_length, dtype=jnp.float32)[:, None] * freqs[None, :]
    return (jnp.cos(angles), jnp.sin(angles))


def rotate(value, cosine, sine):
    half = value.shape[-1] // 2
    first = value[..., :half]
    second = value[..., half:]
    return jnp.concatenate([first * cosine - second * sine, first * sine + second * cosine], -1)


def rotate_back(grad, cosine, sine):
    half = grad.shape[-1] // 2
    first = grad[..., :half]
    second = grad[..., half:]
    return jnp.concatenate([first * cosine + second * sine, second * cosine - first * sine], -1)


def silu_slope(value):
    sigma = jax.nn.sigmoid(value)
    return sigma * (1.0 + value * (1.0 - sigma))


def seg_keep(segments, offset):
    document_length = segments.shape[1]
    moved = jnp.pad(segments, ((0, 0), (offset, 0)), constant_values=-1)[:, :document_length]
    return (moved == segments).astype(jnp.float32)[:, :, None]


def move_down(value, offset):
    document_length = value.shape[1]
    return jnp.pad(value, ((0, 0), (offset, 0), (0, 0)))[:, :document_length]


def move_up(value, offset):
    return jnp.pad(value, ((0, 0), (0, offset), (0, 0)))[:, offset:]


def conv_forward(value, kernel, bias, segments):
    taps = kernel.shape[0]
    total = jnp.zeros_like(value) + bias.astype(jnp.float32)
    for tap in range(taps):
        offset = taps - 1 - tap
        total = total + kernel[tap].astype(jnp.float32) * move_down(value, offset) * seg_keep(
            segments, offset
        )
    return total


def conv_backward(grad, value, kernel, segments):
    taps = kernel.shape[0]
    grad_in = jnp.zeros_like(value)
    kernel_rows = []
    for tap in range(taps):
        offset = taps - 1 - tap
        masked = grad * seg_keep(segments, offset)
        kernel_rows.append(jnp.sum(masked * move_down(value, offset), axis=(0, 1)))
        grad_in = grad_in + kernel[tap].astype(jnp.float32) * move_up(masked, offset)
    return (grad_in, jnp.stack(kernel_rows))


def ssd_parts(step_block, rate, coef_b, coef_c, heads_block, allowed):
    coupling = jnp.einsum("tn,sn->ts", coef_c, coef_b, preferred_element_type=jnp.float32)
    cumulative = jnp.cumsum(step_block * rate, axis=0).T
    difference = cumulative[:, :, None] - cumulative[:, None, :]
    decay = jnp.where(allowed[None], jnp.exp(jnp.where(allowed[None], difference, 0.0)), 0.0)
    mixing = (coupling[None] * decay).astype(jnp.bfloat16)
    driven = (heads_block * step_block.T[:, :, None]).astype(jnp.bfloat16)
    return (coupling, decay, mixing, driven)


def pair_sum(value):
    if lax.axis_size("tensor") == 2:
        other = lax.ppermute(value, "tensor", [(0, 1), (1, 0)])
        return value.astype(jnp.float32) + other.astype(jnp.float32)
    return lax.psum(value, "tensor").astype(jnp.float32)


def swap_bit(value, bit):
    size = lax.axis_size("dp")
    return lax.ppermute(value, "dp", [(i, i ^ bit) for i in range(size)])


def shared_sum(rows, first_shared):
    tail = pair_sum(rows[:, first_shared:]).astype(rows.dtype)
    return jnp.concatenate([rows[:, :first_shared], tail], 1) if first_shared else tail


def tree_sum(value, first_shared=None):
    size = lax.axis_size("dp")
    rows = value.shape[0]
    if size & (size - 1) or rows % (16 * size):
        total = lax.psum(value, "dp")
        return total if first_shared is None else shared_sum(total, first_shared)
    bits = [1 << i for i in range(size.bit_length() - 1)]
    me = lax.axis_index("dp")
    for bit in bits:
        half = value.shape[0] // 2
        low, high = value[:half], value[half:]
        upper = (me & bit) != 0
        got = swap_bit(jnp.where(upper, low, high), bit)
        kept = jnp.where(upper, high, low)
        value = (kept.astype(jnp.float32) + got.astype(jnp.float32)).astype(value.dtype)
    if first_shared is not None:
        value = shared_sum(value, first_shared)
    for bit in reversed(bits):
        upper = (me & bit) != 0
        got = swap_bit(value, bit)
        value = jnp.where(
            upper, jnp.concatenate([got, value], 0), jnp.concatenate([value, got], 0)
        )
    return value


def local(
    tokens,
    segments,
    cotangent,
    input_gain,
    query_weight,
    key_value_weight,
    attnout_weight,
    gating_weight,
    inner_weight,
    state_weight,
    step_weight,
    conv_inner,
    conv_state,
    inner_bias,
    state_bias,
    step_bias,
    decay_log,
    skip_scale,
    mixer_gain,
    mixer_out,
    post_gain,
    gate_weight,
    up_weight,
    down_weight,
):
    seq_count, document_length = segments.shape
    rows = seq_count * document_length
    heads = query_weight.shape[1] // HEAD_SIZE
    ssm_heads = step_weight.shape[1]
    query_group = QUERY_HEADS // KEYVALUE_HEADS
    shared_key_head = lax.axis_index("tensor") * heads // query_group
    scale = HEAD_SIZE ** (-0.5)
    cosine, sine = rotary_tables(document_length)
    positions = jnp.arange(document_length)

    def allowed_of(seg_ids):
        return (positions[:, None] >= positions[None, :]) & (seg_ids[:, None] == seg_ids[None, :])

    inputs = tokens.astype(jnp.float32)
    inv_first = lax.rsqrt(jnp.mean(inputs * inputs, -1, keepdims=True) + EPS)
    unit_first = inputs * inv_first
    in_gain = input_gain.astype(jnp.float32)
    normed = (unit_first * in_gain).astype(jnp.bfloat16)
    key_cols = lax.dynamic_slice_in_dim(key_value_weight, shared_key_head * HEAD_SIZE, HEAD_SIZE, 1)
    value_columns = lax.dynamic_slice_in_dim(
        key_value_weight, (KEYVALUE_HEADS + shared_key_head) * HEAD_SIZE, HEAD_SIZE, 1
    )
    query_pre = matmul(normed, query_weight)
    key_pre = matmul(normed, key_cols)
    value_pre = matmul(normed, value_columns)
    queries = rotate(
        query_pre.reshape(seq_count, document_length, heads, HEAD_SIZE).transpose(0, 2, 1, 3),
        cosine,
        sine,
    ).astype(jnp.bfloat16)
    key_rows = rotate(key_pre.reshape(seq_count, document_length, HEAD_SIZE), cosine, sine).astype(
        jnp.bfloat16
    )
    value_rows = value_pre.reshape(seq_count, document_length, HEAD_SIZE).astype(jnp.bfloat16)

    def attend(seq_item):
        query_block, key_block, value_block, seg_ids = seq_item
        allowed = allowed_of(seg_ids)[None]
        scores = (
            jnp.einsum("htd,sd->hts", query_block, key_block, preferred_element_type=jnp.float32)
            * scale
        )
        scores = jnp.where(allowed, scores, NEG_FILL)
        top = jnp.max(scores, -1, keepdims=True)
        weights = jnp.exp(scores - top)
        total = jnp.sum(weights, -1, keepdims=True)
        probs = (weights / total).astype(jnp.bfloat16)
        attended = jnp.einsum("hts,sd->htd", probs, value_block, preferred_element_type=jnp.float32)
        return (attended.astype(jnp.bfloat16), (top + jnp.log(total))[..., 0])

    attended, logsum = lax.map(attend, (queries, key_rows, value_rows, segments))
    attn_flat = attended.transpose(0, 2, 1, 3).reshape(rows, heads * HEAD_SIZE)
    attn_part = matmul(attn_flat, attnout_weight)
    gating = matmul(normed, gating_weight)
    inner = matmul(normed, inner_weight).reshape(seq_count, document_length, -1)
    state_in = matmul(normed, state_weight).reshape(seq_count, document_length, -1)
    step_raw = matmul(normed, step_weight)
    inner_pre = conv_forward(inner, conv_inner, inner_bias, segments)
    inner_act = jax.nn.silu(inner_pre)
    state_pre = conv_forward(state_in, conv_state, state_bias, segments)
    state_act = jax.nn.silu(state_pre)
    coef_b = state_act[..., :NS].astype(jnp.bfloat16)
    coef_c = state_act[..., NS:].astype(jnp.bfloat16)
    step_arg = step_raw.reshape(seq_count, document_length, ssm_heads) + step_bias.astype(
        jnp.float32
    )
    step = jax.nn.softplus(step_arg)
    rate = -jnp.exp(decay_log.astype(jnp.float32))
    heads_in = inner_act.reshape(seq_count, document_length, ssm_heads, P_SIZE).transpose(
        0, 2, 1, 3
    )

    def scan_forward(seq_item):
        step_block, coef_b_block, coef_c_block, heads_block, seg_ids = seq_item
        parts = ssd_parts(
            step_block, rate, coef_b_block, coef_c_block, heads_block, allowed_of(seg_ids)
        )
        return jnp.einsum("hts,hsp->htp", parts[2], parts[3], preferred_element_type=jnp.float32)

    core = lax.map(scan_forward, (step, coef_b, coef_c, heads_in, segments))
    skip = skip_scale.astype(jnp.float32)[None, :, None, None]
    ssm_out = (core + skip * heads_in).transpose(0, 2, 1, 3).reshape(rows, ssm_heads * P_SIZE)
    sigma_gate = jax.nn.sigmoid(gating)
    gate_act = gating * sigma_gate
    gated = ssm_out * gate_act
    square_sum = pair_sum(jnp.sum(gated * gated, -1))[:, None]
    inv_gate = lax.rsqrt(square_sum / DSSM + EPS)
    mixer_scale = mixer_gain.astype(jnp.float32)
    mixed = (gated * inv_gate * mixer_scale).astype(jnp.bfloat16)
    branch_part = attn_part + matmul(mixed, mixer_out)
    out_gain = post_gain.astype(jnp.float32)
    branch = pair_sum(branch_part.astype(jnp.bfloat16))
    middle = inputs + branch
    inv_second = lax.rsqrt(jnp.mean(middle * middle, -1, keepdims=True) + EPS)
    unit_second = middle * inv_second
    post = (unit_second * out_gain).astype(jnp.bfloat16)
    gate = matmul(post, gate_weight)
    upward = matmul(post, up_weight)
    sigma = jax.nn.sigmoid(gate)
    hidden = (gate * sigma * upward).astype(jnp.bfloat16)
    down_wgrad = jnp.einsum("tf,td->fd", hidden, cotangent, preferred_element_type=jnp.float32)
    hidden_grad = jnp.einsum(
        "td,fd->tf", cotangent, down_weight, preferred_element_type=jnp.float32
    )
    up_act_grad = (hidden_grad * gate * sigma).astype(jnp.bfloat16)
    gate_act_grad = (hidden_grad * upward * sigma * (1.0 + gate * (1.0 - sigma))).astype(
        jnp.bfloat16
    )
    gate_wgrad = jnp.einsum("tc,tf->cf", post, gate_act_grad, preferred_element_type=jnp.float32)
    up_wgrad = jnp.einsum("tc,tf->cf", post, up_act_grad, preferred_element_type=jnp.float32)
    post_part = jnp.einsum(
        "tf,cf->tc", gate_act_grad, gate_weight, preferred_element_type=jnp.float32
    ) + jnp.einsum("tf,cf->tc", up_act_grad, up_weight, preferred_element_type=jnp.float32)
    post_gain_part = jnp.sum(post_part * unit_second, 0)
    post_full = pair_sum(post_part.astype(jnp.bfloat16))
    down_wgrad, gate_wgrad, up_wgrad, post_full = lax.optimization_barrier(
        (
            down_wgrad.astype(jnp.bfloat16),
            gate_wgrad.astype(jnp.bfloat16),
            up_wgrad.astype(jnp.bfloat16),
            post_full,
        )
    )
    down_wgrad, gate_wgrad, up_wgrad = lax.psum((down_wgrad, gate_wgrad, up_wgrad), "dp")
    scaled_post = post_full * out_gain
    middle_grad = cotangent.astype(jnp.float32) + inv_second * (
        scaled_post - unit_second * jnp.mean(scaled_post * unit_second, -1, keepdims=True)
    )
    branch_grad = middle_grad.astype(jnp.bfloat16)
    attnout_wgrad = jnp.einsum(
        "tk,td->kd", attn_flat, branch_grad, preferred_element_type=jnp.float32
    )
    attended_grad = jnp.einsum(
        "td,kd->tk", branch_grad, attnout_weight, preferred_element_type=jnp.float32
    )
    attended_grad = (
        attended_grad.astype(jnp.bfloat16)
        .reshape(seq_count, document_length, heads, HEAD_SIZE)
        .transpose(0, 2, 1, 3)
    )

    def attend_back(seq_item):
        query_block, key_block, value_block, seg_ids, logsum_block, grad_block = seq_item
        allowed = allowed_of(seg_ids)[None]
        scores = (
            jnp.einsum("htd,sd->hts", query_block, key_block, preferred_element_type=jnp.float32)
            * scale
        )
        probs = jnp.where(allowed, jnp.exp(scores - logsum_block[..., None]), 0.0)
        value_grad = jnp.einsum(
            "hts,htd->hsd",
            probs.astype(jnp.bfloat16),
            grad_block,
            preferred_element_type=jnp.float32,
        )
        prob_grad = jnp.einsum(
            "htd,sd->hts", grad_block, value_block, preferred_element_type=jnp.float32
        )
        delta = jnp.sum(probs * prob_grad, -1, keepdims=True)
        score_grad = (probs * (prob_grad - delta)).astype(jnp.bfloat16)
        query_grad = (
            jnp.einsum("hts,sd->htd", score_grad, key_block, preferred_element_type=jnp.float32)
            * scale
        )
        key_grad = (
            jnp.einsum("hts,htd->hsd", score_grad, query_block, preferred_element_type=jnp.float32)
            * scale
        )
        return (query_grad, key_grad, value_grad)

    query_rot_grad, key_rot_grad, value_head_grad = lax.map(
        attend_back, (queries, key_rows, value_rows, segments, logsum, attended_grad)
    )
    query_pre_grad = (
        rotate_back(query_rot_grad, cosine, sine)
        .astype(jnp.bfloat16)
        .transpose(0, 2, 1, 3)
        .reshape(rows, heads * HEAD_SIZE)
    )
    key_pre_grad = rotate_back(key_rot_grad, cosine, sine).astype(jnp.bfloat16)
    value_pre_grad = value_head_grad.astype(jnp.bfloat16)
    normed_seq = normed.reshape(seq_count, document_length, -1)
    query_wgrad = jnp.einsum(
        "tc,tk->ck", normed, query_pre_grad, preferred_element_type=jnp.float32
    )
    key_wgrad = jnp.einsum(
        "slc,shld->cd", normed_seq, key_pre_grad, preferred_element_type=jnp.float32
    )
    value_weight_grad = jnp.einsum(
        "slc,shld->cd", normed_seq, value_pre_grad, preferred_element_type=jnp.float32
    )
    normed_part = (
        jnp.einsum("tk,ck->tc", query_pre_grad, query_weight, preferred_element_type=jnp.float32)
        + jnp.einsum(
            "shld,cd->slc", key_pre_grad, key_cols, preferred_element_type=jnp.float32
        ).reshape(rows, -1)
        + jnp.einsum(
            "shld,cd->slc", value_pre_grad, value_columns, preferred_element_type=jnp.float32
        ).reshape(rows, -1)
    )
    mixout_wgrad = jnp.einsum("tk,td->kd", mixed, branch_grad, preferred_element_type=jnp.float32)
    mixed_grad = jnp.einsum("td,kd->tk", branch_grad, mixer_out, preferred_element_type=jnp.float32)
    mixer_gain_wgrad = jnp.sum(mixed_grad * gated * inv_gate, 0)
    weighted = mixed_grad * mixer_scale
    cross = pair_sum(jnp.sum(weighted * gated, -1))[:, None]
    gated_grad = inv_gate * weighted - gated * (inv_gate * inv_gate * inv_gate) * cross / DSSM
    ssm_grad = gated_grad * gate_act
    gating_act_grad = (
        gated_grad * ssm_out * sigma_gate * (1.0 + gating * (1.0 - sigma_gate))
    ).astype(jnp.bfloat16)
    ssm_heads_grad = ssm_grad.reshape(seq_count, document_length, ssm_heads, P_SIZE).transpose(
        0, 2, 1, 3
    )
    core_grad = ssm_heads_grad.astype(jnp.bfloat16)
    skip_wgrad = jnp.sum(ssm_heads_grad * heads_in, axis=(0, 2, 3))

    def scan_back(seq_item):
        step_block, coef_b_block, coef_c_block, heads_block, seg_ids, core_block = seq_item
        coupling, decay, mixing, driven = ssd_parts(
            step_block, rate, coef_b_block, coef_c_block, heads_block, allowed_of(seg_ids)
        )
        mix_grad = jnp.einsum(
            "htp,hsp->hts", core_block, driven, preferred_element_type=jnp.float32
        )
        driven_grad = jnp.einsum(
            "hts,htp->hsp", mixing, core_block, preferred_element_type=jnp.float32
        )
        rounded = (mix_grad * decay).astype(jnp.bfloat16)
        coef_c_grad = jnp.einsum(
            "hts,sn->tn", rounded, coef_b_block, preferred_element_type=jnp.float32
        )
        coef_b_grad = jnp.einsum(
            "hts,tn->sn", rounded, coef_c_block, preferred_element_type=jnp.float32
        )
        spread = mix_grad * coupling[None] * decay
        cumulative_grad = jnp.sum(spread, 2) - jnp.sum(spread, 1)
        log_grad = jnp.flip(jnp.cumsum(jnp.flip(cumulative_grad, 1), 1), 1)
        heads_grad = driven_grad * step_block.T[:, :, None]
        step_grad = (jnp.sum(driven_grad * heads_block, -1) + log_grad * rate[:, None]).T
        rate_grad = jnp.sum(log_grad * step_block.T, 1)
        return (heads_grad, step_grad, rate_grad, coef_b_grad, coef_c_grad)

    heads_grad, step_grad, rate_grad, coef_b_grad, coef_c_grad = lax.map(
        scan_back, (step, coef_b, coef_c, heads_in, segments, core_grad)
    )
    heads_total = heads_grad + ssm_heads_grad * skip
    inner_act_grad = heads_total.transpose(0, 2, 1, 3).reshape(seq_count, document_length, -1)
    step_total = step_grad * jax.nn.sigmoid(step_arg)
    step_bias_wgrad = jnp.sum(step_total, axis=(0, 1))
    decay_wgrad = jnp.sum(rate_grad, 0) * rate
    step_raw_grad = step_total.reshape(rows, ssm_heads).astype(jnp.bfloat16)
    inner_pre_grad = inner_act_grad * silu_slope(inner_pre)
    inner_bias_wgrad = jnp.sum(inner_pre_grad, axis=(0, 1))
    inner_grad, conv_inner_wgrad = conv_backward(inner_pre_grad, inner, conv_inner, segments)
    inner_grad = inner_grad.reshape(rows, -1).astype(jnp.bfloat16)
    state_act_grad = jnp.concatenate([coef_b_grad, coef_c_grad], -1)
    state_pre_grad = state_act_grad * silu_slope(state_pre)
    state_bias_wgrad = jnp.sum(state_pre_grad, axis=(0, 1))
    state_grad, conv_state_wgrad = conv_backward(state_pre_grad, state_in, conv_state, segments)
    state_grad = state_grad.reshape(rows, -1).astype(jnp.bfloat16)
    gating_wgrad = jnp.einsum(
        "tc,tk->ck", normed, gating_act_grad, preferred_element_type=jnp.float32
    )
    inner_wgrad = jnp.einsum("tc,tk->ck", normed, inner_grad, preferred_element_type=jnp.float32)
    step_wgrad = jnp.einsum("tc,tk->ck", normed, step_raw_grad, preferred_element_type=jnp.float32)
    state_wgrad = jnp.einsum("tc,tk->ck", normed, state_grad, preferred_element_type=jnp.float32)
    normed_part = (
        normed_part
        + jnp.einsum(
            "tk,ck->tc", gating_act_grad, gating_weight, preferred_element_type=jnp.float32
        )
        + jnp.einsum("tk,ck->tc", inner_grad, inner_weight, preferred_element_type=jnp.float32)
        + jnp.einsum("tk,ck->tc", step_raw_grad, step_weight, preferred_element_type=jnp.float32)
        + jnp.einsum("tk,ck->tc", state_grad, state_weight, preferred_element_type=jnp.float32)
    )
    input_gain_part = jnp.sum(normed_part * unit_first, 0)
    normed_full = pair_sum(normed_part.astype(jnp.bfloat16))
    scaled_in = normed_full * in_gain
    tokens_grad = middle_grad + inv_first * (
        scaled_in - unit_first * jnp.mean(scaled_in * unit_first, -1, keepdims=True)
    )
    low = jnp.bfloat16
    if lax.axis_size("tensor") == 2 and KEYVALUE_HEADS == 2:
        keyval_part = jnp.concatenate([key_wgrad, value_weight_grad], 1)
    else:
        keyval_part = jnp.zeros(key_value_weight.shape, jnp.float32)
        keyval_part = lax.dynamic_update_slice_in_dim(
            keyval_part, key_wgrad, shared_key_head * HEAD_SIZE, 1
        )
        keyval_part = lax.dynamic_update_slice_in_dim(
            keyval_part, value_weight_grad, (KEYVALUE_HEADS + shared_key_head) * HEAD_SIZE, 1
        )
        keyval_part = lax.psum(keyval_part, "tensor")
    first_total = tree_sum(
        jnp.concatenate(
            [query_wgrad.astype(low), keyval_part.astype(low), gating_wgrad.astype(low)], 1
        )
    ).astype(jnp.float32)
    second_total = tree_sum(
        jnp.concatenate([attnout_wgrad.astype(low), mixout_wgrad.astype(low)], 0)
    ).astype(jnp.float32)
    width = query_wgrad.shape[1]
    kv_width = keyval_part.shape[1]
    query_wgrad = first_total[:, :width]
    keyval_part = first_total[:, width : width + kv_width]
    gating_wgrad = first_total[:, width + kv_width :]
    attnout_wgrad = second_total[: heads * HEAD_SIZE]
    mixout_wgrad = second_total[heads * HEAD_SIZE :]
    if lax.axis_size("tensor") == 2 and KEYVALUE_HEADS == 2:
        other = lax.ppermute(keyval_part.astype(low), "tensor", [(0, 1), (1, 0)])
        mine = keyval_part.astype(low)
        is_first = lax.axis_index("tensor") == 0
        head_0 = jnp.where(is_first, mine, other)
        head_1 = jnp.where(is_first, other, mine)
        key_value_weight_grad = jnp.concatenate(
            [
                head_0[:, :HEAD_SIZE],
                head_1[:, :HEAD_SIZE],
                head_0[:, HEAD_SIZE:],
                head_1[:, HEAD_SIZE:],
            ],
            1,
        ).astype(jnp.float32)
    else:
        key_value_weight_grad = keyval_part
    own = [
        step_bias_wgrad,
        decay_wgrad,
        skip_wgrad,
        mixer_gain_wgrad,
        inner_bias_wgrad,
        conv_inner_wgrad.reshape(-1),
    ]
    shared = [input_gain_part, post_gain_part, state_bias_wgrad, conv_state_wgrad.reshape(-1)]

    def columns_of(parts):
        flat = jnp.concatenate(parts)
        count = -(-flat.shape[0] // tokens.shape[1])
        flat = jnp.pad(flat, (0, count * tokens.shape[1] - flat.shape[0]))
        return flat.reshape(count, tokens.shape[1]).T

    def parts_of(columns, parts):
        flat = columns.T.reshape(-1)
        found, at = [], 0
        for part in parts:
            found.append(flat[at : at + part.shape[0]])
            at += part.shape[0]
        return found

    own_columns, shared_columns = columns_of(own), columns_of(shared)
    inner_width = inner_wgrad.shape[1]
    own_width = own_columns.shape[1]
    shared_from = -(-(inner_width + ssm_heads + own_width) // 128) * 128
    pad = shared_from - inner_width - ssm_heads - own_width
    third_total = tree_sum(
        jnp.concatenate(
            [
                inner_wgrad.astype(low),
                step_wgrad.astype(low),
                own_columns.astype(low),
                jnp.zeros((tokens.shape[1], pad), low),
                state_wgrad.astype(low),
                shared_columns.astype(low),
            ],
            1,
        ),
        shared_from,
    ).astype(jnp.float32)
    inner_wgrad = third_total[:, :inner_width]
    step_wgrad = third_total[:, inner_width : inner_width + ssm_heads]
    at = inner_width + ssm_heads
    (
        step_bias_wgrad,
        decay_wgrad,
        skip_wgrad,
        mixer_gain_wgrad,
        inner_bias_wgrad,
        conv_inner_flat,
    ) = parts_of(third_total[:, at : at + own_width], own)
    conv_inner_wgrad = conv_inner_flat.reshape(conv_inner.shape)
    state_width = state_wgrad.shape[1]
    state_wgrad = third_total[:, shared_from : shared_from + state_width]
    input_gain_part, post_gain_part, state_bias_wgrad, conv_state_flat = parts_of(
        third_total[:, shared_from + state_width :], shared
    )
    conv_state_wgrad = conv_state_flat.reshape(conv_state.shape)
    down_wgrad = down_wgrad.astype(jnp.float32)
    gate_wgrad = gate_wgrad.astype(jnp.float32)
    up_wgrad = up_wgrad.astype(jnp.float32)
    return (
        tokens_grad,
        input_gain_part,
        query_wgrad,
        key_value_weight_grad,
        attnout_wgrad,
        gating_wgrad,
        inner_wgrad,
        state_wgrad,
        step_wgrad,
        conv_inner_wgrad,
        conv_state_wgrad,
        inner_bias_wgrad,
        state_bias_wgrad,
        step_bias_wgrad,
        decay_wgrad,
        skip_wgrad,
        mixer_gain_wgrad,
        mixout_wgrad,
        post_gain_part,
        gate_wgrad,
        up_wgrad,
        down_wgrad,
    )


CHUNK = 256
LANES = 128
VMEM_BYTES = 56 * 1024 * 1024


def dot_nn(left, right):
    return lax.dot_general(left, right, (((1,), (0,)), ((), ())), preferred_element_type=jnp.float32)


def dot_nt(left, right):
    return lax.dot_general(left, right, (((1,), (1,)), ((), ())), preferred_element_type=jnp.float32)


def dot_tn(left, right):
    return lax.dot_general(left, right, (((0,), (0,)), ((), ())), preferred_element_type=jnp.float32)


def split_two(value):
    high = value.astype(jnp.bfloat16)
    return high, (value - high.astype(jnp.float32)).astype(jnp.bfloat16)


def exact_nn(ones, value):
    high, low = split_two(value)
    return dot_nn(ones, high) + dot_nn(ones, low)


def grid_of(shape):
    return (
        lax.broadcasted_iota(jnp.int32, shape, 0),
        lax.broadcasted_iota(jnp.int32, shape, 1),
    )


def pick(columns, pair):
    rows = columns.shape[0]
    left = jnp.broadcast_to(columns[:, 2 * pair : 2 * pair + 1], (rows, LANES))
    right = jnp.broadcast_to(columns[:, 2 * pair + 1 : 2 * pair + 2], (rows, LANES))
    return jnp.where(grid_of((rows, LANES))[1] < P_SIZE, left, right)


def scan_terms(step, rate, aux):
    row, col = grid_of((CHUNK, CHUNK))
    lower = (row >= col).astype(jnp.bfloat16)
    cumulative = exact_nn(lower, step * rate)
    last = cumulative[CHUNK - 1 : CHUNK]
    enter = jnp.exp(cumulative) * aux[:, 1:2]
    leave = jnp.exp(last - cumulative) * aux[:, 2:3]
    across = jnp.exp(last) * aux[CHUNK - 1 : CHUNK, 1:2]
    return cumulative, enter, leave, across


def scan_kernel(step_ref, coef_ref, act_ref, aux_ref, seg_ref, rate_ref, core_ref, kept_ref, state, moved):
    @pl.when(pl.program_id(0) == 0)
    def _():
        state[...] = jnp.zeros_like(state)

    step = step_ref[...]
    aux = aux_ref[...]
    cumulative, enter, leave, across = scan_terms(step, rate_ref[...], aux)
    cum_rows = cumulative.T
    row, col = grid_of((CHUNK, CHUNK))
    blocked = jnp.where((row >= col) & (aux[:, 0:1] == seg_ref[...]), 0.0, NEG_FILL)
    coef_b = coef_ref[:, :NS]
    coef_c = coef_ref[:, NS:]
    coupling = dot_nt(coef_c, coef_b)
    low_state = state[...].astype(jnp.bfloat16)
    kept_ref[0] = low_state
    carried = dot_nn(coef_c, low_state)
    first = grid_of((CHUNK, LANES))[1] < P_SIZE
    for pair in range(act_ref.shape[1] // LANES):
        at = slice(pair * LANES, (pair + 1) * LANES)
        driven = (act_ref[:, at] * pick(step, pair)).astype(jnp.bfloat16)
        parts = []
        for head in (2 * pair, 2 * pair + 1):
            decay = jnp.exp(cumulative[:, head : head + 1] - cum_rows[head : head + 1] + blocked)
            parts.append(dot_nn((coupling * decay).astype(jnp.bfloat16), driven))
        core_ref[:, at] = jnp.where(first, parts[0], parts[1]) + carried[:, at] * pick(enter, pair)
        moved[:, at] = (driven.astype(jnp.float32) * pick(leave, pair)).astype(jnp.bfloat16)
    fresh = dot_tn(coef_b, moved[...])
    for pair in range(act_ref.shape[1] // LANES):
        at = slice(pair * LANES, (pair + 1) * LANES)
        state[:, at] = state[:, at] * pick(across, pair) + fresh[:, at]


def scan_call(step, coef, act, aux, seg_row, rate):
    rows, width = act.shape
    chunks = rows // CHUNK
    by_chunk = lambda columns: pl.BlockSpec((CHUNK, columns), lambda i: (i, 0))
    return pl.pallas_call(
        scan_kernel,
        grid=(chunks,),
        in_specs=[
            by_chunk(LANES),
            by_chunk(2 * NS),
            by_chunk(width),
            by_chunk(LANES),
            pl.BlockSpec((1, CHUNK), lambda i: (0, i)),
            pl.BlockSpec((1, LANES), lambda i: (0, 0)),
        ],
        out_specs=[by_chunk(width), pl.BlockSpec((1, NS, width), lambda i: (i, 0, 0))],
        out_shape=[
            jax.ShapeDtypeStruct((rows, width), jnp.float32),
            jax.ShapeDtypeStruct((chunks, NS, width), jnp.bfloat16),
        ],
        scratch_shapes=[
            pltpu.VMEM((NS, width), jnp.float32),
            pltpu.VMEM((CHUNK, width), jnp.bfloat16),
        ],
        compiler_params=pltpu.CompilerParams(vmem_limit_bytes=VMEM_BYTES),
        name="scan_forward",
    )(step, coef, act, aux, seg_row, rate)


def scan_back_kernel(
    step_ref,
    coef_ref,
    act_ref,
    aux_ref,
    seg_ref,
    rate_ref,
    skip_ref,
    grad_ref,
    kept_ref,
    act_grad_ref,
    step_grad_ref,
    coef_grad_ref,
    sums_ref,
    skip_sum_ref,
    state_grad,
    moved,
    entered,
    row_sums,
):
    @pl.when(pl.program_id(0) == 0)
    def _():
        state_grad[...] = jnp.zeros_like(state_grad)
        sums_ref[...] = jnp.zeros_like(sums_ref)
        skip_sum_ref[...] = jnp.zeros_like(skip_sum_ref)
        row_sums[...] = jnp.zeros_like(row_sums)

    step = step_ref[...]
    aux = aux_ref[...]
    rate = rate_ref[...]
    cumulative, enter, leave, across = scan_terms(step, rate, aux)
    cum_rows = cumulative.T
    row, col = grid_of((CHUNK, CHUNK))
    blocked = jnp.where((row <= col) & (aux[:, 0:1] == seg_ref[...]), 0.0, NEG_FILL)
    coef_b = coef_ref[:, :NS]
    coef_c = coef_ref[:, NS:]
    coupling = dot_nt(coef_b, coef_c)
    low_state = kept_ref[0]
    carried = dot_nn(coef_c, low_state)
    low_grad = state_grad[...].astype(jnp.bfloat16)
    returned = dot_nn(coef_b, low_grad)
    product = jnp.sum(low_state.astype(jnp.float32) * low_grad.astype(jnp.float32), 0, keepdims=True)
    lane = grid_of((CHUNK, LANES))[1]
    lane_row = grid_of((1, LANES))[1]
    first = lane < P_SIZE
    later = jnp.zeros((CHUNK, LANES), jnp.float32)
    earlier = jnp.zeros((CHUNK, LANES), jnp.float32)
    direct = jnp.zeros((CHUNK, LANES), jnp.float32)
    through = jnp.zeros((1, LANES), jnp.float32)
    coupling_grad = jnp.zeros((CHUNK, CHUNK), jnp.float32)
    for pair in range(act_ref.shape[1] // LANES):
        at = slice(pair * LANES, (pair + 1) * LANES)
        act = act_ref[:, at]
        spread_step = pick(step, pair)
        driven = (act * spread_step).astype(jnp.bfloat16)
        grad = grad_ref[:, at]
        core_grad = grad.astype(jnp.bfloat16)
        core_wide = core_grad.astype(jnp.float32)
        enter_grad = core_wide * pick(enter, pair)
        entered[:, at] = enter_grad.astype(jnp.bfloat16)
        row_part = enter_grad * carried[:, at]
        leave_pair = pick(leave, pair)
        moved[:, at] = (driven.astype(jnp.float32) * leave_pair).astype(jnp.bfloat16)
        back = returned[:, at] * leave_pair
        col_part = back * driven.astype(jnp.float32)
        parts = []
        for head in (2 * pair, 2 * pair + 1):
            mine = first if head % 2 == 0 else ~first
            decay = jnp.exp(cum_rows[head : head + 1] - cumulative[:, head : head + 1] + blocked)
            mix_grad = dot_nt(jnp.where(mine, driven, jnp.zeros_like(driven)), core_grad)
            share = mix_grad * decay
            coupling_grad = coupling_grad + share
            spread = share * coupling
            row_sums[head : head + 1] = jnp.sum(spread, 0, keepdims=True)
            folded = sum(spread[:, k * LANES : (k + 1) * LANES] for k in range(CHUNK // LANES))
            found = jnp.sum(jnp.where(mine, row_part, 0.0) - folded, 1, keepdims=True)
            later = jnp.where(lane == head, found, later)
            parts.append(dot_nn((coupling * decay).astype(jnp.bfloat16), core_grad))
            found = jnp.sum(jnp.where(mine, col_part, 0.0), 1, keepdims=True)
            earlier = jnp.where(lane == head, found, earlier)
        driven_grad = jnp.where(first, parts[0], parts[1]) + back
        act_grad_ref[:, at] = driven_grad * spread_step + grad * skip_ref[:, at]
        skip_sum_ref[:, at] += jnp.sum(grad * act, 0, keepdims=True)
        step_part = driven_grad * act
        product_pair = product[:, at]
        for head in (2 * pair, 2 * pair + 1):
            mine = first if head % 2 == 0 else ~first
            found = jnp.sum(jnp.where(mine, step_part, 0.0), 1, keepdims=True)
            direct = jnp.where(lane == head, found, direct)
            found = jnp.sum(jnp.where(mine[:1], product_pair, 0.0), 1, keepdims=True)
            through = jnp.where(lane_row == head, found, through)
    upper = (row <= col).astype(jnp.bfloat16)
    below = (row > col).astype(jnp.bfloat16)
    high, low = split_two(row_sums[...])
    log_grad = (
        exact_nn(upper, later)
        + dot_nt(upper, high)
        + dot_nt(upper, low)
        + exact_nn(below, earlier)
        + through * across
    )
    step_grad_ref[...] = direct + log_grad * rate
    sums_ref[...] += jnp.sum(log_grad * step, 0, keepdims=True)
    low_coupling = coupling_grad.astype(jnp.bfloat16)
    coef_grad_ref[:, :NS] = dot_nn(low_coupling, coef_c) + dot_nt(moved[...], low_grad)
    coef_grad_ref[:, NS:] = dot_tn(low_coupling, coef_b) + dot_nt(entered[...], low_state)
    fresh = dot_tn(coef_c, entered[...])
    for pair in range(act_ref.shape[1] // LANES):
        at = slice(pair * LANES, (pair + 1) * LANES)
        state_grad[:, at] = state_grad[:, at] * pick(across, pair) + fresh[:, at]


def scan_back_call(step, coef, act, aux, seg_row, rate, skip_row, grad, kept):
    rows, width = act.shape
    chunks = rows // CHUNK
    by_chunk = lambda columns: pl.BlockSpec((CHUNK, columns), lambda i: (chunks - 1 - i, 0))
    one_row = lambda columns: pl.BlockSpec((1, columns), lambda i: (0, 0))
    return pl.pallas_call(
        scan_back_kernel,
        grid=(chunks,),
        in_specs=[
            by_chunk(LANES),
            by_chunk(2 * NS),
            by_chunk(width),
            by_chunk(LANES),
            pl.BlockSpec((1, CHUNK), lambda i: (0, chunks - 1 - i)),
            one_row(LANES),
            one_row(width),
            by_chunk(width),
            pl.BlockSpec((1, NS, width), lambda i: (chunks - 1 - i, 0, 0)),
        ],
        out_specs=[
            by_chunk(width),
            by_chunk(LANES),
            by_chunk(2 * NS),
            one_row(LANES),
            one_row(width),
        ],
        out_shape=[
            jax.ShapeDtypeStruct((rows, width), jnp.float32),
            jax.ShapeDtypeStruct((rows, LANES), jnp.float32),
            jax.ShapeDtypeStruct((rows, 2 * NS), jnp.float32),
            jax.ShapeDtypeStruct((1, LANES), jnp.float32),
            jax.ShapeDtypeStruct((1, width), jnp.float32),
        ],
        scratch_shapes=[
            pltpu.VMEM((NS, width), jnp.float32),
            pltpu.VMEM((CHUNK, width), jnp.bfloat16),
            pltpu.VMEM((CHUNK, width), jnp.bfloat16),
            pltpu.VMEM((LANES, CHUNK), jnp.float32),
        ],
        compiler_params=pltpu.CompilerParams(vmem_limit_bytes=VMEM_BYTES),
        name="scan_backward",
    )(step, coef, act, aux, seg_row, rate, skip_row, grad, kept)


def swap_halves(value):
    width = value.shape[1]
    half = HEAD_SIZE // 2
    up = pltpu.roll(value, width - half, 1)
    down = pltpu.roll(value, half, 1)
    return jnp.where(grid_of(value.shape)[1] % HEAD_SIZE < half, up, down)


def turned(value, cosine, sine):
    return value * cosine + swap_halves(value) * sine


def attend_kernel(query_ref, keyval_ref, seg_ref, seg_col_ref, cos_ref, sin_ref, out_ref, turned_ref, both_ref, log_ref):
    rows = query_ref.shape[0]
    first = grid_of((rows, LANES))[1] < HEAD_SIZE
    keyval = keyval_ref[...]
    moved = pltpu.roll(keyval, HEAD_SIZE, 1)
    keys = turned(jnp.where(first, keyval, moved), cos_ref[...], sin_ref[...]).astype(jnp.bfloat16)
    values = jnp.where(first, moved, keyval).astype(jnp.bfloat16)
    both_ref[:, :LANES] = keys
    both_ref[:, LANES:] = values
    scale = HEAD_SIZE ** (-0.5)
    head_lane = grid_of((CHUNK, LANES))[1]
    first = head_lane < HEAD_SIZE
    for block in range(rows // CHUNK):
        low, high = block * CHUNK, (block + 1) * CHUNK
        row, col = grid_of((CHUNK, high))
        blocked = jnp.where(
            (row + low >= col) & (seg_col_ref[low:high, 0:1] == seg_ref[:, :high]), 0.0, NEG_FILL
        )
        logs = jnp.zeros((CHUNK, LANES), jnp.float32)
        for pair in range(query_ref.shape[1] // LANES):
            at = slice(pair * LANES, (pair + 1) * LANES)
            query = turned(query_ref[low:high, at], cos_ref[low:high], sin_ref[low:high]).astype(
                jnp.bfloat16
            )
            turned_ref[low:high, at] = query
            parts = []
            for head in (2 * pair, 2 * pair + 1):
                mine = first if head % 2 == 0 else ~first
                scores = (
                    dot_nt(jnp.where(mine, query, jnp.zeros_like(query)), keys[:high]) * scale
                    + blocked
                )
                top = jnp.max(scores, 1, keepdims=True)
                weights = jnp.exp(scores - top)
                total = jnp.sum(weights, 1, keepdims=True)
                probs = (weights * (1.0 / total)).astype(jnp.bfloat16)
                parts.append(dot_nn(probs, values[:high]))
                logs = jnp.where(head_lane == head, top + jnp.log(total), logs)
            out_ref[low:high, at] = jnp.where(first, parts[0], parts[1]).astype(jnp.bfloat16)
        log_ref[low:high] = logs


def attend_call(query, keyval, seg_row, aux, cosine, sine):
    rows, width = query.shape
    return pl.pallas_call(
        attend_kernel,
        out_shape=[
            jax.ShapeDtypeStruct((rows, width), jnp.bfloat16),
            jax.ShapeDtypeStruct((rows, width), jnp.bfloat16),
            jax.ShapeDtypeStruct((rows, 2 * LANES), jnp.bfloat16),
            jax.ShapeDtypeStruct((rows, LANES), jnp.float32),
        ],
        compiler_params=pltpu.CompilerParams(vmem_limit_bytes=VMEM_BYTES),
        name="attend_forward",
    )(query, keyval, seg_row, aux, cosine, sine)


def attend_back_kernel(
    query_ref, both_ref, seg_ref, seg_col_ref, cos_ref, sin_ref, log_ref, out_ref, grad_ref,
    query_grad_ref, keyval_grad_ref, key_sum, value_sum,
):
    rows = query_ref.shape[0]
    key_sum[...] = jnp.zeros_like(key_sum)
    value_sum[...] = jnp.zeros_like(value_sum)
    scale = HEAD_SIZE ** (-0.5)
    first = grid_of((CHUNK, LANES))[1] < HEAD_SIZE
    for block in range(rows // CHUNK):
        low, high = block * CHUNK, (block + 1) * CHUNK
        row, col = grid_of((CHUNK, high))
        blocked = jnp.where(
            (row + low >= col) & (seg_col_ref[low:high, 0:1] == seg_ref[:, :high]), 0.0, NEG_FILL
        )
        keys = both_ref[:high, :LANES]
        values = both_ref[:high, LANES:]
        for pair in range(query_ref.shape[1] // LANES):
            at = slice(pair * LANES, (pair + 1) * LANES)
            query = query_ref[low:high, at]
            grad = grad_ref[low:high, at]
            inner = grad.astype(jnp.float32) * out_ref[low:high, at].astype(jnp.float32)
            parts = []
            key_part = None
            for head in (2 * pair, 2 * pair + 1):
                mine = first if head % 2 == 0 else ~first
                query_mine = jnp.where(mine, query, jnp.zeros_like(query))
                grad_mine = jnp.where(mine, grad, jnp.zeros_like(grad))
                scores = dot_nt(query_mine, keys) * scale + blocked
                probs = jnp.exp(scores - log_ref[low:high, head : head + 1])
                delta = jnp.sum(jnp.where(mine, inner, 0.0), 1, keepdims=True)
                prob_grad = dot_nt(grad_mine, values)
                score_grad = (probs * (prob_grad - delta)).astype(jnp.bfloat16)
                parts.append(dot_nn(score_grad, keys) * scale)
                key_sum[:high] += dot_tn(score_grad, query_mine)
                value_sum[:high] += dot_tn(probs.astype(jnp.bfloat16), grad_mine)
            full = jnp.where(first, parts[0], parts[1])
            query_grad_ref[low:high, at] = turned(full, cos_ref[low:high], -sin_ref[low:high]).astype(
                jnp.bfloat16
            )
    wide = grid_of((rows, LANES))[1] < HEAD_SIZE
    key_total = key_sum[...] * scale
    key_total = key_total + pltpu.roll(key_total, HEAD_SIZE, 1)
    key_total = turned(key_total, cos_ref[...], -sin_ref[...])
    value_total = value_sum[...]
    value_total = value_total + pltpu.roll(value_total, HEAD_SIZE, 1)
    keyval_grad_ref[...] = jnp.where(wide, key_total, value_total).astype(jnp.bfloat16)


def attend_back_call(query, both, seg_row, aux, cosine, sine, logs, out, grad):
    rows, width = query.shape
    return pl.pallas_call(
        attend_back_kernel,
        out_shape=[
            jax.ShapeDtypeStruct((rows, width), jnp.bfloat16),
            jax.ShapeDtypeStruct((rows, LANES), jnp.bfloat16),
        ],
        scratch_shapes=[
            pltpu.VMEM((rows, LANES), jnp.float32),
            pltpu.VMEM((rows, LANES), jnp.float32),
        ],
        compiler_params=pltpu.CompilerParams(vmem_limit_bytes=VMEM_BYTES),
        name="attend_backward",
    )(query, both, seg_row, aux, cosine, sine, logs, out, grad)


def halve(value, bit):
    half = value.shape[0] // 2
    upper = (lax.axis_index("dp") & bit) != 0
    got = swap_bit(jnp.where(upper, value[:half], value[half:]), bit)
    kept = jnp.where(upper, value[half:], value[:half])
    return (kept.astype(jnp.float32) + got.astype(jnp.float32)).astype(value.dtype)


def double(value, bit):
    upper = (lax.axis_index("dp") & bit) != 0
    got = swap_bit(value, bit)
    return jnp.concatenate([jnp.where(upper, got, value), jnp.where(upper, value, got)], 0)


def dp_bits():
    size = lax.axis_size("dp")
    return [1 << i for i in range(size.bit_length() - 1)]


def halve_parts(values, bit):
    half = values[0].shape[0] // 2
    upper = (lax.axis_index("dp") & bit) != 0
    got = swap_bit(
        jnp.concatenate([jnp.where(upper, v[:half], v[half:]) for v in values], 1), bit
    )
    kept = jnp.concatenate([jnp.where(upper, v[half:], v[:half]) for v in values], 1)
    return (kept.astype(jnp.float32) + got.astype(jnp.float32)).astype(got.dtype)


def by_rows(value):
    return with_layout_constraint(value, Layout(major_to_minor=(0, 1)))


def tie(*values):
    return lax.optimization_barrier(values)


def conv_rows(value, kernel, bias, keeps):
    taps = kernel.shape[0]
    total = bias.astype(jnp.float32)[None]
    for tap in range(taps):
        offset = taps - 1 - tap
        moved = jnp.pad(value, ((offset, 0), (0, 0)))[: value.shape[0]]
        total = total + kernel[tap].astype(jnp.float32) * moved * keeps[offset]
    return total


def conv_rows_back(grad, value, kernel, keeps):
    taps = kernel.shape[0]
    grad_in = jnp.zeros_like(grad)
    sums = []
    for tap in range(taps):
        offset = taps - 1 - tap
        masked = grad * keeps[offset]
        moved = jnp.pad(value, ((offset, 0), (0, 0)))[: value.shape[0]]
        sums.append(jnp.sum(masked * moved, 0, keepdims=True))
        grad_in = grad_in + kernel[tap].astype(jnp.float32) * jnp.pad(
            masked, ((0, offset), (0, 0))
        )[offset:]
    return grad_in, sums


def product_kernel(*refs):
    left_pairs, right_pairs = [refs[0:2], refs[2:4], refs[2:4]], [(), refs[4:6], refs[6:8]]
    cotangent_ref, out_ref = refs[8], refs[9]
    half = refs[0].shape[0]
    for which in range(3):
        total = None
        for k in range(2):
            left = left_pairs[which][k][...]
            if which == 0:
                right = cotangent_ref[k * half : (k + 1) * half]
            else:
                right = right_pairs[which][k][...]
            part = dot_tn(left, right)
            total = part if total is None else total + part
        out_ref[which] = total.astype(out_ref.dtype)


def product_call(hidden_a, hidden_b, post_a, post_b, gate_a, gate_b, up_a, up_b, cotangent):
    half, model = post_a.shape
    hidden = hidden_a.shape[1]
    columns = pl.BlockSpec((half, CHUNK), lambda i: (0, i))
    whole = pl.BlockSpec((half, hidden), lambda i: (0, 0))
    return pl.pallas_call(
        product_kernel,
        grid=(hidden // CHUNK,),
        in_specs=[columns] * 4 + [whole] * 4 + [pl.BlockSpec((2 * half, model), lambda i: (0, 0))],
        out_specs=pl.BlockSpec((3, CHUNK, model), lambda i: (0, i, 0)),
        out_shape=jax.ShapeDtypeStruct((3, hidden, model), jnp.bfloat16),
        compiler_params=pltpu.CompilerParams(vmem_limit_bytes=VMEM_BYTES),
        name="weight_products",
    )(hidden_a, hidden_b, post_a, post_b, gate_a, gate_b, up_a, up_b, cotangent)


def local_fast(
    tokens,
    segments,
    cotangent,
    input_gain,
    query_weight,
    key_value_weight,
    attnout_weight,
    gating_weight,
    inner_weight,
    state_weight,
    step_weight,
    conv_inner,
    conv_state,
    inner_bias,
    state_bias,
    step_bias,
    decay_log,
    skip_scale,
    mixer_gain,
    mixer_out,
    post_gain,
    gate_weight,
    up_weight,
    down_weight,
):
    low, wide = jnp.bfloat16, jnp.float32
    rows, model = tokens.shape
    heads = query_weight.shape[1] // HEAD_SIZE
    ssm_heads = step_weight.shape[1]
    ssm_width = ssm_heads * P_SIZE
    query_width = heads * HEAD_SIZE
    first_device = lax.axis_index("tensor") == 0
    pick_head = lambda at: jnp.where(
        first_device,
        key_value_weight[:, at : at + HEAD_SIZE],
        key_value_weight[:, at + HEAD_SIZE : at + 2 * HEAD_SIZE],
    )
    keyval_weight = jnp.concatenate([pick_head(0), pick_head(KEYVALUE_HEADS * HEAD_SIZE)], 1)
    lane_pad = ((0, 0), (0, LANES - ssm_heads))
    step_weight_wide = jnp.pad(step_weight, lane_pad)
    step_bias_wide = jnp.pad(step_bias.astype(wide)[None], lane_pad)
    rate = -jnp.exp(decay_log.astype(wide))
    rate_wide = jnp.pad(rate[None], lane_pad)
    skip_row = jnp.repeat(skip_scale.astype(wide), P_SIZE)[None]
    cosine, sine = rotary_tables(rows)
    cosine = jnp.concatenate([cosine] * 4, 1)
    sine = jnp.concatenate([-sine, sine, -sine, sine], 1)
    seg_row = segments.astype(wide)
    seg_chunks = seg_row.reshape(-1, CHUNK)
    ends = seg_chunks[:, -1:]
    starts = jnp.concatenate([jnp.full((1, 1), -1.0, wide), ends[:-1]], 0)
    aux = jnp.stack(
        [seg_chunks, (seg_chunks == starts).astype(wide), (seg_chunks == ends).astype(wide)], -1
    ).reshape(rows, 3)
    aux = jnp.pad(aux, ((0, 0), (0, LANES - 3)))
    keeps = [seg_keep(segments, offset)[0] for offset in range(conv_inner.shape[0])]

    inputs = by_rows(tokens.astype(wide))
    inv_first = lax.rsqrt(jnp.mean(inputs * inputs, -1, keepdims=True) + EPS)
    unit_first = inputs * inv_first
    in_gain = input_gain.astype(wide)
    normed = by_rows((unit_first * in_gain).astype(low))
    inner = matmul(normed, inner_weight)
    state_in = matmul(normed, state_weight)
    step_arg = matmul(normed, step_weight_wide) + step_bias_wide
    gating = matmul(normed, gating_weight)
    inner_pre = conv_rows(inner, conv_inner, inner_bias, keeps)
    inner_act = jax.nn.silu(inner_pre)
    state_pre = conv_rows(state_in, conv_state, state_bias, keeps)
    coef = jax.nn.silu(state_pre).astype(low)
    step = jax.nn.softplus(step_arg)
    core, kept = scan_call(step, coef, inner_act, aux, seg_row, rate_wide)
    ssm_out = core + skip_row * inner_act
    sigma_gate = jax.nn.sigmoid(gating)
    gate_act = gating * sigma_gate
    gated = ssm_out * gate_act
    square_sum = pair_sum(jnp.sum(gated * gated, -1))[:, None]
    query_pre = matmul(normed, query_weight)
    keyval_pre = matmul(normed, keyval_weight)
    attended, queries, both, logs = attend_call(query_pre, keyval_pre, seg_row, aux, cosine, sine)
    attn_part = matmul(attended, attnout_weight)
    inv_gate = lax.rsqrt(square_sum / DSSM + EPS)
    mixer_scale = mixer_gain.astype(wide)
    mixed = (gated * inv_gate * mixer_scale).astype(low)
    branch_part = attn_part + matmul(mixed, mixer_out)
    out_gain = post_gain.astype(wide)
    branch_part = by_rows(branch_part.astype(low))
    half = rows // 2
    spans = [slice(0, half), slice(half, rows)]
    branches = [by_rows(pair_sum(branch_part[span])) for span in spans]
    weight_cat = jnp.concatenate(
        [gating_weight, inner_weight, step_weight_wide, state_weight, query_weight, keyval_weight], 1
    )
    branches[0], weight_cat = tie(branches[0], weight_cat)
    found = []
    for at, span in enumerate(spans):
        middle = inputs[span] + branches[at]
        inv_second = lax.rsqrt(jnp.mean(middle * middle, -1, keepdims=True) + EPS)
        unit_second = middle * inv_second
        post = by_rows((unit_second * out_gain).astype(low))
        gate = matmul(post, gate_weight)
        upward = matmul(post, up_weight)
        sigma = jax.nn.sigmoid(gate)
        hidden = (gate * sigma * upward).astype(low)
        hidden_grad = dot_nt(cotangent[span], down_weight)
        up_act_grad = (hidden_grad * gate * sigma).astype(low)
        gate_act_grad = (hidden_grad * upward * sigma * (1.0 + gate * (1.0 - sigma))).astype(low)
        post_part = dot_nt(gate_act_grad, gate_weight) + dot_nt(up_act_grad, up_weight)
        gain_part = jnp.sum(post_part * unit_second, 0, keepdims=True)
        post_low = by_rows(post_part.astype(low))
        if at == 0:
            branches[1], post_low = tie(branches[1], post_low)
        post_full = by_rows(pair_sum(post_low))
        found.append(
            (post_full, unit_second, inv_second, gain_part, hidden, post, gate_act_grad, up_act_grad)
        )
    post_gain_part = found[0][3] + found[1][3]
    forward_part = product_call(
        *[piece for k in range(4, 8) for piece in (found[0][k], found[1][k])], cotangent
    )
    post_fulls = [found[0][0], found[1][0]]
    post_fulls[1], _ = tie(post_fulls[1], forward_part)
    forward_piece = lax.psum_scatter(
        forward_part.reshape(-1, model), "dp", scatter_dimension=0, tiled=True
    )
    middle_grads = []
    for span, part, post_full in zip(spans, found, post_fulls):
        unit_second, inv_second = part[1], part[2]
        scaled_post = post_full * out_gain
        middle_grads.append(
            cotangent[span].astype(wide)
            + inv_second
            * (scaled_post - unit_second * jnp.mean(scaled_post * unit_second, -1, keepdims=True))
        )
    branch_grad = by_rows(jnp.concatenate([grad.astype(low) for grad in middle_grads], 0))
    middle_grad = jnp.concatenate(middle_grads, 0)
    mixed_grad = dot_nt(branch_grad, mixer_out)
    mixer_gain_part = jnp.sum(mixed_grad * gated * inv_gate, 0, keepdims=True)
    weighted = mixed_grad * mixer_scale
    cross = pair_sum(jnp.sum(weighted * gated, -1))[:, None]
    out_part = dot_tn(jnp.concatenate([attended, mixed], 1), branch_grad).astype(low)
    out_part = by_rows(out_part)
    attended_grad = dot_nt(branch_grad, attnout_weight).astype(low)
    gated_grad = inv_gate * weighted - gated * (inv_gate * inv_gate * inv_gate) * cross / DSSM
    ssm_grad = gated_grad * gate_act
    gating_grad = (
        gated_grad * ssm_out * sigma_gate * (1.0 + gating * (1.0 - sigma_gate))
    ).astype(low)
    gating_part = by_rows(dot_tn(normed, gating_grad).astype(low))
    bits = dp_bits()
    early = halve_parts([out_part, gating_part], bits[0])
    early, ssm_grad = tie(early, ssm_grad)
    early = halve(early, bits[1])
    act_grad, step_grad, coef_grad, rate_sum, skip_sum = scan_back_call(
        step, coef, inner_act, aux, seg_row, rate_wide, skip_row, ssm_grad, kept
    )
    early, act_grad, step_grad, coef_grad, forward_piece = tie(
        early, act_grad, step_grad, coef_grad, forward_piece
    )
    forward_total = lax.all_gather(forward_piece, "dp", axis=0, tiled=True)
    early = halve(early, bits[2])
    step_total = step_grad * jax.nn.sigmoid(step_arg)
    inner_pre_grad = act_grad * silu_slope(inner_pre)
    inner_grad, conv_inner_sums = conv_rows_back(inner_pre_grad, inner, conv_inner, keeps)
    state_pre_grad = coef_grad * silu_slope(state_pre)
    state_grad, conv_state_sums = conv_rows_back(state_pre_grad, state_in, conv_state, keeps)
    scan_cat = jnp.concatenate(
        [inner_grad.astype(low), step_total.astype(low), state_grad.astype(low)], 1
    )
    scan_part = dot_tn(normed, scan_cat).astype(low)
    early, scan_part, attended_grad = tie(early, scan_part, attended_grad)
    early = halve(early, bits[3])
    scan_part = halve(scan_part, bits[0])
    query_grad, keyval_grad = attend_back_call(
        queries, both, seg_row, aux, cosine, sine, logs, attended, attended_grad
    )
    attend_cat = jnp.concatenate([query_grad, keyval_grad], 1)
    attend_part = dot_tn(normed, attend_cat).astype(low)
    early, scan_part, attend_part, attend_cat = tie(early, scan_part, attend_part, attend_cat)
    early = double(early, bits[3])
    scan_part = halve(scan_part, bits[1])
    attend_part = halve(attend_part, bits[0])
    normed_part = dot_nt(jnp.concatenate([gating_grad, scan_cat, attend_cat], 1), weight_cat)
    input_gain_part = jnp.sum(normed_part * unit_first, 0, keepdims=True)
    early, scan_part, attend_part, normed_part, input_gain_part = tie(
        early, scan_part, attend_part, normed_part, input_gain_part
    )
    normed_full = by_rows(pair_sum(by_rows(normed_part.astype(low))))
    own_rows = [
        *conv_inner_sums,
        jnp.sum(inner_pre_grad, 0, keepdims=True),
        mixer_gain_part,
        skip_sum,
        jnp.sum(step_total, 0, keepdims=True),
        rate_sum * rate_wide,
    ]
    shared_rows = [
        input_gain_part,
        post_gain_part,
        *conv_state_sums,
        jnp.sum(state_pre_grad, 0, keepdims=True),
    ]
    small = jnp.concatenate(
        [jnp.pad(row, ((0, 0), (0, model - row.shape[1]))) for row in own_rows + shared_rows], 0
    )
    small = small + swap_bit(small, bits[0])
    early = double(early, bits[2])
    scan_part = halve(scan_part, bits[2])
    attend_part = halve(attend_part, bits[1])
    early, scan_part, attend_part, small = tie(early, scan_part, attend_part, small)
    early = double(early, bits[1])
    scan_part = halve(scan_part, bits[3])
    attend_part = halve(attend_part, bits[2])
    small = small + swap_bit(small, bits[1])
    scan_part, attend_part, small = tie(scan_part, attend_part, small)
    attend_part = halve(attend_part, bits[3])
    small = small + swap_bit(small, bits[2])
    attend_part, small, early, forward_total = tie(attend_part, small, early, forward_total)
    hidden_units = down_weight.shape[0]
    down_wgrad = forward_total[:hidden_units].astype(wide)
    gate_wgrad = forward_total[hidden_units : hidden_units + model].astype(wide)
    up_wgrad = forward_total[hidden_units + model :].astype(wide)
    small = small + swap_bit(small, bits[3])
    scan_piece, attend_piece = scan_part, attend_part
    state_at = ssm_width + LANES
    trade = jnp.concatenate([scan_piece[:, state_at:], attend_piece[:, query_width:]], 1)
    other = lax.ppermute(trade, "tensor", [(0, 1), (1, 0)])
    state_cols = state_weight.shape[1]
    state_piece = (
        trade[:, :state_cols].astype(wide) + other[:, :state_cols].astype(wide)
    ).astype(low)
    mine, theirs = trade[:, state_cols:], other[:, state_cols:]
    head_0 = jnp.where(first_device, mine, theirs)
    head_1 = jnp.where(first_device, theirs, mine)
    late = jnp.concatenate(
        [
            scan_piece[:, :state_at],
            state_piece,
            attend_piece[:, :query_width],
            head_0[:, :HEAD_SIZE],
            head_1[:, :HEAD_SIZE],
            head_0[:, HEAD_SIZE:],
            head_1[:, HEAD_SIZE:],
        ],
        1,
    )
    late, small = tie(late, small)
    late = double(late, bits[3])
    small_other = lax.ppermute(small, "tensor", [(0, 1), (1, 0)])
    is_shared = lax.broadcasted_iota(jnp.int32, small.shape, 0) >= len(own_rows)
    small = small + jnp.where(is_shared, small_other, 0.0)
    late, early, small = tie(late, early, small)
    late = double(late, bits[2])
    early = double(early, bits[0])
    late, early = tie(late, early)
    late = double(late, bits[1])
    early_grads = (
        gate_wgrad,
        up_wgrad,
        down_wgrad,
        early[:query_width, :model].astype(wide),
        early[:, model:].astype(wide),
        early[query_width:, :model].astype(wide),
    )
    scaled_in = normed_full * in_gain
    tokens_grad = middle_grad + inv_first * (
        scaled_in - unit_first * jnp.mean(scaled_in * unit_first, -1, keepdims=True)
    )
    late, tokens_grad, *early_grads = tie(late, tokens_grad, *early_grads)
    late = double(late, bits[0])
    scan_total = late[:, : state_at + state_cols]
    attend_total = late[:, state_at + state_cols :]
    gate_wgrad, up_wgrad, down_wgrad, attnout_grad, gating_wgrad, mixout_grad = early_grads
    count = len(own_rows)
    taps = conv_inner.shape[0]
    return (
        tokens_grad,
        small[count],
        attend_total[:, :query_width].astype(wide),
        attend_total[:, query_width:].astype(wide),
        attnout_grad,
        gating_wgrad,
        scan_total[:, :ssm_width].astype(wide),
        scan_total[:, state_at:].astype(wide),
        scan_total[:, ssm_width : ssm_width + ssm_heads].astype(wide),
        small[:taps, :ssm_width],
        small[count + 2 : count + 2 + taps, :state_cols],
        small[taps, :ssm_width],
        small[count + 2 + taps, :state_cols],
        small[taps + 3, :ssm_heads],
        small[taps + 4, :ssm_heads],
        jnp.sum(small[taps + 2, :ssm_width].reshape(ssm_heads, P_SIZE), 1),
        small[taps + 1, :ssm_width],
        mixout_grad,
        small[count + 1],
        gate_wgrad,
        up_wgrad,
        down_wgrad,
    )


def layer(*arrays):
    tokens, segments, query_weight, step_weight = arrays[0], arrays[1], arrays[4], arrays[10]
    size = lax.axis_size("dp")
    fits = (
        lax.axis_size("tensor") == 2
        and size == 16
        and segments.shape[0] == 1
        and tokens.shape[0] % CHUNK == 0
        and tokens.shape[1] % (16 * size) == 0
        and query_weight.shape[1] == QUERY_HEADS // KEYVALUE_HEADS * HEAD_SIZE
        and KEYVALUE_HEADS == 2
        and arrays[23].shape[0] == tokens.shape[1]
        and step_weight.shape[1] % 2 == 0
        and query_weight.shape[1] + step_weight.shape[1] * P_SIZE == tokens.shape[1]
    )
    return local_fast(*arrays) if fits else local(*arrays)


def solution(mesh):
    placed = (
        P("dp", None),
        P("dp", None),
        P("dp", None),
        P(),
        P(None, "tensor"),
        P(),
        P("tensor", None),
        P(None, "tensor"),
        P(None, "tensor"),
        P(),
        P(None, "tensor"),
        P(None, "tensor"),
        P(),
        P("tensor"),
        P(),
        P("tensor"),
        P("tensor"),
        P("tensor"),
        P("tensor"),
        P("tensor", None),
        P(),
        P(None, "tensor"),
        P(None, "tensor"),
        P("tensor", None),
    )
    return jax.shard_map(
        layer,
        mesh=mesh,
        in_specs=placed,
        out_specs=(
            P("dp", None),
            P(),
            P(None, "tensor"),
            P(),
            P("tensor", None),
            P(None, "tensor"),
            P(None, "tensor"),
            P(),
            P(None, "tensor"),
            P(None, "tensor"),
            P(),
            P("tensor"),
            P(),
            P("tensor"),
            P("tensor"),
            P("tensor"),
            P("tensor"),
            P("tensor", None),
            P(),
            P(None, "tensor"),
            P(None, "tensor"),
            P("tensor", None),
        ),
        check_vma=False,
    )
```

```python
import jax
import jax.numpy as jnp
from jax import lax
from jax.experimental.layout import Layout, with_layout_constraint
from jax.experimental import pallas as pl
from jax.experimental.pallas import tpu as pltpu
from jax.sharding import PartitionSpec as P

QUERY_HEADS = 8
KEYVALUE_HEADS = 2
HEAD_SIZE = 64
P_SIZE = 64
NS = 128
DSSM = 1536


EPS = 1e-05
ROPE_BASE = 100000000000.0
NEG_FILL = -1e30


def matmul(left, right):
    return jnp.dot(left, right, preferred_element_type=jnp.float32)


def rotary_tables(document_length):
    half = HEAD_SIZE // 2
    freqs = jnp.exp(-jnp.log(ROPE_BASE) * (2.0 * jnp.arange(half, dtype=jnp.float32) / HEAD_SIZE))
    angles = jnp.arange(document_length, dtype=jnp.float32)[:, None] * freqs[None, :]
    return (jnp.cos(angles), jnp.sin(angles))


def rotate(value, cosine, sine):
    half = value.shape[-1] // 2
    first = value[..., :half]
    second = value[..., half:]
    return jnp.concatenate([first * cosine - second * sine, first * sine + second * cosine], -1)


def rotate_back(grad, cosine, sine):
    half = grad.shape[-1] // 2
    first = grad[..., :half]
    second = grad[..., half:]
    return jnp.concatenate([first * cosine + second * sine, second * cosine - first * sine], -1)


def silu_slope(value):
    sigma = jax.nn.sigmoid(value)
    return sigma * (1.0 + value * (1.0 - sigma))


def seg_keep(segments, offset):
    document_length = segments.shape[1]
    moved = jnp.pad(segments, ((0, 0), (offset, 0)), constant_values=-1)[:, :document_length]
    return (moved == segments).astype(jnp.float32)[:, :, None]


def move_down(value, offset):
    document_length = value.shape[1]
    return jnp.pad(value, ((0, 0), (offset, 0), (0, 0)))[:, :document_length]


def move_up(value, offset):
    return jnp.pad(value, ((0, 0), (0, offset), (0, 0)))[:, offset:]


def conv_forward(value, kernel, bias, segments):
    taps = kernel.shape[0]
    total = jnp.zeros_like(value) + bias.astype(jnp.float32)
    for tap in range(taps):
        offset = taps - 1 - tap
        total = total + kernel[tap].astype(jnp.float32) * move_down(value, offset) * seg_keep(
            segments, offset
        )
    return total


def conv_backward(grad, value, kernel, segments):
    taps = kernel.shape[0]
    grad_in = jnp.zeros_like(value)
    kernel_rows = []
    for tap in range(taps):
        offset = taps - 1 - tap
        masked = grad * seg_keep(segments, offset)
        kernel_rows.append(jnp.sum(masked * move_down(value, offset), axis=(0, 1)))
        grad_in = grad_in + kernel[tap].astype(jnp.float32) * move_up(masked, offset)
    return (grad_in, jnp.stack(kernel_rows))


def ssd_parts(step_block, rate, coef_b, coef_c, heads_block, allowed):
    coupling = jnp.einsum("tn,sn->ts", coef_c, coef_b, preferred_element_type=jnp.float32)
    cumulative = jnp.cumsum(step_block * rate, axis=0).T
    difference = cumulative[:, :, None] - cumulative[:, None, :]
    decay = jnp.where(allowed[None], jnp.exp(jnp.where(allowed[None], difference, 0.0)), 0.0)
    mixing = (coupling[None] * decay).astype(jnp.bfloat16)
    driven = (heads_block * step_block.T[:, :, None]).astype(jnp.bfloat16)
    return (coupling, decay, mixing, driven)


def pair_sum(value):
    if lax.axis_size("tensor") == 2:
        other = lax.ppermute(value, "tensor", [(0, 1), (1, 0)])
        return value.astype(jnp.float32) + other.astype(jnp.float32)
    return lax.psum(value, "tensor").astype(jnp.float32)


def swap_bit(value, bit):
    size = lax.axis_size("dp")
    return lax.ppermute(value, "dp", [(i, i ^ bit) for i in range(size)])


def shared_sum(rows, first_shared):
    tail = pair_sum(rows[:, first_shared:]).astype(rows.dtype)
    return jnp.concatenate([rows[:, :first_shared], tail], 1) if first_shared else tail


def tree_sum(value, first_shared=None):
    size = lax.axis_size("dp")
    rows = value.shape[0]
    if size & (size - 1) or rows % (16 * size):
        total = lax.psum(value, "dp")
        return total if first_shared is None else shared_sum(total, first_shared)
    bits = [1 << i for i in range(size.bit_length() - 1)]
    me = lax.axis_index("dp")
    for bit in bits:
        half = value.shape[0] // 2
        low, high = value[:half], value[half:]
        upper = (me & bit) != 0
        got = swap_bit(jnp.where(upper, low, high), bit)
        kept = jnp.where(upper, high, low)
        value = (kept.astype(jnp.float32) + got.astype(jnp.float32)).astype(value.dtype)
    if first_shared is not None:
        value = shared_sum(value, first_shared)
    for bit in reversed(bits):
        upper = (me & bit) != 0
        got = swap_bit(value, bit)
        value = jnp.where(
            upper, jnp.concatenate([got, value], 0), jnp.concatenate([value, got], 0)
        )
    return value


def local(
    tokens,
    segments,
    cotangent,
    input_gain,
    query_weight,
    key_value_weight,
    attnout_weight,
    gating_weight,
    inner_weight,
    state_weight,
    step_weight,
    conv_inner,
    conv_state,
    inner_bias,
    state_bias,
    step_bias,
    decay_log,
    skip_scale,
    mixer_gain,
    mixer_out,
    post_gain,
    gate_weight,
    up_weight,
    down_weight,
):
    seq_count, document_length = segments.shape
    rows = seq_count * document_length
    heads = query_weight.shape[1] // HEAD_SIZE
    ssm_heads = step_weight.shape[1]
    query_group = QUERY_HEADS // KEYVALUE_HEADS
    shared_key_head = lax.axis_index("tensor") * heads // query_group
    scale = HEAD_SIZE ** (-0.5)
    cosine, sine = rotary_tables(document_length)
    positions = jnp.arange(document_length)

    def allowed_of(seg_ids):
        return (positions[:, None] >= positions[None, :]) & (seg_ids[:, None] == seg_ids[None, :])

    inputs = tokens.astype(jnp.float32)
    inv_first = lax.rsqrt(jnp.mean(inputs * inputs, -1, keepdims=True) + EPS)
    unit_first = inputs * inv_first
    in_gain = input_gain.astype(jnp.float32)
    normed = (unit_first * in_gain).astype(jnp.bfloat16)
    key_cols = lax.dynamic_slice_in_dim(key_value_weight, shared_key_head * HEAD_SIZE, HEAD_SIZE, 1)
    value_columns = lax.dynamic_slice_in_dim(
        key_value_weight, (KEYVALUE_HEADS + shared_key_head) * HEAD_SIZE, HEAD_SIZE, 1
    )
    query_pre = matmul(normed, query_weight)
    key_pre = matmul(normed, key_cols)
    value_pre = matmul(normed, value_columns)
    queries = rotate(
        query_pre.reshape(seq_count, document_length, heads, HEAD_SIZE).transpose(0, 2, 1, 3),
        cosine,
        sine,
    ).astype(jnp.bfloat16)
    key_rows = rotate(key_pre.reshape(seq_count, document_length, HEAD_SIZE), cosine, sine).astype(
        jnp.bfloat16
    )
    value_rows = value_pre.reshape(seq_count, document_length, HEAD_SIZE).astype(jnp.bfloat16)

    def attend(seq_item):
        query_block, key_block, value_block, seg_ids = seq_item
        allowed = allowed_of(seg_ids)[None]
        scores = (
            jnp.einsum("htd,sd->hts", query_block, key_block, preferred_element_type=jnp.float32)
            * scale
        )
        scores = jnp.where(allowed, scores, NEG_FILL)
        top = jnp.max(scores, -1, keepdims=True)
        weights = jnp.exp(scores - top)
        total = jnp.sum(weights, -1, keepdims=True)
        probs = (weights / total).astype(jnp.bfloat16)
        attended = jnp.einsum("hts,sd->htd", probs, value_block, preferred_element_type=jnp.float32)
        return (attended.astype(jnp.bfloat16), (top + jnp.log(total))[..., 0])

    attended, logsum = lax.map(attend, (queries, key_rows, value_rows, segments))
    attn_flat = attended.transpose(0, 2, 1, 3).reshape(rows, heads * HEAD_SIZE)
    attn_part = matmul(attn_flat, attnout_weight)
    gating = matmul(normed, gating_weight)
    inner = matmul(normed, inner_weight).reshape(seq_count, document_length, -1)
    state_in = matmul(normed, state_weight).reshape(seq_count, document_length, -1)
    step_raw = matmul(normed, step_weight)
    inner_pre = conv_forward(inner, conv_inner, inner_bias, segments)
    inner_act = jax.nn.silu(inner_pre)
    state_pre = conv_forward(state_in, conv_state, state_bias, segments)
    state_act = jax.nn.silu(state_pre)
    coef_b = state_act[..., :NS].astype(jnp.bfloat16)
    coef_c = state_act[..., NS:].astype(jnp.bfloat16)
    step_arg = step_raw.reshape(seq_count, document_length, ssm_heads) + step_bias.astype(
        jnp.float32
    )
    step = jax.nn.softplus(step_arg)
    rate = -jnp.exp(decay_log.astype(jnp.float32))
    heads_in = inner_act.reshape(seq_count, document_length, ssm_heads, P_SIZE).transpose(
        0, 2, 1, 3
    )

    def scan_forward(seq_item):
        step_block, coef_b_block, coef_c_block, heads_block, seg_ids = seq_item
        parts = ssd_parts(
            step_block, rate, coef_b_block, coef_c_block, heads_block, allowed_of(seg_ids)
        )
        return jnp.einsum("hts,hsp->htp", parts[2], parts[3], preferred_element_type=jnp.float32)

    core = lax.map(scan_forward, (step, coef_b, coef_c, heads_in, segments))
    skip = skip_scale.astype(jnp.float32)[None, :, None, None]
    ssm_out = (core + skip * heads_in).transpose(0, 2, 1, 3).reshape(rows, ssm_heads * P_SIZE)
    sigma_gate = jax.nn.sigmoid(gating)
    gate_act = gating * sigma_gate
    gated = ssm_out * gate_act
    square_sum = pair_sum(jnp.sum(gated * gated, -1))[:, None]
    inv_gate = lax.rsqrt(square_sum / DSSM + EPS)
    mixer_scale = mixer_gain.astype(jnp.float32)
    mixed = (gated * inv_gate * mixer_scale).astype(jnp.bfloat16)
    branch_part = attn_part + matmul(mixed, mixer_out)
    out_gain = post_gain.astype(jnp.float32)
    branch = pair_sum(branch_part.astype(jnp.bfloat16))
    middle = inputs + branch
    inv_second = lax.rsqrt(jnp.mean(middle * middle, -1, keepdims=True) + EPS)
    unit_second = middle * inv_second
    post = (unit_second * out_gain).astype(jnp.bfloat16)
    gate = matmul(post, gate_weight)
    upward = matmul(post, up_weight)
    sigma = jax.nn.sigmoid(gate)
    hidden = (gate * sigma * upward).astype(jnp.bfloat16)
    down_wgrad = jnp.einsum("tf,td->fd", hidden, cotangent, preferred_element_type=jnp.float32)
    hidden_grad = jnp.einsum(
        "td,fd->tf", cotangent, down_weight, preferred_element_type=jnp.float32
    )
    up_act_grad = (hidden_grad * gate * sigma).astype(jnp.bfloat16)
    gate_act_grad = (hidden_grad * upward * sigma * (1.0 + gate * (1.0 - sigma))).astype(
        jnp.bfloat16
    )
    gate_wgrad = jnp.einsum("tc,tf->cf", post, gate_act_grad, preferred_element_type=jnp.float32)
    up_wgrad = jnp.einsum("tc,tf->cf", post, up_act_grad, preferred_element_type=jnp.float32)
    post_part = jnp.einsum(
        "tf,cf->tc", gate_act_grad, gate_weight, preferred_element_type=jnp.float32
    ) + jnp.einsum("tf,cf->tc", up_act_grad, up_weight, preferred_element_type=jnp.float32)
    post_gain_part = jnp.sum(post_part * unit_second, 0)
    post_full = pair_sum(post_part.astype(jnp.bfloat16))
    down_wgrad, gate_wgrad, up_wgrad, post_full = lax.optimization_barrier(
        (
            down_wgrad.astype(jnp.bfloat16),
            gate_wgrad.astype(jnp.bfloat16),
            up_wgrad.astype(jnp.bfloat16),
            post_full,
        )
    )
    down_wgrad, gate_wgrad, up_wgrad = lax.psum((down_wgrad, gate_wgrad, up_wgrad), "dp")
    scaled_post = post_full * out_gain
    middle_grad = cotangent.astype(jnp.float32) + inv_second * (
        scaled_post - unit_second * jnp.mean(scaled_post * unit_second, -1, keepdims=True)
    )
    branch_grad = middle_grad.astype(jnp.bfloat16)
    attnout_wgrad = jnp.einsum(
        "tk,td->kd", attn_flat, branch_grad, preferred_element_type=jnp.float32
    )
    attended_grad = jnp.einsum(
        "td,kd->tk", branch_grad, attnout_weight, preferred_element_type=jnp.float32
    )
    attended_grad = (
        attended_grad.astype(jnp.bfloat16)
        .reshape(seq_count, document_length, heads, HEAD_SIZE)
        .transpose(0, 2, 1, 3)
    )

    def attend_back(seq_item):
        query_block, key_block, value_block, seg_ids, logsum_block, grad_block = seq_item
        allowed = allowed_of(seg_ids)[None]
        scores = (
            jnp.einsum("htd,sd->hts", query_block, key_block, preferred_element_type=jnp.float32)
            * scale
        )
        probs = jnp.where(allowed, jnp.exp(scores - logsum_block[..., None]), 0.0)
        value_grad = jnp.einsum(
            "hts,htd->hsd",
            probs.astype(jnp.bfloat16),
            grad_block,
            preferred_element_type=jnp.float32,
        )
        prob_grad = jnp.einsum(
            "htd,sd->hts", grad_block, value_block, preferred_element_type=jnp.float32
        )
        delta = jnp.sum(probs * prob_grad, -1, keepdims=True)
        score_grad = (probs * (prob_grad - delta)).astype(jnp.bfloat16)
        query_grad = (
            jnp.einsum("hts,sd->htd", score_grad, key_block, preferred_element_type=jnp.float32)
            * scale
        )
        key_grad = (
            jnp.einsum("hts,htd->hsd", score_grad, query_block, preferred_element_type=jnp.float32)
            * scale
        )
        return (query_grad, key_grad, value_grad)

    query_rot_grad, key_rot_grad, value_head_grad = lax.map(
        attend_back, (queries, key_rows, value_rows, segments, logsum, attended_grad)
    )
    query_pre_grad = (
        rotate_back(query_rot_grad, cosine, sine)
        .astype(jnp.bfloat16)
        .transpose(0, 2, 1, 3)
        .reshape(rows, heads * HEAD_SIZE)
    )
    key_pre_grad = rotate_back(key_rot_grad, cosine, sine).astype(jnp.bfloat16)
    value_pre_grad = value_head_grad.astype(jnp.bfloat16)
    normed_seq = normed.reshape(seq_count, document_length, -1)
    query_wgrad = jnp.einsum(
        "tc,tk->ck", normed, query_pre_grad, preferred_element_type=jnp.float32
    )
    key_wgrad = jnp.einsum(
        "slc,shld->cd", normed_seq, key_pre_grad, preferred_element_type=jnp.float32
    )
    value_weight_grad = jnp.einsum(
        "slc,shld->cd", normed_seq, value_pre_grad, preferred_element_type=jnp.float32
    )
    normed_part = (
        jnp.einsum("tk,ck->tc", query_pre_grad, query_weight, preferred_element_type=jnp.float32)
        + jnp.einsum(
            "shld,cd->slc", key_pre_grad, key_cols, preferred_element_type=jnp.float32
        ).reshape(rows, -1)
        + jnp.einsum(
            "shld,cd->slc", value_pre_grad, value_columns, preferred_element_type=jnp.float32
        ).reshape(rows, -1)
    )
    mixout_wgrad = jnp.einsum("tk,td->kd", mixed, branch_grad, preferred_element_type=jnp.float32)
    mixed_grad = jnp.einsum("td,kd->tk", branch_grad, mixer_out, preferred_element_type=jnp.float32)
    mixer_gain_wgrad = jnp.sum(mixed_grad * gated * inv_gate, 0)
    weighted = mixed_grad * mixer_scale
    cross = pair_sum(jnp.sum(weighted * gated, -1))[:, None]
    gated_grad = inv_gate * weighted - gated * (inv_gate * inv_gate * inv_gate) * cross / DSSM
    ssm_grad = gated_grad * gate_act
    gating_act_grad = (
        gated_grad * ssm_out * sigma_gate * (1.0 + gating * (1.0 - sigma_gate))
    ).astype(jnp.bfloat16)
    ssm_heads_grad = ssm_grad.reshape(seq_count, document_length, ssm_heads, P_SIZE).transpose(
        0, 2, 1, 3
    )
    core_grad = ssm_heads_grad.astype(jnp.bfloat16)
    skip_wgrad = jnp.sum(ssm_heads_grad * heads_in, axis=(0, 2, 3))

    def scan_back(seq_item):
        step_block, coef_b_block, coef_c_block, heads_block, seg_ids, core_block = seq_item
        coupling, decay, mixing, driven = ssd_parts(
            step_block, rate, coef_b_block, coef_c_block, heads_block, allowed_of(seg_ids)
        )
        mix_grad = jnp.einsum(
            "htp,hsp->hts", core_block, driven, preferred_element_type=jnp.float32
        )
        driven_grad = jnp.einsum(
            "hts,htp->hsp", mixing, core_block, preferred_element_type=jnp.float32
        )
        rounded = (mix_grad * decay).astype(jnp.bfloat16)
        coef_c_grad = jnp.einsum(
            "hts,sn->tn", rounded, coef_b_block, preferred_element_type=jnp.float32
        )
        coef_b_grad = jnp.einsum(
            "hts,tn->sn", rounded, coef_c_block, preferred_element_type=jnp.float32
        )
        spread = mix_grad * coupling[None] * decay
        cumulative_grad = jnp.sum(spread, 2) - jnp.sum(spread, 1)
        log_grad = jnp.flip(jnp.cumsum(jnp.flip(cumulative_grad, 1), 1), 1)
        heads_grad = driven_grad * step_block.T[:, :, None]
        step_grad = (jnp.sum(driven_grad * heads_block, -1) + log_grad * rate[:, None]).T
        rate_grad = jnp.sum(log_grad * step_block.T, 1)
        return (heads_grad, step_grad, rate_grad, coef_b_grad, coef_c_grad)

    heads_grad, step_grad, rate_grad, coef_b_grad, coef_c_grad = lax.map(
        scan_back, (step, coef_b, coef_c, heads_in, segments, core_grad)
    )
    heads_total = heads_grad + ssm_heads_grad * skip
    inner_act_grad = heads_total.transpose(0, 2, 1, 3).reshape(seq_count, document_length, -1)
    step_total = step_grad * jax.nn.sigmoid(step_arg)
    step_bias_wgrad = jnp.sum(step_total, axis=(0, 1))
    decay_wgrad = jnp.sum(rate_grad, 0) * rate
    step_raw_grad = step_total.reshape(rows, ssm_heads).astype(jnp.bfloat16)
    inner_pre_grad = inner_act_grad * silu_slope(inner_pre)
    inner_bias_wgrad = jnp.sum(inner_pre_grad, axis=(0, 1))
    inner_grad, conv_inner_wgrad = conv_backward(inner_pre_grad, inner, conv_inner, segments)
    inner_grad = inner_grad.reshape(rows, -1).astype(jnp.bfloat16)
    state_act_grad = jnp.concatenate([coef_b_grad, coef_c_grad], -1)
    state_pre_grad = state_act_grad * silu_slope(state_pre)
    state_bias_wgrad = jnp.sum(state_pre_grad, axis=(0, 1))
    state_grad, conv_state_wgrad = conv_backward(state_pre_grad, state_in, conv_state, segments)
    state_grad = state_grad.reshape(rows, -1).astype(jnp.bfloat16)
    gating_wgrad = jnp.einsum(
        "tc,tk->ck", normed, gating_act_grad, preferred_element_type=jnp.float32
    )
    inner_wgrad = jnp.einsum("tc,tk->ck", normed, inner_grad, preferred_element_type=jnp.float32)
    step_wgrad = jnp.einsum("tc,tk->ck", normed, step_raw_grad, preferred_element_type=jnp.float32)
    state_wgrad = jnp.einsum("tc,tk->ck", normed, state_grad, preferred_element_type=jnp.float32)
    normed_part = (
        normed_part
        + jnp.einsum(
            "tk,ck->tc", gating_act_grad, gating_weight, preferred_element_type=jnp.float32
        )
        + jnp.einsum("tk,ck->tc", inner_grad, inner_weight, preferred_element_type=jnp.float32)
        + jnp.einsum("tk,ck->tc", step_raw_grad, step_weight, preferred_element_type=jnp.float32)
        + jnp.einsum("tk,ck->tc", state_grad, state_weight, preferred_element_type=jnp.float32)
    )
    input_gain_part = jnp.sum(normed_part * unit_first, 0)
    normed_full = pair_sum(normed_part.astype(jnp.bfloat16))
    scaled_in = normed_full * in_gain
    tokens_grad = middle_grad + inv_first * (
        scaled_in - unit_first * jnp.mean(scaled_in * unit_first, -1, keepdims=True)
    )
    low = jnp.bfloat16
    if lax.axis_size("tensor") == 2 and KEYVALUE_HEADS == 2:
        keyval_part = jnp.concatenate([key_wgrad, value_weight_grad], 1)
    else:
        keyval_part = jnp.zeros(key_value_weight.shape, jnp.float32)
        keyval_part = lax.dynamic_update_slice_in_dim(
            keyval_part, key_wgrad, shared_key_head * HEAD_SIZE, 1
        )
        keyval_part = lax.dynamic_update_slice_in_dim(
            keyval_part, value_weight_grad, (KEYVALUE_HEADS + shared_key_head) * HEAD_SIZE, 1
        )
        keyval_part = lax.psum(keyval_part, "tensor")
    first_total = tree_sum(
        jnp.concatenate(
            [query_wgrad.astype(low), keyval_part.astype(low), gating_wgrad.astype(low)], 1
        )
    ).astype(jnp.float32)
    second_total = tree_sum(
        jnp.concatenate([attnout_wgrad.astype(low), mixout_wgrad.astype(low)], 0)
    ).astype(jnp.float32)
    width = query_wgrad.shape[1]
    kv_width = keyval_part.shape[1]
    query_wgrad = first_total[:, :width]
    keyval_part = first_total[:, width : width + kv_width]
    gating_wgrad = first_total[:, width + kv_width :]
    attnout_wgrad = second_total[: heads * HEAD_SIZE]
    mixout_wgrad = second_total[heads * HEAD_SIZE :]
    if lax.axis_size("tensor") == 2 and KEYVALUE_HEADS == 2:
        other = lax.ppermute(keyval_part.astype(low), "tensor", [(0, 1), (1, 0)])
        mine = keyval_part.astype(low)
        is_first = lax.axis_index("tensor") == 0
        head_0 = jnp.where(is_first, mine, other)
        head_1 = jnp.where(is_first, other, mine)
        key_value_weight_grad = jnp.concatenate(
            [
                head_0[:, :HEAD_SIZE],
                head_1[:, :HEAD_SIZE],
                head_0[:, HEAD_SIZE:],
                head_1[:, HEAD_SIZE:],
            ],
            1,
        ).astype(jnp.float32)
    else:
        key_value_weight_grad = keyval_part
    own = [
        step_bias_wgrad,
        decay_wgrad,
        skip_wgrad,
        mixer_gain_wgrad,
        inner_bias_wgrad,
        conv_inner_wgrad.reshape(-1),
    ]
    shared = [input_gain_part, post_gain_part, state_bias_wgrad, conv_state_wgrad.reshape(-1)]

    def columns_of(parts):
        flat = jnp.concatenate(parts)
        count = -(-flat.shape[0] // tokens.shape[1])
        flat = jnp.pad(flat, (0, count * tokens.shape[1] - flat.shape[0]))
        return flat.reshape(count, tokens.shape[1]).T

    def parts_of(columns, parts):
        flat = columns.T.reshape(-1)
        found, at = [], 0
        for part in parts:
            found.append(flat[at : at + part.shape[0]])
            at += part.shape[0]
        return found

    own_columns, shared_columns = columns_of(own), columns_of(shared)
    inner_width = inner_wgrad.shape[1]
    own_width = own_columns.shape[1]
    shared_from = -(-(inner_width + ssm_heads + own_width) // 128) * 128
    pad = shared_from - inner_width - ssm_heads - own_width
    third_total = tree_sum(
        jnp.concatenate(
            [
                inner_wgrad.astype(low),
                step_wgrad.astype(low),
                own_columns.astype(low),
                jnp.zeros((tokens.shape[1], pad), low),
                state_wgrad.astype(low),
                shared_columns.astype(low),
            ],
            1,
        ),
        shared_from,
    ).astype(jnp.float32)
    inner_wgrad = third_total[:, :inner_width]
    step_wgrad = third_total[:, inner_width : inner_width + ssm_heads]
    at = inner_width + ssm_heads
    (
        step_bias_wgrad,
        decay_wgrad,
        skip_wgrad,
        mixer_gain_wgrad,
        inner_bias_wgrad,
        conv_inner_flat,
    ) = parts_of(third_total[:, at : at + own_width], own)
    conv_inner_wgrad = conv_inner_flat.reshape(conv_inner.shape)
    state_width = state_wgrad.shape[1]
    state_wgrad = third_total[:, shared_from : shared_from + state_width]
    input_gain_part, post_gain_part, state_bias_wgrad, conv_state_flat = parts_of(
        third_total[:, shared_from + state_width :], shared
    )
    conv_state_wgrad = conv_state_flat.reshape(conv_state.shape)
    down_wgrad = down_wgrad.astype(jnp.float32)
    gate_wgrad = gate_wgrad.astype(jnp.float32)
    up_wgrad = up_wgrad.astype(jnp.float32)
    return (
        tokens_grad,
        input_gain_part,
        query_wgrad,
        key_value_weight_grad,
        attnout_wgrad,
        gating_wgrad,
        inner_wgrad,
        state_wgrad,
        step_wgrad,
        conv_inner_wgrad,
        conv_state_wgrad,
        inner_bias_wgrad,
        state_bias_wgrad,
        step_bias_wgrad,
        decay_wgrad,
        skip_wgrad,
        mixer_gain_wgrad,
        mixout_wgrad,
        post_gain_part,
        gate_wgrad,
        up_wgrad,
        down_wgrad,
    )


CHUNK = 256
LANES = 128
VMEM_BYTES = 56 * 1024 * 1024


def dot_nn(left, right):
    return lax.dot_general(left, right, (((1,), (0,)), ((), ())), preferred_element_type=jnp.float32)


def dot_nt(left, right):
    return lax.dot_general(left, right, (((1,), (1,)), ((), ())), preferred_element_type=jnp.float32)


def dot_tn(left, right):
    return lax.dot_general(left, right, (((0,), (0,)), ((), ())), preferred_element_type=jnp.float32)


def split_two(value):
    high = value.astype(jnp.bfloat16)
    return high, (value - high.astype(jnp.float32)).astype(jnp.bfloat16)


def exact_nn(ones, value):
    high, low = split_two(value)
    return dot_nn(ones, high) + dot_nn(ones, low)


def grid_of(shape):
    return (
        lax.broadcasted_iota(jnp.int32, shape, 0),
        lax.broadcasted_iota(jnp.int32, shape, 1),
    )


def pick(columns, pair):
    rows = columns.shape[0]
    left = jnp.broadcast_to(columns[:, 2 * pair : 2 * pair + 1], (rows, LANES))
    right = jnp.broadcast_to(columns[:, 2 * pair + 1 : 2 * pair + 2], (rows, LANES))
    return jnp.where(grid_of((rows, LANES))[1] < P_SIZE, left, right)


def scan_terms(step, rate, aux):
    row, col = grid_of((CHUNK, CHUNK))
    lower = (row >= col).astype(jnp.bfloat16)
    cumulative = exact_nn(lower, step * rate)
    last = cumulative[CHUNK - 1 : CHUNK]
    enter = jnp.exp(cumulative) * aux[:, 1:2]
    leave = jnp.exp(last - cumulative) * aux[:, 2:3]
    across = jnp.exp(last) * aux[CHUNK - 1 : CHUNK, 1:2]
    return cumulative, enter, leave, across


def scan_kernel(step_ref, coef_ref, act_ref, aux_ref, seg_ref, rate_ref, core_ref, kept_ref, state, moved):
    @pl.when(pl.program_id(0) == 0)
    def _():
        state[...] = jnp.zeros_like(state)

    step = step_ref[...]
    aux = aux_ref[...]
    cumulative, enter, leave, across = scan_terms(step, rate_ref[...], aux)
    cum_rows = cumulative.T
    row, col = grid_of((CHUNK, CHUNK))
    blocked = jnp.where((row >= col) & (aux[:, 0:1] == seg_ref[...]), 0.0, NEG_FILL)
    coef_b = coef_ref[:, :NS]
    coef_c = coef_ref[:, NS:]
    coupling = dot_nt(coef_c, coef_b)
    low_state = state[...].astype(jnp.bfloat16)
    kept_ref[0] = low_state
    carried = dot_nn(coef_c, low_state)
    first = grid_of((CHUNK, LANES))[1] < P_SIZE
    for pair in range(act_ref.shape[1] // LANES):
        at = slice(pair * LANES, (pair + 1) * LANES)
        driven = (act_ref[:, at] * pick(step, pair)).astype(jnp.bfloat16)
        parts = []
        for head in (2 * pair, 2 * pair + 1):
            decay = jnp.exp(cumulative[:, head : head + 1] - cum_rows[head : head + 1] + blocked)
            parts.append(dot_nn((coupling * decay).astype(jnp.bfloat16), driven))
        core_ref[:, at] = jnp.where(first, parts[0], parts[1]) + carried[:, at] * pick(enter, pair)
        moved[:, at] = (driven.astype(jnp.float32) * pick(leave, pair)).astype(jnp.bfloat16)
    fresh = dot_tn(coef_b, moved[...])
    for pair in range(act_ref.shape[1] // LANES):
        at = slice(pair * LANES, (pair + 1) * LANES)
        state[:, at] = state[:, at] * pick(across, pair) + fresh[:, at]


def scan_call(step, coef, act, aux, seg_row, rate):
    rows, width = act.shape
    chunks = rows // CHUNK
    by_chunk = lambda columns: pl.BlockSpec((CHUNK, columns), lambda i: (i, 0))
    return pl.pallas_call(
        scan_kernel,
        grid=(chunks,),
        in_specs=[
            by_chunk(LANES),
            by_chunk(2 * NS),
            by_chunk(width),
            by_chunk(LANES),
            pl.BlockSpec((1, CHUNK), lambda i: (0, i)),
            pl.BlockSpec((1, LANES), lambda i: (0, 0)),
        ],
        out_specs=[by_chunk(width), pl.BlockSpec((1, NS, width), lambda i: (i, 0, 0))],
        out_shape=[
            jax.ShapeDtypeStruct((rows, width), jnp.float32),
            jax.ShapeDtypeStruct((chunks, NS, width), jnp.bfloat16),
        ],
        scratch_shapes=[
            pltpu.VMEM((NS, width), jnp.float32),
            pltpu.VMEM((CHUNK, width), jnp.bfloat16),
        ],
        compiler_params=pltpu.CompilerParams(vmem_limit_bytes=VMEM_BYTES),
        name="scan_forward",
    )(step, coef, act, aux, seg_row, rate)


def scan_back_kernel(
    step_ref,
    coef_ref,
    act_ref,
    aux_ref,
    seg_ref,
    rate_ref,
    skip_ref,
    grad_ref,
    kept_ref,
    act_grad_ref,
    step_grad_ref,
    coef_grad_ref,
    sums_ref,
    skip_sum_ref,
    state_grad,
    moved,
    entered,
    row_sums,
):
    @pl.when(pl.program_id(0) == 0)
    def _():
        state_grad[...] = jnp.zeros_like(state_grad)
        sums_ref[...] = jnp.zeros_like(sums_ref)
        skip_sum_ref[...] = jnp.zeros_like(skip_sum_ref)
        row_sums[...] = jnp.zeros_like(row_sums)

    step = step_ref[...]
    aux = aux_ref[...]
    rate = rate_ref[...]
    cumulative, enter, leave, across = scan_terms(step, rate, aux)
    cum_rows = cumulative.T
    row, col = grid_of((CHUNK, CHUNK))
    blocked = jnp.where((row <= col) & (aux[:, 0:1] == seg_ref[...]), 0.0, NEG_FILL)
    coef_b = coef_ref[:, :NS]
    coef_c = coef_ref[:, NS:]
    coupling = dot_nt(coef_b, coef_c)
    low_state = kept_ref[0]
    carried = dot_nn(coef_c, low_state)
    low_grad = state_grad[...].astype(jnp.bfloat16)
    returned = dot_nn(coef_b, low_grad)
    product = jnp.sum(low_state.astype(jnp.float32) * low_grad.astype(jnp.float32), 0, keepdims=True)
    lane = grid_of((CHUNK, LANES))[1]
    lane_row = grid_of((1, LANES))[1]
    first = lane < P_SIZE
    later = jnp.zeros((CHUNK, LANES), jnp.float32)
    earlier = jnp.zeros((CHUNK, LANES), jnp.float32)
    direct = jnp.zeros((CHUNK, LANES), jnp.float32)
    through = jnp.zeros((1, LANES), jnp.float32)
    coupling_grad = jnp.zeros((CHUNK, CHUNK), jnp.float32)
    for pair in range(act_ref.shape[1] // LANES):
        at = slice(pair * LANES, (pair + 1) * LANES)
        act = act_ref[:, at]
        spread_step = pick(step, pair)
        driven = (act * spread_step).astype(jnp.bfloat16)
        grad = grad_ref[:, at]
        core_grad = grad.astype(jnp.bfloat16)
        core_wide = core_grad.astype(jnp.float32)
        enter_grad = core_wide * pick(enter, pair)
        entered[:, at] = enter_grad.astype(jnp.bfloat16)
        row_part = enter_grad * carried[:, at]
        leave_pair = pick(leave, pair)
        moved[:, at] = (driven.astype(jnp.float32) * leave_pair).astype(jnp.bfloat16)
        back = returned[:, at] * leave_pair
        col_part = back * driven.astype(jnp.float32)
        parts = []
        for head in (2 * pair, 2 * pair + 1):
            mine = first if head % 2 == 0 else ~first
            decay = jnp.exp(cum_rows[head : head + 1] - cumulative[:, head : head + 1] + blocked)
            mix_grad = dot_nt(jnp.where(mine, driven, jnp.zeros_like(driven)), core_grad)
            share = mix_grad * decay
            coupling_grad = coupling_grad + share
            spread = share * coupling
            row_sums[head : head + 1] = jnp.sum(spread, 0, keepdims=True)
            folded = sum(spread[:, k * LANES : (k + 1) * LANES] for k in range(CHUNK // LANES))
            found = jnp.sum(jnp.where(mine, row_part, 0.0) - folded, 1, keepdims=True)
            later = jnp.where(lane == head, found, later)
            parts.append(dot_nn((coupling * decay).astype(jnp.bfloat16), core_grad))
            found = jnp.sum(jnp.where(mine, col_part, 0.0), 1, keepdims=True)
            earlier = jnp.where(lane == head, found, earlier)
        driven_grad = jnp.where(first, parts[0], parts[1]) + back
        act_grad_ref[:, at] = driven_grad * spread_step + grad * skip_ref[:, at]
        skip_sum_ref[:, at] += jnp.sum(grad * act, 0, keepdims=True)
        step_part = driven_grad * act
        product_pair = product[:, at]
        for head in (2 * pair, 2 * pair + 1):
            mine = first if head % 2 == 0 else ~first
            found = jnp.sum(jnp.where(mine, step_part, 0.0), 1, keepdims=True)
            direct = jnp.where(lane == head, found, direct)
            found = jnp.sum(jnp.where(mine[:1], product_pair, 0.0), 1, keepdims=True)
            through = jnp.where(lane_row == head, found, through)
    upper = (row <= col).astype(jnp.bfloat16)
    below = (row > col).astype(jnp.bfloat16)
    high, low = split_two(row_sums[...])
    log_grad = (
        exact_nn(upper, later)
        + dot_nt(upper, high)
        + dot_nt(upper, low)
        + exact_nn(below, earlier)
        + through * across
    )
    step_grad_ref[...] = direct + log_grad * rate
    sums_ref[...] += jnp.sum(log_grad * step, 0, keepdims=True)
    low_coupling = coupling_grad.astype(jnp.bfloat16)
    coef_grad_ref[:, :NS] = dot_nn(low_coupling, coef_c) + dot_nt(moved[...], low_grad)
    coef_grad_ref[:, NS:] = dot_tn(low_coupling, coef_b) + dot_nt(entered[...], low_state)
    fresh = dot_tn(coef_c, entered[...])
    for pair in range(act_ref.shape[1] // LANES):
        at = slice(pair * LANES, (pair + 1) * LANES)
        state_grad[:, at] = state_grad[:, at] * pick(across, pair) + fresh[:, at]


def scan_back_call(step, coef, act, aux, seg_row, rate, skip_row, grad, kept):
    rows, width = act.shape
    chunks = rows // CHUNK
    by_chunk = lambda columns: pl.BlockSpec((CHUNK, columns), lambda i: (chunks - 1 - i, 0))
    one_row = lambda columns: pl.BlockSpec((1, columns), lambda i: (0, 0))
    return pl.pallas_call(
        scan_back_kernel,
        grid=(chunks,),
        in_specs=[
            by_chunk(LANES),
            by_chunk(2 * NS),
            by_chunk(width),
            by_chunk(LANES),
            pl.BlockSpec((1, CHUNK), lambda i: (0, chunks - 1 - i)),
            one_row(LANES),
            one_row(width),
            by_chunk(width),
            pl.BlockSpec((1, NS, width), lambda i: (chunks - 1 - i, 0, 0)),
        ],
        out_specs=[
            by_chunk(width),
            by_chunk(LANES),
            by_chunk(2 * NS),
            one_row(LANES),
            one_row(width),
        ],
        out_shape=[
            jax.ShapeDtypeStruct((rows, width), jnp.float32),
            jax.ShapeDtypeStruct((rows, LANES), jnp.float32),
            jax.ShapeDtypeStruct((rows, 2 * NS), jnp.float32),
            jax.ShapeDtypeStruct((1, LANES), jnp.float32),
            jax.ShapeDtypeStruct((1, width), jnp.float32),
        ],
        scratch_shapes=[
            pltpu.VMEM((NS, width), jnp.float32),
            pltpu.VMEM((CHUNK, width), jnp.bfloat16),
            pltpu.VMEM((CHUNK, width), jnp.bfloat16),
            pltpu.VMEM((LANES, CHUNK), jnp.float32),
        ],
        compiler_params=pltpu.CompilerParams(vmem_limit_bytes=VMEM_BYTES),
        name="scan_backward",
    )(step, coef, act, aux, seg_row, rate, skip_row, grad, kept)


def swap_halves(value):
    width = value.shape[1]
    half = HEAD_SIZE // 2
    up = pltpu.roll(value, width - half, 1)
    down = pltpu.roll(value, half, 1)
    return jnp.where(grid_of(value.shape)[1] % HEAD_SIZE < half, up, down)


def turned(value, cosine, sine):
    return value * cosine + swap_halves(value) * sine


def attend_kernel(query_ref, keyval_ref, seg_ref, seg_col_ref, cos_ref, sin_ref, out_ref, turned_ref, both_ref, log_ref):
    rows = query_ref.shape[0]
    first = grid_of((rows, LANES))[1] < HEAD_SIZE
    keyval = keyval_ref[...]
    moved = pltpu.roll(keyval, HEAD_SIZE, 1)
    keys = turned(jnp.where(first, keyval, moved), cos_ref[...], sin_ref[...]).astype(jnp.bfloat16)
    values = jnp.where(first, moved, keyval).astype(jnp.bfloat16)
    both_ref[:, :LANES] = keys
    both_ref[:, LANES:] = values
    scale = HEAD_SIZE ** (-0.5)
    head_lane = grid_of((CHUNK, LANES))[1]
    first = head_lane < HEAD_SIZE
    for block in range(rows // CHUNK):
        low, high = block * CHUNK, (block + 1) * CHUNK
        row, col = grid_of((CHUNK, high))
        blocked = jnp.where(
            (row + low >= col) & (seg_col_ref[low:high, 0:1] == seg_ref[:, :high]), 0.0, NEG_FILL
        )
        logs = jnp.zeros((CHUNK, LANES), jnp.float32)
        for pair in range(query_ref.shape[1] // LANES):
            at = slice(pair * LANES, (pair + 1) * LANES)
            query = turned(query_ref[low:high, at], cos_ref[low:high], sin_ref[low:high]).astype(
                jnp.bfloat16
            )
            turned_ref[low:high, at] = query
            parts = []
            for head in (2 * pair, 2 * pair + 1):
                mine = first if head % 2 == 0 else ~first
                scores = (
                    dot_nt(jnp.where(mine, query, jnp.zeros_like(query)), keys[:high]) * scale
                    + blocked
                )
                top = jnp.max(scores, 1, keepdims=True)
                weights = jnp.exp(scores - top)
                total = jnp.sum(weights, 1, keepdims=True)
                probs = (weights * (1.0 / total)).astype(jnp.bfloat16)
                parts.append(dot_nn(probs, values[:high]))
                logs = jnp.where(head_lane == head, top + jnp.log(total), logs)
            out_ref[low:high, at] = jnp.where(first, parts[0], parts[1]).astype(jnp.bfloat16)
        log_ref[low:high] = logs


def attend_call(query, keyval, seg_row, aux, cosine, sine):
    rows, width = query.shape
    return pl.pallas_call(
        attend_kernel,
        out_shape=[
            jax.ShapeDtypeStruct((rows, width), jnp.bfloat16),
            jax.ShapeDtypeStruct((rows, width), jnp.bfloat16),
            jax.ShapeDtypeStruct((rows, 2 * LANES), jnp.bfloat16),
            jax.ShapeDtypeStruct((rows, LANES), jnp.float32),
        ],
        compiler_params=pltpu.CompilerParams(vmem_limit_bytes=VMEM_BYTES),
        name="attend_forward",
    )(query, keyval, seg_row, aux, cosine, sine)


def attend_back_kernel(
    query_ref, both_ref, seg_ref, seg_col_ref, cos_ref, sin_ref, log_ref, out_ref, grad_ref,
    query_grad_ref, keyval_grad_ref, key_sum, value_sum,
):
    rows = query_ref.shape[0]
    key_sum[...] = jnp.zeros_like(key_sum)
    value_sum[...] = jnp.zeros_like(value_sum)
    scale = HEAD_SIZE ** (-0.5)
    first = grid_of((CHUNK, LANES))[1] < HEAD_SIZE
    for block in range(rows // CHUNK):
        low, high = block * CHUNK, (block + 1) * CHUNK
        row, col = grid_of((CHUNK, high))
        blocked = jnp.where(
            (row + low >= col) & (seg_col_ref[low:high, 0:1] == seg_ref[:, :high]), 0.0, NEG_FILL
        )
        keys = both_ref[:high, :LANES]
        values = both_ref[:high, LANES:]
        for pair in range(query_ref.shape[1] // LANES):
            at = slice(pair * LANES, (pair + 1) * LANES)
            query = query_ref[low:high, at]
            grad = grad_ref[low:high, at]
            inner = grad.astype(jnp.float32) * out_ref[low:high, at].astype(jnp.float32)
            parts = []
            key_part = None
            for head in (2 * pair, 2 * pair + 1):
                mine = first if head % 2 == 0 else ~first
                query_mine = jnp.where(mine, query, jnp.zeros_like(query))
                grad_mine = jnp.where(mine, grad, jnp.zeros_like(grad))
                scores = dot_nt(query_mine, keys) * scale + blocked
                probs = jnp.exp(scores - log_ref[low:high, head : head + 1])
                delta = jnp.sum(jnp.where(mine, inner, 0.0), 1, keepdims=True)
                prob_grad = dot_nt(grad_mine, values)
                score_grad = (probs * (prob_grad - delta)).astype(jnp.bfloat16)
                parts.append(dot_nn(score_grad, keys) * scale)
                key_sum[:high] += dot_tn(score_grad, query_mine)
                value_sum[:high] += dot_tn(probs.astype(jnp.bfloat16), grad_mine)
            full = jnp.where(first, parts[0], parts[1])
            query_grad_ref[low:high, at] = turned(full, cos_ref[low:high], -sin_ref[low:high]).astype(
                jnp.bfloat16
            )
    wide = grid_of((rows, LANES))[1] < HEAD_SIZE
    key_total = key_sum[...] * scale
    key_total = key_total + pltpu.roll(key_total, HEAD_SIZE, 1)
    key_total = turned(key_total, cos_ref[...], -sin_ref[...])
    value_total = value_sum[...]
    value_total = value_total + pltpu.roll(value_total, HEAD_SIZE, 1)
    keyval_grad_ref[...] = jnp.where(wide, key_total, value_total).astype(jnp.bfloat16)


def attend_back_call(query, both, seg_row, aux, cosine, sine, logs, out, grad):
    rows, width = query.shape
    return pl.pallas_call(
        attend_back_kernel,
        out_shape=[
            jax.ShapeDtypeStruct((rows, width), jnp.bfloat16),
            jax.ShapeDtypeStruct((rows, LANES), jnp.bfloat16),
        ],
        scratch_shapes=[
            pltpu.VMEM((rows, LANES), jnp.float32),
            pltpu.VMEM((rows, LANES), jnp.float32),
        ],
        compiler_params=pltpu.CompilerParams(vmem_limit_bytes=VMEM_BYTES),
        name="attend_backward",
    )(query, both, seg_row, aux, cosine, sine, logs, out, grad)


def halve(value, bit):
    half = value.shape[0] // 2
    upper = (lax.axis_index("dp") & bit) != 0
    got = swap_bit(jnp.where(upper, value[:half], value[half:]), bit)
    kept = jnp.where(upper, value[half:], value[:half])
    return (kept.astype(jnp.float32) + got.astype(jnp.float32)).astype(value.dtype)


def double(value, bit):
    upper = (lax.axis_index("dp") & bit) != 0
    got = swap_bit(value, bit)
    return jnp.concatenate([jnp.where(upper, got, value), jnp.where(upper, value, got)], 0)


def dp_bits():
    size = lax.axis_size("dp")
    return [1 << i for i in range(size.bit_length() - 1)]


def halve_parts(values, bit):
    half = values[0].shape[0] // 2
    upper = (lax.axis_index("dp") & bit) != 0
    got = swap_bit(
        jnp.concatenate([jnp.where(upper, v[:half], v[half:]) for v in values], 1), bit
    )
    kept = jnp.concatenate([jnp.where(upper, v[half:], v[:half]) for v in values], 1)
    return (kept.astype(jnp.float32) + got.astype(jnp.float32)).astype(got.dtype)


def by_rows(value):
    return with_layout_constraint(value, Layout(major_to_minor=(0, 1)))


def swap_pair(value):
    return lax.ppermute(value, "tensor", [(0, 1), (1, 0)])


def tie(*values):
    return lax.optimization_barrier(values)


def conv_rows(value, kernel, bias, keeps):
    taps = kernel.shape[0]
    total = bias.astype(jnp.float32)[None]
    for tap in range(taps):
        offset = taps - 1 - tap
        moved = jnp.pad(value, ((offset, 0), (0, 0)))[: value.shape[0]]
        total = total + kernel[tap].astype(jnp.float32) * moved * keeps[offset]
    return total


def conv_sums(grad, value, taps, keeps):
    sums = []
    for tap in range(taps):
        offset = taps - 1 - tap
        moved = jnp.pad(value, ((offset, 0), (0, 0)))[: value.shape[0]]
        sums.append(jnp.sum(grad * keeps[offset] * moved, 0, keepdims=True))
    return sums


def conv_grad(grad, kernel, keeps):
    taps = kernel.shape[0]
    total = jnp.zeros_like(grad)
    for tap in range(taps):
        offset = taps - 1 - tap
        moved = jnp.pad(grad * keeps[offset], ((0, offset), (0, 0)))[offset:]
        total = total + kernel[tap].astype(jnp.float32) * moved
    return total


def product_kernel(*refs):
    left_pairs, right_pairs = [refs[0:2], refs[2:4], refs[2:4]], [(), refs[4:6], refs[6:8]]
    cotangent_ref, out_ref = refs[8], refs[9]
    half = refs[0].shape[0]
    for which in range(3):
        total = None
        for k in range(2):
            left = left_pairs[which][k][...]
            if which == 0:
                right = cotangent_ref[k * half : (k + 1) * half]
            else:
                right = right_pairs[which][k][...]
            part = dot_tn(left, right)
            total = part if total is None else total + part
        out_ref[which] = total.astype(out_ref.dtype)


def product_call(hidden_a, hidden_b, post_a, post_b, gate_a, gate_b, up_a, up_b, cotangent):
    half, model = post_a.shape
    hidden = hidden_a.shape[1]
    columns = pl.BlockSpec((half, CHUNK), lambda i: (0, i))
    whole = pl.BlockSpec((half, hidden), lambda i: (0, 0))
    return pl.pallas_call(
        product_kernel,
        grid=(hidden // CHUNK,),
        in_specs=[columns] * 4 + [whole] * 4 + [pl.BlockSpec((2 * half, model), lambda i: (0, 0))],
        out_specs=pl.BlockSpec((3, CHUNK, model), lambda i: (0, i, 0)),
        out_shape=jax.ShapeDtypeStruct((3, hidden, model), jnp.bfloat16),
        compiler_params=pltpu.CompilerParams(vmem_limit_bytes=VMEM_BYTES),
        name="weight_products",
    )(hidden_a, hidden_b, post_a, post_b, gate_a, gate_b, up_a, up_b, cotangent)


def local_fast(
    tokens,
    segments,
    cotangent,
    input_gain,
    query_weight,
    key_value_weight,
    attnout_weight,
    gating_weight,
    inner_weight,
    state_weight,
    step_weight,
    conv_inner,
    conv_state,
    inner_bias,
    state_bias,
    step_bias,
    decay_log,
    skip_scale,
    mixer_gain,
    mixer_out,
    post_gain,
    gate_weight,
    up_weight,
    down_weight,
):
    low, wide = jnp.bfloat16, jnp.float32
    rows, model = tokens.shape
    heads = query_weight.shape[1] // HEAD_SIZE
    ssm_heads = step_weight.shape[1]
    ssm_width = ssm_heads * P_SIZE
    query_width = heads * HEAD_SIZE
    first_device = lax.axis_index("tensor") == 0
    pick_head = lambda at: jnp.where(
        first_device,
        key_value_weight[:, at : at + HEAD_SIZE],
        key_value_weight[:, at + HEAD_SIZE : at + 2 * HEAD_SIZE],
    )
    keyval_weight = jnp.concatenate([pick_head(0), pick_head(KEYVALUE_HEADS * HEAD_SIZE)], 1)
    lane_pad = ((0, 0), (0, LANES - ssm_heads))
    step_weight_wide = jnp.pad(step_weight, lane_pad)
    step_bias_wide = jnp.pad(step_bias.astype(wide)[None], lane_pad)
    rate = -jnp.exp(decay_log.astype(wide))
    rate_wide = jnp.pad(rate[None], lane_pad)
    skip_row = jnp.repeat(skip_scale.astype(wide), P_SIZE)[None]
    cosine, sine = rotary_tables(rows)
    cosine = jnp.concatenate([cosine] * 4, 1)
    sine = jnp.concatenate([-sine, sine, -sine, sine], 1)
    seg_row = segments.astype(wide)
    seg_chunks = seg_row.reshape(-1, CHUNK)
    ends = seg_chunks[:, -1:]
    starts = jnp.concatenate([jnp.full((1, 1), -1.0, wide), ends[:-1]], 0)
    aux = jnp.stack(
        [seg_chunks, (seg_chunks == starts).astype(wide), (seg_chunks == ends).astype(wide)], -1
    ).reshape(rows, 3)
    aux = jnp.pad(aux, ((0, 0), (0, LANES - 3)))
    keeps = [seg_keep(segments, offset)[0] for offset in range(conv_inner.shape[0])]

    inputs = by_rows(tokens.astype(wide))
    inv_first = lax.rsqrt(jnp.mean(inputs * inputs, -1, keepdims=True) + EPS)
    unit_first = inputs * inv_first
    in_gain = input_gain.astype(wide)
    normed = by_rows((unit_first * in_gain).astype(low))
    inner = matmul(normed, inner_weight)
    state_in = matmul(normed, state_weight)
    step_arg = matmul(normed, step_weight_wide) + step_bias_wide
    gating = matmul(normed, gating_weight)
    inner_pre = conv_rows(inner, conv_inner, inner_bias, keeps)
    inner_act = jax.nn.silu(inner_pre)
    state_pre = conv_rows(state_in, conv_state, state_bias, keeps)
    coef = jax.nn.silu(state_pre).astype(low)
    step = jax.nn.softplus(step_arg)
    core, kept = scan_call(step, coef, inner_act, aux, seg_row, rate_wide)
    ssm_out = core + skip_row * inner_act
    sigma_gate = jax.nn.sigmoid(gating)
    gate_act = gating * sigma_gate
    gated = ssm_out * gate_act
    square_sum = pair_sum(jnp.sum(gated * gated, -1))[:, None]
    query_pre = matmul(normed, query_weight)
    keyval_pre = matmul(normed, keyval_weight)
    attended, queries, both, logs = attend_call(query_pre, keyval_pre, seg_row, aux, cosine, sine)
    attn_part = matmul(attended, attnout_weight)
    inv_gate = lax.rsqrt(square_sum / DSSM + EPS)
    mixer_scale = mixer_gain.astype(wide)
    mixed = (gated * inv_gate * mixer_scale).astype(low)
    branch_part = attn_part + matmul(mixed, mixer_out)
    out_gain = post_gain.astype(wide)
    branch_part = by_rows(branch_part.astype(low))
    half = rows // 2
    spans = [slice(0, half), slice(half, rows)]
    sent = [branch_part[span] for span in spans]
    got = [swap_pair(piece) for piece in sent]
    weight_cat = jnp.concatenate(
        [gating_weight, inner_weight, step_weight_wide, state_weight, query_weight, keyval_weight], 1
    )
    got[0], weight_cat = tie(got[0], weight_cat)
    found = []
    for at, span in enumerate(spans):
        middle = inputs[span] + by_rows(sent[at].astype(wide) + got[at].astype(wide))
        inv_second = lax.rsqrt(jnp.mean(middle * middle, -1, keepdims=True) + EPS)
        unit_second = middle * inv_second
        post = by_rows((unit_second * out_gain).astype(low))
        gate = matmul(post, gate_weight)
        upward = matmul(post, up_weight)
        sigma = jax.nn.sigmoid(gate)
        hidden = (gate * sigma * upward).astype(low)
        hidden_grad = dot_nt(cotangent[span], down_weight)
        up_act_grad = (hidden_grad * gate * sigma).astype(low)
        gate_act_grad = (hidden_grad * upward * sigma * (1.0 + gate * (1.0 - sigma))).astype(low)
        post_part = dot_nt(gate_act_grad, gate_weight) + dot_nt(up_act_grad, up_weight)
        gain_part = jnp.sum(post_part * unit_second, 0, keepdims=True)
        post_low = by_rows(post_part.astype(low))
        if at == 0:
            got[1], post_low = tie(got[1], post_low)
        post_got = swap_pair(post_low)
        found.append(
            (post_low, unit_second, inv_second, gain_part, hidden, post, gate_act_grad, up_act_grad)
        )
        got[at] = post_got
    post_gain_part = found[0][3] + found[1][3]
    forward_part = product_call(
        *[piece for k in range(4, 8) for piece in (found[0][k], found[1][k])], cotangent
    )
    got[1], _ = tie(got[1], forward_part)
    forward_piece = lax.psum_scatter(
        forward_part.reshape(-1, model), "dp", scatter_dimension=0, tiled=True
    )
    middle_grads = []
    for span, part, other in zip(spans, found, got):
        post_low, unit_second, inv_second = part[:3]
        post_full = by_rows(post_low.astype(wide) + other.astype(wide))
        scaled_post = post_full * out_gain
        middle_grads.append(
            cotangent[span].astype(wide)
            + inv_second
            * (scaled_post - unit_second * jnp.mean(scaled_post * unit_second, -1, keepdims=True))
        )
    branch_grad = by_rows(jnp.concatenate([grad.astype(low) for grad in middle_grads], 0))
    middle_grad = jnp.concatenate(middle_grads, 0)
    mixed_grad = dot_nt(branch_grad, mixer_out)
    mixer_gain_part = jnp.sum(mixed_grad * gated * inv_gate, 0, keepdims=True)
    weighted = mixed_grad * mixer_scale
    cross = pair_sum(jnp.sum(weighted * gated, -1))[:, None]
    out_part = dot_tn(jnp.concatenate([attended, mixed], 1), branch_grad).astype(low)
    out_part = by_rows(out_part)
    attended_grad = dot_nt(branch_grad, attnout_weight).astype(low)
    gated_grad = inv_gate * weighted - gated * (inv_gate * inv_gate * inv_gate) * cross / DSSM
    ssm_grad = gated_grad * gate_act
    gating_grad = (
        gated_grad * ssm_out * sigma_gate * (1.0 + gating * (1.0 - sigma_gate))
    ).astype(low)
    gating_part = by_rows(dot_tn(normed, gating_grad).astype(low))
    bits = dp_bits()
    early = halve_parts([out_part, gating_part], bits[0])
    early, ssm_grad = tie(early, ssm_grad)
    early = halve(early, bits[1])
    act_grad, step_grad, coef_grad, rate_sum, skip_sum = scan_back_call(
        step, coef, inner_act, aux, seg_row, rate_wide, skip_row, ssm_grad, kept
    )
    early, act_grad, step_grad, coef_grad, forward_piece = tie(
        early, act_grad, step_grad, coef_grad, forward_piece
    )
    forward_total = lax.all_gather(forward_piece, "dp", axis=0, tiled=True)
    early = halve(early, bits[2])
    step_total = step_grad * jax.nn.sigmoid(step_arg)
    taps = conv_inner.shape[0]
    inner_pre_grad = act_grad * silu_slope(inner_pre)
    conv_inner_sums = conv_sums(inner_pre_grad, inner, taps, keeps)
    inner_bias_part = jnp.sum(inner_pre_grad, 0, keepdims=True)
    state_pre_grad = coef_grad * silu_slope(state_pre)
    conv_state_sums = conv_sums(state_pre_grad, state_in, taps, keeps)
    state_bias_part = jnp.sum(state_pre_grad, 0, keepdims=True)
    early, act_grad, coef_grad, *sums = tie(
        early, act_grad, coef_grad, inner_bias_part, state_bias_part, *conv_inner_sums, *conv_state_sums
    )
    inner_bias_part, state_bias_part = sums[:2]
    conv_inner_sums, conv_state_sums = sums[2 : 2 + taps], sums[2 + taps :]
    early = halve(early, bits[3])
    inner_grad = conv_grad(act_grad * silu_slope(inner_pre), conv_inner, keeps)
    state_grad = conv_grad(coef_grad * silu_slope(state_pre), conv_state, keeps)
    scan_cat = jnp.concatenate(
        [inner_grad.astype(low), step_total.astype(low), state_grad.astype(low)], 1
    )
    scan_part = dot_tn(normed, scan_cat).astype(low)
    early, scan_part, attended_grad = tie(early, scan_part, attended_grad)
    early = double(early, bits[3])
    scan_part = halve(scan_part, bits[0])
    query_grad, keyval_grad = attend_back_call(
        queries, both, seg_row, aux, cosine, sine, logs, attended, attended_grad
    )
    attend_cat = jnp.concatenate([query_grad, keyval_grad], 1)
    attend_part = dot_tn(normed, attend_cat).astype(low)
    early, scan_part, attend_part, attend_cat = tie(early, scan_part, attend_part, attend_cat)
    early = double(early, bits[2])
    scan_part = halve(scan_part, bits[1])
    attend_part = halve(attend_part, bits[0])
    normed_part = dot_nt(jnp.concatenate([gating_grad, scan_cat, attend_cat], 1), weight_cat)
    input_gain_part = jnp.sum(normed_part * unit_first, 0, keepdims=True)
    early, scan_part, attend_part, normed_part, input_gain_part = tie(
        early, scan_part, attend_part, normed_part, input_gain_part
    )
    normed_full = by_rows(pair_sum(by_rows(normed_part.astype(low))))
    own_rows = [
        *conv_inner_sums,
        inner_bias_part,
        mixer_gain_part,
        skip_sum,
        jnp.sum(step_total, 0, keepdims=True),
        rate_sum * rate_wide,
    ]
    shared_rows = [
        input_gain_part,
        post_gain_part,
        *conv_state_sums,
        state_bias_part,
    ]
    small = jnp.concatenate(
        [jnp.pad(row, ((0, 0), (0, model - row.shape[1]))) for row in own_rows + shared_rows], 0
    )
    small = small + swap_bit(small, bits[0])
    early = double(early, bits[1])
    scan_part = halve(scan_part, bits[2])
    attend_part = halve(attend_part, bits[1])
    scan_part, attend_part, small = tie(scan_part, attend_part, small)
    scan_part = halve(scan_part, bits[3])
    attend_part = halve(attend_part, bits[2])
    small = small + swap_bit(small, bits[1])
    scan_part, attend_part, small, early = tie(scan_part, attend_part, small, early)
    early = double(early, bits[0])
    attend_part = halve(attend_part, bits[3])
    small = small + swap_bit(small, bits[2])
    attend_part, small, forward_total = tie(attend_part, small, forward_total)
    hidden_units = down_weight.shape[0]
    down_wgrad = forward_total[:hidden_units].astype(wide)
    gate_wgrad = forward_total[hidden_units : hidden_units + model].astype(wide)
    up_wgrad = forward_total[hidden_units + model :].astype(wide)
    small = small + swap_bit(small, bits[3])
    scan_piece, attend_piece = scan_part, attend_part
    state_at = ssm_width + LANES
    trade = jnp.concatenate([scan_piece[:, state_at:], attend_piece[:, query_width:]], 1)
    other = lax.ppermute(trade, "tensor", [(0, 1), (1, 0)])
    state_cols = state_weight.shape[1]
    state_piece = (
        trade[:, :state_cols].astype(wide) + other[:, :state_cols].astype(wide)
    ).astype(low)
    mine, theirs = trade[:, state_cols:], other[:, state_cols:]
    head_0 = jnp.where(first_device, mine, theirs)
    head_1 = jnp.where(first_device, theirs, mine)
    late = jnp.concatenate(
        [
            scan_piece[:, :state_at],
            state_piece,
            attend_piece[:, :query_width],
            head_0[:, :HEAD_SIZE],
            head_1[:, :HEAD_SIZE],
            head_0[:, HEAD_SIZE:],
            head_1[:, HEAD_SIZE:],
        ],
        1,
    )
    late, small = tie(late, small)
    late = double(late, bits[3])
    small_other = lax.ppermute(small, "tensor", [(0, 1), (1, 0)])
    is_shared = lax.broadcasted_iota(jnp.int32, small.shape, 0) >= len(own_rows)
    small = small + jnp.where(is_shared, small_other, 0.0)
    late, early, small = tie(late, early, small)
    late = double(late, bits[2])
    (late,) = tie(late)
    late = double(late, bits[1])
    early_grads = (
        gate_wgrad,
        up_wgrad,
        down_wgrad,
        early[:query_width, :model].astype(wide),
        early[:, model:].astype(wide),
        early[query_width:, :model].astype(wide),
    )
    scaled_in = normed_full * in_gain
    tokens_grad = middle_grad + inv_first * (
        scaled_in - unit_first * jnp.mean(scaled_in * unit_first, -1, keepdims=True)
    )
    late, tokens_grad, *early_grads = tie(late, tokens_grad, *early_grads)
    late = double(late, bits[0])
    scan_total = late[:, : state_at + state_cols]
    attend_total = late[:, state_at + state_cols :]
    gate_wgrad, up_wgrad, down_wgrad, attnout_grad, gating_wgrad, mixout_grad = early_grads
    count = len(own_rows)
    return (
        tokens_grad,
        small[count],
        attend_total[:, :query_width].astype(wide),
        attend_total[:, query_width:].astype(wide),
        attnout_grad,
        gating_wgrad,
        scan_total[:, :ssm_width].astype(wide),
        scan_total[:, state_at:].astype(wide),
        scan_total[:, ssm_width : ssm_width + ssm_heads].astype(wide),
        small[:taps, :ssm_width],
        small[count + 2 : count + 2 + taps, :state_cols],
        small[taps, :ssm_width],
        small[count + 2 + taps, :state_cols],
        small[taps + 3, :ssm_heads],
        small[taps + 4, :ssm_heads],
        jnp.sum(small[taps + 2, :ssm_width].reshape(ssm_heads, P_SIZE), 1),
        small[taps + 1, :ssm_width],
        mixout_grad,
        small[count + 1],
        gate_wgrad,
        up_wgrad,
        down_wgrad,
    )


def layer(*arrays):
    tokens, segments, query_weight, step_weight = arrays[0], arrays[1], arrays[4], arrays[10]
    size = lax.axis_size("dp")
    fits = (
        lax.axis_size("tensor") == 2
        and size == 16
        and segments.shape[0] == 1
        and tokens.shape[0] % CHUNK == 0
        and tokens.shape[1] % (16 * size) == 0
        and query_weight.shape[1] == QUERY_HEADS // KEYVALUE_HEADS * HEAD_SIZE
        and KEYVALUE_HEADS == 2
        and arrays[23].shape[0] == tokens.shape[1]
        and step_weight.shape[1] % 2 == 0
        and query_weight.shape[1] + step_weight.shape[1] * P_SIZE == tokens.shape[1]
    )
    return local_fast(*arrays) if fits else local(*arrays)


def solution(mesh):
    placed = (
        P("dp", None),
        P("dp", None),
        P("dp", None),
        P(),
        P(None, "tensor"),
        P(),
        P("tensor", None),
        P(None, "tensor"),
        P(None, "tensor"),
        P(),
        P(None, "tensor"),
        P(None, "tensor"),
        P(),
        P("tensor"),
        P(),
        P("tensor"),
        P("tensor"),
        P("tensor"),
        P("tensor"),
        P("tensor", None),
        P(),
        P(None, "tensor"),
        P(None, "tensor"),
        P("tensor", None),
    )
    return jax.shard_map(
        layer,
        mesh=mesh,
        in_specs=placed,
        out_specs=(
            P("dp", None),
            P(),
            P(None, "tensor"),
            P(),
            P("tensor", None),
            P(None, "tensor"),
            P(None, "tensor"),
            P(),
            P(None, "tensor"),
            P(None, "tensor"),
            P(),
            P("tensor"),
            P(),
            P("tensor"),
            P("tensor"),
            P("tensor"),
            P("tensor"),
            P("tensor", None),
            P(),
            P(None, "tensor"),
            P(None, "tensor"),
            P("tensor", None),
        ),
        check_vma=False,
    )
```

```python
import jax
import jax.numpy as jnp
from jax import lax
from jax.experimental.layout import Layout, with_layout_constraint
from jax.experimental import pallas as pl
from jax.experimental.pallas import tpu as pltpu
from jax.sharding import PartitionSpec as P

QUERY_HEADS = 8
KEYVALUE_HEADS = 2
HEAD_SIZE = 64
P_SIZE = 64
NS = 128
DSSM = 1536


EPS = 1e-05
ROPE_BASE = 100000000000.0
NEG_FILL = -1e30


def matmul(left, right):
    return jnp.dot(left, right, preferred_element_type=jnp.float32)


def rotary_tables(document_length):
    half = HEAD_SIZE // 2
    freqs = jnp.exp(-jnp.log(ROPE_BASE) * (2.0 * jnp.arange(half, dtype=jnp.float32) / HEAD_SIZE))
    angles = jnp.arange(document_length, dtype=jnp.float32)[:, None] * freqs[None, :]
    return (jnp.cos(angles), jnp.sin(angles))


def rotate(value, cosine, sine):
    half = value.shape[-1] // 2
    first = value[..., :half]
    second = value[..., half:]
    return jnp.concatenate([first * cosine - second * sine, first * sine + second * cosine], -1)


def rotate_back(grad, cosine, sine):
    half = grad.shape[-1] // 2
    first = grad[..., :half]
    second = grad[..., half:]
    return jnp.concatenate([first * cosine + second * sine, second * cosine - first * sine], -1)


def silu_slope(value):
    sigma = jax.nn.sigmoid(value)
    return sigma * (1.0 + value * (1.0 - sigma))


def seg_keep(segments, offset):
    document_length = segments.shape[1]
    moved = jnp.pad(segments, ((0, 0), (offset, 0)), constant_values=-1)[:, :document_length]
    return (moved == segments).astype(jnp.float32)[:, :, None]


def move_down(value, offset):
    document_length = value.shape[1]
    return jnp.pad(value, ((0, 0), (offset, 0), (0, 0)))[:, :document_length]


def move_up(value, offset):
    return jnp.pad(value, ((0, 0), (0, offset), (0, 0)))[:, offset:]


def conv_forward(value, kernel, bias, segments):
    taps = kernel.shape[0]
    total = jnp.zeros_like(value) + bias.astype(jnp.float32)
    for tap in range(taps):
        offset = taps - 1 - tap
        total = total + kernel[tap].astype(jnp.float32) * move_down(value, offset) * seg_keep(
            segments, offset
        )
    return total


def conv_backward(grad, value, kernel, segments):
    taps = kernel.shape[0]
    grad_in = jnp.zeros_like(value)
    kernel_rows = []
    for tap in range(taps):
        offset = taps - 1 - tap
        masked = grad * seg_keep(segments, offset)
        kernel_rows.append(jnp.sum(masked * move_down(value, offset), axis=(0, 1)))
        grad_in = grad_in + kernel[tap].astype(jnp.float32) * move_up(masked, offset)
    return (grad_in, jnp.stack(kernel_rows))


def ssd_parts(step_block, rate, coef_b, coef_c, heads_block, allowed):
    coupling = jnp.einsum("tn,sn->ts", coef_c, coef_b, preferred_element_type=jnp.float32)
    cumulative = jnp.cumsum(step_block * rate, axis=0).T
    difference = cumulative[:, :, None] - cumulative[:, None, :]
    decay = jnp.where(allowed[None], jnp.exp(jnp.where(allowed[None], difference, 0.0)), 0.0)
    mixing = (coupling[None] * decay).astype(jnp.bfloat16)
    driven = (heads_block * step_block.T[:, :, None]).astype(jnp.bfloat16)
    return (coupling, decay, mixing, driven)


def pair_sum(value):
    if lax.axis_size("tensor") == 2:
        other = lax.ppermute(value, "tensor", [(0, 1), (1, 0)])
        return value.astype(jnp.float32) + other.astype(jnp.float32)
    return lax.psum(value, "tensor").astype(jnp.float32)


def swap_bit(value, bit):
    size = lax.axis_size("dp")
    return lax.ppermute(value, "dp", [(i, i ^ bit) for i in range(size)])


def shared_sum(rows, first_shared):
    tail = pair_sum(rows[:, first_shared:]).astype(rows.dtype)
    return jnp.concatenate([rows[:, :first_shared], tail], 1) if first_shared else tail


def tree_sum(value, first_shared=None):
    size = lax.axis_size("dp")
    rows = value.shape[0]
    if size & (size - 1) or rows % (16 * size):
        total = lax.psum(value, "dp")
        return total if first_shared is None else shared_sum(total, first_shared)
    bits = [1 << i for i in range(size.bit_length() - 1)]
    me = lax.axis_index("dp")
    for bit in bits:
        half = value.shape[0] // 2
        low, high = value[:half], value[half:]
        upper = (me & bit) != 0
        got = swap_bit(jnp.where(upper, low, high), bit)
        kept = jnp.where(upper, high, low)
        value = (kept.astype(jnp.float32) + got.astype(jnp.float32)).astype(value.dtype)
    if first_shared is not None:
        value = shared_sum(value, first_shared)
    for bit in reversed(bits):
        upper = (me & bit) != 0
        got = swap_bit(value, bit)
        value = jnp.where(
            upper, jnp.concatenate([got, value], 0), jnp.concatenate([value, got], 0)
        )
    return value


def local(
    tokens,
    segments,
    cotangent,
    input_gain,
    query_weight,
    key_value_weight,
    attnout_weight,
    gating_weight,
    inner_weight,
    state_weight,
    step_weight,
    conv_inner,
    conv_state,
    inner_bias,
    state_bias,
    step_bias,
    decay_log,
    skip_scale,
    mixer_gain,
    mixer_out,
    post_gain,
    gate_weight,
    up_weight,
    down_weight,
):
    seq_count, document_length = segments.shape
    rows = seq_count * document_length
    heads = query_weight.shape[1] // HEAD_SIZE
    ssm_heads = step_weight.shape[1]
    query_group = QUERY_HEADS // KEYVALUE_HEADS
    shared_key_head = lax.axis_index("tensor") * heads // query_group
    scale = HEAD_SIZE ** (-0.5)
    cosine, sine = rotary_tables(document_length)
    positions = jnp.arange(document_length)

    def allowed_of(seg_ids):
        return (positions[:, None] >= positions[None, :]) & (seg_ids[:, None] == seg_ids[None, :])

    inputs = tokens.astype(jnp.float32)
    inv_first = lax.rsqrt(jnp.mean(inputs * inputs, -1, keepdims=True) + EPS)
    unit_first = inputs * inv_first
    in_gain = input_gain.astype(jnp.float32)
    normed = (unit_first * in_gain).astype(jnp.bfloat16)
    key_cols = lax.dynamic_slice_in_dim(key_value_weight, shared_key_head * HEAD_SIZE, HEAD_SIZE, 1)
    value_columns = lax.dynamic_slice_in_dim(
        key_value_weight, (KEYVALUE_HEADS + shared_key_head) * HEAD_SIZE, HEAD_SIZE, 1
    )
    query_pre = matmul(normed, query_weight)
    key_pre = matmul(normed, key_cols)
    value_pre = matmul(normed, value_columns)
    queries = rotate(
        query_pre.reshape(seq_count, document_length, heads, HEAD_SIZE).transpose(0, 2, 1, 3),
        cosine,
        sine,
    ).astype(jnp.bfloat16)
    key_rows = rotate(key_pre.reshape(seq_count, document_length, HEAD_SIZE), cosine, sine).astype(
        jnp.bfloat16
    )
    value_rows = value_pre.reshape(seq_count, document_length, HEAD_SIZE).astype(jnp.bfloat16)

    def attend(seq_item):
        query_block, key_block, value_block, seg_ids = seq_item
        allowed = allowed_of(seg_ids)[None]
        scores = (
            jnp.einsum("htd,sd->hts", query_block, key_block, preferred_element_type=jnp.float32)
            * scale
        )
        scores = jnp.where(allowed, scores, NEG_FILL)
        top = jnp.max(scores, -1, keepdims=True)
        weights = jnp.exp(scores - top)
        total = jnp.sum(weights, -1, keepdims=True)
        probs = (weights / total).astype(jnp.bfloat16)
        attended = jnp.einsum("hts,sd->htd", probs, value_block, preferred_element_type=jnp.float32)
        return (attended.astype(jnp.bfloat16), (top + jnp.log(total))[..., 0])

    attended, logsum = lax.map(attend, (queries, key_rows, value_rows, segments))
    attn_flat = attended.transpose(0, 2, 1, 3).reshape(rows, heads * HEAD_SIZE)
    attn_part = matmul(attn_flat, attnout_weight)
    gating = matmul(normed, gating_weight)
    inner = matmul(normed, inner_weight).reshape(seq_count, document_length, -1)
    state_in = matmul(normed, state_weight).reshape(seq_count, document_length, -1)
    step_raw = matmul(normed, step_weight)
    inner_pre = conv_forward(inner, conv_inner, inner_bias, segments)
    inner_act = jax.nn.silu(inner_pre)
    state_pre = conv_forward(state_in, conv_state, state_bias, segments)
    state_act = jax.nn.silu(state_pre)
    coef_b = state_act[..., :NS].astype(jnp.bfloat16)
    coef_c = state_act[..., NS:].astype(jnp.bfloat16)
    step_arg = step_raw.reshape(seq_count, document_length, ssm_heads) + step_bias.astype(
        jnp.float32
    )
    step = jax.nn.softplus(step_arg)
    rate = -jnp.exp(decay_log.astype(jnp.float32))
    heads_in = inner_act.reshape(seq_count, document_length, ssm_heads, P_SIZE).transpose(
        0, 2, 1, 3
    )

    def scan_forward(seq_item):
        step_block, coef_b_block, coef_c_block, heads_block, seg_ids = seq_item
        parts = ssd_parts(
            step_block, rate, coef_b_block, coef_c_block, heads_block, allowed_of(seg_ids)
        )
        return jnp.einsum("hts,hsp->htp", parts[2], parts[3], preferred_element_type=jnp.float32)

    core = lax.map(scan_forward, (step, coef_b, coef_c, heads_in, segments))
    skip = skip_scale.astype(jnp.float32)[None, :, None, None]
    ssm_out = (core + skip * heads_in).transpose(0, 2, 1, 3).reshape(rows, ssm_heads * P_SIZE)
    sigma_gate = jax.nn.sigmoid(gating)
    gate_act = gating * sigma_gate
    gated = ssm_out * gate_act
    square_sum = pair_sum(jnp.sum(gated * gated, -1))[:, None]
    inv_gate = lax.rsqrt(square_sum / DSSM + EPS)
    mixer_scale = mixer_gain.astype(jnp.float32)
    mixed = (gated * inv_gate * mixer_scale).astype(jnp.bfloat16)
    branch_part = attn_part + matmul(mixed, mixer_out)
    out_gain = post_gain.astype(jnp.float32)
    branch = pair_sum(branch_part.astype(jnp.bfloat16))
    middle = inputs + branch
    inv_second = lax.rsqrt(jnp.mean(middle * middle, -1, keepdims=True) + EPS)
    unit_second = middle * inv_second
    post = (unit_second * out_gain).astype(jnp.bfloat16)
    gate = matmul(post, gate_weight)
    upward = matmul(post, up_weight)
    sigma = jax.nn.sigmoid(gate)
    hidden = (gate * sigma * upward).astype(jnp.bfloat16)
    down_wgrad = jnp.einsum("tf,td->fd", hidden, cotangent, preferred_element_type=jnp.float32)
    hidden_grad = jnp.einsum(
        "td,fd->tf", cotangent, down_weight, preferred_element_type=jnp.float32
    )
    up_act_grad = (hidden_grad * gate * sigma).astype(jnp.bfloat16)
    gate_act_grad = (hidden_grad * upward * sigma * (1.0 + gate * (1.0 - sigma))).astype(
        jnp.bfloat16
    )
    gate_wgrad = jnp.einsum("tc,tf->cf", post, gate_act_grad, preferred_element_type=jnp.float32)
    up_wgrad = jnp.einsum("tc,tf->cf", post, up_act_grad, preferred_element_type=jnp.float32)
    post_part = jnp.einsum(
        "tf,cf->tc", gate_act_grad, gate_weight, preferred_element_type=jnp.float32
    ) + jnp.einsum("tf,cf->tc", up_act_grad, up_weight, preferred_element_type=jnp.float32)
    post_gain_part = jnp.sum(post_part * unit_second, 0)
    post_full = pair_sum(post_part.astype(jnp.bfloat16))
    down_wgrad, gate_wgrad, up_wgrad, post_full = lax.optimization_barrier(
        (
            down_wgrad.astype(jnp.bfloat16),
            gate_wgrad.astype(jnp.bfloat16),
            up_wgrad.astype(jnp.bfloat16),
            post_full,
        )
    )
    down_wgrad, gate_wgrad, up_wgrad = lax.psum((down_wgrad, gate_wgrad, up_wgrad), "dp")
    scaled_post = post_full * out_gain
    middle_grad = cotangent.astype(jnp.float32) + inv_second * (
        scaled_post - unit_second * jnp.mean(scaled_post * unit_second, -1, keepdims=True)
    )
    branch_grad = middle_grad.astype(jnp.bfloat16)
    attnout_wgrad = jnp.einsum(
        "tk,td->kd", attn_flat, branch_grad, preferred_element_type=jnp.float32
    )
    attended_grad = jnp.einsum(
        "td,kd->tk", branch_grad, attnout_weight, preferred_element_type=jnp.float32
    )
    attended_grad = (
        attended_grad.astype(jnp.bfloat16)
        .reshape(seq_count, document_length, heads, HEAD_SIZE)
        .transpose(0, 2, 1, 3)
    )

    def attend_back(seq_item):
        query_block, key_block, value_block, seg_ids, logsum_block, grad_block = seq_item
        allowed = allowed_of(seg_ids)[None]
        scores = (
            jnp.einsum("htd,sd->hts", query_block, key_block, preferred_element_type=jnp.float32)
            * scale
        )
        probs = jnp.where(allowed, jnp.exp(scores - logsum_block[..., None]), 0.0)
        value_grad = jnp.einsum(
            "hts,htd->hsd",
            probs.astype(jnp.bfloat16),
            grad_block,
            preferred_element_type=jnp.float32,
        )
        prob_grad = jnp.einsum(
            "htd,sd->hts", grad_block, value_block, preferred_element_type=jnp.float32
        )
        delta = jnp.sum(probs * prob_grad, -1, keepdims=True)
        score_grad = (probs * (prob_grad - delta)).astype(jnp.bfloat16)
        query_grad = (
            jnp.einsum("hts,sd->htd", score_grad, key_block, preferred_element_type=jnp.float32)
            * scale
        )
        key_grad = (
            jnp.einsum("hts,htd->hsd", score_grad, query_block, preferred_element_type=jnp.float32)
            * scale
        )
        return (query_grad, key_grad, value_grad)

    query_rot_grad, key_rot_grad, value_head_grad = lax.map(
        attend_back, (queries, key_rows, value_rows, segments, logsum, attended_grad)
    )
    query_pre_grad = (
        rotate_back(query_rot_grad, cosine, sine)
        .astype(jnp.bfloat16)
        .transpose(0, 2, 1, 3)
        .reshape(rows, heads * HEAD_SIZE)
    )
    key_pre_grad = rotate_back(key_rot_grad, cosine, sine).astype(jnp.bfloat16)
    value_pre_grad = value_head_grad.astype(jnp.bfloat16)
    normed_seq = normed.reshape(seq_count, document_length, -1)
    query_wgrad = jnp.einsum(
        "tc,tk->ck", normed, query_pre_grad, preferred_element_type=jnp.float32
    )
    key_wgrad = jnp.einsum(
        "slc,shld->cd", normed_seq, key_pre_grad, preferred_element_type=jnp.float32
    )
    value_weight_grad = jnp.einsum(
        "slc,shld->cd", normed_seq, value_pre_grad, preferred_element_type=jnp.float32
    )
    normed_part = (
        jnp.einsum("tk,ck->tc", query_pre_grad, query_weight, preferred_element_type=jnp.float32)
        + jnp.einsum(
            "shld,cd->slc", key_pre_grad, key_cols, preferred_element_type=jnp.float32
        ).reshape(rows, -1)
        + jnp.einsum(
            "shld,cd->slc", value_pre_grad, value_columns, preferred_element_type=jnp.float32
        ).reshape(rows, -1)
    )
    mixout_wgrad = jnp.einsum("tk,td->kd", mixed, branch_grad, preferred_element_type=jnp.float32)
    mixed_grad = jnp.einsum("td,kd->tk", branch_grad, mixer_out, preferred_element_type=jnp.float32)
    mixer_gain_wgrad = jnp.sum(mixed_grad * gated * inv_gate, 0)
    weighted = mixed_grad * mixer_scale
    cross = pair_sum(jnp.sum(weighted * gated, -1))[:, None]
    gated_grad = inv_gate * weighted - gated * (inv_gate * inv_gate * inv_gate) * cross / DSSM
    ssm_grad = gated_grad * gate_act
    gating_act_grad = (
        gated_grad * ssm_out * sigma_gate * (1.0 + gating * (1.0 - sigma_gate))
    ).astype(jnp.bfloat16)
    ssm_heads_grad = ssm_grad.reshape(seq_count, document_length, ssm_heads, P_SIZE).transpose(
        0, 2, 1, 3
    )
    core_grad = ssm_heads_grad.astype(jnp.bfloat16)
    skip_wgrad = jnp.sum(ssm_heads_grad * heads_in, axis=(0, 2, 3))

    def scan_back(seq_item):
        step_block, coef_b_block, coef_c_block, heads_block, seg_ids, core_block = seq_item
        coupling, decay, mixing, driven = ssd_parts(
            step_block, rate, coef_b_block, coef_c_block, heads_block, allowed_of(seg_ids)
        )
        mix_grad = jnp.einsum(
            "htp,hsp->hts", core_block, driven, preferred_element_type=jnp.float32
        )
        driven_grad = jnp.einsum(
            "hts,htp->hsp", mixing, core_block, preferred_element_type=jnp.float32
        )
        rounded = (mix_grad * decay).astype(jnp.bfloat16)
        coef_c_grad = jnp.einsum(
            "hts,sn->tn", rounded, coef_b_block, preferred_element_type=jnp.float32
        )
        coef_b_grad = jnp.einsum(
            "hts,tn->sn", rounded, coef_c_block, preferred_element_type=jnp.float32
        )
        spread = mix_grad * coupling[None] * decay
        cumulative_grad = jnp.sum(spread, 2) - jnp.sum(spread, 1)
        log_grad = jnp.flip(jnp.cumsum(jnp.flip(cumulative_grad, 1), 1), 1)
        heads_grad = driven_grad * step_block.T[:, :, None]
        step_grad = (jnp.sum(driven_grad * heads_block, -1) + log_grad * rate[:, None]).T
        rate_grad = jnp.sum(log_grad * step_block.T, 1)
        return (heads_grad, step_grad, rate_grad, coef_b_grad, coef_c_grad)

    heads_grad, step_grad, rate_grad, coef_b_grad, coef_c_grad = lax.map(
        scan_back, (step, coef_b, coef_c, heads_in, segments, core_grad)
    )
    heads_total = heads_grad + ssm_heads_grad * skip
    inner_act_grad = heads_total.transpose(0, 2, 1, 3).reshape(seq_count, document_length, -1)
    step_total = step_grad * jax.nn.sigmoid(step_arg)
    step_bias_wgrad = jnp.sum(step_total, axis=(0, 1))
    decay_wgrad = jnp.sum(rate_grad, 0) * rate
    step_raw_grad = step_total.reshape(rows, ssm_heads).astype(jnp.bfloat16)
    inner_pre_grad = inner_act_grad * silu_slope(inner_pre)
    inner_bias_wgrad = jnp.sum(inner_pre_grad, axis=(0, 1))
    inner_grad, conv_inner_wgrad = conv_backward(inner_pre_grad, inner, conv_inner, segments)
    inner_grad = inner_grad.reshape(rows, -1).astype(jnp.bfloat16)
    state_act_grad = jnp.concatenate([coef_b_grad, coef_c_grad], -1)
    state_pre_grad = state_act_grad * silu_slope(state_pre)
    state_bias_wgrad = jnp.sum(state_pre_grad, axis=(0, 1))
    state_grad, conv_state_wgrad = conv_backward(state_pre_grad, state_in, conv_state, segments)
    state_grad = state_grad.reshape(rows, -1).astype(jnp.bfloat16)
    gating_wgrad = jnp.einsum(
        "tc,tk->ck", normed, gating_act_grad, preferred_element_type=jnp.float32
    )
    inner_wgrad = jnp.einsum("tc,tk->ck", normed, inner_grad, preferred_element_type=jnp.float32)
    step_wgrad = jnp.einsum("tc,tk->ck", normed, step_raw_grad, preferred_element_type=jnp.float32)
    state_wgrad = jnp.einsum("tc,tk->ck", normed, state_grad, preferred_element_type=jnp.float32)
    normed_part = (
        normed_part
        + jnp.einsum(
            "tk,ck->tc", gating_act_grad, gating_weight, preferred_element_type=jnp.float32
        )
        + jnp.einsum("tk,ck->tc", inner_grad, inner_weight, preferred_element_type=jnp.float32)
        + jnp.einsum("tk,ck->tc", step_raw_grad, step_weight, preferred_element_type=jnp.float32)
        + jnp.einsum("tk,ck->tc", state_grad, state_weight, preferred_element_type=jnp.float32)
    )
    input_gain_part = jnp.sum(normed_part * unit_first, 0)
    normed_full = pair_sum(normed_part.astype(jnp.bfloat16))
    scaled_in = normed_full * in_gain
    tokens_grad = middle_grad + inv_first * (
        scaled_in - unit_first * jnp.mean(scaled_in * unit_first, -1, keepdims=True)
    )
    low = jnp.bfloat16
    if lax.axis_size("tensor") == 2 and KEYVALUE_HEADS == 2:
        keyval_part = jnp.concatenate([key_wgrad, value_weight_grad], 1)
    else:
        keyval_part = jnp.zeros(key_value_weight.shape, jnp.float32)
        keyval_part = lax.dynamic_update_slice_in_dim(
            keyval_part, key_wgrad, shared_key_head * HEAD_SIZE, 1
        )
        keyval_part = lax.dynamic_update_slice_in_dim(
            keyval_part, value_weight_grad, (KEYVALUE_HEADS + shared_key_head) * HEAD_SIZE, 1
        )
        keyval_part = lax.psum(keyval_part, "tensor")
    first_total = tree_sum(
        jnp.concatenate(
            [query_wgrad.astype(low), keyval_part.astype(low), gating_wgrad.astype(low)], 1
        )
    ).astype(jnp.float32)
    second_total = tree_sum(
        jnp.concatenate([attnout_wgrad.astype(low), mixout_wgrad.astype(low)], 0)
    ).astype(jnp.float32)
    width = query_wgrad.shape[1]
    kv_width = keyval_part.shape[1]
    query_wgrad = first_total[:, :width]
    keyval_part = first_total[:, width : width + kv_width]
    gating_wgrad = first_total[:, width + kv_width :]
    attnout_wgrad = second_total[: heads * HEAD_SIZE]
    mixout_wgrad = second_total[heads * HEAD_SIZE :]
    if lax.axis_size("tensor") == 2 and KEYVALUE_HEADS == 2:
        other = lax.ppermute(keyval_part.astype(low), "tensor", [(0, 1), (1, 0)])
        mine = keyval_part.astype(low)
        is_first = lax.axis_index("tensor") == 0
        head_0 = jnp.where(is_first, mine, other)
        head_1 = jnp.where(is_first, other, mine)
        key_value_weight_grad = jnp.concatenate(
            [
                head_0[:, :HEAD_SIZE],
                head_1[:, :HEAD_SIZE],
                head_0[:, HEAD_SIZE:],
                head_1[:, HEAD_SIZE:],
            ],
            1,
        ).astype(jnp.float32)
    else:
        key_value_weight_grad = keyval_part
    own = [
        step_bias_wgrad,
        decay_wgrad,
        skip_wgrad,
        mixer_gain_wgrad,
        inner_bias_wgrad,
        conv_inner_wgrad.reshape(-1),
    ]
    shared = [input_gain_part, post_gain_part, state_bias_wgrad, conv_state_wgrad.reshape(-1)]

    def columns_of(parts):
        flat = jnp.concatenate(parts)
        count = -(-flat.shape[0] // tokens.shape[1])
        flat = jnp.pad(flat, (0, count * tokens.shape[1] - flat.shape[0]))
        return flat.reshape(count, tokens.shape[1]).T

    def parts_of(columns, parts):
        flat = columns.T.reshape(-1)
        found, at = [], 0
        for part in parts:
            found.append(flat[at : at + part.shape[0]])
            at += part.shape[0]
        return found

    own_columns, shared_columns = columns_of(own), columns_of(shared)
    inner_width = inner_wgrad.shape[1]
    own_width = own_columns.shape[1]
    shared_from = -(-(inner_width + ssm_heads + own_width) // 128) * 128
    pad = shared_from - inner_width - ssm_heads - own_width
    third_total = tree_sum(
        jnp.concatenate(
            [
                inner_wgrad.astype(low),
                step_wgrad.astype(low),
                own_columns.astype(low),
                jnp.zeros((tokens.shape[1], pad), low),
                state_wgrad.astype(low),
                shared_columns.astype(low),
            ],
            1,
        ),
        shared_from,
    ).astype(jnp.float32)
    inner_wgrad = third_total[:, :inner_width]
    step_wgrad = third_total[:, inner_width : inner_width + ssm_heads]
    at = inner_width + ssm_heads
    (
        step_bias_wgrad,
        decay_wgrad,
        skip_wgrad,
        mixer_gain_wgrad,
        inner_bias_wgrad,
        conv_inner_flat,
    ) = parts_of(third_total[:, at : at + own_width], own)
    conv_inner_wgrad = conv_inner_flat.reshape(conv_inner.shape)
    state_width = state_wgrad.shape[1]
    state_wgrad = third_total[:, shared_from : shared_from + state_width]
    input_gain_part, post_gain_part, state_bias_wgrad, conv_state_flat = parts_of(
        third_total[:, shared_from + state_width :], shared
    )
    conv_state_wgrad = conv_state_flat.reshape(conv_state.shape)
    down_wgrad = down_wgrad.astype(jnp.float32)
    gate_wgrad = gate_wgrad.astype(jnp.float32)
    up_wgrad = up_wgrad.astype(jnp.float32)
    return (
        tokens_grad,
        input_gain_part,
        query_wgrad,
        key_value_weight_grad,
        attnout_wgrad,
        gating_wgrad,
        inner_wgrad,
        state_wgrad,
        step_wgrad,
        conv_inner_wgrad,
        conv_state_wgrad,
        inner_bias_wgrad,
        state_bias_wgrad,
        step_bias_wgrad,
        decay_wgrad,
        skip_wgrad,
        mixer_gain_wgrad,
        mixout_wgrad,
        post_gain_part,
        gate_wgrad,
        up_wgrad,
        down_wgrad,
    )


CHUNK = 256
LANES = 128
VMEM_BYTES = 56 * 1024 * 1024


def dot_nn(left, right):
    return lax.dot_general(left, right, (((1,), (0,)), ((), ())), preferred_element_type=jnp.float32)


def dot_nt(left, right):
    return lax.dot_general(left, right, (((1,), (1,)), ((), ())), preferred_element_type=jnp.float32)


def dot_tn(left, right):
    return lax.dot_general(left, right, (((0,), (0,)), ((), ())), preferred_element_type=jnp.float32)


def split_two(value):
    high = value.astype(jnp.bfloat16)
    return high, (value - high.astype(jnp.float32)).astype(jnp.bfloat16)


def exact_nn(ones, value):
    high, low = split_two(value)
    return dot_nn(ones, high) + dot_nn(ones, low)


def grid_of(shape):
    return (
        lax.broadcasted_iota(jnp.int32, shape, 0),
        lax.broadcasted_iota(jnp.int32, shape, 1),
    )


def pick(columns, pair):
    rows = columns.shape[0]
    left = jnp.broadcast_to(columns[:, 2 * pair : 2 * pair + 1], (rows, LANES))
    right = jnp.broadcast_to(columns[:, 2 * pair + 1 : 2 * pair + 2], (rows, LANES))
    return jnp.where(grid_of((rows, LANES))[1] < P_SIZE, left, right)


def scan_terms(step, rate, aux):
    row, col = grid_of((CHUNK, CHUNK))
    lower = (row >= col).astype(jnp.bfloat16)
    cumulative = exact_nn(lower, step * rate)
    last = cumulative[CHUNK - 1 : CHUNK]
    enter = jnp.exp(cumulative) * aux[:, 1:2]
    leave = jnp.exp(last - cumulative) * aux[:, 2:3]
    across = jnp.exp(last) * aux[CHUNK - 1 : CHUNK, 1:2]
    return cumulative, enter, leave, across


def scan_kernel(step_ref, coef_ref, act_ref, aux_ref, seg_ref, rate_ref, core_ref, kept_ref, state, moved):
    @pl.when(pl.program_id(0) == 0)
    def _():
        state[...] = jnp.zeros_like(state)

    step = step_ref[...]
    aux = aux_ref[...]
    cumulative, enter, leave, across = scan_terms(step, rate_ref[...], aux)
    cum_rows = cumulative.T
    row, col = grid_of((CHUNK, CHUNK))
    blocked = jnp.where((row >= col) & (aux[:, 0:1] == seg_ref[...]), 0.0, NEG_FILL)
    coef_b = coef_ref[:, :NS]
    coef_c = coef_ref[:, NS:]
    coupling = dot_nt(coef_c, coef_b)
    low_state = state[...].astype(jnp.bfloat16)
    kept_ref[0] = low_state
    carried = dot_nn(coef_c, low_state)
    first = grid_of((CHUNK, LANES))[1] < P_SIZE
    for pair in range(act_ref.shape[1] // LANES):
        at = slice(pair * LANES, (pair + 1) * LANES)
        driven = (act_ref[:, at] * pick(step, pair)).astype(jnp.bfloat16)
        parts = []
        for head in (2 * pair, 2 * pair + 1):
            decay = jnp.exp(cumulative[:, head : head + 1] - cum_rows[head : head + 1] + blocked)
            parts.append(dot_nn((coupling * decay).astype(jnp.bfloat16), driven))
        core_ref[:, at] = jnp.where(first, parts[0], parts[1]) + carried[:, at] * pick(enter, pair)
        moved[:, at] = (driven.astype(jnp.float32) * pick(leave, pair)).astype(jnp.bfloat16)
    fresh = dot_tn(coef_b, moved[...])
    for pair in range(act_ref.shape[1] // LANES):
        at = slice(pair * LANES, (pair + 1) * LANES)
        state[:, at] = state[:, at] * pick(across, pair) + fresh[:, at]


def scan_call(step, coef, act, aux, seg_row, rate):
    rows, width = act.shape
    chunks = rows // CHUNK
    by_chunk = lambda columns: pl.BlockSpec((CHUNK, columns), lambda i: (i, 0))
    return pl.pallas_call(
        scan_kernel,
        grid=(chunks,),
        in_specs=[
            by_chunk(LANES),
            by_chunk(2 * NS),
            by_chunk(width),
            by_chunk(LANES),
            pl.BlockSpec((1, CHUNK), lambda i: (0, i)),
            pl.BlockSpec((1, LANES), lambda i: (0, 0)),
        ],
        out_specs=[by_chunk(width), pl.BlockSpec((1, NS, width), lambda i: (i, 0, 0))],
        out_shape=[
            jax.ShapeDtypeStruct((rows, width), jnp.float32),
            jax.ShapeDtypeStruct((chunks, NS, width), jnp.bfloat16),
        ],
        scratch_shapes=[
            pltpu.VMEM((NS, width), jnp.float32),
            pltpu.VMEM((CHUNK, width), jnp.bfloat16),
        ],
        compiler_params=pltpu.CompilerParams(vmem_limit_bytes=VMEM_BYTES),
        name="scan_forward",
    )(step, coef, act, aux, seg_row, rate)


def scan_back_kernel(
    step_ref,
    coef_ref,
    act_ref,
    aux_ref,
    seg_ref,
    rate_ref,
    skip_ref,
    grad_ref,
    kept_ref,
    act_grad_ref,
    step_grad_ref,
    coef_grad_ref,
    sums_ref,
    skip_sum_ref,
    state_grad,
    moved,
    entered,
    row_sums,
):
    @pl.when(pl.program_id(0) == 0)
    def _():
        state_grad[...] = jnp.zeros_like(state_grad)
        sums_ref[...] = jnp.zeros_like(sums_ref)
        skip_sum_ref[...] = jnp.zeros_like(skip_sum_ref)
        row_sums[...] = jnp.zeros_like(row_sums)

    step = step_ref[...]
    aux = aux_ref[...]
    rate = rate_ref[...]
    cumulative, enter, leave, across = scan_terms(step, rate, aux)
    cum_rows = cumulative.T
    row, col = grid_of((CHUNK, CHUNK))
    blocked = jnp.where((row <= col) & (aux[:, 0:1] == seg_ref[...]), 0.0, NEG_FILL)
    coef_b = coef_ref[:, :NS]
    coef_c = coef_ref[:, NS:]
    coupling = dot_nt(coef_b, coef_c)
    low_state = kept_ref[0]
    carried = dot_nn(coef_c, low_state)
    low_grad = state_grad[...].astype(jnp.bfloat16)
    returned = dot_nn(coef_b, low_grad)
    product = jnp.sum(low_state.astype(jnp.float32) * low_grad.astype(jnp.float32), 0, keepdims=True)
    lane = grid_of((CHUNK, LANES))[1]
    lane_row = grid_of((1, LANES))[1]
    first = lane < P_SIZE
    later = jnp.zeros((CHUNK, LANES), jnp.float32)
    earlier = jnp.zeros((CHUNK, LANES), jnp.float32)
    direct = jnp.zeros((CHUNK, LANES), jnp.float32)
    through = jnp.zeros((1, LANES), jnp.float32)
    coupling_grad = jnp.zeros((CHUNK, CHUNK), jnp.float32)
    for pair in range(act_ref.shape[1] // LANES):
        at = slice(pair * LANES, (pair + 1) * LANES)
        act = act_ref[:, at]
        spread_step = pick(step, pair)
        driven = (act * spread_step).astype(jnp.bfloat16)
        grad = grad_ref[:, at]
        core_grad = grad.astype(jnp.bfloat16)
        core_wide = core_grad.astype(jnp.float32)
        enter_grad = core_wide * pick(enter, pair)
        entered[:, at] = enter_grad.astype(jnp.bfloat16)
        row_part = enter_grad * carried[:, at]
        leave_pair = pick(leave, pair)
        moved[:, at] = (driven.astype(jnp.float32) * leave_pair).astype(jnp.bfloat16)
        back = returned[:, at] * leave_pair
        col_part = back * driven.astype(jnp.float32)
        parts = []
        for head in (2 * pair, 2 * pair + 1):
            mine = first if head % 2 == 0 else ~first
            decay = jnp.exp(cum_rows[head : head + 1] - cumulative[:, head : head + 1] + blocked)
            mix_grad = dot_nt(jnp.where(mine, driven, jnp.zeros_like(driven)), core_grad)
            share = mix_grad * decay
            coupling_grad = coupling_grad + share
            spread = share * coupling
            row_sums[head : head + 1] = jnp.sum(spread, 0, keepdims=True)
            folded = sum(spread[:, k * LANES : (k + 1) * LANES] for k in range(CHUNK // LANES))
            found = jnp.sum(jnp.where(mine, row_part, 0.0) - folded, 1, keepdims=True)
            later = jnp.where(lane == head, found, later)
            parts.append(dot_nn((coupling * decay).astype(jnp.bfloat16), core_grad))
            found = jnp.sum(jnp.where(mine, col_part, 0.0), 1, keepdims=True)
            earlier = jnp.where(lane == head, found, earlier)
        driven_grad = jnp.where(first, parts[0], parts[1]) + back
        act_grad_ref[:, at] = driven_grad * spread_step + grad * skip_ref[:, at]
        skip_sum_ref[:, at] += jnp.sum(grad * act, 0, keepdims=True)
        step_part = driven_grad * act
        product_pair = product[:, at]
        for head in (2 * pair, 2 * pair + 1):
            mine = first if head % 2 == 0 else ~first
            found = jnp.sum(jnp.where(mine, step_part, 0.0), 1, keepdims=True)
            direct = jnp.where(lane == head, found, direct)
            found = jnp.sum(jnp.where(mine[:1], product_pair, 0.0), 1, keepdims=True)
            through = jnp.where(lane_row == head, found, through)
    upper = (row <= col).astype(jnp.bfloat16)
    below = (row > col).astype(jnp.bfloat16)
    high, low = split_two(row_sums[...])
    log_grad = (
        exact_nn(upper, later)
        + dot_nt(upper, high)
        + dot_nt(upper, low)
        + exact_nn(below, earlier)
        + through * across
    )
    step_grad_ref[...] = direct + log_grad * rate
    sums_ref[...] += jnp.sum(log_grad * step, 0, keepdims=True)
    low_coupling = coupling_grad.astype(jnp.bfloat16)
    coef_grad_ref[:, :NS] = dot_nn(low_coupling, coef_c) + dot_nt(moved[...], low_grad)
    coef_grad_ref[:, NS:] = dot_tn(low_coupling, coef_b) + dot_nt(entered[...], low_state)
    fresh = dot_tn(coef_c, entered[...])
    for pair in range(act_ref.shape[1] // LANES):
        at = slice(pair * LANES, (pair + 1) * LANES)
        state_grad[:, at] = state_grad[:, at] * pick(across, pair) + fresh[:, at]


def scan_back_call(step, coef, act, aux, seg_row, rate, skip_row, grad, kept):
    rows, width = act.shape
    chunks = rows // CHUNK
    by_chunk = lambda columns: pl.BlockSpec((CHUNK, columns), lambda i: (chunks - 1 - i, 0))
    one_row = lambda columns: pl.BlockSpec((1, columns), lambda i: (0, 0))
    return pl.pallas_call(
        scan_back_kernel,
        grid=(chunks,),
        in_specs=[
            by_chunk(LANES),
            by_chunk(2 * NS),
            by_chunk(width),
            by_chunk(LANES),
            pl.BlockSpec((1, CHUNK), lambda i: (0, chunks - 1 - i)),
            one_row(LANES),
            one_row(width),
            by_chunk(width),
            pl.BlockSpec((1, NS, width), lambda i: (chunks - 1 - i, 0, 0)),
        ],
        out_specs=[
            by_chunk(width),
            by_chunk(LANES),
            by_chunk(2 * NS),
            one_row(LANES),
            one_row(width),
        ],
        out_shape=[
            jax.ShapeDtypeStruct((rows, width), jnp.float32),
            jax.ShapeDtypeStruct((rows, LANES), jnp.float32),
            jax.ShapeDtypeStruct((rows, 2 * NS), jnp.float32),
            jax.ShapeDtypeStruct((1, LANES), jnp.float32),
            jax.ShapeDtypeStruct((1, width), jnp.float32),
        ],
        scratch_shapes=[
            pltpu.VMEM((NS, width), jnp.float32),
            pltpu.VMEM((CHUNK, width), jnp.bfloat16),
            pltpu.VMEM((CHUNK, width), jnp.bfloat16),
            pltpu.VMEM((LANES, CHUNK), jnp.float32),
        ],
        compiler_params=pltpu.CompilerParams(vmem_limit_bytes=VMEM_BYTES),
        name="scan_backward",
    )(step, coef, act, aux, seg_row, rate, skip_row, grad, kept)


def swap_halves(value):
    width = value.shape[1]
    half = HEAD_SIZE // 2
    up = pltpu.roll(value, width - half, 1)
    down = pltpu.roll(value, half, 1)
    return jnp.where(grid_of(value.shape)[1] % HEAD_SIZE < half, up, down)


def turned(value, cosine, sine):
    return value * cosine + swap_halves(value) * sine


def attend_kernel(query_ref, keyval_ref, seg_ref, seg_col_ref, cos_ref, sin_ref, out_ref, turned_ref, both_ref, log_ref):
    rows = query_ref.shape[0]
    first = grid_of((rows, LANES))[1] < HEAD_SIZE
    keyval = keyval_ref[...]
    moved = pltpu.roll(keyval, HEAD_SIZE, 1)
    keys = turned(jnp.where(first, keyval, moved), cos_ref[...], sin_ref[...]).astype(jnp.bfloat16)
    values = jnp.where(first, moved, keyval).astype(jnp.bfloat16)
    both_ref[:, :LANES] = keys
    both_ref[:, LANES:] = values
    scale = HEAD_SIZE ** (-0.5)
    head_lane = grid_of((CHUNK, LANES))[1]
    first = head_lane < HEAD_SIZE
    for block in range(rows // CHUNK):
        low, high = block * CHUNK, (block + 1) * CHUNK
        row, col = grid_of((CHUNK, high))
        blocked = jnp.where(
            (row + low >= col) & (seg_col_ref[low:high, 0:1] == seg_ref[:, :high]), 0.0, NEG_FILL
        )
        logs = jnp.zeros((CHUNK, LANES), jnp.float32)
        for pair in range(query_ref.shape[1] // LANES):
            at = slice(pair * LANES, (pair + 1) * LANES)
            query = turned(query_ref[low:high, at], cos_ref[low:high], sin_ref[low:high]).astype(
                jnp.bfloat16
            )
            turned_ref[low:high, at] = query
            parts = []
            for head in (2 * pair, 2 * pair + 1):
                mine = first if head % 2 == 0 else ~first
                scores = (
                    dot_nt(jnp.where(mine, query, jnp.zeros_like(query)), keys[:high]) * scale
                    + blocked
                )
                top = jnp.max(scores, 1, keepdims=True)
                weights = jnp.exp(scores - top)
                total = jnp.sum(weights, 1, keepdims=True)
                probs = (weights * (1.0 / total)).astype(jnp.bfloat16)
                parts.append(dot_nn(probs, values[:high]))
                logs = jnp.where(head_lane == head, top + jnp.log(total), logs)
            out_ref[low:high, at] = jnp.where(first, parts[0], parts[1]).astype(jnp.bfloat16)
        log_ref[low:high] = logs


def attend_call(query, keyval, seg_row, aux, cosine, sine):
    rows, width = query.shape
    return pl.pallas_call(
        attend_kernel,
        out_shape=[
            jax.ShapeDtypeStruct((rows, width), jnp.bfloat16),
            jax.ShapeDtypeStruct((rows, width), jnp.bfloat16),
            jax.ShapeDtypeStruct((rows, 2 * LANES), jnp.bfloat16),
            jax.ShapeDtypeStruct((rows, LANES), jnp.float32),
        ],
        compiler_params=pltpu.CompilerParams(vmem_limit_bytes=VMEM_BYTES),
        name="attend_forward",
    )(query, keyval, seg_row, aux, cosine, sine)


def attend_back_kernel(
    query_ref, both_ref, seg_ref, seg_col_ref, cos_ref, sin_ref, log_ref, out_ref, grad_ref,
    query_grad_ref, keyval_grad_ref, key_sum, value_sum,
):
    rows = query_ref.shape[0]
    key_sum[...] = jnp.zeros_like(key_sum)
    value_sum[...] = jnp.zeros_like(value_sum)
    scale = HEAD_SIZE ** (-0.5)
    first = grid_of((CHUNK, LANES))[1] < HEAD_SIZE
    for block in range(rows // CHUNK):
        low, high = block * CHUNK, (block + 1) * CHUNK
        row, col = grid_of((CHUNK, high))
        blocked = jnp.where(
            (row + low >= col) & (seg_col_ref[low:high, 0:1] == seg_ref[:, :high]), 0.0, NEG_FILL
        )
        keys = both_ref[:high, :LANES]
        values = both_ref[:high, LANES:]
        for pair in range(query_ref.shape[1] // LANES):
            at = slice(pair * LANES, (pair + 1) * LANES)
            query = query_ref[low:high, at]
            grad = grad_ref[low:high, at]
            inner = grad.astype(jnp.float32) * out_ref[low:high, at].astype(jnp.float32)
            parts = []
            key_part = None
            for head in (2 * pair, 2 * pair + 1):
                mine = first if head % 2 == 0 else ~first
                query_mine = jnp.where(mine, query, jnp.zeros_like(query))
                grad_mine = jnp.where(mine, grad, jnp.zeros_like(grad))
                scores = dot_nt(query_mine, keys) * scale + blocked
                probs = jnp.exp(scores - log_ref[low:high, head : head + 1])
                delta = jnp.sum(jnp.where(mine, inner, 0.0), 1, keepdims=True)
                prob_grad = dot_nt(grad_mine, values)
                score_grad = (probs * (prob_grad - delta)).astype(jnp.bfloat16)
                parts.append(dot_nn(score_grad, keys) * scale)
                key_sum[:high] += dot_tn(score_grad, query_mine)
                value_sum[:high] += dot_tn(probs.astype(jnp.bfloat16), grad_mine)
            full = jnp.where(first, parts[0], parts[1])
            query_grad_ref[low:high, at] = turned(full, cos_ref[low:high], -sin_ref[low:high]).astype(
                jnp.bfloat16
            )
    wide = grid_of((rows, LANES))[1] < HEAD_SIZE
    key_total = key_sum[...] * scale
    key_total = key_total + pltpu.roll(key_total, HEAD_SIZE, 1)
    key_total = turned(key_total, cos_ref[...], -sin_ref[...])
    value_total = value_sum[...]
    value_total = value_total + pltpu.roll(value_total, HEAD_SIZE, 1)
    keyval_grad_ref[...] = jnp.where(wide, key_total, value_total).astype(jnp.bfloat16)


def attend_back_call(query, both, seg_row, aux, cosine, sine, logs, out, grad):
    rows, width = query.shape
    return pl.pallas_call(
        attend_back_kernel,
        out_shape=[
            jax.ShapeDtypeStruct((rows, width), jnp.bfloat16),
            jax.ShapeDtypeStruct((rows, LANES), jnp.bfloat16),
        ],
        scratch_shapes=[
            pltpu.VMEM((rows, LANES), jnp.float32),
            pltpu.VMEM((rows, LANES), jnp.float32),
        ],
        compiler_params=pltpu.CompilerParams(vmem_limit_bytes=VMEM_BYTES),
        name="attend_backward",
    )(query, both, seg_row, aux, cosine, sine, logs, out, grad)


def halve(value, bit):
    half = value.shape[0] // 2
    upper = (lax.axis_index("dp") & bit) != 0
    got = swap_bit(jnp.where(upper, value[:half], value[half:]), bit)
    kept = jnp.where(upper, value[half:], value[:half])
    return (kept.astype(jnp.float32) + got.astype(jnp.float32)).astype(value.dtype)


def double(value, bit):
    upper = (lax.axis_index("dp") & bit) != 0
    got = swap_bit(value, bit)
    return jnp.concatenate([jnp.where(upper, got, value), jnp.where(upper, value, got)], 0)


def dp_bits():
    size = lax.axis_size("dp")
    return [1 << i for i in range(size.bit_length() - 1)]


def halve_parts(values, bit):
    half = values[0].shape[0] // 2
    upper = (lax.axis_index("dp") & bit) != 0
    got = swap_bit(
        jnp.concatenate([jnp.where(upper, v[:half], v[half:]) for v in values], 1), bit
    )
    kept = jnp.concatenate([jnp.where(upper, v[half:], v[:half]) for v in values], 1)
    return (kept.astype(jnp.float32) + got.astype(jnp.float32)).astype(got.dtype)


def by_rows(value):
    return with_layout_constraint(value, Layout(major_to_minor=(0, 1)))


def swap_pair(value):
    return lax.ppermute(value, "tensor", [(0, 1), (1, 0)])


def tie(*values):
    return lax.optimization_barrier(values)


def conv_rows(value, kernel, bias, keeps):
    taps = kernel.shape[0]
    total = bias.astype(jnp.float32)[None]
    for tap in range(taps):
        offset = taps - 1 - tap
        moved = jnp.pad(value, ((offset, 0), (0, 0)))[: value.shape[0]]
        total = total + kernel[tap].astype(jnp.float32) * moved * keeps[offset]
    return total


def conv_sums(grad, value, taps, keeps):
    sums = []
    for tap in range(taps):
        offset = taps - 1 - tap
        moved = jnp.pad(value, ((offset, 0), (0, 0)))[: value.shape[0]]
        sums.append(jnp.sum(grad * keeps[offset] * moved, 0, keepdims=True))
    return sums


def conv_grad(grad, kernel, keeps):
    taps = kernel.shape[0]
    total = jnp.zeros_like(grad)
    for tap in range(taps):
        offset = taps - 1 - tap
        moved = jnp.pad(grad * keeps[offset], ((0, offset), (0, 0)))[offset:]
        total = total + kernel[tap].astype(jnp.float32) * moved
    return total


def product_kernel(*refs):
    left_pairs, right_pairs = [refs[0:2], refs[2:4], refs[2:4]], [(), refs[4:6], refs[6:8]]
    cotangent_ref, out_ref = refs[8], refs[9]
    half = refs[0].shape[0]
    for which in range(3):
        total = None
        for k in range(2):
            left = left_pairs[which][k][...]
            if which == 0:
                right = cotangent_ref[k * half : (k + 1) * half]
            else:
                right = right_pairs[which][k][...]
            part = dot_tn(left, right)
            total = part if total is None else total + part
        out_ref[which] = total.astype(out_ref.dtype)


def product_call(hidden_a, hidden_b, post_a, post_b, gate_a, gate_b, up_a, up_b, cotangent):
    half, model = post_a.shape
    hidden = hidden_a.shape[1]
    columns = pl.BlockSpec((half, CHUNK), lambda i: (0, i))
    whole = pl.BlockSpec((half, hidden), lambda i: (0, 0))
    return pl.pallas_call(
        product_kernel,
        grid=(hidden // CHUNK,),
        in_specs=[columns] * 4 + [whole] * 4 + [pl.BlockSpec((2 * half, model), lambda i: (0, 0))],
        out_specs=pl.BlockSpec((3, CHUNK, model), lambda i: (0, i, 0)),
        out_shape=jax.ShapeDtypeStruct((3, hidden, model), jnp.bfloat16),
        compiler_params=pltpu.CompilerParams(vmem_limit_bytes=VMEM_BYTES),
        name="weight_products",
    )(hidden_a, hidden_b, post_a, post_b, gate_a, gate_b, up_a, up_b, cotangent)


def local_fast(
    tokens,
    segments,
    cotangent,
    input_gain,
    query_weight,
    key_value_weight,
    attnout_weight,
    gating_weight,
    inner_weight,
    state_weight,
    step_weight,
    conv_inner,
    conv_state,
    inner_bias,
    state_bias,
    step_bias,
    decay_log,
    skip_scale,
    mixer_gain,
    mixer_out,
    post_gain,
    gate_weight,
    up_weight,
    down_weight,
):
    low, wide = jnp.bfloat16, jnp.float32
    rows, model = tokens.shape
    heads = query_weight.shape[1] // HEAD_SIZE
    ssm_heads = step_weight.shape[1]
    ssm_width = ssm_heads * P_SIZE
    query_width = heads * HEAD_SIZE
    first_device = lax.axis_index("tensor") == 0
    pick_head = lambda at: jnp.where(
        first_device,
        key_value_weight[:, at : at + HEAD_SIZE],
        key_value_weight[:, at + HEAD_SIZE : at + 2 * HEAD_SIZE],
    )
    keyval_weight = jnp.concatenate([pick_head(0), pick_head(KEYVALUE_HEADS * HEAD_SIZE)], 1)
    lane_pad = ((0, 0), (0, LANES - ssm_heads))
    step_weight_wide = jnp.pad(step_weight, lane_pad)
    step_bias_wide = jnp.pad(step_bias.astype(wide)[None], lane_pad)
    rate = -jnp.exp(decay_log.astype(wide))
    rate_wide = jnp.pad(rate[None], lane_pad)
    skip_row = jnp.repeat(skip_scale.astype(wide), P_SIZE)[None]
    cosine, sine = rotary_tables(rows)
    cosine = jnp.concatenate([cosine] * 4, 1)
    sine = jnp.concatenate([-sine, sine, -sine, sine], 1)
    seg_row = segments.astype(wide)
    seg_chunks = seg_row.reshape(-1, CHUNK)
    ends = seg_chunks[:, -1:]
    starts = jnp.concatenate([jnp.full((1, 1), -1.0, wide), ends[:-1]], 0)
    aux = jnp.stack(
        [seg_chunks, (seg_chunks == starts).astype(wide), (seg_chunks == ends).astype(wide)], -1
    ).reshape(rows, 3)
    aux = jnp.pad(aux, ((0, 0), (0, LANES - 3)))
    keeps = [seg_keep(segments, offset)[0] for offset in range(conv_inner.shape[0])]

    inputs = by_rows(tokens.astype(wide))
    inv_first = lax.rsqrt(jnp.mean(inputs * inputs, -1, keepdims=True) + EPS)
    unit_first = inputs * inv_first
    in_gain = input_gain.astype(wide)
    normed = by_rows((unit_first * in_gain).astype(low))
    inner = matmul(normed, inner_weight)
    state_in = matmul(normed, state_weight)
    step_arg = matmul(normed, step_weight_wide) + step_bias_wide
    gating = matmul(normed, gating_weight)
    inner_pre = conv_rows(inner, conv_inner, inner_bias, keeps)
    inner_act = jax.nn.silu(inner_pre)
    state_pre = conv_rows(state_in, conv_state, state_bias, keeps)
    coef = jax.nn.silu(state_pre).astype(low)
    step = jax.nn.softplus(step_arg)
    core, kept = scan_call(step, coef, inner_act, aux, seg_row, rate_wide)
    ssm_out = core + skip_row * inner_act
    sigma_gate = jax.nn.sigmoid(gating)
    gate_act = gating * sigma_gate
    gated = ssm_out * gate_act
    square_sum = pair_sum(jnp.sum(gated * gated, -1))[:, None]
    query_pre = matmul(normed, query_weight)
    keyval_pre = matmul(normed, keyval_weight)
    attended, queries, both, logs = attend_call(query_pre, keyval_pre, seg_row, aux, cosine, sine)
    attn_part = matmul(attended, attnout_weight)
    inv_gate = lax.rsqrt(square_sum / DSSM + EPS)
    mixer_scale = mixer_gain.astype(wide)
    mixed = (gated * inv_gate * mixer_scale).astype(low)
    branch_part = attn_part + matmul(mixed, mixer_out)
    out_gain = post_gain.astype(wide)
    branch_part = by_rows(branch_part.astype(low))
    half = rows // 2
    spans = [slice(0, half), slice(half, rows)]
    sent = [branch_part[span] for span in spans]
    got = [swap_pair(piece) for piece in sent]
    weight_cat = jnp.concatenate(
        [gating_weight, inner_weight, step_weight_wide, state_weight, query_weight, keyval_weight], 1
    )
    got[0], weight_cat = tie(got[0], weight_cat)
    found = []
    for at, span in enumerate(spans):
        middle = inputs[span] + by_rows(sent[at].astype(wide) + got[at].astype(wide))
        inv_second = lax.rsqrt(jnp.mean(middle * middle, -1, keepdims=True) + EPS)
        unit_second = middle * inv_second
        post = by_rows((unit_second * out_gain).astype(low))
        gate = matmul(post, gate_weight)
        upward = matmul(post, up_weight)
        sigma = jax.nn.sigmoid(gate)
        hidden = (gate * sigma * upward).astype(low)
        hidden_grad = dot_nt(cotangent[span], down_weight)
        up_act_grad = (hidden_grad * gate * sigma).astype(low)
        gate_act_grad = (hidden_grad * upward * sigma * (1.0 + gate * (1.0 - sigma))).astype(low)
        post_part = dot_nt(gate_act_grad, gate_weight) + dot_nt(up_act_grad, up_weight)
        gain_part = jnp.sum(post_part * unit_second, 0, keepdims=True)
        post_low = by_rows(post_part.astype(low))
        if at == 0:
            got[1], post_low = tie(got[1], post_low)
        else:
            got[0], post_low = tie(got[0], post_low)
        post_got = swap_pair(post_low)
        found.append(
            (post_low, unit_second, inv_second, gain_part, hidden, post, gate_act_grad, up_act_grad)
        )
        got[at] = post_got
    post_gain_part = found[0][3] + found[1][3]
    forward_part = product_call(
        *[piece for k in range(4, 8) for piece in (found[0][k], found[1][k])], cotangent
    )
    got[1], _ = tie(got[1], forward_part)
    forward_piece = lax.psum_scatter(
        forward_part.reshape(-1, model), "dp", scatter_dimension=0, tiled=True
    )
    middle_grads = []
    for span, part, other in zip(spans, found, got):
        post_low, unit_second, inv_second = part[:3]
        post_full = by_rows(post_low.astype(wide) + other.astype(wide))
        scaled_post = post_full * out_gain
        middle_grads.append(
            cotangent[span].astype(wide)
            + inv_second
            * (scaled_post - unit_second * jnp.mean(scaled_post * unit_second, -1, keepdims=True))
        )
    branch_grad = by_rows(jnp.concatenate([grad.astype(low) for grad in middle_grads], 0))
    middle_grad = jnp.concatenate(middle_grads, 0)
    mixed_grad = dot_nt(branch_grad, mixer_out)
    mixer_gain_part = jnp.sum(mixed_grad * gated * inv_gate, 0, keepdims=True)
    weighted = mixed_grad * mixer_scale
    cross = pair_sum(jnp.sum(weighted * gated, -1))[:, None]
    out_part = dot_tn(jnp.concatenate([attended, mixed], 1), branch_grad).astype(low)
    out_part = by_rows(out_part)
    attended_grad = dot_nt(branch_grad, attnout_weight).astype(low)
    gated_grad = inv_gate * weighted - gated * (inv_gate * inv_gate * inv_gate) * cross / DSSM
    ssm_grad = gated_grad * gate_act
    gating_grad = (
        gated_grad * ssm_out * sigma_gate * (1.0 + gating * (1.0 - sigma_gate))
    ).astype(low)
    gating_part = by_rows(dot_tn(normed, gating_grad).astype(low))
    bits = dp_bits()
    early = halve_parts([out_part, gating_part], bits[0])
    early, ssm_grad = tie(early, ssm_grad)
    early = halve(early, bits[1])
    act_grad, step_grad, coef_grad, rate_sum, skip_sum = scan_back_call(
        step, coef, inner_act, aux, seg_row, rate_wide, skip_row, ssm_grad, kept
    )
    early, act_grad, step_grad, coef_grad, forward_piece = tie(
        early, act_grad, step_grad, coef_grad, forward_piece
    )
    forward_total = lax.all_gather(forward_piece, "dp", axis=0, tiled=True)
    early = halve(early, bits[2])
    step_total = step_grad * jax.nn.sigmoid(step_arg)
    taps = conv_inner.shape[0]
    inner_pre_grad = act_grad * silu_slope(inner_pre)
    conv_inner_sums = conv_sums(inner_pre_grad, inner, taps, keeps)
    inner_bias_part = jnp.sum(inner_pre_grad, 0, keepdims=True)
    state_pre_grad = coef_grad * silu_slope(state_pre)
    conv_state_sums = conv_sums(state_pre_grad, state_in, taps, keeps)
    state_bias_part = jnp.sum(state_pre_grad, 0, keepdims=True)
    early, act_grad, coef_grad, *sums = tie(
        early, act_grad, coef_grad, inner_bias_part, state_bias_part, *conv_inner_sums, *conv_state_sums
    )
    inner_bias_part, state_bias_part = sums[:2]
    conv_inner_sums, conv_state_sums = sums[2 : 2 + taps], sums[2 + taps :]
    early = halve(early, bits[3])
    inner_grad = conv_grad(act_grad * silu_slope(inner_pre), conv_inner, keeps)
    state_grad = conv_grad(coef_grad * silu_slope(state_pre), conv_state, keeps)
    scan_cat = jnp.concatenate(
        [inner_grad.astype(low), step_total.astype(low), state_grad.astype(low)], 1
    )
    scan_part = dot_tn(normed, scan_cat).astype(low)
    early, scan_part, attended_grad = tie(early, scan_part, attended_grad)
    early = double(early, bits[3])
    scan_part = halve(scan_part, bits[0])
    query_grad, keyval_grad = attend_back_call(
        queries, both, seg_row, aux, cosine, sine, logs, attended, attended_grad
    )
    attend_cat = jnp.concatenate([query_grad, keyval_grad], 1)
    attend_part = dot_tn(normed, attend_cat).astype(low)
    early, scan_part, attend_part, attend_cat = tie(early, scan_part, attend_part, attend_cat)
    early = double(early, bits[2])
    scan_part = halve(scan_part, bits[1])
    attend_part = halve(attend_part, bits[0])
    normed_part = dot_nt(jnp.concatenate([gating_grad, scan_cat, attend_cat], 1), weight_cat)
    input_gain_part = jnp.sum(normed_part * unit_first, 0, keepdims=True)
    early, scan_part, attend_part, normed_part, input_gain_part = tie(
        early, scan_part, attend_part, normed_part, input_gain_part
    )
    normed_low = by_rows(normed_part.astype(low))
    quarter = rows // 4
    normed_first = swap_pair(normed_low[:quarter])
    own_rows = [
        *conv_inner_sums,
        inner_bias_part,
        mixer_gain_part,
        skip_sum,
        jnp.sum(step_total, 0, keepdims=True),
        rate_sum * rate_wide,
    ]
    shared_rows = [
        input_gain_part,
        post_gain_part,
        *conv_state_sums,
        state_bias_part,
    ]
    small = jnp.concatenate(
        [jnp.pad(row, ((0, 0), (0, model - row.shape[1]))) for row in own_rows + shared_rows], 0
    )
    small = small + swap_bit(small, bits[0])
    early = double(early, bits[1])
    scan_part = halve(scan_part, bits[2])
    attend_part = halve(attend_part, bits[1])
    scan_part, attend_part, small, normed_first, normed_low = tie(
        scan_part, attend_part, small, normed_first, normed_low
    )
    normed_second = swap_pair(normed_low[quarter:half])
    scan_part = halve(scan_part, bits[3])
    attend_part = halve(attend_part, bits[2])
    small = small + swap_bit(small, bits[1])
    scan_part, attend_part, small, normed_second = tie(
        scan_part, attend_part, small, normed_second
    )
    attend_part = halve(attend_part, bits[3])
    small = small + swap_bit(small, bits[2])
    attend_part, small, early = tie(attend_part, small, early)
    small = small + swap_bit(small, bits[3])
    scan_piece, attend_piece = scan_part, attend_part
    state_at = ssm_width + LANES
    trade = jnp.concatenate([scan_piece[:, state_at:], attend_piece[:, query_width:]], 1)
    other = swap_pair(trade)
    other, normed_rest = tie(other, normed_low[half:])
    normed_got = [normed_first, normed_second, swap_pair(normed_rest)]
    state_cols = state_weight.shape[1]
    state_piece = (
        trade[:, :state_cols].astype(wide) + other[:, :state_cols].astype(wide)
    ).astype(low)
    mine, theirs = trade[:, state_cols:], other[:, state_cols:]
    head_0 = jnp.where(first_device, mine, theirs)
    head_1 = jnp.where(first_device, theirs, mine)
    late = jnp.concatenate(
        [
            scan_piece[:, :state_at],
            state_piece,
            attend_piece[:, :query_width],
            head_0[:, :HEAD_SIZE],
            head_1[:, :HEAD_SIZE],
            head_0[:, HEAD_SIZE:],
            head_1[:, HEAD_SIZE:],
        ],
        1,
    )
    late, small, early = tie(late, small, early)
    early = double(early, bits[0])
    late = double(late, bits[3])
    small_other = lax.ppermute(small, "tensor", [(0, 1), (1, 0)])
    is_shared = lax.broadcasted_iota(jnp.int32, small.shape, 0) >= len(own_rows)
    small = small + jnp.where(is_shared, small_other, 0.0)
    late, early, small = tie(late, early, small)
    late = double(late, bits[2])
    late, forward_total = tie(late, forward_total)
    hidden_units = down_weight.shape[0]
    down_wgrad = forward_total[:hidden_units].astype(wide)
    gate_wgrad = forward_total[hidden_units : hidden_units + model].astype(wide)
    up_wgrad = forward_total[hidden_units + model :].astype(wide)
    late = double(late, bits[1])
    early_grads = (
        gate_wgrad,
        up_wgrad,
        down_wgrad,
        early[:query_width, :model].astype(wide),
        early[:, model:].astype(wide),
        early[query_width:, :model].astype(wide),
    )
    normed_full = by_rows(normed_low.astype(wide) + jnp.concatenate(normed_got, 0).astype(wide))
    scaled_in = normed_full * in_gain
    tokens_grad = middle_grad + inv_first * (
        scaled_in - unit_first * jnp.mean(scaled_in * unit_first, -1, keepdims=True)
    )
    late, tokens_grad, *early_grads = tie(late, tokens_grad, *early_grads)
    late = double(late, bits[0])
    scan_total = late[:, : state_at + state_cols]
    attend_total = late[:, state_at + state_cols :]
    gate_wgrad, up_wgrad, down_wgrad, attnout_grad, gating_wgrad, mixout_grad = early_grads
    count = len(own_rows)
    return (
        tokens_grad,
        small[count],
        attend_total[:, :query_width].astype(wide),
        attend_total[:, query_width:].astype(wide),
        attnout_grad,
        gating_wgrad,
        scan_total[:, :ssm_width].astype(wide),
        scan_total[:, state_at:].astype(wide),
        scan_total[:, ssm_width : ssm_width + ssm_heads].astype(wide),
        small[:taps, :ssm_width],
        small[count + 2 : count + 2 + taps, :state_cols],
        small[taps, :ssm_width],
        small[count + 2 + taps, :state_cols],
        small[taps + 3, :ssm_heads],
        small[taps + 4, :ssm_heads],
        jnp.sum(small[taps + 2, :ssm_width].reshape(ssm_heads, P_SIZE), 1),
        small[taps + 1, :ssm_width],
        mixout_grad,
        small[count + 1],
        gate_wgrad,
        up_wgrad,
        down_wgrad,
    )


def layer(*arrays):
    tokens, segments, query_weight, step_weight = arrays[0], arrays[1], arrays[4], arrays[10]
    size = lax.axis_size("dp")
    fits = (
        lax.axis_size("tensor") == 2
        and size == 16
        and segments.shape[0] == 1
        and tokens.shape[0] % CHUNK == 0
        and tokens.shape[1] % (16 * size) == 0
        and query_weight.shape[1] == QUERY_HEADS // KEYVALUE_HEADS * HEAD_SIZE
        and KEYVALUE_HEADS == 2
        and arrays[23].shape[0] == tokens.shape[1]
        and step_weight.shape[1] % 2 == 0
        and query_weight.shape[1] + step_weight.shape[1] * P_SIZE == tokens.shape[1]
    )
    return local_fast(*arrays) if fits else local(*arrays)


def solution(mesh):
    placed = (
        P("dp", None),
        P("dp", None),
        P("dp", None),
        P(),
        P(None, "tensor"),
        P(),
        P("tensor", None),
        P(None, "tensor"),
        P(None, "tensor"),
        P(),
        P(None, "tensor"),
        P(None, "tensor"),
        P(),
        P("tensor"),
        P(),
        P("tensor"),
        P("tensor"),
        P("tensor"),
        P("tensor"),
        P("tensor", None),
        P(),
        P(None, "tensor"),
        P(None, "tensor"),
        P("tensor", None),
    )
    return jax.shard_map(
        layer,
        mesh=mesh,
        in_specs=placed,
        out_specs=(
            P("dp", None),
            P(),
            P(None, "tensor"),
            P(),
            P("tensor", None),
            P(None, "tensor"),
            P(None, "tensor"),
            P(),
            P(None, "tensor"),
            P(None, "tensor"),
            P(),
            P("tensor"),
            P(),
            P("tensor"),
            P("tensor"),
            P("tensor"),
            P("tensor"),
            P("tensor", None),
            P(),
            P(None, "tensor"),
            P(None, "tensor"),
            P("tensor", None),
        ),
        check_vma=False,
    )
```

```python
import jax
import jax.numpy as jnp
from jax import lax
from jax.experimental.layout import Layout, with_layout_constraint
from jax.experimental import pallas as pl
from jax.experimental.pallas import tpu as pltpu
from jax.sharding import PartitionSpec as P

QUERY_HEADS = 8
KEYVALUE_HEADS = 2
HEAD_SIZE = 64
P_SIZE = 64
NS = 128
DSSM = 1536


EPS = 1e-05
ROPE_BASE = 100000000000.0
NEG_FILL = -1e30


def matmul(left, right):
    return jnp.dot(left, right, preferred_element_type=jnp.float32)


def rotary_tables(document_length):
    half = HEAD_SIZE // 2
    freqs = jnp.exp(-jnp.log(ROPE_BASE) * (2.0 * jnp.arange(half, dtype=jnp.float32) / HEAD_SIZE))
    angles = jnp.arange(document_length, dtype=jnp.float32)[:, None] * freqs[None, :]
    return (jnp.cos(angles), jnp.sin(angles))


def rotate(value, cosine, sine):
    half = value.shape[-1] // 2
    first = value[..., :half]
    second = value[..., half:]
    return jnp.concatenate([first * cosine - second * sine, first * sine + second * cosine], -1)


def rotate_back(grad, cosine, sine):
    half = grad.shape[-1] // 2
    first = grad[..., :half]
    second = grad[..., half:]
    return jnp.concatenate([first * cosine + second * sine, second * cosine - first * sine], -1)


def silu_slope(value):
    sigma = jax.nn.sigmoid(value)
    return sigma * (1.0 + value * (1.0 - sigma))


def seg_keep(segments, offset):
    document_length = segments.shape[1]
    moved = jnp.pad(segments, ((0, 0), (offset, 0)), constant_values=-1)[:, :document_length]
    return (moved == segments).astype(jnp.float32)[:, :, None]


def move_down(value, offset):
    document_length = value.shape[1]
    return jnp.pad(value, ((0, 0), (offset, 0), (0, 0)))[:, :document_length]


def move_up(value, offset):
    return jnp.pad(value, ((0, 0), (0, offset), (0, 0)))[:, offset:]


def conv_forward(value, kernel, bias, segments):
    taps = kernel.shape[0]
    total = jnp.zeros_like(value) + bias.astype(jnp.float32)
    for tap in range(taps):
        offset = taps - 1 - tap
        total = total + kernel[tap].astype(jnp.float32) * move_down(value, offset) * seg_keep(
            segments, offset
        )
    return total


def conv_backward(grad, value, kernel, segments):
    taps = kernel.shape[0]
    grad_in = jnp.zeros_like(value)
    kernel_rows = []
    for tap in range(taps):
        offset = taps - 1 - tap
        masked = grad * seg_keep(segments, offset)
        kernel_rows.append(jnp.sum(masked * move_down(value, offset), axis=(0, 1)))
        grad_in = grad_in + kernel[tap].astype(jnp.float32) * move_up(masked, offset)
    return (grad_in, jnp.stack(kernel_rows))


def ssd_parts(step_block, rate, coef_b, coef_c, heads_block, allowed):
    coupling = jnp.einsum("tn,sn->ts", coef_c, coef_b, preferred_element_type=jnp.float32)
    cumulative = jnp.cumsum(step_block * rate, axis=0).T
    difference = cumulative[:, :, None] - cumulative[:, None, :]
    decay = jnp.where(allowed[None], jnp.exp(jnp.where(allowed[None], difference, 0.0)), 0.0)
    mixing = (coupling[None] * decay).astype(jnp.bfloat16)
    driven = (heads_block * step_block.T[:, :, None]).astype(jnp.bfloat16)
    return (coupling, decay, mixing, driven)


def pair_sum(value):
    if lax.axis_size("tensor") == 2:
        other = lax.ppermute(value, "tensor", [(0, 1), (1, 0)])
        return value.astype(jnp.float32) + other.astype(jnp.float32)
    return lax.psum(value, "tensor").astype(jnp.float32)


def swap_bit(value, bit):
    size = lax.axis_size("dp")
    return lax.ppermute(value, "dp", [(i, i ^ bit) for i in range(size)])


def shared_sum(rows, first_shared):
    tail = pair_sum(rows[:, first_shared:]).astype(rows.dtype)
    return jnp.concatenate([rows[:, :first_shared], tail], 1) if first_shared else tail


def tree_sum(value, first_shared=None):
    size = lax.axis_size("dp")
    rows = value.shape[0]
    if size & (size - 1) or rows % (16 * size):
        total = lax.psum(value, "dp")
        return total if first_shared is None else shared_sum(total, first_shared)
    bits = [1 << i for i in range(size.bit_length() - 1)]
    me = lax.axis_index("dp")
    for bit in bits:
        half = value.shape[0] // 2
        low, high = value[:half], value[half:]
        upper = (me & bit) != 0
        got = swap_bit(jnp.where(upper, low, high), bit)
        kept = jnp.where(upper, high, low)
        value = (kept.astype(jnp.float32) + got.astype(jnp.float32)).astype(value.dtype)
    if first_shared is not None:
        value = shared_sum(value, first_shared)
    for bit in reversed(bits):
        upper = (me & bit) != 0
        got = swap_bit(value, bit)
        value = jnp.where(
            upper, jnp.concatenate([got, value], 0), jnp.concatenate([value, got], 0)
        )
    return value


def local(
    tokens,
    segments,
    cotangent,
    input_gain,
    query_weight,
    key_value_weight,
    attnout_weight,
    gating_weight,
    inner_weight,
    state_weight,
    step_weight,
    conv_inner,
    conv_state,
    inner_bias,
    state_bias,
    step_bias,
    decay_log,
    skip_scale,
    mixer_gain,
    mixer_out,
    post_gain,
    gate_weight,
    up_weight,
    down_weight,
):
    seq_count, document_length = segments.shape
    rows = seq_count * document_length
    heads = query_weight.shape[1] // HEAD_SIZE
    ssm_heads = step_weight.shape[1]
    query_group = QUERY_HEADS // KEYVALUE_HEADS
    shared_key_head = lax.axis_index("tensor") * heads // query_group
    scale = HEAD_SIZE ** (-0.5)
    cosine, sine = rotary_tables(document_length)
    positions = jnp.arange(document_length)

    def allowed_of(seg_ids):
        return (positions[:, None] >= positions[None, :]) & (seg_ids[:, None] == seg_ids[None, :])

    inputs = tokens.astype(jnp.float32)
    inv_first = lax.rsqrt(jnp.mean(inputs * inputs, -1, keepdims=True) + EPS)
    unit_first = inputs * inv_first
    in_gain = input_gain.astype(jnp.float32)
    normed = (unit_first * in_gain).astype(jnp.bfloat16)
    key_cols = lax.dynamic_slice_in_dim(key_value_weight, shared_key_head * HEAD_SIZE, HEAD_SIZE, 1)
    value_columns = lax.dynamic_slice_in_dim(
        key_value_weight, (KEYVALUE_HEADS + shared_key_head) * HEAD_SIZE, HEAD_SIZE, 1
    )
    query_pre = matmul(normed, query_weight)
    key_pre = matmul(normed, key_cols)
    value_pre = matmul(normed, value_columns)
    queries = rotate(
        query_pre.reshape(seq_count, document_length, heads, HEAD_SIZE).transpose(0, 2, 1, 3),
        cosine,
        sine,
    ).astype(jnp.bfloat16)
    key_rows = rotate(key_pre.reshape(seq_count, document_length, HEAD_SIZE), cosine, sine).astype(
        jnp.bfloat16
    )
    value_rows = value_pre.reshape(seq_count, document_length, HEAD_SIZE).astype(jnp.bfloat16)

    def attend(seq_item):
        query_block, key_block, value_block, seg_ids = seq_item
        allowed = allowed_of(seg_ids)[None]
        scores = (
            jnp.einsum("htd,sd->hts", query_block, key_block, preferred_element_type=jnp.float32)
            * scale
        )
        scores = jnp.where(allowed, scores, NEG_FILL)
        top = jnp.max(scores, -1, keepdims=True)
        weights = jnp.exp(scores - top)
        total = jnp.sum(weights, -1, keepdims=True)
        probs = (weights / total).astype(jnp.bfloat16)
        attended = jnp.einsum("hts,sd->htd", probs, value_block, preferred_element_type=jnp.float32)
        return (attended.astype(jnp.bfloat16), (top + jnp.log(total))[..., 0])

    attended, logsum = lax.map(attend, (queries, key_rows, value_rows, segments))
    attn_flat = attended.transpose(0, 2, 1, 3).reshape(rows, heads * HEAD_SIZE)
    attn_part = matmul(attn_flat, attnout_weight)
    gating = matmul(normed, gating_weight)
    inner = matmul(normed, inner_weight).reshape(seq_count, document_length, -1)
    state_in = matmul(normed, state_weight).reshape(seq_count, document_length, -1)
    step_raw = matmul(normed, step_weight)
    inner_pre = conv_forward(inner, conv_inner, inner_bias, segments)
    inner_act = jax.nn.silu(inner_pre)
    state_pre = conv_forward(state_in, conv_state, state_bias, segments)
    state_act = jax.nn.silu(state_pre)
    coef_b = state_act[..., :NS].astype(jnp.bfloat16)
    coef_c = state_act[..., NS:].astype(jnp.bfloat16)
    step_arg = step_raw.reshape(seq_count, document_length, ssm_heads) + step_bias.astype(
        jnp.float32
    )
    step = jax.nn.softplus(step_arg)
    rate = -jnp.exp(decay_log.astype(jnp.float32))
    heads_in = inner_act.reshape(seq_count, document_length, ssm_heads, P_SIZE).transpose(
        0, 2, 1, 3
    )

    def scan_forward(seq_item):
        step_block, coef_b_block, coef_c_block, heads_block, seg_ids = seq_item
        parts = ssd_parts(
            step_block, rate, coef_b_block, coef_c_block, heads_block, allowed_of(seg_ids)
        )
        return jnp.einsum("hts,hsp->htp", parts[2], parts[3], preferred_element_type=jnp.float32)

    core = lax.map(scan_forward, (step, coef_b, coef_c, heads_in, segments))
    skip = skip_scale.astype(jnp.float32)[None, :, None, None]
    ssm_out = (core + skip * heads_in).transpose(0, 2, 1, 3).reshape(rows, ssm_heads * P_SIZE)
    sigma_gate = jax.nn.sigmoid(gating)
    gate_act = gating * sigma_gate
    gated = ssm_out * gate_act
    square_sum = pair_sum(jnp.sum(gated * gated, -1))[:, None]
    inv_gate = lax.rsqrt(square_sum / DSSM + EPS)
    mixer_scale = mixer_gain.astype(jnp.float32)
    mixed = (gated * inv_gate * mixer_scale).astype(jnp.bfloat16)
    branch_part = attn_part + matmul(mixed, mixer_out)
    out_gain = post_gain.astype(jnp.float32)
    branch = pair_sum(branch_part.astype(jnp.bfloat16))
    middle = inputs + branch
    inv_second = lax.rsqrt(jnp.mean(middle * middle, -1, keepdims=True) + EPS)
    unit_second = middle * inv_second
    post = (unit_second * out_gain).astype(jnp.bfloat16)
    gate = matmul(post, gate_weight)
    upward = matmul(post, up_weight)
    sigma = jax.nn.sigmoid(gate)
    hidden = (gate * sigma * upward).astype(jnp.bfloat16)
    down_wgrad = jnp.einsum("tf,td->fd", hidden, cotangent, preferred_element_type=jnp.float32)
    hidden_grad = jnp.einsum(
        "td,fd->tf", cotangent, down_weight, preferred_element_type=jnp.float32
    )
    up_act_grad = (hidden_grad * gate * sigma).astype(jnp.bfloat16)
    gate_act_grad = (hidden_grad * upward * sigma * (1.0 + gate * (1.0 - sigma))).astype(
        jnp.bfloat16
    )
    gate_wgrad = jnp.einsum("tc,tf->cf", post, gate_act_grad, preferred_element_type=jnp.float32)
    up_wgrad = jnp.einsum("tc,tf->cf", post, up_act_grad, preferred_element_type=jnp.float32)
    post_part = jnp.einsum(
        "tf,cf->tc", gate_act_grad, gate_weight, preferred_element_type=jnp.float32
    ) + jnp.einsum("tf,cf->tc", up_act_grad, up_weight, preferred_element_type=jnp.float32)
    post_gain_part = jnp.sum(post_part * unit_second, 0)
    post_full = pair_sum(post_part.astype(jnp.bfloat16))
    down_wgrad, gate_wgrad, up_wgrad, post_full = lax.optimization_barrier(
        (
            down_wgrad.astype(jnp.bfloat16),
            gate_wgrad.astype(jnp.bfloat16),
            up_wgrad.astype(jnp.bfloat16),
            post_full,
        )
    )
    down_wgrad, gate_wgrad, up_wgrad = lax.psum((down_wgrad, gate_wgrad, up_wgrad), "dp")
    scaled_post = post_full * out_gain
    middle_grad = cotangent.astype(jnp.float32) + inv_second * (
        scaled_post - unit_second * jnp.mean(scaled_post * unit_second, -1, keepdims=True)
    )
    branch_grad = middle_grad.astype(jnp.bfloat16)
    attnout_wgrad = jnp.einsum(
        "tk,td->kd", attn_flat, branch_grad, preferred_element_type=jnp.float32
    )
    attended_grad = jnp.einsum(
        "td,kd->tk", branch_grad, attnout_weight, preferred_element_type=jnp.float32
    )
    attended_grad = (
        attended_grad.astype(jnp.bfloat16)
        .reshape(seq_count, document_length, heads, HEAD_SIZE)
        .transpose(0, 2, 1, 3)
    )

    def attend_back(seq_item):
        query_block, key_block, value_block, seg_ids, logsum_block, grad_block = seq_item
        allowed = allowed_of(seg_ids)[None]
        scores = (
            jnp.einsum("htd,sd->hts", query_block, key_block, preferred_element_type=jnp.float32)
            * scale
        )
        probs = jnp.where(allowed, jnp.exp(scores - logsum_block[..., None]), 0.0)
        value_grad = jnp.einsum(
            "hts,htd->hsd",
            probs.astype(jnp.bfloat16),
            grad_block,
            preferred_element_type=jnp.float32,
        )
        prob_grad = jnp.einsum(
            "htd,sd->hts", grad_block, value_block, preferred_element_type=jnp.float32
        )
        delta = jnp.sum(probs * prob_grad, -1, keepdims=True)
        score_grad = (probs * (prob_grad - delta)).astype(jnp.bfloat16)
        query_grad = (
            jnp.einsum("hts,sd->htd", score_grad, key_block, preferred_element_type=jnp.float32)
            * scale
        )
        key_grad = (
            jnp.einsum("hts,htd->hsd", score_grad, query_block, preferred_element_type=jnp.float32)
            * scale
        )
        return (query_grad, key_grad, value_grad)

    query_rot_grad, key_rot_grad, value_head_grad = lax.map(
        attend_back, (queries, key_rows, value_rows, segments, logsum, attended_grad)
    )
    query_pre_grad = (
        rotate_back(query_rot_grad, cosine, sine)
        .astype(jnp.bfloat16)
        .transpose(0, 2, 1, 3)
        .reshape(rows, heads * HEAD_SIZE)
    )
    key_pre_grad = rotate_back(key_rot_grad, cosine, sine).astype(jnp.bfloat16)
    value_pre_grad = value_head_grad.astype(jnp.bfloat16)
    normed_seq = normed.reshape(seq_count, document_length, -1)
    query_wgrad = jnp.einsum(
        "tc,tk->ck", normed, query_pre_grad, preferred_element_type=jnp.float32
    )
    key_wgrad = jnp.einsum(
        "slc,shld->cd", normed_seq, key_pre_grad, preferred_element_type=jnp.float32
    )
    value_weight_grad = jnp.einsum(
        "slc,shld->cd", normed_seq, value_pre_grad, preferred_element_type=jnp.float32
    )
    normed_part = (
        jnp.einsum("tk,ck->tc", query_pre_grad, query_weight, preferred_element_type=jnp.float32)
        + jnp.einsum(
            "shld,cd->slc", key_pre_grad, key_cols, preferred_element_type=jnp.float32
        ).reshape(rows, -1)
        + jnp.einsum(
            "shld,cd->slc", value_pre_grad, value_columns, preferred_element_type=jnp.float32
        ).reshape(rows, -1)
    )
    mixout_wgrad = jnp.einsum("tk,td->kd", mixed, branch_grad, preferred_element_type=jnp.float32)
    mixed_grad = jnp.einsum("td,kd->tk", branch_grad, mixer_out, preferred_element_type=jnp.float32)
    mixer_gain_wgrad = jnp.sum(mixed_grad * gated * inv_gate, 0)
    weighted = mixed_grad * mixer_scale
    cross = pair_sum(jnp.sum(weighted * gated, -1))[:, None]
    gated_grad = inv_gate * weighted - gated * (inv_gate * inv_gate * inv_gate) * cross / DSSM
    ssm_grad = gated_grad * gate_act
    gating_act_grad = (
        gated_grad * ssm_out * sigma_gate * (1.0 + gating * (1.0 - sigma_gate))
    ).astype(jnp.bfloat16)
    ssm_heads_grad = ssm_grad.reshape(seq_count, document_length, ssm_heads, P_SIZE).transpose(
        0, 2, 1, 3
    )
    core_grad = ssm_heads_grad.astype(jnp.bfloat16)
    skip_wgrad = jnp.sum(ssm_heads_grad * heads_in, axis=(0, 2, 3))

    def scan_back(seq_item):
        step_block, coef_b_block, coef_c_block, heads_block, seg_ids, core_block = seq_item
        coupling, decay, mixing, driven = ssd_parts(
            step_block, rate, coef_b_block, coef_c_block, heads_block, allowed_of(seg_ids)
        )
        mix_grad = jnp.einsum(
            "htp,hsp->hts", core_block, driven, preferred_element_type=jnp.float32
        )
        driven_grad = jnp.einsum(
            "hts,htp->hsp", mixing, core_block, preferred_element_type=jnp.float32
        )
        rounded = (mix_grad * decay).astype(jnp.bfloat16)
        coef_c_grad = jnp.einsum(
            "hts,sn->tn", rounded, coef_b_block, preferred_element_type=jnp.float32
        )
        coef_b_grad = jnp.einsum(
            "hts,tn->sn", rounded, coef_c_block, preferred_element_type=jnp.float32
        )
        spread = mix_grad * coupling[None] * decay
        cumulative_grad = jnp.sum(spread, 2) - jnp.sum(spread, 1)
        log_grad = jnp.flip(jnp.cumsum(jnp.flip(cumulative_grad, 1), 1), 1)
        heads_grad = driven_grad * step_block.T[:, :, None]
        step_grad = (jnp.sum(driven_grad * heads_block, -1) + log_grad * rate[:, None]).T
        rate_grad = jnp.sum(log_grad * step_block.T, 1)
        return (heads_grad, step_grad, rate_grad, coef_b_grad, coef_c_grad)

    heads_grad, step_grad, rate_grad, coef_b_grad, coef_c_grad = lax.map(
        scan_back, (step, coef_b, coef_c, heads_in, segments, core_grad)
    )
    heads_total = heads_grad + ssm_heads_grad * skip
    inner_act_grad = heads_total.transpose(0, 2, 1, 3).reshape(seq_count, document_length, -1)
    step_total = step_grad * jax.nn.sigmoid(step_arg)
    step_bias_wgrad = jnp.sum(step_total, axis=(0, 1))
    decay_wgrad = jnp.sum(rate_grad, 0) * rate
    step_raw_grad = step_total.reshape(rows, ssm_heads).astype(jnp.bfloat16)
    inner_pre_grad = inner_act_grad * silu_slope(inner_pre)
    inner_bias_wgrad = jnp.sum(inner_pre_grad, axis=(0, 1))
    inner_grad, conv_inner_wgrad = conv_backward(inner_pre_grad, inner, conv_inner, segments)
    inner_grad = inner_grad.reshape(rows, -1).astype(jnp.bfloat16)
    state_act_grad = jnp.concatenate([coef_b_grad, coef_c_grad], -1)
    state_pre_grad = state_act_grad * silu_slope(state_pre)
    state_bias_wgrad = jnp.sum(state_pre_grad, axis=(0, 1))
    state_grad, conv_state_wgrad = conv_backward(state_pre_grad, state_in, conv_state, segments)
    state_grad = state_grad.reshape(rows, -1).astype(jnp.bfloat16)
    gating_wgrad = jnp.einsum(
        "tc,tk->ck", normed, gating_act_grad, preferred_element_type=jnp.float32
    )
    inner_wgrad = jnp.einsum("tc,tk->ck", normed, inner_grad, preferred_element_type=jnp.float32)
    step_wgrad = jnp.einsum("tc,tk->ck", normed, step_raw_grad, preferred_element_type=jnp.float32)
    state_wgrad = jnp.einsum("tc,tk->ck", normed, state_grad, preferred_element_type=jnp.float32)
    normed_part = (
        normed_part
        + jnp.einsum(
            "tk,ck->tc", gating_act_grad, gating_weight, preferred_element_type=jnp.float32
        )
        + jnp.einsum("tk,ck->tc", inner_grad, inner_weight, preferred_element_type=jnp.float32)
        + jnp.einsum("tk,ck->tc", step_raw_grad, step_weight, preferred_element_type=jnp.float32)
        + jnp.einsum("tk,ck->tc", state_grad, state_weight, preferred_element_type=jnp.float32)
    )
    input_gain_part = jnp.sum(normed_part * unit_first, 0)
    normed_full = pair_sum(normed_part.astype(jnp.bfloat16))
    scaled_in = normed_full * in_gain
    tokens_grad = middle_grad + inv_first * (
        scaled_in - unit_first * jnp.mean(scaled_in * unit_first, -1, keepdims=True)
    )
    low = jnp.bfloat16
    if lax.axis_size("tensor") == 2 and KEYVALUE_HEADS == 2:
        keyval_part = jnp.concatenate([key_wgrad, value_weight_grad], 1)
    else:
        keyval_part = jnp.zeros(key_value_weight.shape, jnp.float32)
        keyval_part = lax.dynamic_update_slice_in_dim(
            keyval_part, key_wgrad, shared_key_head * HEAD_SIZE, 1
        )
        keyval_part = lax.dynamic_update_slice_in_dim(
            keyval_part, value_weight_grad, (KEYVALUE_HEADS + shared_key_head) * HEAD_SIZE, 1
        )
        keyval_part = lax.psum(keyval_part, "tensor")
    first_total = tree_sum(
        jnp.concatenate(
            [query_wgrad.astype(low), keyval_part.astype(low), gating_wgrad.astype(low)], 1
        )
    ).astype(jnp.float32)
    second_total = tree_sum(
        jnp.concatenate([attnout_wgrad.astype(low), mixout_wgrad.astype(low)], 0)
    ).astype(jnp.float32)
    width = query_wgrad.shape[1]
    kv_width = keyval_part.shape[1]
    query_wgrad = first_total[:, :width]
    keyval_part = first_total[:, width : width + kv_width]
    gating_wgrad = first_total[:, width + kv_width :]
    attnout_wgrad = second_total[: heads * HEAD_SIZE]
    mixout_wgrad = second_total[heads * HEAD_SIZE :]
    if lax.axis_size("tensor") == 2 and KEYVALUE_HEADS == 2:
        other = lax.ppermute(keyval_part.astype(low), "tensor", [(0, 1), (1, 0)])
        mine = keyval_part.astype(low)
        is_first = lax.axis_index("tensor") == 0
        head_0 = jnp.where(is_first, mine, other)
        head_1 = jnp.where(is_first, other, mine)
        key_value_weight_grad = jnp.concatenate(
            [
                head_0[:, :HEAD_SIZE],
                head_1[:, :HEAD_SIZE],
                head_0[:, HEAD_SIZE:],
                head_1[:, HEAD_SIZE:],
            ],
            1,
        ).astype(jnp.float32)
    else:
        key_value_weight_grad = keyval_part
    own = [
        step_bias_wgrad,
        decay_wgrad,
        skip_wgrad,
        mixer_gain_wgrad,
        inner_bias_wgrad,
        conv_inner_wgrad.reshape(-1),
    ]
    shared = [input_gain_part, post_gain_part, state_bias_wgrad, conv_state_wgrad.reshape(-1)]

    def columns_of(parts):
        flat = jnp.concatenate(parts)
        count = -(-flat.shape[0] // tokens.shape[1])
        flat = jnp.pad(flat, (0, count * tokens.shape[1] - flat.shape[0]))
        return flat.reshape(count, tokens.shape[1]).T

    def parts_of(columns, parts):
        flat = columns.T.reshape(-1)
        found, at = [], 0
        for part in parts:
            found.append(flat[at : at + part.shape[0]])
            at += part.shape[0]
        return found

    own_columns, shared_columns = columns_of(own), columns_of(shared)
    inner_width = inner_wgrad.shape[1]
    own_width = own_columns.shape[1]
    shared_from = -(-(inner_width + ssm_heads + own_width) // 128) * 128
    pad = shared_from - inner_width - ssm_heads - own_width
    third_total = tree_sum(
        jnp.concatenate(
            [
                inner_wgrad.astype(low),
                step_wgrad.astype(low),
                own_columns.astype(low),
                jnp.zeros((tokens.shape[1], pad), low),
                state_wgrad.astype(low),
                shared_columns.astype(low),
            ],
            1,
        ),
        shared_from,
    ).astype(jnp.float32)
    inner_wgrad = third_total[:, :inner_width]
    step_wgrad = third_total[:, inner_width : inner_width + ssm_heads]
    at = inner_width + ssm_heads
    (
        step_bias_wgrad,
        decay_wgrad,
        skip_wgrad,
        mixer_gain_wgrad,
        inner_bias_wgrad,
        conv_inner_flat,
    ) = parts_of(third_total[:, at : at + own_width], own)
    conv_inner_wgrad = conv_inner_flat.reshape(conv_inner.shape)
    state_width = state_wgrad.shape[1]
    state_wgrad = third_total[:, shared_from : shared_from + state_width]
    input_gain_part, post_gain_part, state_bias_wgrad, conv_state_flat = parts_of(
        third_total[:, shared_from + state_width :], shared
    )
    conv_state_wgrad = conv_state_flat.reshape(conv_state.shape)
    down_wgrad = down_wgrad.astype(jnp.float32)
    gate_wgrad = gate_wgrad.astype(jnp.float32)
    up_wgrad = up_wgrad.astype(jnp.float32)
    return (
        tokens_grad,
        input_gain_part,
        query_wgrad,
        key_value_weight_grad,
        attnout_wgrad,
        gating_wgrad,
        inner_wgrad,
        state_wgrad,
        step_wgrad,
        conv_inner_wgrad,
        conv_state_wgrad,
        inner_bias_wgrad,
        state_bias_wgrad,
        step_bias_wgrad,
        decay_wgrad,
        skip_wgrad,
        mixer_gain_wgrad,
        mixout_wgrad,
        post_gain_part,
        gate_wgrad,
        up_wgrad,
        down_wgrad,
    )


CHUNK = 256
LANES = 128
VMEM_BYTES = 56 * 1024 * 1024


def dot_nn(left, right):
    return lax.dot_general(left, right, (((1,), (0,)), ((), ())), preferred_element_type=jnp.float32)


def dot_nt(left, right):
    return lax.dot_general(left, right, (((1,), (1,)), ((), ())), preferred_element_type=jnp.float32)


def dot_tn(left, right):
    return lax.dot_general(left, right, (((0,), (0,)), ((), ())), preferred_element_type=jnp.float32)


def split_two(value):
    high = value.astype(jnp.bfloat16)
    return high, (value - high.astype(jnp.float32)).astype(jnp.bfloat16)


def exact_nn(ones, value):
    high, low = split_two(value)
    return dot_nn(ones, high) + dot_nn(ones, low)


def grid_of(shape):
    return (
        lax.broadcasted_iota(jnp.int32, shape, 0),
        lax.broadcasted_iota(jnp.int32, shape, 1),
    )


def pick(columns, pair):
    rows = columns.shape[0]
    left = jnp.broadcast_to(columns[:, 2 * pair : 2 * pair + 1], (rows, LANES))
    right = jnp.broadcast_to(columns[:, 2 * pair + 1 : 2 * pair + 2], (rows, LANES))
    return jnp.where(grid_of((rows, LANES))[1] < P_SIZE, left, right)


def scan_terms(step, rate, aux):
    row, col = grid_of((CHUNK, CHUNK))
    lower = (row >= col).astype(jnp.bfloat16)
    cumulative = exact_nn(lower, step * rate)
    last = cumulative[CHUNK - 1 : CHUNK]
    enter = jnp.exp(cumulative) * aux[:, 1:2]
    leave = jnp.exp(last - cumulative) * aux[:, 2:3]
    across = jnp.exp(last) * aux[CHUNK - 1 : CHUNK, 1:2]
    return cumulative, enter, leave, across


def scan_kernel(step_ref, coef_ref, act_ref, aux_ref, seg_ref, rate_ref, core_ref, kept_ref, state, moved):
    @pl.when(pl.program_id(0) == 0)
    def _():
        state[...] = jnp.zeros_like(state)

    step = step_ref[...]
    aux = aux_ref[...]
    cumulative, enter, leave, across = scan_terms(step, rate_ref[...], aux)
    cum_rows = cumulative.T
    row, col = grid_of((CHUNK, CHUNK))
    blocked = jnp.where((row >= col) & (aux[:, 0:1] == seg_ref[...]), 0.0, NEG_FILL)
    coef_b = coef_ref[:, :NS]
    coef_c = coef_ref[:, NS:]
    coupling = dot_nt(coef_c, coef_b)
    low_state = state[...].astype(jnp.bfloat16)
    kept_ref[0] = low_state
    carried = dot_nn(coef_c, low_state)
    first = grid_of((CHUNK, LANES))[1] < P_SIZE
    for pair in range(act_ref.shape[1] // LANES):
        at = slice(pair * LANES, (pair + 1) * LANES)
        driven = (act_ref[:, at] * pick(step, pair)).astype(jnp.bfloat16)
        parts = []
        for head in (2 * pair, 2 * pair + 1):
            decay = jnp.exp(cumulative[:, head : head + 1] - cum_rows[head : head + 1] + blocked)
            parts.append(dot_nn((coupling * decay).astype(jnp.bfloat16), driven))
        core_ref[:, at] = jnp.where(first, parts[0], parts[1]) + carried[:, at] * pick(enter, pair)
        moved[:, at] = (driven.astype(jnp.float32) * pick(leave, pair)).astype(jnp.bfloat16)
    fresh = dot_tn(coef_b, moved[...])
    for pair in range(act_ref.shape[1] // LANES):
        at = slice(pair * LANES, (pair + 1) * LANES)
        state[:, at] = state[:, at] * pick(across, pair) + fresh[:, at]


def scan_call(step, coef, act, aux, seg_row, rate):
    rows, width = act.shape
    chunks = rows // CHUNK
    by_chunk = lambda columns: pl.BlockSpec((CHUNK, columns), lambda i: (i, 0))
    return pl.pallas_call(
        scan_kernel,
        grid=(chunks,),
        in_specs=[
            by_chunk(LANES),
            by_chunk(2 * NS),
            by_chunk(width),
            by_chunk(LANES),
            pl.BlockSpec((1, CHUNK), lambda i: (0, i)),
            pl.BlockSpec((1, LANES), lambda i: (0, 0)),
        ],
        out_specs=[by_chunk(width), pl.BlockSpec((1, NS, width), lambda i: (i, 0, 0))],
        out_shape=[
            jax.ShapeDtypeStruct((rows, width), jnp.float32),
            jax.ShapeDtypeStruct((chunks, NS, width), jnp.bfloat16),
        ],
        scratch_shapes=[
            pltpu.VMEM((NS, width), jnp.float32),
            pltpu.VMEM((CHUNK, width), jnp.bfloat16),
        ],
        compiler_params=pltpu.CompilerParams(vmem_limit_bytes=VMEM_BYTES),
        name="scan_forward",
    )(step, coef, act, aux, seg_row, rate)


def scan_back_kernel(
    step_ref,
    coef_ref,
    act_ref,
    aux_ref,
    seg_ref,
    rate_ref,
    skip_ref,
    grad_ref,
    kept_ref,
    act_grad_ref,
    step_grad_ref,
    coef_grad_ref,
    sums_ref,
    skip_sum_ref,
    state_grad,
    moved,
    entered,
    row_sums,
):
    @pl.when(pl.program_id(0) == 0)
    def _():
        state_grad[...] = jnp.zeros_like(state_grad)
        sums_ref[...] = jnp.zeros_like(sums_ref)
        skip_sum_ref[...] = jnp.zeros_like(skip_sum_ref)
        row_sums[...] = jnp.zeros_like(row_sums)

    step = step_ref[...]
    aux = aux_ref[...]
    rate = rate_ref[...]
    cumulative, enter, leave, across = scan_terms(step, rate, aux)
    cum_rows = cumulative.T
    row, col = grid_of((CHUNK, CHUNK))
    blocked = jnp.where((row <= col) & (aux[:, 0:1] == seg_ref[...]), 0.0, NEG_FILL)
    coef_b = coef_ref[:, :NS]
    coef_c = coef_ref[:, NS:]
    coupling = dot_nt(coef_b, coef_c)
    low_state = kept_ref[0]
    carried = dot_nn(coef_c, low_state)
    low_grad = state_grad[...].astype(jnp.bfloat16)
    returned = dot_nn(coef_b, low_grad)
    product = jnp.sum(low_state.astype(jnp.float32) * low_grad.astype(jnp.float32), 0, keepdims=True)
    lane = grid_of((CHUNK, LANES))[1]
    lane_row = grid_of((1, LANES))[1]
    first = lane < P_SIZE
    later = jnp.zeros((CHUNK, LANES), jnp.float32)
    earlier = jnp.zeros((CHUNK, LANES), jnp.float32)
    direct = jnp.zeros((CHUNK, LANES), jnp.float32)
    through = jnp.zeros((1, LANES), jnp.float32)
    coupling_grad = jnp.zeros((CHUNK, CHUNK), jnp.float32)
    for pair in range(act_ref.shape[1] // LANES):
        at = slice(pair * LANES, (pair + 1) * LANES)
        act = act_ref[:, at]
        spread_step = pick(step, pair)
        driven = (act * spread_step).astype(jnp.bfloat16)
        grad = grad_ref[:, at]
        core_grad = grad.astype(jnp.bfloat16)
        core_wide = core_grad.astype(jnp.float32)
        enter_grad = core_wide * pick(enter, pair)
        entered[:, at] = enter_grad.astype(jnp.bfloat16)
        row_part = enter_grad * carried[:, at]
        leave_pair = pick(leave, pair)
        moved[:, at] = (driven.astype(jnp.float32) * leave_pair).astype(jnp.bfloat16)
        back = returned[:, at] * leave_pair
        col_part = back * driven.astype(jnp.float32)
        parts = []
        for head in (2 * pair, 2 * pair + 1):
            mine = first if head % 2 == 0 else ~first
            decay = jnp.exp(cum_rows[head : head + 1] - cumulative[:, head : head + 1] + blocked)
            mix_grad = dot_nt(jnp.where(mine, driven, jnp.zeros_like(driven)), core_grad)
            share = mix_grad * decay
            coupling_grad = coupling_grad + share
            spread = share * coupling
            row_sums[head : head + 1] = jnp.sum(spread, 0, keepdims=True)
            folded = sum(spread[:, k * LANES : (k + 1) * LANES] for k in range(CHUNK // LANES))
            found = jnp.sum(jnp.where(mine, row_part, 0.0) - folded, 1, keepdims=True)
            later = jnp.where(lane == head, found, later)
            parts.append(dot_nn((coupling * decay).astype(jnp.bfloat16), core_grad))
            found = jnp.sum(jnp.where(mine, col_part, 0.0), 1, keepdims=True)
            earlier = jnp.where(lane == head, found, earlier)
        driven_grad = jnp.where(first, parts[0], parts[1]) + back
        act_grad_ref[:, at] = driven_grad * spread_step + grad * skip_ref[:, at]
        skip_sum_ref[:, at] += jnp.sum(grad * act, 0, keepdims=True)
        step_part = driven_grad * act
        product_pair = product[:, at]
        for head in (2 * pair, 2 * pair + 1):
            mine = first if head % 2 == 0 else ~first
            found = jnp.sum(jnp.where(mine, step_part, 0.0), 1, keepdims=True)
            direct = jnp.where(lane == head, found, direct)
            found = jnp.sum(jnp.where(mine[:1], product_pair, 0.0), 1, keepdims=True)
            through = jnp.where(lane_row == head, found, through)
    upper = (row <= col).astype(jnp.bfloat16)
    below = (row > col).astype(jnp.bfloat16)
    high, low = split_two(row_sums[...])
    log_grad = (
        exact_nn(upper, later)
        + dot_nt(upper, high)
        + dot_nt(upper, low)
        + exact_nn(below, earlier)
        + through * across
    )
    step_grad_ref[...] = direct + log_grad * rate
    sums_ref[...] += jnp.sum(log_grad * step, 0, keepdims=True)
    low_coupling = coupling_grad.astype(jnp.bfloat16)
    coef_grad_ref[:, :NS] = dot_nn(low_coupling, coef_c) + dot_nt(moved[...], low_grad)
    coef_grad_ref[:, NS:] = dot_tn(low_coupling, coef_b) + dot_nt(entered[...], low_state)
    fresh = dot_tn(coef_c, entered[...])
    for pair in range(act_ref.shape[1] // LANES):
        at = slice(pair * LANES, (pair + 1) * LANES)
        state_grad[:, at] = state_grad[:, at] * pick(across, pair) + fresh[:, at]


def scan_back_call(step, coef, act, aux, seg_row, rate, skip_row, grad, kept):
    rows, width = act.shape
    chunks = rows // CHUNK
    by_chunk = lambda columns: pl.BlockSpec((CHUNK, columns), lambda i: (chunks - 1 - i, 0))
    one_row = lambda columns: pl.BlockSpec((1, columns), lambda i: (0, 0))
    return pl.pallas_call(
        scan_back_kernel,
        grid=(chunks,),
        in_specs=[
            by_chunk(LANES),
            by_chunk(2 * NS),
            by_chunk(width),
            by_chunk(LANES),
            pl.BlockSpec((1, CHUNK), lambda i: (0, chunks - 1 - i)),
            one_row(LANES),
            one_row(width),
            by_chunk(width),
            pl.BlockSpec((1, NS, width), lambda i: (chunks - 1 - i, 0, 0)),
        ],
        out_specs=[
            by_chunk(width),
            by_chunk(LANES),
            by_chunk(2 * NS),
            one_row(LANES),
            one_row(width),
        ],
        out_shape=[
            jax.ShapeDtypeStruct((rows, width), jnp.float32),
            jax.ShapeDtypeStruct((rows, LANES), jnp.float32),
            jax.ShapeDtypeStruct((rows, 2 * NS), jnp.float32),
            jax.ShapeDtypeStruct((1, LANES), jnp.float32),
            jax.ShapeDtypeStruct((1, width), jnp.float32),
        ],
        scratch_shapes=[
            pltpu.VMEM((NS, width), jnp.float32),
            pltpu.VMEM((CHUNK, width), jnp.bfloat16),
            pltpu.VMEM((CHUNK, width), jnp.bfloat16),
            pltpu.VMEM((LANES, CHUNK), jnp.float32),
        ],
        compiler_params=pltpu.CompilerParams(vmem_limit_bytes=VMEM_BYTES),
        name="scan_backward",
    )(step, coef, act, aux, seg_row, rate, skip_row, grad, kept)


def swap_halves(value):
    width = value.shape[1]
    half = HEAD_SIZE // 2
    up = pltpu.roll(value, width - half, 1)
    down = pltpu.roll(value, half, 1)
    return jnp.where(grid_of(value.shape)[1] % HEAD_SIZE < half, up, down)


def turned(value, cosine, sine):
    return value * cosine + swap_halves(value) * sine


def attend_kernel(query_ref, keyval_ref, seg_ref, seg_col_ref, cos_ref, sin_ref, out_ref, turned_ref, both_ref, log_ref):
    rows = query_ref.shape[0]
    first = grid_of((rows, LANES))[1] < HEAD_SIZE
    keyval = keyval_ref[...]
    moved = pltpu.roll(keyval, HEAD_SIZE, 1)
    keys = turned(jnp.where(first, keyval, moved), cos_ref[...], sin_ref[...]).astype(jnp.bfloat16)
    values = jnp.where(first, moved, keyval).astype(jnp.bfloat16)
    both_ref[:, :LANES] = keys
    both_ref[:, LANES:] = values
    scale = HEAD_SIZE ** (-0.5)
    head_lane = grid_of((CHUNK, LANES))[1]
    first = head_lane < HEAD_SIZE
    for block in range(rows // CHUNK):
        low, high = block * CHUNK, (block + 1) * CHUNK
        row, col = grid_of((CHUNK, high))
        blocked = jnp.where(
            (row + low >= col) & (seg_col_ref[low:high, 0:1] == seg_ref[:, :high]), 0.0, NEG_FILL
        )
        logs = jnp.zeros((CHUNK, LANES), jnp.float32)
        for pair in range(query_ref.shape[1] // LANES):
            at = slice(pair * LANES, (pair + 1) * LANES)
            query = turned(query_ref[low:high, at], cos_ref[low:high], sin_ref[low:high]).astype(
                jnp.bfloat16
            )
            turned_ref[low:high, at] = query
            parts = []
            for head in (2 * pair, 2 * pair + 1):
                mine = first if head % 2 == 0 else ~first
                scores = (
                    dot_nt(jnp.where(mine, query, jnp.zeros_like(query)), keys[:high]) * scale
                    + blocked
                )
                top = jnp.max(scores, 1, keepdims=True)
                weights = jnp.exp(scores - top)
                total = jnp.sum(weights, 1, keepdims=True)
                probs = (weights * (1.0 / total)).astype(jnp.bfloat16)
                parts.append(dot_nn(probs, values[:high]))
                logs = jnp.where(head_lane == head, top + jnp.log(total), logs)
            out_ref[low:high, at] = jnp.where(first, parts[0], parts[1]).astype(jnp.bfloat16)
        log_ref[low:high] = logs


def attend_call(query, keyval, seg_row, aux, cosine, sine):
    rows, width = query.shape
    return pl.pallas_call(
        attend_kernel,
        out_shape=[
            jax.ShapeDtypeStruct((rows, width), jnp.bfloat16),
            jax.ShapeDtypeStruct((rows, width), jnp.bfloat16),
            jax.ShapeDtypeStruct((rows, 2 * LANES), jnp.bfloat16),
            jax.ShapeDtypeStruct((rows, LANES), jnp.float32),
        ],
        compiler_params=pltpu.CompilerParams(vmem_limit_bytes=VMEM_BYTES),
        name="attend_forward",
    )(query, keyval, seg_row, aux, cosine, sine)


def attend_back_kernel(
    query_ref, both_ref, seg_ref, seg_col_ref, cos_ref, sin_ref, log_ref, out_ref, grad_ref,
    query_grad_ref, keyval_grad_ref, key_sum, value_sum,
):
    rows = query_ref.shape[0]
    key_sum[...] = jnp.zeros_like(key_sum)
    value_sum[...] = jnp.zeros_like(value_sum)
    scale = HEAD_SIZE ** (-0.5)
    first = grid_of((CHUNK, LANES))[1] < HEAD_SIZE
    for block in range(rows // CHUNK):
        low, high = block * CHUNK, (block + 1) * CHUNK
        row, col = grid_of((CHUNK, high))
        blocked = jnp.where(
            (row + low >= col) & (seg_col_ref[low:high, 0:1] == seg_ref[:, :high]), 0.0, NEG_FILL
        )
        keys = both_ref[:high, :LANES]
        values = both_ref[:high, LANES:]
        for pair in range(query_ref.shape[1] // LANES):
            at = slice(pair * LANES, (pair + 1) * LANES)
            query = query_ref[low:high, at]
            grad = grad_ref[low:high, at]
            inner = grad.astype(jnp.float32) * out_ref[low:high, at].astype(jnp.float32)
            parts = []
            key_part = None
            for head in (2 * pair, 2 * pair + 1):
                mine = first if head % 2 == 0 else ~first
                query_mine = jnp.where(mine, query, jnp.zeros_like(query))
                grad_mine = jnp.where(mine, grad, jnp.zeros_like(grad))
                scores = dot_nt(query_mine, keys) * scale + blocked
                probs = jnp.exp(scores - log_ref[low:high, head : head + 1])
                delta = jnp.sum(jnp.where(mine, inner, 0.0), 1, keepdims=True)
                prob_grad = dot_nt(grad_mine, values)
                score_grad = (probs * (prob_grad - delta)).astype(jnp.bfloat16)
                parts.append(dot_nn(score_grad, keys) * scale)
                key_sum[:high] += dot_tn(score_grad, query_mine)
                value_sum[:high] += dot_tn(probs.astype(jnp.bfloat16), grad_mine)
            full = jnp.where(first, parts[0], parts[1])
            query_grad_ref[low:high, at] = turned(full, cos_ref[low:high], -sin_ref[low:high]).astype(
                jnp.bfloat16
            )
    wide = grid_of((rows, LANES))[1] < HEAD_SIZE
    key_total = key_sum[...] * scale
    key_total = key_total + pltpu.roll(key_total, HEAD_SIZE, 1)
    key_total = turned(key_total, cos_ref[...], -sin_ref[...])
    value_total = value_sum[...]
    value_total = value_total + pltpu.roll(value_total, HEAD_SIZE, 1)
    keyval_grad_ref[...] = jnp.where(wide, key_total, value_total).astype(jnp.bfloat16)


def attend_back_call(query, both, seg_row, aux, cosine, sine, logs, out, grad):
    rows, width = query.shape
    return pl.pallas_call(
        attend_back_kernel,
        out_shape=[
            jax.ShapeDtypeStruct((rows, width), jnp.bfloat16),
            jax.ShapeDtypeStruct((rows, LANES), jnp.bfloat16),
        ],
        scratch_shapes=[
            pltpu.VMEM((rows, LANES), jnp.float32),
            pltpu.VMEM((rows, LANES), jnp.float32),
        ],
        compiler_params=pltpu.CompilerParams(vmem_limit_bytes=VMEM_BYTES),
        name="attend_backward",
    )(query, both, seg_row, aux, cosine, sine, logs, out, grad)


def halve(value, bit):
    half = value.shape[0] // 2
    upper = (lax.axis_index("dp") & bit) != 0
    got = swap_bit(jnp.where(upper, value[:half], value[half:]), bit)
    kept = jnp.where(upper, value[half:], value[:half])
    return (kept.astype(jnp.float32) + got.astype(jnp.float32)).astype(value.dtype)


def double(value, bit):
    upper = (lax.axis_index("dp") & bit) != 0
    got = swap_bit(value, bit)
    return jnp.concatenate([jnp.where(upper, got, value), jnp.where(upper, value, got)], 0)


def dp_bits():
    size = lax.axis_size("dp")
    return [1 << i for i in range(size.bit_length() - 1)]


def halve_parts(values, bit):
    half = values[0].shape[0] // 2
    upper = (lax.axis_index("dp") & bit) != 0
    got = swap_bit(
        jnp.concatenate([jnp.where(upper, v[:half], v[half:]) for v in values], 1), bit
    )
    kept = jnp.concatenate([jnp.where(upper, v[half:], v[:half]) for v in values], 1)
    return (kept.astype(jnp.float32) + got.astype(jnp.float32)).astype(got.dtype)


def by_rows(value):
    return with_layout_constraint(value, Layout(major_to_minor=(0, 1)))


def swap_pair(value):
    return lax.ppermute(value, "tensor", [(0, 1), (1, 0)])


def tie(*values):
    return lax.optimization_barrier(values)


def conv_rows(value, kernel, bias, keeps):
    taps = kernel.shape[0]
    total = bias.astype(jnp.float32)[None]
    for tap in range(taps):
        offset = taps - 1 - tap
        moved = jnp.pad(value, ((offset, 0), (0, 0)))[: value.shape[0]]
        total = total + kernel[tap].astype(jnp.float32) * moved * keeps[offset]
    return total


def conv_sums(grad, value, taps, keeps):
    sums = []
    for tap in range(taps):
        offset = taps - 1 - tap
        moved = jnp.pad(value, ((offset, 0), (0, 0)))[: value.shape[0]]
        sums.append(jnp.sum(grad * keeps[offset] * moved, 0, keepdims=True))
    return sums


def conv_grad(grad, kernel, keeps):
    taps = kernel.shape[0]
    total = jnp.zeros_like(grad)
    for tap in range(taps):
        offset = taps - 1 - tap
        moved = jnp.pad(grad * keeps[offset], ((0, offset), (0, 0)))[offset:]
        total = total + kernel[tap].astype(jnp.float32) * moved
    return total


def product_kernel(*refs):
    left_pairs, right_pairs = [refs[0:2], refs[2:4], refs[2:4]], [(), refs[4:6], refs[6:8]]
    cotangent_ref, out_ref = refs[8], refs[9]
    half = refs[0].shape[0]
    for which in range(3):
        total = None
        for k in range(2):
            left = left_pairs[which][k][...]
            if which == 0:
                right = cotangent_ref[k * half : (k + 1) * half]
            else:
                right = right_pairs[which][k][...]
            part = dot_tn(left, right)
            total = part if total is None else total + part
        out_ref[which] = total.astype(out_ref.dtype)


def product_call(hidden_a, hidden_b, post_a, post_b, gate_a, gate_b, up_a, up_b, cotangent):
    half, model = post_a.shape
    hidden = hidden_a.shape[1]
    columns = pl.BlockSpec((half, CHUNK), lambda i: (0, i))
    whole = pl.BlockSpec((half, hidden), lambda i: (0, 0))
    return pl.pallas_call(
        product_kernel,
        grid=(hidden // CHUNK,),
        in_specs=[columns] * 4 + [whole] * 4 + [pl.BlockSpec((2 * half, model), lambda i: (0, 0))],
        out_specs=pl.BlockSpec((3, CHUNK, model), lambda i: (0, i, 0)),
        out_shape=jax.ShapeDtypeStruct((3, hidden, model), jnp.bfloat16),
        compiler_params=pltpu.CompilerParams(vmem_limit_bytes=VMEM_BYTES),
        name="weight_products",
    )(hidden_a, hidden_b, post_a, post_b, gate_a, gate_b, up_a, up_b, cotangent)


def local_fast(
    tokens,
    segments,
    cotangent,
    input_gain,
    query_weight,
    key_value_weight,
    attnout_weight,
    gating_weight,
    inner_weight,
    state_weight,
    step_weight,
    conv_inner,
    conv_state,
    inner_bias,
    state_bias,
    step_bias,
    decay_log,
    skip_scale,
    mixer_gain,
    mixer_out,
    post_gain,
    gate_weight,
    up_weight,
    down_weight,
):
    low, wide = jnp.bfloat16, jnp.float32
    rows, model = tokens.shape
    heads = query_weight.shape[1] // HEAD_SIZE
    ssm_heads = step_weight.shape[1]
    ssm_width = ssm_heads * P_SIZE
    query_width = heads * HEAD_SIZE
    first_device = lax.axis_index("tensor") == 0
    pick_head = lambda at: jnp.where(
        first_device,
        key_value_weight[:, at : at + HEAD_SIZE],
        key_value_weight[:, at + HEAD_SIZE : at + 2 * HEAD_SIZE],
    )
    keyval_weight = jnp.concatenate([pick_head(0), pick_head(KEYVALUE_HEADS * HEAD_SIZE)], 1)
    lane_pad = ((0, 0), (0, LANES - ssm_heads))
    step_weight_wide = jnp.pad(step_weight, lane_pad)
    step_bias_wide = jnp.pad(step_bias.astype(wide)[None], lane_pad)
    rate = -jnp.exp(decay_log.astype(wide))
    rate_wide = jnp.pad(rate[None], lane_pad)
    skip_row = jnp.repeat(skip_scale.astype(wide), P_SIZE)[None]
    cosine, sine = rotary_tables(rows)
    cosine = jnp.concatenate([cosine] * 4, 1)
    sine = jnp.concatenate([-sine, sine, -sine, sine], 1)
    seg_row = segments.astype(wide)
    seg_chunks = seg_row.reshape(-1, CHUNK)
    ends = seg_chunks[:, -1:]
    starts = jnp.concatenate([jnp.full((1, 1), -1.0, wide), ends[:-1]], 0)
    aux = jnp.stack(
        [seg_chunks, (seg_chunks == starts).astype(wide), (seg_chunks == ends).astype(wide)], -1
    ).reshape(rows, 3)
    aux = jnp.pad(aux, ((0, 0), (0, LANES - 3)))
    keeps = [seg_keep(segments, offset)[0] for offset in range(conv_inner.shape[0])]

    inputs = by_rows(tokens.astype(wide))
    inv_first = lax.rsqrt(jnp.mean(inputs * inputs, -1, keepdims=True) + EPS)
    unit_first = inputs * inv_first
    in_gain = input_gain.astype(wide)
    normed = by_rows((unit_first * in_gain).astype(low))
    inner = matmul(normed, inner_weight)
    state_in = matmul(normed, state_weight)
    step_arg = matmul(normed, step_weight_wide) + step_bias_wide
    gating = matmul(normed, gating_weight)
    inner_pre = conv_rows(inner, conv_inner, inner_bias, keeps)
    inner_act = jax.nn.silu(inner_pre)
    state_pre = conv_rows(state_in, conv_state, state_bias, keeps)
    coef = jax.nn.silu(state_pre).astype(low)
    step = jax.nn.softplus(step_arg)
    core, kept = scan_call(step, coef, inner_act, aux, seg_row, rate_wide)
    ssm_out = core + skip_row * inner_act
    sigma_gate = jax.nn.sigmoid(gating)
    gate_act = gating * sigma_gate
    gated = ssm_out * gate_act
    square_sum = pair_sum(jnp.sum(gated * gated, -1))[:, None]
    query_pre = matmul(normed, query_weight)
    keyval_pre = matmul(normed, keyval_weight)
    attended, queries, both, logs = attend_call(query_pre, keyval_pre, seg_row, aux, cosine, sine)
    attn_part = matmul(attended, attnout_weight)
    inv_gate = lax.rsqrt(square_sum / DSSM + EPS)
    mixer_scale = mixer_gain.astype(wide)
    mixed = (gated * inv_gate * mixer_scale).astype(low)
    branch_part = attn_part + matmul(mixed, mixer_out)
    out_gain = post_gain.astype(wide)
    branch_part = by_rows(branch_part.astype(low))
    half = rows // 2
    spans = [slice(0, half), slice(half, rows)]
    sent = [branch_part[span] for span in spans]
    got = [swap_pair(piece) for piece in sent]
    weight_cat = jnp.concatenate(
        [gating_weight, inner_weight, step_weight_wide, state_weight, query_weight, keyval_weight], 1
    )
    got[0], weight_cat = tie(got[0], weight_cat)
    found = []
    for at, span in enumerate(spans):
        middle = inputs[span] + by_rows(sent[at].astype(wide) + got[at].astype(wide))
        inv_second = lax.rsqrt(jnp.mean(middle * middle, -1, keepdims=True) + EPS)
        unit_second = middle * inv_second
        post = by_rows((unit_second * out_gain).astype(low))
        gate = matmul(post, gate_weight)
        upward = matmul(post, up_weight)
        sigma = jax.nn.sigmoid(gate)
        hidden = (gate * sigma * upward).astype(low)
        hidden_grad = dot_nt(cotangent[span], down_weight)
        up_act_grad = (hidden_grad * gate * sigma).astype(low)
        gate_act_grad = (hidden_grad * upward * sigma * (1.0 + gate * (1.0 - sigma))).astype(low)
        post_part = dot_nt(gate_act_grad, gate_weight) + dot_nt(up_act_grad, up_weight)
        gain_part = jnp.sum(post_part * unit_second, 0, keepdims=True)
        post_low = by_rows(post_part.astype(low))
        if at == 0:
            got[1], post_low = tie(got[1], post_low)
        else:
            got[0], post_low = tie(got[0], post_low)
        post_got = swap_pair(post_low)
        found.append(
            (post_low, unit_second, inv_second, gain_part, hidden, post, gate_act_grad, up_act_grad)
        )
        got[at] = post_got
    post_gain_part = found[0][3] + found[1][3]
    forward_part = product_call(
        *[piece for k in range(4, 8) for piece in (found[0][k], found[1][k])], cotangent
    )
    got[1], _ = tie(got[1], forward_part)
    forward_piece = lax.psum_scatter(
        forward_part.reshape(-1, model), "dp", scatter_dimension=0, tiled=True
    )
    middle_grads = []
    for span, part, other in zip(spans, found, got):
        post_low, unit_second, inv_second = part[:3]
        post_full = by_rows(post_low.astype(wide) + other.astype(wide))
        scaled_post = post_full * out_gain
        middle_grads.append(
            cotangent[span].astype(wide)
            + inv_second
            * (scaled_post - unit_second * jnp.mean(scaled_post * unit_second, -1, keepdims=True))
        )
    branch_grad = by_rows(jnp.concatenate([grad.astype(low) for grad in middle_grads], 0))
    middle_grad = jnp.concatenate(middle_grads, 0)
    mixed_grad = dot_nt(branch_grad, mixer_out)
    mixer_gain_part = jnp.sum(mixed_grad * gated * inv_gate, 0, keepdims=True)
    weighted = mixed_grad * mixer_scale
    cross = pair_sum(jnp.sum(weighted * gated, -1))[:, None]
    out_part = dot_tn(jnp.concatenate([attended, mixed], 1), branch_grad).astype(low)
    out_part = by_rows(out_part)
    attended_grad = dot_nt(branch_grad, attnout_weight).astype(low)
    gated_grad = inv_gate * weighted - gated * (inv_gate * inv_gate * inv_gate) * cross / DSSM
    ssm_grad = gated_grad * gate_act
    gating_grad = (
        gated_grad * ssm_out * sigma_gate * (1.0 + gating * (1.0 - sigma_gate))
    ).astype(low)
    gating_part = by_rows(dot_tn(normed, gating_grad).astype(low))
    bits = dp_bits()
    early = halve_parts([out_part, gating_part], bits[0])
    early, ssm_grad = tie(early, ssm_grad)
    early = halve(early, bits[1])
    act_grad, step_grad, coef_grad, rate_sum, skip_sum = scan_back_call(
        step, coef, inner_act, aux, seg_row, rate_wide, skip_row, ssm_grad, kept
    )
    early, act_grad, step_grad, coef_grad, forward_piece = tie(
        early, act_grad, step_grad, coef_grad, forward_piece
    )
    forward_total = lax.all_gather(forward_piece, "dp", axis=0, tiled=True)
    early = halve(early, bits[2])
    step_total = step_grad * jax.nn.sigmoid(step_arg)
    taps = conv_inner.shape[0]
    inner_pre_grad = act_grad * silu_slope(inner_pre)
    conv_inner_sums = conv_sums(inner_pre_grad, inner, taps, keeps)
    inner_bias_part = jnp.sum(inner_pre_grad, 0, keepdims=True)
    state_pre_grad = coef_grad * silu_slope(state_pre)
    conv_state_sums = conv_sums(state_pre_grad, state_in, taps, keeps)
    state_bias_part = jnp.sum(state_pre_grad, 0, keepdims=True)
    early, act_grad, coef_grad, *sums = tie(
        early, act_grad, coef_grad, inner_bias_part, state_bias_part, *conv_inner_sums, *conv_state_sums
    )
    inner_bias_part, state_bias_part = sums[:2]
    conv_inner_sums, conv_state_sums = sums[2 : 2 + taps], sums[2 + taps :]
    early = halve(early, bits[3])
    inner_grad = conv_grad(act_grad * silu_slope(inner_pre), conv_inner, keeps)
    state_grad = conv_grad(coef_grad * silu_slope(state_pre), conv_state, keeps)
    scan_cat = jnp.concatenate(
        [inner_grad.astype(low), step_total.astype(low), state_grad.astype(low)], 1
    )
    scan_part = dot_tn(normed, scan_cat).astype(low)
    early, scan_part, attended_grad = tie(early, scan_part, attended_grad)
    early = double(early, bits[3])
    scan_part = halve(scan_part, bits[0])
    query_grad, keyval_grad = attend_back_call(
        queries, both, seg_row, aux, cosine, sine, logs, attended, attended_grad
    )
    attend_cat = jnp.concatenate([query_grad, keyval_grad], 1)
    attend_part = dot_tn(normed, attend_cat).astype(low)
    early, scan_part, attend_part, attend_cat = tie(early, scan_part, attend_part, attend_cat)
    early = double(early, bits[2])
    scan_part = halve(scan_part, bits[1])
    attend_part = halve(attend_part, bits[0])
    normed_part = dot_nt(jnp.concatenate([gating_grad, scan_cat, attend_cat], 1), weight_cat)
    input_gain_part = jnp.sum(normed_part * unit_first, 0, keepdims=True)
    early, scan_part, attend_part, normed_part, input_gain_part = tie(
        early, scan_part, attend_part, normed_part, input_gain_part
    )
    normed_low = by_rows(normed_part.astype(low))
    quarter = rows // 4
    normed_first = swap_pair(normed_low[:quarter])
    own_rows = [
        *conv_inner_sums,
        inner_bias_part,
        mixer_gain_part,
        skip_sum,
        jnp.sum(step_total, 0, keepdims=True),
        rate_sum * rate_wide,
    ]
    shared_rows = [
        input_gain_part,
        post_gain_part,
        *conv_state_sums,
        state_bias_part,
    ]
    small = jnp.concatenate(
        [jnp.pad(row, ((0, 0), (0, model - row.shape[1]))) for row in own_rows + shared_rows], 0
    )
    small = small + swap_bit(small, bits[0])
    early = double(early, bits[1])
    scan_part = halve(scan_part, bits[2])
    attend_part = halve(attend_part, bits[1])
    scan_part, attend_part, small, normed_first, normed_low = tie(
        scan_part, attend_part, small, normed_first, normed_low
    )
    normed_second = swap_pair(normed_low[quarter:half])
    scan_part = halve(scan_part, bits[3])
    attend_part = halve(attend_part, bits[2])
    small = small + swap_bit(small, bits[1])
    scan_part, attend_part, small, normed_second = tie(
        scan_part, attend_part, small, normed_second
    )
    attend_part = halve(attend_part, bits[3])
    small = small + swap_bit(small, bits[2])
    attend_part, small, early = tie(attend_part, small, early)
    small = small + swap_bit(small, bits[3])
    scan_piece, attend_piece = scan_part, attend_part
    state_at = ssm_width + LANES
    trade = jnp.concatenate([scan_piece[:, state_at:], attend_piece[:, query_width:]], 1)
    other = swap_pair(trade)
    other, normed_rest = tie(other, normed_low[half:])
    normed_got = [normed_first, normed_second, swap_pair(normed_rest)]
    state_cols = state_weight.shape[1]
    state_piece = (
        trade[:, :state_cols].astype(wide) + other[:, :state_cols].astype(wide)
    ).astype(low)
    mine, theirs = trade[:, state_cols:], other[:, state_cols:]
    head_0 = jnp.where(first_device, mine, theirs)
    head_1 = jnp.where(first_device, theirs, mine)
    late = jnp.concatenate(
        [
            scan_piece[:, :state_at],
            state_piece,
            attend_piece[:, :query_width],
            head_0[:, :HEAD_SIZE],
            head_1[:, :HEAD_SIZE],
            head_0[:, HEAD_SIZE:],
            head_1[:, HEAD_SIZE:],
        ],
        1,
    )
    late, small, early = tie(late, small, early)
    early = double(early, bits[0])
    late = double(late, bits[3])
    small_other = lax.ppermute(small, "tensor", [(0, 1), (1, 0)])
    is_shared = lax.broadcasted_iota(jnp.int32, small.shape, 0) >= len(own_rows)
    small = small + jnp.where(is_shared, small_other, 0.0)
    late, early = tie(late, early)
    late = double(late, bits[2])
    late, forward_total = tie(late, forward_total)
    hidden_units = down_weight.shape[0]
    down_wgrad = forward_total[:hidden_units].astype(wide)
    gate_wgrad = forward_total[hidden_units : hidden_units + model].astype(wide)
    up_wgrad = forward_total[hidden_units + model :].astype(wide)
    late = double(late, bits[1])
    early_grads = (
        gate_wgrad,
        up_wgrad,
        down_wgrad,
        early[:query_width, :model].astype(wide),
        early[:, model:].astype(wide),
        early[query_width:, :model].astype(wide),
    )
    normed_full = by_rows(normed_low.astype(wide) + jnp.concatenate(normed_got, 0).astype(wide))
    scaled_in = normed_full * in_gain
    tokens_grad = middle_grad + inv_first * (
        scaled_in - unit_first * jnp.mean(scaled_in * unit_first, -1, keepdims=True)
    )
    late, tokens_grad, *early_grads = tie(late, tokens_grad, *early_grads)
    late = double(late, bits[0])
    scan_total = late[:, : state_at + state_cols]
    attend_total = late[:, state_at + state_cols :]
    gate_wgrad, up_wgrad, down_wgrad, attnout_grad, gating_wgrad, mixout_grad = early_grads
    count = len(own_rows)
    return (
        tokens_grad,
        small[count],
        attend_total[:, :query_width].astype(wide),
        attend_total[:, query_width:].astype(wide),
        attnout_grad,
        gating_wgrad,
        scan_total[:, :ssm_width].astype(wide),
        scan_total[:, state_at:].astype(wide),
        scan_total[:, ssm_width : ssm_width + ssm_heads].astype(wide),
        small[:taps, :ssm_width],
        small[count + 2 : count + 2 + taps, :state_cols],
        small[taps, :ssm_width],
        small[count + 2 + taps, :state_cols],
        small[taps + 3, :ssm_heads],
        small[taps + 4, :ssm_heads],
        jnp.sum(small[taps + 2, :ssm_width].reshape(ssm_heads, P_SIZE), 1),
        small[taps + 1, :ssm_width],
        mixout_grad,
        small[count + 1],
        gate_wgrad,
        up_wgrad,
        down_wgrad,
    )


def layer(*arrays):
    tokens, segments, query_weight, step_weight = arrays[0], arrays[1], arrays[4], arrays[10]
    size = lax.axis_size("dp")
    fits = (
        lax.axis_size("tensor") == 2
        and size == 16
        and segments.shape[0] == 1
        and tokens.shape[0] % CHUNK == 0
        and tokens.shape[1] % (16 * size) == 0
        and query_weight.shape[1] == QUERY_HEADS // KEYVALUE_HEADS * HEAD_SIZE
        and KEYVALUE_HEADS == 2
        and arrays[23].shape[0] == tokens.shape[1]
        and step_weight.shape[1] % 2 == 0
        and query_weight.shape[1] + step_weight.shape[1] * P_SIZE == tokens.shape[1]
    )
    return local_fast(*arrays) if fits else local(*arrays)


def solution(mesh):
    placed = (
        P("dp", None),
        P("dp", None),
        P("dp", None),
        P(),
        P(None, "tensor"),
        P(),
        P("tensor", None),
        P(None, "tensor"),
        P(None, "tensor"),
        P(),
        P(None, "tensor"),
        P(None, "tensor"),
        P(),
        P("tensor"),
        P(),
        P("tensor"),
        P("tensor"),
        P("tensor"),
        P("tensor"),
        P("tensor", None),
        P(),
        P(None, "tensor"),
        P(None, "tensor"),
        P("tensor", None),
    )
    return jax.shard_map(
        layer,
        mesh=mesh,
        in_specs=placed,
        out_specs=(
            P("dp", None),
            P(),
            P(None, "tensor"),
            P(),
            P("tensor", None),
            P(None, "tensor"),
            P(None, "tensor"),
            P(),
            P(None, "tensor"),
            P(None, "tensor"),
            P(),
            P("tensor"),
            P(),
            P("tensor"),
            P("tensor"),
            P("tensor"),
            P("tensor"),
            P("tensor", None),
            P(),
            P(None, "tensor"),
            P(None, "tensor"),
            P("tensor", None),
        ),
        check_vma=False,
    )
```

```python
import jax
import jax.numpy as jnp
from jax import lax
from jax.experimental.layout import Layout, with_layout_constraint
from jax.experimental import pallas as pl
from jax.experimental.pallas import tpu as pltpu
from jax.sharding import PartitionSpec as P

QUERY_HEADS = 8
KEYVALUE_HEADS = 2
HEAD_SIZE = 64
P_SIZE = 64
NS = 128
DSSM = 1536


EPS = 1e-05
ROPE_BASE = 100000000000.0
NEG_FILL = -1e30


def matmul(left, right):
    return jnp.dot(left, right, preferred_element_type=jnp.float32)


def rotary_tables(document_length):
    half = HEAD_SIZE // 2
    freqs = jnp.exp(-jnp.log(ROPE_BASE) * (2.0 * jnp.arange(half, dtype=jnp.float32) / HEAD_SIZE))
    angles = jnp.arange(document_length, dtype=jnp.float32)[:, None] * freqs[None, :]
    return (jnp.cos(angles), jnp.sin(angles))


def rotate(value, cosine, sine):
    half = value.shape[-1] // 2
    first = value[..., :half]
    second = value[..., half:]
    return jnp.concatenate([first * cosine - second * sine, first * sine + second * cosine], -1)


def rotate_back(grad, cosine, sine):
    half = grad.shape[-1] // 2
    first = grad[..., :half]
    second = grad[..., half:]
    return jnp.concatenate([first * cosine + second * sine, second * cosine - first * sine], -1)


def silu_slope(value):
    sigma = jax.nn.sigmoid(value)
    return sigma * (1.0 + value * (1.0 - sigma))


def seg_keep(segments, offset):
    document_length = segments.shape[1]
    moved = jnp.pad(segments, ((0, 0), (offset, 0)), constant_values=-1)[:, :document_length]
    return (moved == segments).astype(jnp.float32)[:, :, None]


def move_down(value, offset):
    document_length = value.shape[1]
    return jnp.pad(value, ((0, 0), (offset, 0), (0, 0)))[:, :document_length]


def move_up(value, offset):
    return jnp.pad(value, ((0, 0), (0, offset), (0, 0)))[:, offset:]


def conv_forward(value, kernel, bias, segments):
    taps = kernel.shape[0]
    total = jnp.zeros_like(value) + bias.astype(jnp.float32)
    for tap in range(taps):
        offset = taps - 1 - tap
        total = total + kernel[tap].astype(jnp.float32) * move_down(value, offset) * seg_keep(
            segments, offset
        )
    return total


def conv_backward(grad, value, kernel, segments):
    taps = kernel.shape[0]
    grad_in = jnp.zeros_like(value)
    kernel_rows = []
    for tap in range(taps):
        offset = taps - 1 - tap
        masked = grad * seg_keep(segments, offset)
        kernel_rows.append(jnp.sum(masked * move_down(value, offset), axis=(0, 1)))
        grad_in = grad_in + kernel[tap].astype(jnp.float32) * move_up(masked, offset)
    return (grad_in, jnp.stack(kernel_rows))


def ssd_parts(step_block, rate, coef_b, coef_c, heads_block, allowed):
    coupling = jnp.einsum("tn,sn->ts", coef_c, coef_b, preferred_element_type=jnp.float32)
    cumulative = jnp.cumsum(step_block * rate, axis=0).T
    difference = cumulative[:, :, None] - cumulative[:, None, :]
    decay = jnp.where(allowed[None], jnp.exp(jnp.where(allowed[None], difference, 0.0)), 0.0)
    mixing = (coupling[None] * decay).astype(jnp.bfloat16)
    driven = (heads_block * step_block.T[:, :, None]).astype(jnp.bfloat16)
    return (coupling, decay, mixing, driven)


def pair_sum(value):
    if lax.axis_size("tensor") == 2:
        other = lax.ppermute(value, "tensor", [(0, 1), (1, 0)])
        return value.astype(jnp.float32) + other.astype(jnp.float32)
    return lax.psum(value, "tensor").astype(jnp.float32)


def swap_bit(value, bit):
    size = lax.axis_size("dp")
    return lax.ppermute(value, "dp", [(i, i ^ bit) for i in range(size)])


def shared_sum(rows, first_shared):
    tail = pair_sum(rows[:, first_shared:]).astype(rows.dtype)
    return jnp.concatenate([rows[:, :first_shared], tail], 1) if first_shared else tail


def tree_sum(value, first_shared=None):
    size = lax.axis_size("dp")
    rows = value.shape[0]
    if size & (size - 1) or rows % (16 * size):
        total = lax.psum(value, "dp")
        return total if first_shared is None else shared_sum(total, first_shared)
    bits = [1 << i for i in range(size.bit_length() - 1)]
    me = lax.axis_index("dp")
    for bit in bits:
        half = value.shape[0] // 2
        low, high = value[:half], value[half:]
        upper = (me & bit) != 0
        got = swap_bit(jnp.where(upper, low, high), bit)
        kept = jnp.where(upper, high, low)
        value = (kept.astype(jnp.float32) + got.astype(jnp.float32)).astype(value.dtype)
    if first_shared is not None:
        value = shared_sum(value, first_shared)
    for bit in reversed(bits):
        upper = (me & bit) != 0
        got = swap_bit(value, bit)
        value = jnp.where(
            upper, jnp.concatenate([got, value], 0), jnp.concatenate([value, got], 0)
        )
    return value


def local(
    tokens,
    segments,
    cotangent,
    input_gain,
    query_weight,
    key_value_weight,
    attnout_weight,
    gating_weight,
    inner_weight,
    state_weight,
    step_weight,
    conv_inner,
    conv_state,
    inner_bias,
    state_bias,
    step_bias,
    decay_log,
    skip_scale,
    mixer_gain,
    mixer_out,
    post_gain,
    gate_weight,
    up_weight,
    down_weight,
):
    seq_count, document_length = segments.shape
    rows = seq_count * document_length
    heads = query_weight.shape[1] // HEAD_SIZE
    ssm_heads = step_weight.shape[1]
    query_group = QUERY_HEADS // KEYVALUE_HEADS
    shared_key_head = lax.axis_index("tensor") * heads // query_group
    scale = HEAD_SIZE ** (-0.5)
    cosine, sine = rotary_tables(document_length)
    positions = jnp.arange(document_length)

    def allowed_of(seg_ids):
        return (positions[:, None] >= positions[None, :]) & (seg_ids[:, None] == seg_ids[None, :])

    inputs = tokens.astype(jnp.float32)
    inv_first = lax.rsqrt(jnp.mean(inputs * inputs, -1, keepdims=True) + EPS)
    unit_first = inputs * inv_first
    in_gain = input_gain.astype(jnp.float32)
    normed = (unit_first * in_gain).astype(jnp.bfloat16)
    key_cols = lax.dynamic_slice_in_dim(key_value_weight, shared_key_head * HEAD_SIZE, HEAD_SIZE, 1)
    value_columns = lax.dynamic_slice_in_dim(
        key_value_weight, (KEYVALUE_HEADS + shared_key_head) * HEAD_SIZE, HEAD_SIZE, 1
    )
    query_pre = matmul(normed, query_weight)
    key_pre = matmul(normed, key_cols)
    value_pre = matmul(normed, value_columns)
    queries = rotate(
        query_pre.reshape(seq_count, document_length, heads, HEAD_SIZE).transpose(0, 2, 1, 3),
        cosine,
        sine,
    ).astype(jnp.bfloat16)
    key_rows = rotate(key_pre.reshape(seq_count, document_length, HEAD_SIZE), cosine, sine).astype(
        jnp.bfloat16
    )
    value_rows = value_pre.reshape(seq_count, document_length, HEAD_SIZE).astype(jnp.bfloat16)

    def attend(seq_item):
        query_block, key_block, value_block, seg_ids = seq_item
        allowed = allowed_of(seg_ids)[None]
        scores = (
            jnp.einsum("htd,sd->hts", query_block, key_block, preferred_element_type=jnp.float32)
            * scale
        )
        scores = jnp.where(allowed, scores, NEG_FILL)
        top = jnp.max(scores, -1, keepdims=True)
        weights = jnp.exp(scores - top)
        total = jnp.sum(weights, -1, keepdims=True)
        probs = (weights / total).astype(jnp.bfloat16)
        attended = jnp.einsum("hts,sd->htd", probs, value_block, preferred_element_type=jnp.float32)
        return (attended.astype(jnp.bfloat16), (top + jnp.log(total))[..., 0])

    attended, logsum = lax.map(attend, (queries, key_rows, value_rows, segments))
    attn_flat = attended.transpose(0, 2, 1, 3).reshape(rows, heads * HEAD_SIZE)
    attn_part = matmul(attn_flat, attnout_weight)
    gating = matmul(normed, gating_weight)
    inner = matmul(normed, inner_weight).reshape(seq_count, document_length, -1)
    state_in = matmul(normed, state_weight).reshape(seq_count, document_length, -1)
    step_raw = matmul(normed, step_weight)
    inner_pre = conv_forward(inner, conv_inner, inner_bias, segments)
    inner_act = jax.nn.silu(inner_pre)
    state_pre = conv_forward(state_in, conv_state, state_bias, segments)
    state_act = jax.nn.silu(state_pre)
    coef_b = state_act[..., :NS].astype(jnp.bfloat16)
    coef_c = state_act[..., NS:].astype(jnp.bfloat16)
    step_arg = step_raw.reshape(seq_count, document_length, ssm_heads) + step_bias.astype(
        jnp.float32
    )
    step = jax.nn.softplus(step_arg)
    rate = -jnp.exp(decay_log.astype(jnp.float32))
    heads_in = inner_act.reshape(seq_count, document_length, ssm_heads, P_SIZE).transpose(
        0, 2, 1, 3
    )

    def scan_forward(seq_item):
        step_block, coef_b_block, coef_c_block, heads_block, seg_ids = seq_item
        parts = ssd_parts(
            step_block, rate, coef_b_block, coef_c_block, heads_block, allowed_of(seg_ids)
        )
        return jnp.einsum("hts,hsp->htp", parts[2], parts[3], preferred_element_type=jnp.float32)

    core = lax.map(scan_forward, (step, coef_b, coef_c, heads_in, segments))
    skip = skip_scale.astype(jnp.float32)[None, :, None, None]
    ssm_out = (core + skip * heads_in).transpose(0, 2, 1, 3).reshape(rows, ssm_heads * P_SIZE)
    sigma_gate = jax.nn.sigmoid(gating)
    gate_act = gating * sigma_gate
    gated = ssm_out * gate_act
    square_sum = pair_sum(jnp.sum(gated * gated, -1))[:, None]
    inv_gate = lax.rsqrt(square_sum / DSSM + EPS)
    mixer_scale = mixer_gain.astype(jnp.float32)
    mixed = (gated * inv_gate * mixer_scale).astype(jnp.bfloat16)
    branch_part = attn_part + matmul(mixed, mixer_out)
    out_gain = post_gain.astype(jnp.float32)
    branch = pair_sum(branch_part.astype(jnp.bfloat16))
    middle = inputs + branch
    inv_second = lax.rsqrt(jnp.mean(middle * middle, -1, keepdims=True) + EPS)
    unit_second = middle * inv_second
    post = (unit_second * out_gain).astype(jnp.bfloat16)
    gate = matmul(post, gate_weight)
    upward = matmul(post, up_weight)
    sigma = jax.nn.sigmoid(gate)
    hidden = (gate * sigma * upward).astype(jnp.bfloat16)
    down_wgrad = jnp.einsum("tf,td->fd", hidden, cotangent, preferred_element_type=jnp.float32)
    hidden_grad = jnp.einsum(
        "td,fd->tf", cotangent, down_weight, preferred_element_type=jnp.float32
    )
    up_act_grad = (hidden_grad * gate * sigma).astype(jnp.bfloat16)
    gate_act_grad = (hidden_grad * upward * sigma * (1.0 + gate * (1.0 - sigma))).astype(
        jnp.bfloat16
    )
    gate_wgrad = jnp.einsum("tc,tf->cf", post, gate_act_grad, preferred_element_type=jnp.float32)
    up_wgrad = jnp.einsum("tc,tf->cf", post, up_act_grad, preferred_element_type=jnp.float32)
    post_part = jnp.einsum(
        "tf,cf->tc", gate_act_grad, gate_weight, preferred_element_type=jnp.float32
    ) + jnp.einsum("tf,cf->tc", up_act_grad, up_weight, preferred_element_type=jnp.float32)
    post_gain_part = jnp.sum(post_part * unit_second, 0)
    post_full = pair_sum(post_part.astype(jnp.bfloat16))
    down_wgrad, gate_wgrad, up_wgrad, post_full = lax.optimization_barrier(
        (
            down_wgrad.astype(jnp.bfloat16),
            gate_wgrad.astype(jnp.bfloat16),
            up_wgrad.astype(jnp.bfloat16),
            post_full,
        )
    )
    down_wgrad, gate_wgrad, up_wgrad = lax.psum((down_wgrad, gate_wgrad, up_wgrad), "dp")
    scaled_post = post_full * out_gain
    middle_grad = cotangent.astype(jnp.float32) + inv_second * (
        scaled_post - unit_second * jnp.mean(scaled_post * unit_second, -1, keepdims=True)
    )
    branch_grad = middle_grad.astype(jnp.bfloat16)
    attnout_wgrad = jnp.einsum(
        "tk,td->kd", attn_flat, branch_grad, preferred_element_type=jnp.float32
    )
    attended_grad = jnp.einsum(
        "td,kd->tk", branch_grad, attnout_weight, preferred_element_type=jnp.float32
    )
    attended_grad = (
        attended_grad.astype(jnp.bfloat16)
        .reshape(seq_count, document_length, heads, HEAD_SIZE)
        .transpose(0, 2, 1, 3)
    )

    def attend_back(seq_item):
        query_block, key_block, value_block, seg_ids, logsum_block, grad_block = seq_item
        allowed = allowed_of(seg_ids)[None]
        scores = (
            jnp.einsum("htd,sd->hts", query_block, key_block, preferred_element_type=jnp.float32)
            * scale
        )
        probs = jnp.where(allowed, jnp.exp(scores - logsum_block[..., None]), 0.0)
        value_grad = jnp.einsum(
            "hts,htd->hsd",
            probs.astype(jnp.bfloat16),
            grad_block,
            preferred_element_type=jnp.float32,
        )
        prob_grad = jnp.einsum(
            "htd,sd->hts", grad_block, value_block, preferred_element_type=jnp.float32
        )
        delta = jnp.sum(probs * prob_grad, -1, keepdims=True)
        score_grad = (probs * (prob_grad - delta)).astype(jnp.bfloat16)
        query_grad = (
            jnp.einsum("hts,sd->htd", score_grad, key_block, preferred_element_type=jnp.float32)
            * scale
        )
        key_grad = (
            jnp.einsum("hts,htd->hsd", score_grad, query_block, preferred_element_type=jnp.float32)
            * scale
        )
        return (query_grad, key_grad, value_grad)

    query_rot_grad, key_rot_grad, value_head_grad = lax.map(
        attend_back, (queries, key_rows, value_rows, segments, logsum, attended_grad)
    )
    query_pre_grad = (
        rotate_back(query_rot_grad, cosine, sine)
        .astype(jnp.bfloat16)
        .transpose(0, 2, 1, 3)
        .reshape(rows, heads * HEAD_SIZE)
    )
    key_pre_grad = rotate_back(key_rot_grad, cosine, sine).astype(jnp.bfloat16)
    value_pre_grad = value_head_grad.astype(jnp.bfloat16)
    normed_seq = normed.reshape(seq_count, document_length, -1)
    query_wgrad = jnp.einsum(
        "tc,tk->ck", normed, query_pre_grad, preferred_element_type=jnp.float32
    )
    key_wgrad = jnp.einsum(
        "slc,shld->cd", normed_seq, key_pre_grad, preferred_element_type=jnp.float32
    )
    value_weight_grad = jnp.einsum(
        "slc,shld->cd", normed_seq, value_pre_grad, preferred_element_type=jnp.float32
    )
    normed_part = (
        jnp.einsum("tk,ck->tc", query_pre_grad, query_weight, preferred_element_type=jnp.float32)
        + jnp.einsum(
            "shld,cd->slc", key_pre_grad, key_cols, preferred_element_type=jnp.float32
        ).reshape(rows, -1)
        + jnp.einsum(
            "shld,cd->slc", value_pre_grad, value_columns, preferred_element_type=jnp.float32
        ).reshape(rows, -1)
    )
    mixout_wgrad = jnp.einsum("tk,td->kd", mixed, branch_grad, preferred_element_type=jnp.float32)
    mixed_grad = jnp.einsum("td,kd->tk", branch_grad, mixer_out, preferred_element_type=jnp.float32)
    mixer_gain_wgrad = jnp.sum(mixed_grad * gated * inv_gate, 0)
    weighted = mixed_grad * mixer_scale
    cross = pair_sum(jnp.sum(weighted * gated, -1))[:, None]
    gated_grad = inv_gate * weighted - gated * (inv_gate * inv_gate * inv_gate) * cross / DSSM
    ssm_grad = gated_grad * gate_act
    gating_act_grad = (
        gated_grad * ssm_out * sigma_gate * (1.0 + gating * (1.0 - sigma_gate))
    ).astype(jnp.bfloat16)
    ssm_heads_grad = ssm_grad.reshape(seq_count, document_length, ssm_heads, P_SIZE).transpose(
        0, 2, 1, 3
    )
    core_grad = ssm_heads_grad.astype(jnp.bfloat16)
    skip_wgrad = jnp.sum(ssm_heads_grad * heads_in, axis=(0, 2, 3))

    def scan_back(seq_item):
        step_block, coef_b_block, coef_c_block, heads_block, seg_ids, core_block = seq_item
        coupling, decay, mixing, driven = ssd_parts(
            step_block, rate, coef_b_block, coef_c_block, heads_block, allowed_of(seg_ids)
        )
        mix_grad = jnp.einsum(
            "htp,hsp->hts", core_block, driven, preferred_element_type=jnp.float32
        )
        driven_grad = jnp.einsum(
            "hts,htp->hsp", mixing, core_block, preferred_element_type=jnp.float32
        )
        rounded = (mix_grad * decay).astype(jnp.bfloat16)
        coef_c_grad = jnp.einsum(
            "hts,sn->tn", rounded, coef_b_block, preferred_element_type=jnp.float32
        )
        coef_b_grad = jnp.einsum(
            "hts,tn->sn", rounded, coef_c_block, preferred_element_type=jnp.float32
        )
        spread = mix_grad * coupling[None] * decay
        cumulative_grad = jnp.sum(spread, 2) - jnp.sum(spread, 1)
        log_grad = jnp.flip(jnp.cumsum(jnp.flip(cumulative_grad, 1), 1), 1)
        heads_grad = driven_grad * step_block.T[:, :, None]
        step_grad = (jnp.sum(driven_grad * heads_block, -1) + log_grad * rate[:, None]).T
        rate_grad = jnp.sum(log_grad * step_block.T, 1)
        return (heads_grad, step_grad, rate_grad, coef_b_grad, coef_c_grad)

    heads_grad, step_grad, rate_grad, coef_b_grad, coef_c_grad = lax.map(
        scan_back, (step, coef_b, coef_c, heads_in, segments, core_grad)
    )
    heads_total = heads_grad + ssm_heads_grad * skip
    inner_act_grad = heads_total.transpose(0, 2, 1, 3).reshape(seq_count, document_length, -1)
    step_total = step_grad * jax.nn.sigmoid(step_arg)
    step_bias_wgrad = jnp.sum(step_total, axis=(0, 1))
    decay_wgrad = jnp.sum(rate_grad, 0) * rate
    step_raw_grad = step_total.reshape(rows, ssm_heads).astype(jnp.bfloat16)
    inner_pre_grad = inner_act_grad * silu_slope(inner_pre)
    inner_bias_wgrad = jnp.sum(inner_pre_grad, axis=(0, 1))
    inner_grad, conv_inner_wgrad = conv_backward(inner_pre_grad, inner, conv_inner, segments)
    inner_grad = inner_grad.reshape(rows, -1).astype(jnp.bfloat16)
    state_act_grad = jnp.concatenate([coef_b_grad, coef_c_grad], -1)
    state_pre_grad = state_act_grad * silu_slope(state_pre)
    state_bias_wgrad = jnp.sum(state_pre_grad, axis=(0, 1))
    state_grad, conv_state_wgrad = conv_backward(state_pre_grad, state_in, conv_state, segments)
    state_grad = state_grad.reshape(rows, -1).astype(jnp.bfloat16)
    gating_wgrad = jnp.einsum(
        "tc,tk->ck", normed, gating_act_grad, preferred_element_type=jnp.float32
    )
    inner_wgrad = jnp.einsum("tc,tk->ck", normed, inner_grad, preferred_element_type=jnp.float32)
    step_wgrad = jnp.einsum("tc,tk->ck", normed, step_raw_grad, preferred_element_type=jnp.float32)
    state_wgrad = jnp.einsum("tc,tk->ck", normed, state_grad, preferred_element_type=jnp.float32)
    normed_part = (
        normed_part
        + jnp.einsum(
            "tk,ck->tc", gating_act_grad, gating_weight, preferred_element_type=jnp.float32
        )
        + jnp.einsum("tk,ck->tc", inner_grad, inner_weight, preferred_element_type=jnp.float32)
        + jnp.einsum("tk,ck->tc", step_raw_grad, step_weight, preferred_element_type=jnp.float32)
        + jnp.einsum("tk,ck->tc", state_grad, state_weight, preferred_element_type=jnp.float32)
    )
    input_gain_part = jnp.sum(normed_part * unit_first, 0)
    normed_full = pair_sum(normed_part.astype(jnp.bfloat16))
    scaled_in = normed_full * in_gain
    tokens_grad = middle_grad + inv_first * (
        scaled_in - unit_first * jnp.mean(scaled_in * unit_first, -1, keepdims=True)
    )
    low = jnp.bfloat16
    if lax.axis_size("tensor") == 2 and KEYVALUE_HEADS == 2:
        keyval_part = jnp.concatenate([key_wgrad, value_weight_grad], 1)
    else:
        keyval_part = jnp.zeros(key_value_weight.shape, jnp.float32)
        keyval_part = lax.dynamic_update_slice_in_dim(
            keyval_part, key_wgrad, shared_key_head * HEAD_SIZE, 1
        )
        keyval_part = lax.dynamic_update_slice_in_dim(
            keyval_part, value_weight_grad, (KEYVALUE_HEADS + shared_key_head) * HEAD_SIZE, 1
        )
        keyval_part = lax.psum(keyval_part, "tensor")
    first_total = tree_sum(
        jnp.concatenate(
            [query_wgrad.astype(low), keyval_part.astype(low), gating_wgrad.astype(low)], 1
        )
    ).astype(jnp.float32)
    second_total = tree_sum(
        jnp.concatenate([attnout_wgrad.astype(low), mixout_wgrad.astype(low)], 0)
    ).astype(jnp.float32)
    width = query_wgrad.shape[1]
    kv_width = keyval_part.shape[1]
    query_wgrad = first_total[:, :width]
    keyval_part = first_total[:, width : width + kv_width]
    gating_wgrad = first_total[:, width + kv_width :]
    attnout_wgrad = second_total[: heads * HEAD_SIZE]
    mixout_wgrad = second_total[heads * HEAD_SIZE :]
    if lax.axis_size("tensor") == 2 and KEYVALUE_HEADS == 2:
        other = lax.ppermute(keyval_part.astype(low), "tensor", [(0, 1), (1, 0)])
        mine = keyval_part.astype(low)
        is_first = lax.axis_index("tensor") == 0
        head_0 = jnp.where(is_first, mine, other)
        head_1 = jnp.where(is_first, other, mine)
        key_value_weight_grad = jnp.concatenate(
            [
                head_0[:, :HEAD_SIZE],
                head_1[:, :HEAD_SIZE],
                head_0[:, HEAD_SIZE:],
                head_1[:, HEAD_SIZE:],
            ],
            1,
        ).astype(jnp.float32)
    else:
        key_value_weight_grad = keyval_part
    own = [
        step_bias_wgrad,
        decay_wgrad,
        skip_wgrad,
        mixer_gain_wgrad,
        inner_bias_wgrad,
        conv_inner_wgrad.reshape(-1),
    ]
    shared = [input_gain_part, post_gain_part, state_bias_wgrad, conv_state_wgrad.reshape(-1)]

    def columns_of(parts):
        flat = jnp.concatenate(parts)
        count = -(-flat.shape[0] // tokens.shape[1])
        flat = jnp.pad(flat, (0, count * tokens.shape[1] - flat.shape[0]))
        return flat.reshape(count, tokens.shape[1]).T

    def parts_of(columns, parts):
        flat = columns.T.reshape(-1)
        found, at = [], 0
        for part in parts:
            found.append(flat[at : at + part.shape[0]])
            at += part.shape[0]
        return found

    own_columns, shared_columns = columns_of(own), columns_of(shared)
    inner_width = inner_wgrad.shape[1]
    own_width = own_columns.shape[1]
    shared_from = -(-(inner_width + ssm_heads + own_width) // 128) * 128
    pad = shared_from - inner_width - ssm_heads - own_width
    third_total = tree_sum(
        jnp.concatenate(
            [
                inner_wgrad.astype(low),
                step_wgrad.astype(low),
                own_columns.astype(low),
                jnp.zeros((tokens.shape[1], pad), low),
                state_wgrad.astype(low),
                shared_columns.astype(low),
            ],
            1,
        ),
        shared_from,
    ).astype(jnp.float32)
    inner_wgrad = third_total[:, :inner_width]
    step_wgrad = third_total[:, inner_width : inner_width + ssm_heads]
    at = inner_width + ssm_heads
    (
        step_bias_wgrad,
        decay_wgrad,
        skip_wgrad,
        mixer_gain_wgrad,
        inner_bias_wgrad,
        conv_inner_flat,
    ) = parts_of(third_total[:, at : at + own_width], own)
    conv_inner_wgrad = conv_inner_flat.reshape(conv_inner.shape)
    state_width = state_wgrad.shape[1]
    state_wgrad = third_total[:, shared_from : shared_from + state_width]
    input_gain_part, post_gain_part, state_bias_wgrad, conv_state_flat = parts_of(
        third_total[:, shared_from + state_width :], shared
    )
    conv_state_wgrad = conv_state_flat.reshape(conv_state.shape)
    down_wgrad = down_wgrad.astype(jnp.float32)
    gate_wgrad = gate_wgrad.astype(jnp.float32)
    up_wgrad = up_wgrad.astype(jnp.float32)
    return (
        tokens_grad,
        input_gain_part,
        query_wgrad,
        key_value_weight_grad,
        attnout_wgrad,
        gating_wgrad,
        inner_wgrad,
        state_wgrad,
        step_wgrad,
        conv_inner_wgrad,
        conv_state_wgrad,
        inner_bias_wgrad,
        state_bias_wgrad,
        step_bias_wgrad,
        decay_wgrad,
        skip_wgrad,
        mixer_gain_wgrad,
        mixout_wgrad,
        post_gain_part,
        gate_wgrad,
        up_wgrad,
        down_wgrad,
    )


CHUNK = 256
LANES = 128
VMEM_BYTES = 56 * 1024 * 1024


def dot_nn(left, right):
    return lax.dot_general(left, right, (((1,), (0,)), ((), ())), preferred_element_type=jnp.float32)


def dot_nt(left, right):
    return lax.dot_general(left, right, (((1,), (1,)), ((), ())), preferred_element_type=jnp.float32)


def dot_tn(left, right):
    return lax.dot_general(left, right, (((0,), (0,)), ((), ())), preferred_element_type=jnp.float32)


def split_two(value):
    high = value.astype(jnp.bfloat16)
    return high, (value - high.astype(jnp.float32)).astype(jnp.bfloat16)


def exact_nn(ones, value):
    high, low = split_two(value)
    return dot_nn(ones, high) + dot_nn(ones, low)


def grid_of(shape):
    return (
        lax.broadcasted_iota(jnp.int32, shape, 0),
        lax.broadcasted_iota(jnp.int32, shape, 1),
    )


def pick(columns, pair):
    rows = columns.shape[0]
    left = jnp.broadcast_to(columns[:, 2 * pair : 2 * pair + 1], (rows, LANES))
    right = jnp.broadcast_to(columns[:, 2 * pair + 1 : 2 * pair + 2], (rows, LANES))
    return jnp.where(grid_of((rows, LANES))[1] < P_SIZE, left, right)


def scan_terms(step, rate, aux):
    row, col = grid_of((CHUNK, CHUNK))
    lower = (row >= col).astype(jnp.bfloat16)
    cumulative = exact_nn(lower, step * rate)
    last = cumulative[CHUNK - 1 : CHUNK]
    enter = jnp.exp(cumulative) * aux[:, 1:2]
    leave = jnp.exp(last - cumulative) * aux[:, 2:3]
    across = jnp.exp(last) * aux[CHUNK - 1 : CHUNK, 1:2]
    return cumulative, enter, leave, across


def scan_kernel(step_ref, coef_ref, act_ref, aux_ref, seg_ref, rate_ref, core_ref, kept_ref, state, moved):
    @pl.when(pl.program_id(0) == 0)
    def _():
        state[...] = jnp.zeros_like(state)

    step = step_ref[...]
    aux = aux_ref[...]
    cumulative, enter, leave, across = scan_terms(step, rate_ref[...], aux)
    cum_rows = cumulative.T
    row, col = grid_of((CHUNK, CHUNK))
    blocked = jnp.where((row >= col) & (aux[:, 0:1] == seg_ref[...]), 0.0, NEG_FILL)
    coef_b = coef_ref[:, :NS]
    coef_c = coef_ref[:, NS:]
    coupling = dot_nt(coef_c, coef_b)
    low_state = state[...].astype(jnp.bfloat16)
    kept_ref[0] = low_state
    carried = dot_nn(coef_c, low_state)
    first = grid_of((CHUNK, LANES))[1] < P_SIZE
    for pair in range(act_ref.shape[1] // LANES):
        at = slice(pair * LANES, (pair + 1) * LANES)
        driven = (act_ref[:, at] * pick(step, pair)).astype(jnp.bfloat16)
        parts = []
        for head in (2 * pair, 2 * pair + 1):
            decay = jnp.exp(cumulative[:, head : head + 1] - cum_rows[head : head + 1] + blocked)
            parts.append(dot_nn((coupling * decay).astype(jnp.bfloat16), driven))
        core_ref[:, at] = jnp.where(first, parts[0], parts[1]) + carried[:, at] * pick(enter, pair)
        moved[:, at] = (driven.astype(jnp.float32) * pick(leave, pair)).astype(jnp.bfloat16)
    fresh = dot_tn(coef_b, moved[...])
    for pair in range(act_ref.shape[1] // LANES):
        at = slice(pair * LANES, (pair + 1) * LANES)
        state[:, at] = state[:, at] * pick(across, pair) + fresh[:, at]


def scan_call(step, coef, act, aux, seg_row, rate):
    rows, width = act.shape
    chunks = rows // CHUNK
    by_chunk = lambda columns: pl.BlockSpec((CHUNK, columns), lambda i: (i, 0))
    return pl.pallas_call(
        scan_kernel,
        grid=(chunks,),
        in_specs=[
            by_chunk(LANES),
            by_chunk(2 * NS),
            by_chunk(width),
            by_chunk(LANES),
            pl.BlockSpec((1, CHUNK), lambda i: (0, i)),
            pl.BlockSpec((1, LANES), lambda i: (0, 0)),
        ],
        out_specs=[by_chunk(width), pl.BlockSpec((1, NS, width), lambda i: (i, 0, 0))],
        out_shape=[
            jax.ShapeDtypeStruct((rows, width), jnp.float32),
            jax.ShapeDtypeStruct((chunks, NS, width), jnp.bfloat16),
        ],
        scratch_shapes=[
            pltpu.VMEM((NS, width), jnp.float32),
            pltpu.VMEM((CHUNK, width), jnp.bfloat16),
        ],
        compiler_params=pltpu.CompilerParams(vmem_limit_bytes=VMEM_BYTES),
        name="scan_forward",
    )(step, coef, act, aux, seg_row, rate)


def scan_back_kernel(
    step_ref,
    coef_ref,
    act_ref,
    aux_ref,
    seg_ref,
    rate_ref,
    skip_ref,
    grad_ref,
    kept_ref,
    act_grad_ref,
    step_grad_ref,
    coef_grad_ref,
    sums_ref,
    skip_sum_ref,
    state_grad,
    moved,
    entered,
    row_sums,
):
    @pl.when(pl.program_id(0) == 0)
    def _():
        state_grad[...] = jnp.zeros_like(state_grad)
        sums_ref[...] = jnp.zeros_like(sums_ref)
        skip_sum_ref[...] = jnp.zeros_like(skip_sum_ref)
        row_sums[...] = jnp.zeros_like(row_sums)

    step = step_ref[...]
    aux = aux_ref[...]
    rate = rate_ref[...]
    cumulative, enter, leave, across = scan_terms(step, rate, aux)
    cum_rows = cumulative.T
    row, col = grid_of((CHUNK, CHUNK))
    blocked = jnp.where((row <= col) & (aux[:, 0:1] == seg_ref[...]), 0.0, NEG_FILL)
    coef_b = coef_ref[:, :NS]
    coef_c = coef_ref[:, NS:]
    coupling = dot_nt(coef_b, coef_c)
    low_state = kept_ref[0]
    carried = dot_nn(coef_c, low_state)
    low_grad = state_grad[...].astype(jnp.bfloat16)
    returned = dot_nn(coef_b, low_grad)
    product = jnp.sum(low_state.astype(jnp.float32) * low_grad.astype(jnp.float32), 0, keepdims=True)
    lane = grid_of((CHUNK, LANES))[1]
    lane_row = grid_of((1, LANES))[1]
    first = lane < P_SIZE
    later = jnp.zeros((CHUNK, LANES), jnp.float32)
    earlier = jnp.zeros((CHUNK, LANES), jnp.float32)
    direct = jnp.zeros((CHUNK, LANES), jnp.float32)
    through = jnp.zeros((1, LANES), jnp.float32)
    coupling_grad = jnp.zeros((CHUNK, CHUNK), jnp.float32)
    for pair in range(act_ref.shape[1] // LANES):
        at = slice(pair * LANES, (pair + 1) * LANES)
        act = act_ref[:, at]
        spread_step = pick(step, pair)
        driven = (act * spread_step).astype(jnp.bfloat16)
        grad = grad_ref[:, at]
        core_grad = grad.astype(jnp.bfloat16)
        core_wide = core_grad.astype(jnp.float32)
        enter_grad = core_wide * pick(enter, pair)
        entered[:, at] = enter_grad.astype(jnp.bfloat16)
        row_part = enter_grad * carried[:, at]
        leave_pair = pick(leave, pair)
        moved[:, at] = (driven.astype(jnp.float32) * leave_pair).astype(jnp.bfloat16)
        back = returned[:, at] * leave_pair
        col_part = back * driven.astype(jnp.float32)
        parts = []
        for head in (2 * pair, 2 * pair + 1):
            mine = first if head % 2 == 0 else ~first
            decay = jnp.exp(cum_rows[head : head + 1] - cumulative[:, head : head + 1] + blocked)
            mix_grad = dot_nt(jnp.where(mine, driven, jnp.zeros_like(driven)), core_grad)
            share = mix_grad * decay
            coupling_grad = coupling_grad + share
            spread = share * coupling
            row_sums[head : head + 1] = jnp.sum(spread, 0, keepdims=True)
            folded = sum(spread[:, k * LANES : (k + 1) * LANES] for k in range(CHUNK // LANES))
            found = jnp.sum(jnp.where(mine, row_part, 0.0) - folded, 1, keepdims=True)
            later = jnp.where(lane == head, found, later)
            parts.append(dot_nn((coupling * decay).astype(jnp.bfloat16), core_grad))
            found = jnp.sum(jnp.where(mine, col_part, 0.0), 1, keepdims=True)
            earlier = jnp.where(lane == head, found, earlier)
        driven_grad = jnp.where(first, parts[0], parts[1]) + back
        act_grad_ref[:, at] = driven_grad * spread_step + grad * skip_ref[:, at]
        skip_sum_ref[:, at] += jnp.sum(grad * act, 0, keepdims=True)
        step_part = driven_grad * act
        product_pair = product[:, at]
        for head in (2 * pair, 2 * pair + 1):
            mine = first if head % 2 == 0 else ~first
            found = jnp.sum(jnp.where(mine, step_part, 0.0), 1, keepdims=True)
            direct = jnp.where(lane == head, found, direct)
            found = jnp.sum(jnp.where(mine[:1], product_pair, 0.0), 1, keepdims=True)
            through = jnp.where(lane_row == head, found, through)
    upper = (row <= col).astype(jnp.bfloat16)
    below = (row > col).astype(jnp.bfloat16)
    high, low = split_two(row_sums[...])
    log_grad = (
        exact_nn(upper, later)
        + dot_nt(upper, high)
        + dot_nt(upper, low)
        + exact_nn(below, earlier)
        + through * across
    )
    step_grad_ref[...] = direct + log_grad * rate
    sums_ref[...] += jnp.sum(log_grad * step, 0, keepdims=True)
    low_coupling = coupling_grad.astype(jnp.bfloat16)
    coef_grad_ref[:, :NS] = dot_nn(low_coupling, coef_c) + dot_nt(moved[...], low_grad)
    coef_grad_ref[:, NS:] = dot_tn(low_coupling, coef_b) + dot_nt(entered[...], low_state)
    fresh = dot_tn(coef_c, entered[...])
    for pair in range(act_ref.shape[1] // LANES):
        at = slice(pair * LANES, (pair + 1) * LANES)
        state_grad[:, at] = state_grad[:, at] * pick(across, pair) + fresh[:, at]


def scan_back_call(step, coef, act, aux, seg_row, rate, skip_row, grad, kept):
    rows, width = act.shape
    chunks = rows // CHUNK
    by_chunk = lambda columns: pl.BlockSpec((CHUNK, columns), lambda i: (chunks - 1 - i, 0))
    one_row = lambda columns: pl.BlockSpec((1, columns), lambda i: (0, 0))
    return pl.pallas_call(
        scan_back_kernel,
        grid=(chunks,),
        in_specs=[
            by_chunk(LANES),
            by_chunk(2 * NS),
            by_chunk(width),
            by_chunk(LANES),
            pl.BlockSpec((1, CHUNK), lambda i: (0, chunks - 1 - i)),
            one_row(LANES),
            one_row(width),
            by_chunk(width),
            pl.BlockSpec((1, NS, width), lambda i: (chunks - 1 - i, 0, 0)),
        ],
        out_specs=[
            by_chunk(width),
            by_chunk(LANES),
            by_chunk(2 * NS),
            one_row(LANES),
            one_row(width),
        ],
        out_shape=[
            jax.ShapeDtypeStruct((rows, width), jnp.float32),
            jax.ShapeDtypeStruct((rows, LANES), jnp.float32),
            jax.ShapeDtypeStruct((rows, 2 * NS), jnp.float32),
            jax.ShapeDtypeStruct((1, LANES), jnp.float32),
            jax.ShapeDtypeStruct((1, width), jnp.float32),
        ],
        scratch_shapes=[
            pltpu.VMEM((NS, width), jnp.float32),
            pltpu.VMEM((CHUNK, width), jnp.bfloat16),
            pltpu.VMEM((CHUNK, width), jnp.bfloat16),
            pltpu.VMEM((LANES, CHUNK), jnp.float32),
        ],
        compiler_params=pltpu.CompilerParams(vmem_limit_bytes=VMEM_BYTES),
        name="scan_backward",
    )(step, coef, act, aux, seg_row, rate, skip_row, grad, kept)


def swap_halves(value):
    width = value.shape[1]
    half = HEAD_SIZE // 2
    up = pltpu.roll(value, width - half, 1)
    down = pltpu.roll(value, half, 1)
    return jnp.where(grid_of(value.shape)[1] % HEAD_SIZE < half, up, down)


def turned(value, cosine, sine):
    return value * cosine + swap_halves(value) * sine


def attend_kernel(query_ref, keyval_ref, seg_ref, seg_col_ref, cos_ref, sin_ref, out_ref, turned_ref, both_ref, log_ref):
    rows = query_ref.shape[0]
    first = grid_of((rows, LANES))[1] < HEAD_SIZE
    keyval = keyval_ref[...]
    moved = pltpu.roll(keyval, HEAD_SIZE, 1)
    keys = turned(jnp.where(first, keyval, moved), cos_ref[...], sin_ref[...]).astype(jnp.bfloat16)
    values = jnp.where(first, moved, keyval).astype(jnp.bfloat16)
    both_ref[:, :LANES] = keys
    both_ref[:, LANES:] = values
    scale = HEAD_SIZE ** (-0.5)
    head_lane = grid_of((CHUNK, LANES))[1]
    first = head_lane < HEAD_SIZE
    for block in range(rows // CHUNK):
        low, high = block * CHUNK, (block + 1) * CHUNK
        row, col = grid_of((CHUNK, high))
        blocked = jnp.where(
            (row + low >= col) & (seg_col_ref[low:high, 0:1] == seg_ref[:, :high]), 0.0, NEG_FILL
        )
        logs = jnp.zeros((CHUNK, LANES), jnp.float32)
        for pair in range(query_ref.shape[1] // LANES):
            at = slice(pair * LANES, (pair + 1) * LANES)
            query = turned(query_ref[low:high, at], cos_ref[low:high], sin_ref[low:high]).astype(
                jnp.bfloat16
            )
            turned_ref[low:high, at] = query
            parts = []
            for head in (2 * pair, 2 * pair + 1):
                mine = first if head % 2 == 0 else ~first
                scores = (
                    dot_nt(jnp.where(mine, query, jnp.zeros_like(query)), keys[:high]) * scale
                    + blocked
                )
                top = jnp.max(scores, 1, keepdims=True)
                weights = jnp.exp(scores - top)
                total = jnp.sum(weights, 1, keepdims=True)
                probs = (weights * (1.0 / total)).astype(jnp.bfloat16)
                parts.append(dot_nn(probs, values[:high]))
                logs = jnp.where(head_lane == head, top + jnp.log(total), logs)
            out_ref[low:high, at] = jnp.where(first, parts[0], parts[1]).astype(jnp.bfloat16)
        log_ref[low:high] = logs


def attend_call(query, keyval, seg_row, aux, cosine, sine):
    rows, width = query.shape
    return pl.pallas_call(
        attend_kernel,
        out_shape=[
            jax.ShapeDtypeStruct((rows, width), jnp.bfloat16),
            jax.ShapeDtypeStruct((rows, width), jnp.bfloat16),
            jax.ShapeDtypeStruct((rows, 2 * LANES), jnp.bfloat16),
            jax.ShapeDtypeStruct((rows, LANES), jnp.float32),
        ],
        compiler_params=pltpu.CompilerParams(vmem_limit_bytes=VMEM_BYTES),
        name="attend_forward",
    )(query, keyval, seg_row, aux, cosine, sine)


def attend_back_kernel(
    query_ref, both_ref, seg_ref, seg_col_ref, cos_ref, sin_ref, log_ref, out_ref, grad_ref,
    query_grad_ref, keyval_grad_ref, key_sum, value_sum,
):
    rows = query_ref.shape[0]
    key_sum[...] = jnp.zeros_like(key_sum)
    value_sum[...] = jnp.zeros_like(value_sum)
    scale = HEAD_SIZE ** (-0.5)
    first = grid_of((CHUNK, LANES))[1] < HEAD_SIZE
    for block in range(rows // CHUNK):
        low, high = block * CHUNK, (block + 1) * CHUNK
        row, col = grid_of((CHUNK, high))
        blocked = jnp.where(
            (row + low >= col) & (seg_col_ref[low:high, 0:1] == seg_ref[:, :high]), 0.0, NEG_FILL
        )
        keys = both_ref[:high, :LANES]
        values = both_ref[:high, LANES:]
        for pair in range(query_ref.shape[1] // LANES):
            at = slice(pair * LANES, (pair + 1) * LANES)
            query = query_ref[low:high, at]
            grad = grad_ref[low:high, at]
            inner = grad.astype(jnp.float32) * out_ref[low:high, at].astype(jnp.float32)
            parts = []
            key_part = None
            for head in (2 * pair, 2 * pair + 1):
                mine = first if head % 2 == 0 else ~first
                query_mine = jnp.where(mine, query, jnp.zeros_like(query))
                grad_mine = jnp.where(mine, grad, jnp.zeros_like(grad))
                scores = dot_nt(query_mine, keys) * scale + blocked
                probs = jnp.exp(scores - log_ref[low:high, head : head + 1])
                delta = jnp.sum(jnp.where(mine, inner, 0.0), 1, keepdims=True)
                prob_grad = dot_nt(grad_mine, values)
                score_grad = (probs * (prob_grad - delta)).astype(jnp.bfloat16)
                parts.append(dot_nn(score_grad, keys) * scale)
                key_sum[:high] += dot_tn(score_grad, query_mine)
                value_sum[:high] += dot_tn(probs.astype(jnp.bfloat16), grad_mine)
            full = jnp.where(first, parts[0], parts[1])
            query_grad_ref[low:high, at] = turned(full, cos_ref[low:high], -sin_ref[low:high]).astype(
                jnp.bfloat16
            )
    wide = grid_of((rows, LANES))[1] < HEAD_SIZE
    key_total = key_sum[...] * scale
    key_total = key_total + pltpu.roll(key_total, HEAD_SIZE, 1)
    key_total = turned(key_total, cos_ref[...], -sin_ref[...])
    value_total = value_sum[...]
    value_total = value_total + pltpu.roll(value_total, HEAD_SIZE, 1)
    keyval_grad_ref[...] = jnp.where(wide, key_total, value_total).astype(jnp.bfloat16)


def attend_back_call(query, both, seg_row, aux, cosine, sine, logs, out, grad):
    rows, width = query.shape
    return pl.pallas_call(
        attend_back_kernel,
        out_shape=[
            jax.ShapeDtypeStruct((rows, width), jnp.bfloat16),
            jax.ShapeDtypeStruct((rows, LANES), jnp.bfloat16),
        ],
        scratch_shapes=[
            pltpu.VMEM((rows, LANES), jnp.float32),
            pltpu.VMEM((rows, LANES), jnp.float32),
        ],
        compiler_params=pltpu.CompilerParams(vmem_limit_bytes=VMEM_BYTES),
        name="attend_backward",
    )(query, both, seg_row, aux, cosine, sine, logs, out, grad)


def halve(value, bit):
    half = value.shape[0] // 2
    upper = (lax.axis_index("dp") & bit) != 0
    got = swap_bit(jnp.where(upper, value[:half], value[half:]), bit)
    kept = jnp.where(upper, value[half:], value[:half])
    return (kept.astype(jnp.float32) + got.astype(jnp.float32)).astype(value.dtype)


def double(value, bit):
    upper = (lax.axis_index("dp") & bit) != 0
    got = swap_bit(value, bit)
    return jnp.concatenate([jnp.where(upper, got, value), jnp.where(upper, value, got)], 0)


def dp_bits():
    size = lax.axis_size("dp")
    return [1 << i for i in range(size.bit_length() - 1)]


def halve_parts(values, bit):
    half = values[0].shape[0] // 2
    upper = (lax.axis_index("dp") & bit) != 0
    got = swap_bit(
        jnp.concatenate([jnp.where(upper, v[:half], v[half:]) for v in values], 1), bit
    )
    kept = jnp.concatenate([jnp.where(upper, v[half:], v[:half]) for v in values], 1)
    return (kept.astype(jnp.float32) + got.astype(jnp.float32)).astype(got.dtype)


def by_rows(value):
    return with_layout_constraint(value, Layout(major_to_minor=(0, 1)))


def swap_pair(value):
    return lax.ppermute(value, "tensor", [(0, 1), (1, 0)])


def tie(*values):
    return lax.optimization_barrier(values)


def conv_rows(value, kernel, bias, keeps):
    taps = kernel.shape[0]
    total = bias.astype(jnp.float32)[None]
    for tap in range(taps):
        offset = taps - 1 - tap
        moved = jnp.pad(value, ((offset, 0), (0, 0)))[: value.shape[0]]
        total = total + kernel[tap].astype(jnp.float32) * moved * keeps[offset]
    return total


def conv_sums(grad, value, taps, keeps):
    sums = []
    for tap in range(taps):
        offset = taps - 1 - tap
        moved = jnp.pad(value, ((offset, 0), (0, 0)))[: value.shape[0]]
        sums.append(jnp.sum(grad * keeps[offset] * moved, 0, keepdims=True))
    return sums


def conv_grad(grad, kernel, keeps):
    taps = kernel.shape[0]
    total = jnp.zeros_like(grad)
    for tap in range(taps):
        offset = taps - 1 - tap
        moved = jnp.pad(grad * keeps[offset], ((0, offset), (0, 0)))[offset:]
        total = total + kernel[tap].astype(jnp.float32) * moved
    return total


def product_kernel(*refs):
    left_pairs, right_pairs = [refs[0:2], refs[2:4], refs[2:4]], [(), refs[4:6], refs[6:8]]
    cotangent_ref, out_ref = refs[8], refs[9]
    half = refs[0].shape[0]
    for which in range(3):
        total = None
        for k in range(2):
            left = left_pairs[which][k][...]
            if which == 0:
                right = cotangent_ref[k * half : (k + 1) * half]
            else:
                right = right_pairs[which][k][...]
            part = dot_tn(left, right)
            total = part if total is None else total + part
        out_ref[which] = total.astype(out_ref.dtype)


def product_call(hidden_a, hidden_b, post_a, post_b, gate_a, gate_b, up_a, up_b, cotangent):
    half, model = post_a.shape
    hidden = hidden_a.shape[1]
    columns = pl.BlockSpec((half, CHUNK), lambda i: (0, i))
    whole = pl.BlockSpec((half, hidden), lambda i: (0, 0))
    return pl.pallas_call(
        product_kernel,
        grid=(hidden // CHUNK,),
        in_specs=[columns] * 4 + [whole] * 4 + [pl.BlockSpec((2 * half, model), lambda i: (0, 0))],
        out_specs=pl.BlockSpec((3, CHUNK, model), lambda i: (0, i, 0)),
        out_shape=jax.ShapeDtypeStruct((3, hidden, model), jnp.bfloat16),
        compiler_params=pltpu.CompilerParams(vmem_limit_bytes=VMEM_BYTES),
        name="weight_products",
    )(hidden_a, hidden_b, post_a, post_b, gate_a, gate_b, up_a, up_b, cotangent)


def local_fast(
    tokens,
    segments,
    cotangent,
    input_gain,
    query_weight,
    key_value_weight,
    attnout_weight,
    gating_weight,
    inner_weight,
    state_weight,
    step_weight,
    conv_inner,
    conv_state,
    inner_bias,
    state_bias,
    step_bias,
    decay_log,
    skip_scale,
    mixer_gain,
    mixer_out,
    post_gain,
    gate_weight,
    up_weight,
    down_weight,
):
    low, wide = jnp.bfloat16, jnp.float32
    rows, model = tokens.shape
    heads = query_weight.shape[1] // HEAD_SIZE
    ssm_heads = step_weight.shape[1]
    ssm_width = ssm_heads * P_SIZE
    query_width = heads * HEAD_SIZE
    first_device = lax.axis_index("tensor") == 0
    pick_head = lambda at: jnp.where(
        first_device,
        key_value_weight[:, at : at + HEAD_SIZE],
        key_value_weight[:, at + HEAD_SIZE : at + 2 * HEAD_SIZE],
    )
    keyval_weight = jnp.concatenate([pick_head(0), pick_head(KEYVALUE_HEADS * HEAD_SIZE)], 1)
    lane_pad = ((0, 0), (0, LANES - ssm_heads))
    step_weight_wide = jnp.pad(step_weight, lane_pad)
    step_bias_wide = jnp.pad(step_bias.astype(wide)[None], lane_pad)
    rate = -jnp.exp(decay_log.astype(wide))
    rate_wide = jnp.pad(rate[None], lane_pad)
    skip_row = jnp.repeat(skip_scale.astype(wide), P_SIZE)[None]
    cosine, sine = rotary_tables(rows)
    cosine = jnp.concatenate([cosine] * 4, 1)
    sine = jnp.concatenate([-sine, sine, -sine, sine], 1)
    seg_row = segments.astype(wide)
    seg_chunks = seg_row.reshape(-1, CHUNK)
    ends = seg_chunks[:, -1:]
    starts = jnp.concatenate([jnp.full((1, 1), -1.0, wide), ends[:-1]], 0)
    aux = jnp.stack(
        [seg_chunks, (seg_chunks == starts).astype(wide), (seg_chunks == ends).astype(wide)], -1
    ).reshape(rows, 3)
    aux = jnp.pad(aux, ((0, 0), (0, LANES - 3)))
    keeps = [seg_keep(segments, offset)[0] for offset in range(conv_inner.shape[0])]

    inputs = by_rows(tokens.astype(wide))
    inv_first = lax.rsqrt(jnp.mean(inputs * inputs, -1, keepdims=True) + EPS)
    unit_first = inputs * inv_first
    in_gain = input_gain.astype(wide)
    normed = by_rows((unit_first * in_gain).astype(low))
    inner = matmul(normed, inner_weight)
    state_in = matmul(normed, state_weight)
    step_arg = matmul(normed, step_weight_wide) + step_bias_wide
    gating = matmul(normed, gating_weight)
    inner_pre = conv_rows(inner, conv_inner, inner_bias, keeps)
    inner_act = jax.nn.silu(inner_pre)
    state_pre = conv_rows(state_in, conv_state, state_bias, keeps)
    coef = jax.nn.silu(state_pre).astype(low)
    step = jax.nn.softplus(step_arg)
    core, kept = scan_call(step, coef, inner_act, aux, seg_row, rate_wide)
    ssm_out = core + skip_row * inner_act
    sigma_gate = jax.nn.sigmoid(gating)
    gate_act = gating * sigma_gate
    gated = ssm_out * gate_act
    square_sum = pair_sum(jnp.sum(gated * gated, -1))[:, None]
    query_pre = matmul(normed, query_weight)
    keyval_pre = matmul(normed, keyval_weight)
    attended, queries, both, logs = attend_call(query_pre, keyval_pre, seg_row, aux, cosine, sine)
    attn_part = matmul(attended, attnout_weight)
    inv_gate = lax.rsqrt(square_sum / DSSM + EPS)
    mixer_scale = mixer_gain.astype(wide)
    mixed = (gated * inv_gate * mixer_scale).astype(low)
    branch_part = attn_part + matmul(mixed, mixer_out)
    out_gain = post_gain.astype(wide)
    branch_part = by_rows(branch_part.astype(low))
    half = rows // 2
    spans = [slice(0, half), slice(half, rows)]
    sent = [branch_part[span] for span in spans]
    got = [swap_pair(piece) for piece in sent]
    weight_cat = jnp.concatenate(
        [gating_weight, inner_weight, step_weight_wide, state_weight, query_weight, keyval_weight], 1
    )
    got[0], weight_cat = tie(got[0], weight_cat)
    found = []
    for at, span in enumerate(spans):
        middle = inputs[span] + by_rows(sent[at].astype(wide) + got[at].astype(wide))
        inv_second = lax.rsqrt(jnp.mean(middle * middle, -1, keepdims=True) + EPS)
        unit_second = middle * inv_second
        post = by_rows((unit_second * out_gain).astype(low))
        gate = matmul(post, gate_weight)
        upward = matmul(post, up_weight)
        sigma = jax.nn.sigmoid(gate)
        hidden = (gate * sigma * upward).astype(low)
        hidden_grad = dot_nt(cotangent[span], down_weight)
        up_act_grad = (hidden_grad * gate * sigma).astype(low)
        gate_act_grad = (hidden_grad * upward * sigma * (1.0 + gate * (1.0 - sigma))).astype(low)
        post_part = dot_nt(gate_act_grad, gate_weight) + dot_nt(up_act_grad, up_weight)
        gain_part = jnp.sum(post_part * unit_second, 0, keepdims=True)
        post_low = by_rows(post_part.astype(low))
        if at == 0:
            got[1], post_low = tie(got[1], post_low)
        else:
            got[0], post_low = tie(got[0], post_low)
        post_got = swap_pair(post_low)
        found.append(
            (post_low, unit_second, inv_second, gain_part, hidden, post, gate_act_grad, up_act_grad)
        )
        got[at] = post_got
    post_gain_part = found[0][3] + found[1][3]
    forward_part = product_call(
        *[piece for k in range(4, 8) for piece in (found[0][k], found[1][k])], cotangent
    )
    got[1], _ = tie(got[1], forward_part)
    forward_piece = lax.psum_scatter(
        forward_part.reshape(-1, model), "dp", scatter_dimension=0, tiled=True
    )
    middle_grads = []
    for span, part, other in zip(spans, found, got):
        post_low, unit_second, inv_second = part[:3]
        post_full = by_rows(post_low.astype(wide) + other.astype(wide))
        scaled_post = post_full * out_gain
        middle_grads.append(
            cotangent[span].astype(wide)
            + inv_second
            * (scaled_post - unit_second * jnp.mean(scaled_post * unit_second, -1, keepdims=True))
        )
    branch_grad = by_rows(jnp.concatenate([grad.astype(low) for grad in middle_grads], 0))
    middle_grad = jnp.concatenate(middle_grads, 0)
    mixed_grad = dot_nt(branch_grad, mixer_out)
    mixer_gain_part = jnp.sum(mixed_grad * gated * inv_gate, 0, keepdims=True)
    weighted = mixed_grad * mixer_scale
    cross = pair_sum(jnp.sum(weighted * gated, -1))[:, None]
    out_part = dot_tn(jnp.concatenate([attended, mixed], 1), branch_grad).astype(low)
    out_part = by_rows(out_part)
    attended_grad = dot_nt(branch_grad, attnout_weight).astype(low)
    gated_grad = inv_gate * weighted - gated * (inv_gate * inv_gate * inv_gate) * cross / DSSM
    ssm_grad = gated_grad * gate_act
    gating_grad = (
        gated_grad * ssm_out * sigma_gate * (1.0 + gating * (1.0 - sigma_gate))
    ).astype(low)
    gating_part = by_rows(dot_tn(normed, gating_grad).astype(low))
    bits = dp_bits()
    early = halve_parts([out_part, gating_part], bits[0])
    early, ssm_grad = tie(early, ssm_grad)
    early = halve(early, bits[1])
    act_grad, step_grad, coef_grad, rate_sum, skip_sum = scan_back_call(
        step, coef, inner_act, aux, seg_row, rate_wide, skip_row, ssm_grad, kept
    )
    early, act_grad, step_grad, coef_grad, forward_piece = tie(
        early, act_grad, step_grad, coef_grad, forward_piece
    )
    forward_total = lax.all_gather(forward_piece, "dp", axis=0, tiled=True)
    early = halve(early, bits[2])
    step_total = step_grad * jax.nn.sigmoid(step_arg)
    taps = conv_inner.shape[0]
    inner_pre_grad = act_grad * silu_slope(inner_pre)
    conv_inner_sums = conv_sums(inner_pre_grad, inner, taps, keeps)
    inner_bias_part = jnp.sum(inner_pre_grad, 0, keepdims=True)
    state_pre_grad = coef_grad * silu_slope(state_pre)
    conv_state_sums = conv_sums(state_pre_grad, state_in, taps, keeps)
    state_bias_part = jnp.sum(state_pre_grad, 0, keepdims=True)
    early, act_grad, coef_grad, *sums = tie(
        early, act_grad, coef_grad, inner_bias_part, state_bias_part, *conv_inner_sums, *conv_state_sums
    )
    inner_bias_part, state_bias_part = sums[:2]
    conv_inner_sums, conv_state_sums = sums[2 : 2 + taps], sums[2 + taps :]
    early = halve(early, bits[3])
    inner_grad = conv_grad(act_grad * silu_slope(inner_pre), conv_inner, keeps)
    state_grad = conv_grad(coef_grad * silu_slope(state_pre), conv_state, keeps)
    scan_cat = jnp.concatenate(
        [inner_grad.astype(low), step_total.astype(low), state_grad.astype(low)], 1
    )
    scan_part = dot_tn(normed, scan_cat).astype(low)
    early, scan_part, attended_grad = tie(early, scan_part, attended_grad)
    early = double(early, bits[3])
    scan_part = halve(scan_part, bits[0])
    query_grad, keyval_grad = attend_back_call(
        queries, both, seg_row, aux, cosine, sine, logs, attended, attended_grad
    )
    attend_cat = jnp.concatenate([query_grad, keyval_grad], 1)
    attend_part = dot_tn(normed, attend_cat).astype(low)
    early, scan_part, attend_part, attend_cat = tie(early, scan_part, attend_part, attend_cat)
    early = double(early, bits[2])
    scan_part = halve(scan_part, bits[1])
    attend_part = halve(attend_part, bits[0])
    normed_part = dot_nt(jnp.concatenate([gating_grad, scan_cat, attend_cat], 1), weight_cat)
    input_gain_part = jnp.sum(normed_part * unit_first, 0, keepdims=True)
    early, scan_part, attend_part, normed_part, input_gain_part = tie(
        early, scan_part, attend_part, normed_part, input_gain_part
    )
    normed_low = by_rows(normed_part.astype(low))
    quarter = rows // 4
    normed_first = swap_pair(normed_low[:quarter])
    own_rows = [
        *conv_inner_sums,
        inner_bias_part,
        mixer_gain_part,
        skip_sum,
        jnp.sum(step_total, 0, keepdims=True),
        rate_sum * rate_wide,
    ]
    shared_rows = [
        input_gain_part,
        post_gain_part,
        *conv_state_sums,
        state_bias_part,
    ]
    small = jnp.concatenate(
        [jnp.pad(row, ((0, 0), (0, model - row.shape[1]))) for row in own_rows + shared_rows], 0
    )
    small = small + swap_bit(small, bits[0])
    early = double(early, bits[1])
    scan_part = halve(scan_part, bits[2])
    attend_part = halve(attend_part, bits[1])
    scan_part, attend_part, small, normed_first, normed_low = tie(
        scan_part, attend_part, small, normed_first, normed_low
    )
    normed_second = swap_pair(normed_low[quarter:half])
    scan_part = halve(scan_part, bits[3])
    attend_part = halve(attend_part, bits[2])
    small = small + swap_bit(small, bits[1])
    scan_part, attend_part, small, normed_second = tie(
        scan_part, attend_part, small, normed_second
    )
    attend_part = halve(attend_part, bits[3])
    small = small + swap_bit(small, bits[2])
    attend_part, small, early = tie(attend_part, small, early)
    small = small + swap_bit(small, bits[3])
    scan_piece, attend_piece = scan_part, attend_part
    state_at = ssm_width + LANES
    trade = jnp.concatenate([scan_piece[:, state_at:], attend_piece[:, query_width:]], 1)
    other = swap_pair(trade)
    other, normed_rest = tie(other, normed_low[half:])
    normed_got = [normed_first, normed_second, swap_pair(normed_rest)]
    state_cols = state_weight.shape[1]
    state_piece = (
        trade[:, :state_cols].astype(wide) + other[:, :state_cols].astype(wide)
    ).astype(low)
    mine, theirs = trade[:, state_cols:], other[:, state_cols:]
    head_0 = jnp.where(first_device, mine, theirs)
    head_1 = jnp.where(first_device, theirs, mine)
    late = jnp.concatenate(
        [
            scan_piece[:, :state_at],
            state_piece,
            attend_piece[:, :query_width],
            head_0[:, :HEAD_SIZE],
            head_1[:, :HEAD_SIZE],
            head_0[:, HEAD_SIZE:],
            head_1[:, HEAD_SIZE:],
        ],
        1,
    )
    late, small, early = tie(late, small, early)
    early = double(early, bits[0])
    late = double(late, bits[3])
    small_other = lax.ppermute(small, "tensor", [(0, 1), (1, 0)])
    is_shared = lax.broadcasted_iota(jnp.int32, small.shape, 0) >= len(own_rows)
    small = small + jnp.where(is_shared, small_other, 0.0)
    late, early = tie(late, early)
    late = double(late, bits[2])
    late, forward_total, normed_got[2] = tie(late, forward_total, normed_got[2])
    hidden_units = down_weight.shape[0]
    down_wgrad = forward_total[:hidden_units].astype(wide)
    gate_wgrad = forward_total[hidden_units : hidden_units + model].astype(wide)
    up_wgrad = forward_total[hidden_units + model :].astype(wide)
    late = double(late, bits[1])
    early_grads = (
        gate_wgrad,
        up_wgrad,
        down_wgrad,
        early[:query_width, :model].astype(wide),
        early[:, model:].astype(wide),
        early[query_width:, :model].astype(wide),
    )
    normed_full = by_rows(normed_low.astype(wide) + jnp.concatenate(normed_got, 0).astype(wide))
    scaled_in = normed_full * in_gain
    tokens_grad = middle_grad + inv_first * (
        scaled_in - unit_first * jnp.mean(scaled_in * unit_first, -1, keepdims=True)
    )
    late, tokens_grad, *early_grads = tie(late, tokens_grad, *early_grads)
    late = double(late, bits[0])
    scan_total = late[:, : state_at + state_cols]
    attend_total = late[:, state_at + state_cols :]
    gate_wgrad, up_wgrad, down_wgrad, attnout_grad, gating_wgrad, mixout_grad = early_grads
    count = len(own_rows)
    return (
        tokens_grad,
        small[count],
        attend_total[:, :query_width].astype(wide),
        attend_total[:, query_width:].astype(wide),
        attnout_grad,
        gating_wgrad,
        scan_total[:, :ssm_width].astype(wide),
        scan_total[:, state_at:].astype(wide),
        scan_total[:, ssm_width : ssm_width + ssm_heads].astype(wide),
        small[:taps, :ssm_width],
        small[count + 2 : count + 2 + taps, :state_cols],
        small[taps, :ssm_width],
        small[count + 2 + taps, :state_cols],
        small[taps + 3, :ssm_heads],
        small[taps + 4, :ssm_heads],
        jnp.sum(small[taps + 2, :ssm_width].reshape(ssm_heads, P_SIZE), 1),
        small[taps + 1, :ssm_width],
        mixout_grad,
        small[count + 1],
        gate_wgrad,
        up_wgrad,
        down_wgrad,
    )


def layer(*arrays):
    tokens, segments, query_weight, step_weight = arrays[0], arrays[1], arrays[4], arrays[10]
    size = lax.axis_size("dp")
    fits = (
        lax.axis_size("tensor") == 2
        and size == 16
        and segments.shape[0] == 1
        and tokens.shape[0] % CHUNK == 0
        and tokens.shape[1] % (16 * size) == 0
        and query_weight.shape[1] == QUERY_HEADS // KEYVALUE_HEADS * HEAD_SIZE
        and KEYVALUE_HEADS == 2
        and arrays[23].shape[0] == tokens.shape[1]
        and step_weight.shape[1] % 2 == 0
        and query_weight.shape[1] + step_weight.shape[1] * P_SIZE == tokens.shape[1]
    )
    return local_fast(*arrays) if fits else local(*arrays)


def solution(mesh):
    placed = (
        P("dp", None),
        P("dp", None),
        P("dp", None),
        P(),
        P(None, "tensor"),
        P(),
        P("tensor", None),
        P(None, "tensor"),
        P(None, "tensor"),
        P(),
        P(None, "tensor"),
        P(None, "tensor"),
        P(),
        P("tensor"),
        P(),
        P("tensor"),
        P("tensor"),
        P("tensor"),
        P("tensor"),
        P("tensor", None),
        P(),
        P(None, "tensor"),
        P(None, "tensor"),
        P("tensor", None),
    )
    return jax.shard_map(
        layer,
        mesh=mesh,
        in_specs=placed,
        out_specs=(
            P("dp", None),
            P(),
            P(None, "tensor"),
            P(),
            P("tensor", None),
            P(None, "tensor"),
            P(None, "tensor"),
            P(),
            P(None, "tensor"),
            P(None, "tensor"),
            P(),
            P("tensor"),
            P(),
            P("tensor"),
            P("tensor"),
            P("tensor"),
            P("tensor"),
            P("tensor", None),
            P(),
            P(None, "tensor"),
            P(None, "tensor"),
            P("tensor", None),
        ),
        check_vma=False,
    )
```
